32 devices in a mesh: rep: 4 (over x, core), fsdp: 8 (over z, y).
Axes of the slice: x: 2, y: 2, z: 4, core: 2. Of those that a mesh axis runs over, the one named last changes fastest.
Arguments:
- layer_input: bfloat16 [16384, 1536], P(('rep', 'fsdp')), may hold values from -6 to 6
- first_gain: float32 [1536], replicated, may hold values from 0.25 to 1.75
- qkv_weight: bfloat16 [1536, 4608], P('fsdp'), may hold values from -0.15625 to 0.15625
- conv_kernel: float32 [16, 6, 11], replicated, may hold values from -0.6 to 1.6
- head_mixing: float32 [8, 2, 2], replicated, may hold values from 0.25 to 1
- group_gain: float32 [1536], replicated, may hold values from 0.25 to 1.75
- out_weight: bfloat16 [1536, 1536], P('fsdp'), may hold values from -0.15625 to 0.15625
- second_gain: float32 [1536], replicated, may hold values from 0.25 to 1.75
- inner_weight: bfloat16 [1536, 8192], P('fsdp'), may hold values from -0.15625 to 0.15625
- down_weight: bfloat16 [4096, 1536], P('fsdp'), may hold values from -0.09375 to 0.09375
- doc_lengths: int32 [32, 4], P(('rep', 'fsdp')), may hold values from 1 to 256, 512 in all within a row
- cotangent: bfloat16 [16384, 1536], P(('rep', 'fsdp')), may hold values from -6 to 6
Outputs:
- layer_output: bfloat16 [16384, 1536], P(('rep', 'fsdp'))
- grad_input: float32 [16384, 1536], P(('rep', 'fsdp'))
- grad_first: float32 [1536], replicated
- grad_qkv: float32 [1536, 4608], P('fsdp')
- grad_kernel: float32 [16, 6, 11], replicated
- grad_mixing: float32 [8, 2, 2], replicated
- grad_group: float32 [1536], replicated
- grad_proj: float32 [1536, 1536], P('fsdp')
- grad_second: float32 [1536], replicated
- grad_inner: float32 [1536, 8192], P('fsdp')
- grad_down: float32 [4096, 1536], P('fsdp')
The draws below stay inside these ranges and needn't reach their ends.
Inputs may be any that keep to these rules, and one draw needn't show every extreme that they name: `doc_lengths`: each sequence's lengths sum to 512, and its largest is 256.
All inputs are finite; a program needn't handle non-finite values.
Results may differ from the reference program's by a relative error of at most 0.02.
Values may be sent and summed in bfloat16 or wider, within the bound.
A program may use at most 320 MiB of HBM per device.

```python
import math
import jax
import jax.numpy as jnp
import numpy as np
from jax import lax

D = 1536
HEADS = 16
HEAD_DIM = 96
FF = 4096
CQ = 6
CK = 11
SEQ = 512
DOCS = 4
SEQS = 32
TOKENS = 16384


def draw_conv_kernel(key, part):
    key = jax.random.fold_in(key, 11)
    jitter = 0.15 * jax.random.truncated_normal(key, -4.0, 4.0, (HEADS, CQ, CK), jnp.float32)
    first_row = lax.broadcasted_iota(jnp.int32, (HEADS, CQ, CK), 1) == 0
    centre = lax.broadcasted_iota(jnp.int32, (HEADS, CQ, CK), 2) == CK // 2
    return jitter + jnp.where(first_row & centre, 1.0, 0.0)


def block_levels(stream_key, extent, cuts, low, top_value):
    def one(dim, shards_of):
        draws = jax.random.uniform(jax.random.fold_in(jax.random.fold_in(stream_key, 6), dim), (shards_of,), jnp.float32, low / len(cuts), top_value / len(cuts))
        return jnp.repeat(jnp.exp(draws), extent[dim] // shards_of).reshape((-1,) + (1,) * (len(extent) - dim - 1))

    loudness = one(*cuts[0])
    for cut in cuts[1:]:
        loudness = loudness * one(*cut)
    return loudness


def length_profile(count, total, bound, slope):
    weights = [(1 << 20) // math.isqrt(grade ** slope) + 1 for grade in range(2, count + 1)]
    surplus, given = total - bound - (count - 1), [1] * (count - 1)
    while surplus > 0:
        free = [i for i in range(count - 1) if given[i] < bound]
        pool, budget = sum([weights[i] for i in free]), surplus
        for i in free:
            more = min(bound - given[i], max(1, budget * weights[i] // pool), surplus)
            given[i] = given[i] + more
            surplus = surplus - more
    return np.array([bound] + given)


def uneven_parts(key, number_of, total, reach, lean):
    if number_of == 2:
        one = jax.random.randint(key, (), max(1, total - reach), min(reach, total - 1) + 1)
        return jnp.stack([one, total - one])
    tallies = jnp.asarray(length_profile(number_of, total, reach, lean), jnp.int32)
    couples = (number_of - 1) // 2
    giver, receiver = tallies[1:1 + 2 * couples:2], tallies[2:2 + 2 * couples:2]
    margin = jnp.minimum(giver - 1, reach - receiver)
    moved = jax.random.randint(jax.random.fold_in(key, 1), (couples,), 0, 1 << 20) % (margin + 1)
    tallies = tallies.at[1:1 + 2 * couples:2].set(giver - moved).at[2:2 + 2 * couples:2].set(receiver + moved)
    return tallies[jax.random.permutation(jax.random.fold_in(key, 2), number_of)]


def bell_draw(rng, extent, scale, most, shards=(), kind=jnp.bfloat16):
    gain = block_levels(rng, extent, shards, -0.22, 0.18) if shards else 1.0
    values = jax.random.normal(rng, extent, jnp.float32) * scale * gain
    return jnp.minimum(jnp.maximum(values, -most), most).astype(kind)


def setup_inputs(seed: int = 0) -> dict:
    seeds = jax.random.split(jax.random.key(seed), 13)
    return {
        "layer_input": bell_draw(seeds[0], (TOKENS, D), 1.0, 6.0, ((0, 32),)),
        "first_gain": jnp.clip(1.0 + 0.15 * jax.random.normal(seeds[1], (D,), jnp.float32), 0.25, 1.75),
        "qkv_weight": bell_draw(seeds[2], (D, 3 * D), D ** -0.5, 0.15625, ((0, 8),)),
        "conv_kernel": draw_conv_kernel(jax.random.fold_in(seeds[12], 71), 0),
        "head_mixing": jnp.clip(jax.random.uniform(seeds[4], (HEADS // 2, 2, 2), jnp.float32, 0.25, 1.0), 0.25, 1.0),
        "group_gain": jnp.clip(1.0 + 0.15 * jax.random.normal(seeds[5], (D,), jnp.float32), 0.25, 1.75),
        "out_weight": bell_draw(seeds[6], (D, D), D ** -0.5, 0.15625, ((0, 8),)),
        "second_gain": jnp.clip(1.0 + 0.15 * jax.random.normal(seeds[7], (D,), jnp.float32), 0.25, 1.75),
        "inner_weight": bell_draw(seeds[8], (D, 2 * FF), D ** -0.5, 0.15625, ((0, 8),)),
        "down_weight": bell_draw(seeds[9], (FF, D), FF ** -0.5, 0.09375, ((0, 8),)),
        "doc_lengths": jax.vmap(lambda own: uneven_parts(own, DOCS, SEQ, SEQ // 2, 2))(jax.random.split(seeds[10], SEQS)).reshape((SEQS, DOCS)).astype(jnp.int32),
        "cotangent": bell_draw(seeds[11], (TOKENS, D), 1.0, 6.0, ((0, 32),)),
    }


PRECISE = lax.Precision.HIGHEST
EPSILON = 1e-05

@jax.custom_vjp
def low(v):
    return lax.optimization_barrier(v.astype(jnp.bfloat16)).astype(jnp.float32)

@jax.custom_vjp
def low_back(v):
    return v

def low_keep(v):
    return (low(v), None)

def low_pass(kept, grad):
    return (grad,)

def back_keep(v):
    return (v, None)

def back_low(kept, grad):
    return (low(grad),)
low.defvjp(low_keep, low_pass)
low_back.defvjp(back_keep, back_low)

def rms_norm(values, gains):
    return values * lax.rsqrt(lax.optimization_barrier(jnp.mean(values * values, axis=-1, keepdims=True)) + EPSILON) * gains

def group_norm(values, gains):
    count_rows = values.shape[0]
    per_head = values.reshape(count_rows, HEADS, values.shape[1] // HEADS)
    centred = per_head - lax.optimization_barrier(jnp.mean(per_head, axis=-1, keepdims=True))
    spread = lax.optimization_barrier(jnp.mean(centred * centred, axis=-1, keepdims=True))
    return (centred * lax.rsqrt(spread + EPSILON)).reshape(count_rows, values.shape[1]) * gains

def swiglu(gate_up):
    middle_col = gate_up.shape[1] // 2
    return jax.nn.silu(gate_up[:, :middle_col]) * gate_up[:, middle_col:]

def shift_rows(values, amount):
    if amount == 0:
        return values
    filler = jnp.zeros(values.shape[:-2] + (amount, values.shape[-1]), values.dtype)
    return jnp.concatenate([filler, values[..., :-amount, :]], axis=-2)

def shift_cols(values, amount):
    if amount == 0:
        return values
    if amount > 0:
        filler = jnp.zeros(values.shape[:-1] + (amount,), values.dtype)
        return jnp.concatenate([filler, values[..., :-amount]], axis=-1)
    filler = jnp.zeros(values.shape[:-1] + (-amount,), values.dtype)
    return jnp.concatenate([values[..., -amount:], filler], axis=-1)

def mask_tables(length_row, seq_len, lags):
    ends = jnp.cumsum(length_row)[:-1]
    places = jnp.arange(seq_len, dtype=jnp.int32)
    segment = lax.optimization_barrier(jnp.sum((places[:, None] >= ends[None, :]).astype(jnp.int32), axis=1))
    allowed = (places[None, :] <= places[:, None]) & (segment[:, None] == segment[None, :])
    padded = jnp.concatenate([jnp.full((lags,), -1, jnp.int32), segment])
    row_keep = jnp.stack([padded[lags - row_shift:lags - row_shift + seq_len] == segment for row_shift in range(lags)])
    return (allowed, row_keep.astype(jnp.float32))

def score_mix(scores, kernel, mixing, allowed, row_keep):
    masked = jnp.where(allowed, scores, 0.0)
    centre = kernel.shape[2] // 2
    shifted = [shift_rows(masked, row_shift) * row_keep[row_shift][:, None] for row_shift in range(kernel.shape[1])]
    summed = jnp.zeros_like(scores)
    for column in range(kernel.shape[2]):
        partial_sum = shifted[0] * kernel[:, 0, column][:, None, None]
        for row_shift in range(1, kernel.shape[1]):
            partial_sum = partial_sum + shifted[row_shift] * kernel[:, row_shift, column][:, None, None]
        summed = summed + shift_cols(partial_sum, column - centre)
    logits = jnp.where(allowed, summed, -1e+30)
    largest = lax.optimization_barrier(jnp.max(logits, axis=-1, keepdims=True))
    weights = jnp.exp(logits - largest)
    probability = weights / lax.optimization_barrier(jnp.sum(weights, axis=-1, keepdims=True))
    return lax.optimization_barrier(jnp.sum(mixing[:, :, None, None] * probability[None], axis=1))

def by_groups(matrix):
    seq_len = matrix.shape[0]
    return matrix.reshape(seq_len, HEADS // 2, 2, HEAD_DIM).transpose(1, 2, 0, 3)

def attend(query, keys, values, conv_kernel, head_mixing, allowed, row_keep):
    score_scale = 1.0 / math.sqrt(HEAD_DIM)

    def one_group(operands):
        q_group, k_group, v_group, k_conv, m_group = operands
        scores = jnp.einsum('hid,hjd->hij', q_group, k_group, precision=PRECISE) * score_scale
        scores = low_back(scores)
        probability = low(score_mix(scores, k_conv, m_group, allowed, row_keep))
        return jnp.einsum('hij,hjd->hid', probability, v_group, precision=PRECISE)
    blocks = lax.map(jax.checkpoint(one_group), (by_groups(query), by_groups(keys), by_groups(values), conv_kernel.reshape(HEADS // 2, 2, CQ, CK), head_mixing))
    return blocks.transpose(2, 0, 1, 3).reshape(blocks.shape[2], HEADS * HEAD_DIM)

def layer(inputs, first_gain, qkv_weight, conv_kernel, head_mixing, group_gain, out_weight, second_gain, inner_weight, down_weight, allowed, row_keep):
    width = inputs.shape[1]
    normed = low(rms_norm(inputs, first_gain))
    projected = low_back(low(jnp.dot(normed, qkv_weight, precision=PRECISE)))
    attended = attend(projected[:, :width], projected[:, width:2 * width], projected[:, 2 * width:], conv_kernel, head_mixing, allowed, row_keep)
    attended = low_back(attended)
    grouped = low(group_norm(attended, group_gain))
    branch = low_back(jnp.dot(grouped, out_weight, precision=PRECISE))
    middle = inputs + branch
    second = low(rms_norm(middle, second_gain))
    gate_up = low_back(jnp.dot(second, inner_weight, precision=PRECISE))
    hidden = low(swiglu(gate_up))
    return middle + jnp.dot(hidden, down_weight, precision=PRECISE)

def reference(layer_input, first_gain, qkv_weight, conv_kernel, head_mixing, group_gain, out_weight, second_gain, inner_weight, down_weight, doc_lengths, cotangent):
    params = tuple((weight_arg.astype(jnp.float32) for weight_arg in (first_gain, qkv_weight, conv_kernel, head_mixing, group_gain, out_weight, second_gain, inner_weight, down_weight)))
    sequences = layer_input.astype(jnp.float32).reshape(SEQS, SEQ, D)
    returned = cotangent.astype(jnp.float32).reshape(SEQS, SEQ, D)

    def per_sequence(carry, operands):
        inputs, length_row, upstream = operands
        allowed, row_keep = mask_tables(length_row, SEQ, CQ)

        def forward(inputs_arg, *weights):
            return layer(inputs_arg, *weights, allowed, row_keep)
        result, pull = jax.vjp(forward, inputs, *params)
        grads = pull(upstream)
        carry = tuple((summed + fresh for summed, fresh in zip(carry, grads[1:])))
        return (carry, (result.astype(jnp.bfloat16), grads[0]))
    initial = tuple((jnp.zeros_like(weight_arg) for weight_arg in params))
    totals, (outputs, input_grads) = lax.scan(per_sequence, initial, (sequences, doc_lengths, returned))
    return (outputs.reshape(TOKENS, D), input_grads.reshape(TOKENS, D), totals[0], totals[1], totals[2], totals[3], totals[4], totals[5], totals[6], totals[7], totals[8])
```

```python
import functools, math
import jax, jax.numpy as jnp
from jax import lax
from jax.experimental import pallas as pl
from jax.experimental.pallas import tpu as pltpu
from jax.sharding import PartitionSpec as P

HEADS = 16
HEAD_DIM = 96
CQ = 6
CK = 11
EPSILON = 1e-05
LANE = 128
QUAD = 4
SCALE = 1.0 / math.sqrt(HEAD_DIM)
F32 = jnp.float32
BF16 = jnp.bfloat16


def row_sets(seq):
    return [
        (r, min(r + LANE, 3 * LANE), max(0, r - 2 * LANE)) for r in range(0, seq, LANE)
    ]


def nt(a, b):
    return lax.dot_general(a, b, (((1,), (1,)), ((), ())), preferred_element_type=F32)


def nn(a, b):
    return jnp.dot(a, b, preferred_element_type=F32)


def fill_masks(docs_ref, masks, seq):
    ends = []
    total = jnp.int32(0)
    for d in range(docs_ref.shape[1] - 1):
        total = total + docs_ref[0, d]
        ends.append(total)
    for r0, width, c0 in row_sets(seq):
        rows = r0 + lax.broadcasted_iota(jnp.int32, (LANE, 1), 0)
        cols = c0 + lax.broadcasted_iota(jnp.int32, (1, width), 1)
        row_doc = sum((rows >= e).astype(jnp.int32) for e in ends)
        col_doc = sum((cols >= e).astype(jnp.int32) for e in ends)
        same = row_doc == col_doc
        for a in range(CQ):
            masks[a, r0 : r0 + LANE, :width] = jnp.where(
                same & (rows - cols >= a), 1.0, 0.0
            ).astype(BF16)


def circulant_masks():
    gap = lax.broadcasted_iota(jnp.int32, (LANE, LANE), 1) - lax.broadcasted_iota(
        jnp.int32, (LANE, LANE), 0
    )
    half = CK // 2
    return (jnp.abs(gap) <= half, gap <= half - LANE, gap >= LANE - half)


def circulant(taps):
    wide = jnp.broadcast_to(taps, (LANE, LANE))
    return pltpu.roll(wide, 0, axis=1, stride=1, stride_axis=0)


def fill_toeplitz(taps_ref, head, band, blocks):
    near, after, before = circulant_masks()
    for a in range(CQ):
        whole = circulant(taps_ref[head, a : a + 1, :])
        parts = {
            0: jnp.where(near, whole, 0.0).astype(BF16),
            1: jnp.where(after, whole, 0.0).astype(BF16),
            -1: jnp.where(before, whole, 0.0).astype(BF16),
        }
        for r in range(blocks):
            for c in range(blocks):
                part = parts.get(c - r)
                if part is not None:
                    yield a, r, c, part


def fill_forward_band(taps_ref, head, band):
    for a, r, c, part in fill_toeplitz(taps_ref, head, band, 3):
        at = (r * CQ + a) * LANE
        band[at : at + LANE, c * LANE : (c + 1) * LANE] = part


def fill_backward_band(taps_ref, head, band):
    for a, r, c, part in fill_toeplitz(taps_ref, head, band, 3):
        at = (c * CQ + a) * LANE
        band[r * LANE : (r + 1) * LANE, at : at + LANE] = part


def shifted_rows(query):
    wide = query.astype(F32)
    return [query] + [pltpu.roll(wide, a, axis=0).astype(BF16) for a in range(1, CQ)]


def masked_scores(shifted, keys, masks, r0, width, c0):
    left = jnp.concatenate([shifted[a, r0 : r0 + LANE] for a in range(CQ)], axis=0)
    scores = nt(left, keys[c0 : c0 + width]).astype(BF16)
    return left, [
        scores[a * LANE : (a + 1) * LANE] * masks[a, r0 : r0 + LANE, :width]
        for a in range(CQ)
    ]


def by_window(parts, width):
    return jnp.concatenate(
        [
            parts[a][:, b * LANE : (b + 1) * LANE]
            for b in range(width // LANE)
            for a in range(CQ)
        ],
        axis=1,
    )


def forward_kernel(
    docs_ref, mix_ref, taps_ref, gain_ref, q_ref, k_ref, v_ref,
    grouped_ref, attended_ref, soft_ref,
    masks, band, qs, ks, vs, shifted, outs, normed,
):
    seq = q_ref.shape[0]
    quad = pl.program_id(0)

    @pl.when(quad == 0)
    def _():
        fill_masks(docs_ref, masks, seq)
        band[...] = jnp.zeros_like(band)

    for h in range(QUAD):
        at = slice(h * HEAD_DIM, (h + 1) * HEAD_DIM)
        qs[h] = q_ref[:, at]
        ks[h] = k_ref[:, at]
        vs[h] = v_ref[:, at]

    sets = row_sets(seq)

    def pair(p, carry):
        group = quad * 2 + p
        for r in range(2):
            h = 2 * p + r
            fill_forward_band(taps_ref, quad * QUAD + h, band)
            for a, rows in enumerate(shifted_rows(qs[h])):
                shifted[a] = rows
            keys = ks[h]
            lefts = []
            for r0, width, c0 in sets:
                _, parts = masked_scores(shifted, keys, masks, r0, width, c0)
                lefts.append((width, by_window(parts, width)))
            convs = []
            i = 0
            while i < len(sets):
                width = sets[i][1]
                n = 1
                while i + n < len(sets) and sets[i + n][1] == width:
                    n += 1
                left = jnp.concatenate([lefts[i + m][1] for m in range(n)], axis=0)
                conv = nn(left, band[: width * CQ, :width])
                convs += [conv[m * LANE : (m + 1) * LANE] for m in range(n)]
                i += n
            for (r0, width, c0), conv in zip(sets, convs):
                logits = jnp.where(
                    masks[0, r0 : r0 + LANE, :width].astype(F32) > 0, conv, -1e30
                )
                weights = jnp.exp(logits - jnp.max(logits, axis=1, keepdims=True))
                soft = weights * (1.0 / jnp.sum(weights, axis=1, keepdims=True))
                soft_ref[h, r0 : r0 + LANE, :width] = soft.astype(BF16)
        for r in range(2):
            h = 2 * p + r
            values = vs[h]
            for r0, width, c0 in sets:
                mixed = (
                    mix_ref[group, 2 * r] * soft_ref[2 * p, r0 : r0 + LANE, :width].astype(F32)
                    + mix_ref[group, 2 * r + 1] * soft_ref[2 * p + 1, r0 : r0 + LANE, :width].astype(F32)
                ).astype(BF16)
                outs[h, r0 : r0 + LANE] = nn(mixed, values[c0 : c0 + width])
        return carry

    lax.fori_loop(0, 2, pair, 0)
    wholes, grouped = [], []
    for h in range(QUAD):
        attended = outs[h]
        centred = attended - jnp.mean(attended, axis=1, keepdims=True)
        var = jnp.mean(centred * centred, axis=1, keepdims=True)
        wholes.append(attended)
        grouped.append(centred * lax.rsqrt(var + EPSILON))
    attended_ref[...] = jnp.concatenate(wholes, axis=1)
    grouped_ref[...] = (jnp.concatenate(grouped, axis=1) * gain_ref[...]).astype(BF16)


def pad_taps(kernel):
    padded = jnp.pad(kernel * SCALE, ((0, 0), (0, 2), (0, LANE - CK)))
    return jnp.roll(padded, -(CK // 2), axis=2)


def attend_forward(projected, conv_kernel, head_mixing, docs, gain):
    seq = projected.shape[0]
    width = projected.shape[1] // 3
    block = QUAD * HEAD_DIM
    quads = HEADS // QUAD
    whole = pl.BlockSpec(memory_space=pltpu.VMEM)
    smem = pl.BlockSpec(memory_space=pltpu.SMEM)

    def columns(first):
        return pl.BlockSpec((seq, block), lambda i: (0, first * quads + i))

    return pl.pallas_call(
        forward_kernel,
        grid=(quads,),
        out_shape=[
            jax.ShapeDtypeStruct((seq, width), BF16),
            jax.ShapeDtypeStruct((seq, width), F32),
            jax.ShapeDtypeStruct((HEADS, seq, 3 * LANE), BF16),
        ],
        in_specs=[
            smem, smem, whole,
            pl.BlockSpec((1, block), lambda i: (0, i)),
            columns(0), columns(1), columns(2),
        ],
        out_specs=[
            columns(0), columns(0),
            pl.BlockSpec((QUAD, seq, 3 * LANE), lambda i: (i, 0, 0)),
        ],
        scratch_shapes=[
            pltpu.VMEM((CQ, seq, 3 * LANE), BF16),
            pltpu.VMEM((3 * LANE * CQ, 3 * LANE), BF16),
            pltpu.VMEM((QUAD, seq, HEAD_DIM), BF16),
            pltpu.VMEM((QUAD, seq, HEAD_DIM), BF16),
            pltpu.VMEM((QUAD, seq, HEAD_DIM), BF16),
            pltpu.VMEM((CQ, seq, HEAD_DIM), BF16),
            pltpu.VMEM((QUAD, seq, HEAD_DIM), F32),
            pltpu.VMEM((8, LANE), F32),
        ],
        compiler_params=pltpu.CompilerParams(vmem_limit_bytes=48 * 1024 * 1024),
    )(
        docs, head_mixing.reshape(HEADS // 2, 4), pad_taps(conv_kernel), gain.reshape(1, width),
        projected, projected, projected,
    )


def backward_kernel(
    docs_ref, mix_ref, taps_ref, gain_ref, q_ref, k_ref, v_ref, attended_ref, d_grouped_ref, soft_ref,
    dq_ref, dk_ref, dv_ref, grad_gain_ref, grad_taps_ref, grad_mix_ref,
    masks, band, qs, ks, vs, ds, shifted, d_heads, d_rows, d_cols, diagonal,
):
    seq = q_ref.shape[0]
    quad = pl.program_id(0)

    @pl.when(quad == 0)
    def _():
        fill_masks(docs_ref, masks, seq)
        band[...] = jnp.zeros_like(band)

    gains = []
    for h in range(QUAD):
        at = slice(h * HEAD_DIM, (h + 1) * HEAD_DIM)
        qs[h] = q_ref[:, at]
        ks[h] = k_ref[:, at]
        vs[h] = v_ref[:, at]
        attended = attended_ref[:, at]
        d_grouped = d_grouped_ref[:, at]
        centred = attended - jnp.mean(attended, axis=1, keepdims=True)
        var = jnp.mean(centred * centred, axis=1, keepdims=True)
        scale = lax.rsqrt(var + EPSILON)
        unit = centred * scale
        gains.append(jnp.sum(d_grouped * unit, axis=0, keepdims=True))
        w = d_grouped * gain_ref[:, at]
        d_attended = scale * (
            w
            - jnp.mean(w, axis=1, keepdims=True)
            - unit * jnp.mean(w * unit, axis=1, keepdims=True)
        )
        ds[h] = d_attended.astype(BF16)
    grad_gain_ref[...] = jnp.concatenate(gains, axis=1)

    sets = row_sets(seq)
    up = lax.broadcasted_iota(jnp.int32, (LANE, LANE), 0)
    across = lax.broadcasted_iota(jnp.int32, (LANE, LANE), 1)
    flip = jnp.where(up + across == LANE - 1, 1.0, 0.0).astype(BF16)
    gap = up + across - (LANE - 1)
    keeps = {0: jnp.abs(gap) <= CK // 2, 1: gap <= CK // 2 - LANE, -1: gap >= LANE - CK // 2}

    def pair(p, carry):
        group = quad * 2 + p
        mix = [[mix_ref[group, 2 * r + s] for s in range(2)] for r in range(2)]
        upstream_t = [ds[2 * p + r].T for r in range(2)]
        grad_mix = [[jnp.zeros((1, 1), F32) for _ in range(2)] for _ in range(2)]
        for r in range(2):
            d_cols[r] = jnp.zeros_like(d_cols[r])
        for r0, width, c0 in sets:
            rows = slice(r0, r0 + LANE)
            soft = [soft_ref[2 * p + s, rows, :width].astype(F32) for s in range(2)]
            d_prob, sums = [], []
            for r in range(2):
                dp = nt(ds[2 * p + r, rows], vs[2 * p + r, c0 : c0 + width])
                d_prob.append(dp)
                sums.append([jnp.sum(dp * soft[s], axis=1, keepdims=True) for s in range(2)])
                for s in range(2):
                    grad_mix[r][s] += jnp.sum(sums[r][s], axis=0, keepdims=True)
                mixed = (mix[r][0] * soft[0] + mix[r][1] * soft[1]).astype(BF16)
                d_cols[r, :, c0 : c0 + width] += nn(upstream_t[r][:, r0 : r0 + LANE], mixed)
            for s in range(2):
                d_soft = mix[0][s] * d_prob[0] + mix[1][s] * d_prob[1]
                inner = mix[0][s] * sums[0][s] + mix[1][s] * sums[1][s]
                d_conv = soft[s] * (d_soft - inner)
                d_rows[s, rows, :width] = d_conv.astype(BF16)
        lane = lax.broadcasted_iota(jnp.int32, (1, LANE), 1)
        line = jnp.zeros((1, LANE), F32)
        for r in range(2):
            for s in range(2):
                line = line + jnp.where(lane == 2 * r + s, grad_mix[r][s], 0.0)
        grad_mix_ref[0, pl.ds(p, 1), :] = line
        for r in range(2):
            d_heads[2, 2 * p + r] = d_cols[r].T

        for r in range(2):
            h = 2 * p + r
            fill_backward_band(taps_ref, quad * QUAD + h, band)
            for a, moved in enumerate(shifted_rows(qs[h])):
                shifted[a] = moved
            keys = ks[h]
            d_cols[0] = jnp.zeros_like(d_cols[0])
            diagonal[...] = jnp.zeros_like(diagonal)
            d_query = []
            for r0, width, c0 in sets:
                rows = slice(r0, r0 + LANE)
                left, parts = masked_scores(shifted, keys, masks, r0, width, c0)
                d_conv = d_rows[r, rows, :width]
                blocks = width // LANE
                flipped = jnp.concatenate(
                    [
                        nt(flip, d_conv[:, b * LANE : (b + 1) * LANE]).astype(BF16)
                        for b in range(blocks)
                    ],
                    axis=0,
                )
                taken = nn(flipped, by_window(parts, width))
                for a in range(CQ):
                    total = diagonal[a]
                    for jb in range(blocks):
                        for qb in range(blocks):
                            if abs(jb - qb) > 1:
                                continue
                            at = (qb * CQ + a) * LANE
                            one = taken[jb * LANE : (jb + 1) * LANE, at : at + LANE]
                            total = total + jnp.where(keeps[qb - jb], one, 0.0)
                    diagonal[a] = total
                spread = nn(d_conv, band[:width, : width * CQ]).astype(BF16)
                stacked = jnp.concatenate(
                    [
                        jnp.concatenate(
                            [
                                spread[:, (b * CQ + a) * LANE : (b * CQ + a + 1) * LANE]
                                for b in range(blocks)
                            ],
                            axis=1,
                        )
                        * masks[a, rows, :width]
                        for a in range(CQ)
                    ],
                    axis=0,
                )
                d_query.append(nn(stacked, keys[c0 : c0 + width]))
                d_cols[0, :, c0 : c0 + width] += nn(left.T, stacked)
            total = None
            for a in range(CQ):
                whole = jnp.concatenate([d[a * LANE : (a + 1) * LANE] for d in d_query], axis=0)
                if a:
                    whole = pltpu.roll(whole, seq - a, axis=0)
                total = whole if total is None else total + whole
            d_heads[0, h] = total
            d_heads[1, h] = d_cols[0].T
            for a in range(CQ):
                aligned = pltpu.roll(diagonal[a], 0, axis=1, stride=1, stride_axis=0)
                grad_taps_ref[h, a : a + 1, :] = jnp.sum(aligned, axis=0, keepdims=True)
        return carry

    lax.fori_loop(0, 2, pair, 0)
    for out, n in ((dq_ref, 0), (dk_ref, 1), (dv_ref, 2)):
        out[...] = jnp.concatenate([d_heads[n, h] for h in range(QUAD)], axis=1).astype(BF16)


def attend_backward(projected, conv_kernel, head_mixing, docs, gain, attended, d_grouped, soft):
    seq = projected.shape[0]
    width = projected.shape[1] // 3
    block = QUAD * HEAD_DIM
    quads = HEADS // QUAD
    whole = pl.BlockSpec(memory_space=pltpu.VMEM)
    smem = pl.BlockSpec(memory_space=pltpu.SMEM)

    def columns(first):
        return pl.BlockSpec((seq, block), lambda i: (0, first * quads + i))

    dq, dk, dv, grad_gain, grad_taps, grad_mix = pl.pallas_call(
        backward_kernel,
        grid=(quads,),
        out_shape=[
            jax.ShapeDtypeStruct((seq, width), BF16),
            jax.ShapeDtypeStruct((seq, width), BF16),
            jax.ShapeDtypeStruct((seq, width), BF16),
            jax.ShapeDtypeStruct((1, width), F32),
            jax.ShapeDtypeStruct((HEADS, 8, LANE), F32),
            jax.ShapeDtypeStruct((quads, 8, LANE), F32),
        ],
        in_specs=[
            smem, smem, whole,
            pl.BlockSpec((1, block), lambda i: (0, i)),
            columns(0), columns(1), columns(2), columns(0), columns(0),
            pl.BlockSpec((QUAD, seq, 3 * LANE), lambda i: (i, 0, 0)),
        ],
        out_specs=[
            columns(0), columns(0), columns(0),
            pl.BlockSpec((1, block), lambda i: (0, i)),
            pl.BlockSpec((QUAD, 8, LANE), lambda i: (i, 0, 0)),
            pl.BlockSpec((1, 8, LANE), lambda i: (i, 0, 0)),
        ],
        scratch_shapes=[
            pltpu.VMEM((CQ, seq, 3 * LANE), BF16),
            pltpu.VMEM((3 * LANE, 3 * LANE * CQ), BF16),
            pltpu.VMEM((QUAD, seq, HEAD_DIM), BF16),
            pltpu.VMEM((QUAD, seq, HEAD_DIM), BF16),
            pltpu.VMEM((QUAD, seq, HEAD_DIM), BF16),
            pltpu.VMEM((QUAD, seq, HEAD_DIM), BF16),
            pltpu.VMEM((CQ, seq, HEAD_DIM), BF16),
            pltpu.VMEM((3, QUAD, seq, HEAD_DIM), F32),
            pltpu.VMEM((2, seq, 3 * LANE), BF16),
            pltpu.VMEM((2, HEAD_DIM, seq), F32),
            pltpu.VMEM((CQ, LANE, LANE), F32),
        ],
        compiler_params=pltpu.CompilerParams(vmem_limit_bytes=56 * 1024 * 1024),
    )(
        docs, head_mixing.reshape(HEADS // 2, 4), pad_taps(conv_kernel[:, :, ::-1]), gain.reshape(1, width),
        projected, projected, projected, attended, d_grouped, soft,
    )
    return (
        dq, dk, dv, grad_gain.reshape(width),
        jnp.roll(grad_taps, CK // 2 + 1, axis=2)[:, :CQ, :CK][:, :, ::-1] * SCALE,
        grad_mix[:, :2, :4].reshape(HEADS // 2, 2, 2),
    )


def rms_norm(values, gains):
    return values * lax.rsqrt(jnp.mean(values * values, axis=-1, keepdims=True) + EPSILON) * gains


def swiglu(gate_up):
    middle_col = gate_up.shape[1] // 2
    return jax.nn.silu(gate_up[:, :middle_col]) * gate_up[:, middle_col:]


def project(operand, weight):
    return jnp.dot(
        operand,
        lax.all_gather(weight, "fsdp", axis=0, tiled=True),
        preferred_element_type=jnp.float32,
    )


def project_back(upstream, weight):
    return lax.dot_general(
        upstream,
        lax.all_gather(weight, "fsdp", axis=0, tiled=True),
        (((1,), (1,)), ((), ())),
        preferred_element_type=jnp.float32,
    )


def weight_grad(operand, upstream):
    return lax.psum_scatter(
        lax.dot_general(
            operand, upstream, (((0,), (0,)), ((), ())), preferred_element_type=jnp.float32
        ).astype(jnp.bfloat16),
        "fsdp",
        scatter_dimension=0,
        tiled=True,
    ).astype(jnp.float32)


def body(
    layer_input,
    first_gain,
    qkv_weight,
    conv_kernel,
    head_mixing,
    group_gain,
    out_weight,
    second_gain,
    inner_weight,
    down_weight,
    doc_lengths,
    cotangent,
):
    inputs = layer_input.astype(jnp.float32)
    normed_value, first_pull = jax.vjp(rms_norm, inputs, first_gain)
    normed = normed_value.astype(jnp.bfloat16)
    projected = project(normed, qkv_weight).astype(jnp.bfloat16)
    grouped, attended, soft = attend_forward(
        projected, conv_kernel, head_mixing, doc_lengths, group_gain
    )
    middle = inputs + project(grouped, out_weight)
    second_value, second_pull = jax.vjp(rms_norm, middle, second_gain)
    second = second_value.astype(jnp.bfloat16)
    gate_up = project(second, inner_weight)
    hidden_value, swiglu_pull = jax.vjp(swiglu, gate_up)
    hidden = hidden_value.astype(jnp.bfloat16)
    layer_output = (middle + project(hidden, down_weight)).astype(jnp.bfloat16)
    upstream = cotangent.astype(jnp.float32)
    grad_down = weight_grad(hidden, cotangent)
    d_hidden = project_back(cotangent, down_weight)
    d_gate_up = swiglu_pull(d_hidden)[0].astype(jnp.bfloat16)
    grad_inner = weight_grad(second, d_gate_up)
    d_second = project_back(d_gate_up, inner_weight)
    d_middle, grad_second = second_pull(d_second)
    d_middle = upstream + d_middle
    d_branch = d_middle.astype(jnp.bfloat16)
    grad_proj = weight_grad(grouped, d_branch)
    d_grouped = project_back(d_branch, out_weight)
    d_query, d_keys, d_values, grad_group, grad_kernel, grad_mixing = attend_backward(
        projected, conv_kernel, head_mixing, doc_lengths, group_gain, attended, d_grouped, soft
    )
    d_projected = jnp.concatenate([d_query, d_keys, d_values], axis=1)
    grad_qkv = weight_grad(normed, d_projected)
    d_normed = project_back(d_projected, qkv_weight)
    d_inputs, grad_first = first_pull(d_normed)
    grad_input = d_middle + d_inputs
    small = lax.psum(
        (grad_first, grad_kernel, grad_mixing, grad_group, grad_second), ("rep", "fsdp")
    )
    shards = (grad_qkv, grad_proj, grad_inner, grad_down)
    shards = (
        lax.psum(shards[0].astype(jnp.bfloat16), "rep").astype(jnp.float32),
        lax.psum(shards[1].astype(jnp.bfloat16), "rep").astype(jnp.float32),
        lax.psum(shards[2].astype(jnp.bfloat16), "rep").astype(jnp.float32),
        lax.psum(shards[3].astype(jnp.bfloat16), "rep").astype(jnp.float32),
    )
    return (
        layer_output,
        grad_input,
        small[0],
        shards[0],
        small[1],
        small[2],
        small[3],
        shards[1],
        small[4],
        shards[2],
        shards[3],
    )


def solution(mesh):
    placed = (
        P(("rep", "fsdp"), None),
        P(),
        P("fsdp", None),
        P(),
        P(),
        P(),
        P("fsdp", None),
        P(),
        P("fsdp", None),
        P("fsdp", None),
        P(("rep", "fsdp"), None),
        P(("rep", "fsdp"), None),
    )
    return jax.shard_map(
        body,
        mesh=mesh,
        in_specs=placed,
        out_specs=(
            P(("rep", "fsdp"), None),
            P(("rep", "fsdp"), None),
            P(),
            P("fsdp", None),
            P(),
            P(),
            P(),
            P("fsdp", None),
            P(),
            P("fsdp", None),
            P("fsdp", None),
        ),
        check_vma=False,
    )
```

```python
import functools, math
import jax, jax.numpy as jnp
from jax import lax
from jax.experimental import pallas as pl
from jax.experimental.pallas import tpu as pltpu
from jax.sharding import PartitionSpec as P

HEADS = 16
HEAD_DIM = 96
CQ = 6
CK = 11
EPSILON = 1e-05
LANE = 128
QUAD = 4
LAG = 1
SCALE = 1.0 / math.sqrt(HEAD_DIM)
F32 = jnp.float32
BF16 = jnp.bfloat16


def row_sets(seq):
    return [
        (r, min(r + LANE, 3 * LANE), max(0, r - 2 * LANE)) for r in range(0, seq, LANE)
    ]


def nt(a, b):
    return lax.dot_general(a, b, (((1,), (1,)), ((), ())), preferred_element_type=F32)


def nn(a, b):
    return jnp.dot(a, b, preferred_element_type=F32)


def fill_masks(docs_ref, masks, seq):
    ends = []
    total = jnp.int32(0)
    for d in range(docs_ref.shape[1] - 1):
        total = total + docs_ref[0, d]
        ends.append(total)
    for r0, width, c0 in row_sets(seq):
        rows = r0 + lax.broadcasted_iota(jnp.int32, (LANE, 1), 0)
        cols = c0 + lax.broadcasted_iota(jnp.int32, (1, width), 1)
        row_doc = sum((rows >= e).astype(jnp.int32) for e in ends)
        col_doc = sum((cols >= e).astype(jnp.int32) for e in ends)
        same = row_doc == col_doc
        for a in range(CQ):
            masks[a, r0 : r0 + LANE, :width] = jnp.where(
                same & (rows - cols >= a), 1.0, 0.0
            ).astype(BF16)


def circulant_masks():
    gap = lax.broadcasted_iota(jnp.int32, (LANE, LANE), 1) - lax.broadcasted_iota(
        jnp.int32, (LANE, LANE), 0
    )
    half = CK // 2
    return (jnp.abs(gap) <= half, gap <= half - LANE, gap >= LANE - half)


def circulant(taps):
    wide = jnp.broadcast_to(taps, (LANE, LANE))
    return pltpu.roll(wide, 0, axis=1, stride=1, stride_axis=0)


def fill_toeplitz(taps_ref, head, band, blocks):
    near, after, before = circulant_masks()
    for a in range(CQ):
        whole = circulant(taps_ref[head, a : a + 1, :])
        parts = {
            0: jnp.where(near, whole, 0.0).astype(BF16),
            1: jnp.where(after, whole, 0.0).astype(BF16),
            -1: jnp.where(before, whole, 0.0).astype(BF16),
        }
        for r in range(blocks):
            for c in range(blocks):
                part = parts.get(c - r)
                if part is not None:
                    yield a, r, c, part


def fill_forward_band(taps_ref, head, band):
    for a, r, c, part in fill_toeplitz(taps_ref, head, band, 3):
        at = (r * CQ + a) * LANE
        band[at : at + LANE, c * LANE : (c + 1) * LANE] = part


def fill_backward_band(taps_ref, head, band):
    for a, r, c, part in fill_toeplitz(taps_ref, head, band, 3):
        at = (c * CQ + a) * LANE
        band[r * LANE : (r + 1) * LANE, at : at + LANE] = part


def shifted_rows(query):
    wide = query.astype(F32)
    return [query] + [pltpu.roll(wide, a, axis=0).astype(BF16) for a in range(1, CQ)]


def masked_scores(shifted, keys, masks, r0, width, c0):
    left = jnp.concatenate([shifted[a, r0 : r0 + LANE] for a in range(CQ)], axis=0)
    scores = nt(left, keys[c0 : c0 + width]).astype(BF16)
    return left, [
        scores[a * LANE : (a + 1) * LANE] * masks[a, r0 : r0 + LANE, :width]
        for a in range(CQ)
    ]


def by_window(parts, width):
    return jnp.concatenate(
        [
            parts[a][:, b * LANE : (b + 1) * LANE]
            for b in range(width // LANE)
            for a in range(CQ)
        ],
        axis=1,
    )


def forward_kernel(
    docs_ref, mix_ref, taps_ref, gain_ref, q_ref, k_ref, v_ref,
    grouped_ref, attended_ref, soft_ref,
    masks, band, qs, ks, vs, shifted, outs, normed,
):
    seq = q_ref.shape[0]
    quad = pl.program_id(0)

    @pl.when(quad == 0)
    def _():
        fill_masks(docs_ref, masks, seq)
        band[...] = jnp.zeros_like(band)

    for h in range(QUAD):
        at = slice(h * HEAD_DIM, (h + 1) * HEAD_DIM)
        qs[h] = q_ref[:, at]
        ks[h] = k_ref[:, at]
        vs[h] = v_ref[:, at]

    sets = row_sets(seq)

    def pair(p, carry):
        group = quad * 2 + p
        for r in range(2):
            h = 2 * p + r
            fill_forward_band(taps_ref, quad * QUAD + h, band)
            for a, rows in enumerate(shifted_rows(qs[h])):
                shifted[a] = rows
            keys = ks[h]
            lefts = []
            for r0, width, c0 in sets:
                _, parts = masked_scores(shifted, keys, masks, r0, width, c0)
                lefts.append((width, by_window(parts, width)))
            convs = []
            i = 0
            while i < len(sets):
                width = sets[i][1]
                n = 1
                while i + n < len(sets) and sets[i + n][1] == width:
                    n += 1
                left = jnp.concatenate([lefts[i + m][1] for m in range(n)], axis=0)
                conv = nn(left, band[: width * CQ, :width])
                convs += [conv[m * LANE : (m + 1) * LANE] for m in range(n)]
                i += n
            for (r0, width, c0), conv in zip(sets, convs):
                logits = jnp.where(
                    masks[0, r0 : r0 + LANE, :width].astype(F32) > 0, conv, -1e30
                )
                weights = jnp.exp(logits - jnp.max(logits, axis=1, keepdims=True))
                soft = weights * (1.0 / jnp.sum(weights, axis=1, keepdims=True))
                soft_ref[h, r0 : r0 + LANE, :width] = soft.astype(BF16)
        for r in range(2):
            h = 2 * p + r
            values = vs[h]
            for r0, width, c0 in sets:
                mixed = (
                    mix_ref[group, 2 * r] * soft_ref[2 * p, r0 : r0 + LANE, :width].astype(F32)
                    + mix_ref[group, 2 * r + 1] * soft_ref[2 * p + 1, r0 : r0 + LANE, :width].astype(F32)
                ).astype(BF16)
                outs[h, r0 : r0 + LANE] = nn(mixed, values[c0 : c0 + width])
        return carry

    lax.fori_loop(0, 2, pair, 0)
    wholes, grouped = [], []
    for h in range(QUAD):
        attended = outs[h]
        centred = attended - jnp.mean(attended, axis=1, keepdims=True)
        var = jnp.mean(centred * centred, axis=1, keepdims=True)
        wholes.append(attended)
        grouped.append(centred * lax.rsqrt(var + EPSILON))
    attended_ref[...] = jnp.concatenate(wholes, axis=1)
    grouped_ref[...] = (jnp.concatenate(grouped, axis=1) * gain_ref[...]).astype(BF16)


def pad_taps(kernel):
    padded = jnp.pad(kernel * SCALE, ((0, 0), (0, 2), (0, LANE - CK)))
    return jnp.roll(padded, -(CK // 2), axis=2)


def attend_forward(projected, conv_kernel, head_mixing, docs, gain):
    seq = projected.shape[0]
    width = projected.shape[1] // 3
    block = QUAD * HEAD_DIM
    quads = HEADS // QUAD
    whole = pl.BlockSpec(memory_space=pltpu.VMEM)
    smem = pl.BlockSpec(memory_space=pltpu.SMEM)

    def columns(first):
        return pl.BlockSpec((seq, block), lambda i: (0, first * quads + i))

    return pl.pallas_call(
        forward_kernel,
        grid=(quads,),
        out_shape=[
            jax.ShapeDtypeStruct((seq, width), BF16),
            jax.ShapeDtypeStruct((seq, width), F32),
            jax.ShapeDtypeStruct((HEADS, seq, 3 * LANE), BF16),
        ],
        in_specs=[
            smem, smem, whole,
            pl.BlockSpec((1, block), lambda i: (0, i)),
            columns(0), columns(1), columns(2),
        ],
        out_specs=[
            columns(0), columns(0),
            pl.BlockSpec((QUAD, seq, 3 * LANE), lambda i: (i, 0, 0)),
        ],
        scratch_shapes=[
            pltpu.VMEM((CQ, seq, 3 * LANE), BF16),
            pltpu.VMEM((3 * LANE * CQ, 3 * LANE), BF16),
            pltpu.VMEM((QUAD, seq, HEAD_DIM), BF16),
            pltpu.VMEM((QUAD, seq, HEAD_DIM), BF16),
            pltpu.VMEM((QUAD, seq, HEAD_DIM), BF16),
            pltpu.VMEM((CQ, seq, HEAD_DIM), BF16),
            pltpu.VMEM((QUAD, seq, HEAD_DIM), F32),
            pltpu.VMEM((8, LANE), F32),
        ],
        compiler_params=pltpu.CompilerParams(vmem_limit_bytes=48 * 1024 * 1024),
    )(
        docs, head_mixing.reshape(HEADS // 2, 4), pad_taps(conv_kernel), gain.reshape(1, width),
        projected, projected, projected,
    )


def backward_kernel(
    docs_ref, mix_ref, taps_ref, gain_ref, q_ref, k_ref, v_ref, attended_ref, d_grouped_ref, soft_ref,
    dq_ref, dk_ref, dv_ref, grad_gain_ref, grad_taps_ref, grad_mix_ref,
    masks, band, qs, ks, vs, ds, shifted, d_heads, d_rows, d_cols, diagonal,
):
    seq = q_ref.shape[0]
    quad = pl.program_id(0)

    @pl.when(quad == 0)
    def _():
        fill_masks(docs_ref, masks, seq)
        band[...] = jnp.zeros_like(band)

    gains = []
    for h in range(QUAD):
        at = slice(h * HEAD_DIM, (h + 1) * HEAD_DIM)
        qs[h] = q_ref[:, at]
        ks[h] = k_ref[:, at]
        vs[h] = v_ref[:, at]
        attended = attended_ref[:, at]
        d_grouped = d_grouped_ref[:, at]
        centred = attended - jnp.mean(attended, axis=1, keepdims=True)
        var = jnp.mean(centred * centred, axis=1, keepdims=True)
        scale = lax.rsqrt(var + EPSILON)
        unit = centred * scale
        gains.append(jnp.sum(d_grouped * unit, axis=0, keepdims=True))
        w = d_grouped * gain_ref[:, at]
        d_attended = scale * (
            w
            - jnp.mean(w, axis=1, keepdims=True)
            - unit * jnp.mean(w * unit, axis=1, keepdims=True)
        )
        ds[h] = d_attended.astype(BF16)
    grad_gain_ref[...] = jnp.concatenate(gains, axis=1)

    sets = row_sets(seq)
    up = lax.broadcasted_iota(jnp.int32, (LANE, LANE), 0)
    across = lax.broadcasted_iota(jnp.int32, (LANE, LANE), 1)
    flip = jnp.where(up + across == LANE - 1, 1.0, 0.0).astype(BF16)
    gap = up + across - (LANE - 1)
    keeps = {0: jnp.abs(gap) <= CK // 2, 1: gap <= CK // 2 - LANE, -1: gap >= LANE - CK // 2}

    def pair(p, carry):
        group = quad * 2 + p
        mix = [[mix_ref[group, 2 * r + s] for s in range(2)] for r in range(2)]
        upstream_t = [ds[2 * p + r].T for r in range(2)]
        grad_mix = [[jnp.zeros((1, 1), F32) for _ in range(2)] for _ in range(2)]
        for r in range(2):
            d_cols[r] = jnp.zeros_like(d_cols[r])
        for r0, width, c0 in sets:
            rows = slice(r0, r0 + LANE)
            soft = [soft_ref[2 * p + s, rows, :width].astype(F32) for s in range(2)]
            d_prob, sums = [], []
            for r in range(2):
                dp = nt(ds[2 * p + r, rows], vs[2 * p + r, c0 : c0 + width])
                d_prob.append(dp)
                sums.append([jnp.sum(dp * soft[s], axis=1, keepdims=True) for s in range(2)])
                for s in range(2):
                    grad_mix[r][s] += jnp.sum(sums[r][s], axis=0, keepdims=True)
                mixed = (mix[r][0] * soft[0] + mix[r][1] * soft[1]).astype(BF16)
                d_cols[r, :, c0 : c0 + width] += nn(upstream_t[r][:, r0 : r0 + LANE], mixed)
            for s in range(2):
                d_soft = mix[0][s] * d_prob[0] + mix[1][s] * d_prob[1]
                inner = mix[0][s] * sums[0][s] + mix[1][s] * sums[1][s]
                d_conv = soft[s] * (d_soft - inner)
                d_rows[s, rows, :width] = d_conv.astype(BF16)
        lane = lax.broadcasted_iota(jnp.int32, (1, LANE), 1)
        line = jnp.zeros((1, LANE), F32)
        for r in range(2):
            for s in range(2):
                line = line + jnp.where(lane == 2 * r + s, grad_mix[r][s], 0.0)
        grad_mix_ref[0, pl.ds(p, 1), :] = line
        for r in range(2):
            d_heads[2, 2 * p + r] = d_cols[r].T

        for r in range(2):
            h = 2 * p + r
            fill_backward_band(taps_ref, quad * QUAD + h, band)
            for a, moved in enumerate(shifted_rows(qs[h])):
                shifted[a] = moved
            keys = ks[h]
            d_cols[0] = jnp.zeros_like(d_cols[0])
            diagonal[...] = jnp.zeros_like(diagonal)
            d_query = []
            for r0, width, c0 in sets:
                rows = slice(r0, r0 + LANE)
                left, parts = masked_scores(shifted, keys, masks, r0, width, c0)
                d_conv = d_rows[r, rows, :width]
                blocks = width // LANE
                flipped = jnp.concatenate(
                    [
                        nt(flip, d_conv[:, b * LANE : (b + 1) * LANE]).astype(BF16)
                        for b in range(blocks)
                    ],
                    axis=0,
                )
                taken = nn(flipped, by_window(parts, width))
                for a in range(CQ):
                    total = diagonal[a]
                    for jb in range(blocks):
                        for qb in range(blocks):
                            if abs(jb - qb) > 1:
                                continue
                            at = (qb * CQ + a) * LANE
                            one = taken[jb * LANE : (jb + 1) * LANE, at : at + LANE]
                            total = total + jnp.where(keeps[qb - jb], one, 0.0)
                    diagonal[a] = total
                spread = nn(d_conv, band[:width, : width * CQ]).astype(BF16)
                stacked = jnp.concatenate(
                    [
                        jnp.concatenate(
                            [
                                spread[:, (b * CQ + a) * LANE : (b * CQ + a + 1) * LANE]
                                for b in range(blocks)
                            ],
                            axis=1,
                        )
                        * masks[a, rows, :width]
                        for a in range(CQ)
                    ],
                    axis=0,
                )
                d_query.append(nn(stacked, keys[c0 : c0 + width]))
                d_cols[0, :, c0 : c0 + width] += nn(left.T, stacked)
            total = None
            for a in range(CQ):
                whole = jnp.concatenate([d[a * LANE : (a + 1) * LANE] for d in d_query], axis=0)
                if a:
                    whole = pltpu.roll(whole, seq - a, axis=0)
                total = whole if total is None else total + whole
            d_heads[0, h] = total
            d_heads[1, h] = d_cols[0].T
            for a in range(CQ):
                aligned = pltpu.roll(diagonal[a], 0, axis=1, stride=1, stride_axis=0)
                grad_taps_ref[h, a : a + 1, :] = jnp.sum(aligned, axis=0, keepdims=True)
        return carry

    lax.fori_loop(0, 2, pair, 0)
    for out, n in ((dq_ref, 0), (dk_ref, 1), (dv_ref, 2)):
        out[...] = jnp.concatenate([d_heads[n, h] for h in range(QUAD)], axis=1).astype(BF16)


def attend_backward(projected, conv_kernel, head_mixing, docs, gain, attended, d_grouped, soft):
    seq = projected.shape[0]
    width = projected.shape[1] // 3
    block = QUAD * HEAD_DIM
    quads = HEADS // QUAD
    whole = pl.BlockSpec(memory_space=pltpu.VMEM)
    smem = pl.BlockSpec(memory_space=pltpu.SMEM)

    def columns(first):
        return pl.BlockSpec((seq, block), lambda i: (0, first * quads + i))

    dq, dk, dv, grad_gain, grad_taps, grad_mix = pl.pallas_call(
        backward_kernel,
        grid=(quads,),
        out_shape=[
            jax.ShapeDtypeStruct((seq, width), BF16),
            jax.ShapeDtypeStruct((seq, width), BF16),
            jax.ShapeDtypeStruct((seq, width), BF16),
            jax.ShapeDtypeStruct((1, width), F32),
            jax.ShapeDtypeStruct((HEADS, 8, LANE), F32),
            jax.ShapeDtypeStruct((quads, 8, LANE), F32),
        ],
        in_specs=[
            smem, smem, whole,
            pl.BlockSpec((1, block), lambda i: (0, i)),
            columns(0), columns(1), columns(2), columns(0), columns(0),
            pl.BlockSpec((QUAD, seq, 3 * LANE), lambda i: (i, 0, 0)),
        ],
        out_specs=[
            columns(0), columns(0), columns(0),
            pl.BlockSpec((1, block), lambda i: (0, i)),
            pl.BlockSpec((QUAD, 8, LANE), lambda i: (i, 0, 0)),
            pl.BlockSpec((1, 8, LANE), lambda i: (i, 0, 0)),
        ],
        scratch_shapes=[
            pltpu.VMEM((CQ, seq, 3 * LANE), BF16),
            pltpu.VMEM((3 * LANE, 3 * LANE * CQ), BF16),
            pltpu.VMEM((QUAD, seq, HEAD_DIM), BF16),
            pltpu.VMEM((QUAD, seq, HEAD_DIM), BF16),
            pltpu.VMEM((QUAD, seq, HEAD_DIM), BF16),
            pltpu.VMEM((QUAD, seq, HEAD_DIM), BF16),
            pltpu.VMEM((CQ, seq, HEAD_DIM), BF16),
            pltpu.VMEM((3, QUAD, seq, HEAD_DIM), F32),
            pltpu.VMEM((2, seq, 3 * LANE), BF16),
            pltpu.VMEM((2, HEAD_DIM, seq), F32),
            pltpu.VMEM((CQ, LANE, LANE), F32),
        ],
        compiler_params=pltpu.CompilerParams(vmem_limit_bytes=56 * 1024 * 1024),
    )(
        docs, head_mixing.reshape(HEADS // 2, 4), pad_taps(conv_kernel[:, :, ::-1]), gain.reshape(1, width),
        projected, projected, projected, attended, d_grouped, soft,
    )
    return (
        dq, dk, dv, grad_gain.reshape(width),
        jnp.roll(grad_taps, CK // 2 + 1, axis=2)[:, :CQ, :CK][:, :, ::-1] * SCALE,
        grad_mix[:, :2, :4].reshape(HEADS // 2, 2, 2),
    )


MESH = pl.DeviceIdType.MESH


def ring_index(place, n):
    place = lax.rem(place + 2 * n, n)
    return jnp.where(place < n // 2, 2 * place, 2 * (n - 1 - place) + 1)


def ring_place(index, n):
    half = lax.div(index, 2)
    return jnp.where(lax.rem(index, 2) == 0, half, n - 1 - half)


class Ring:
    def __init__(self, n):
        self.n = n
        rep = lax.axis_index("rep")
        self.x, self.core = lax.div(rep, 2), lax.rem(rep, 2)
        index = lax.axis_index("fsdp")
        self.index = index
        self.place = ring_place(index, n)
        self.right = (rep, ring_index(self.place + 1, n))
        self.left = (rep, ring_index(self.place - 1, n))
        self.sibling = (self.x * 2 + 1 - self.core, index)
        self.across = ((1 - self.x) * 2 + self.core, index)

    def meet(self):
        barrier = pltpu.get_barrier_semaphore()
        for other in (self.right, self.left, self.sibling, self.across):
            pl.semaphore_signal(barrier, inc=1, device_id=other, device_id_type=MESH)
        pl.semaphore_wait(barrier, 4)


def send(src, dst, send_sem, recv_sem, device):
    return pltpu.make_async_remote_copy(
        src_ref=src, dst_ref=dst, send_sem=send_sem, recv_sem=recv_sem,
        device_id=device, device_id_type=MESH,
    )


def cols(start, size):
    return pl.ds(pl.multiple_of(start, LANE), size)


class Gather:
    def __init__(self, ring, weights, fulls, widths, sems):
        self.ring, self.weights, self.fulls = ring, weights, fulls
        self.axes, self.widths = zip(*widths)
        (self.own, self.ring_send, self.ring_recv, self.core_send, self.core_recv, self.x_send, self.x_recv) = sems

    def windows(self, i):
        ring = self.ring
        half = self.weights[i].shape[self.axes[i]] // 2
        w = self.widths[i]
        base = ring.core * half
        part = half - 2 * w
        first = base + jnp.where(ring.x == 0, 0, half - w)
        second = base + jnp.where(ring.x == 0, w, half - 2 * w)
        give = base + jnp.where(ring.x == 0, 0, half - part)
        take = base + jnp.where(ring.x == 0, half - part, 0)
        return w, part, first, second, give, take

    def block(self, i, index, start, width):
        rows = self.weights[i].shape[0]
        if self.axes[i] == 0:
            return self.fulls[i].at[pl.ds(pl.multiple_of(index * rows + start, 16), width), :]
        return self.fulls[i].at[pl.ds(pl.multiple_of(index * rows, 16), rows), cols(start, width)]

    def piece(self, i, start, width):
        if self.axes[i] == 0:
            return self.weights[i].at[pl.ds(pl.multiple_of(start, 16), width), :]
        return self.weights[i].at[:, cols(start, width)]

    def ring_copy(self, i, d, k, source):
        ring = self.ring
        w, _, first, second, _, _ = self.windows(i)
        start = second if d else first
        index = ring_index(ring.place + (k if d else -k), ring.n)
        there = self.block(i, index, start, w)
        src = self.piece(i, start, w) if source else there
        return send(src, there, self.ring_send.at[i, d, k], self.ring_recv.at[i, d, k], ring.left if d else ring.right)

    def core_copy(self, i, d, k):
        ring = self.ring
        w, part, first, second, _, take = self.windows(i)
        start, width = ((first, w), (second, w), (take, part))[d]
        index = ring_index(ring.place + (k + 1 if d == 1 else -k - 1), ring.n)
        there = self.block(i, index, start, width)
        return send(there, there, self.core_send.at[i, d, k], self.core_recv.at[i, d, k], ring.sibling)

    def x_copy(self, i, k):
        ring = self.ring
        _, part, _, _, give, _ = self.windows(i)
        there = self.block(i, ring_index(ring.place - k - 1, ring.n), give, part)
        return send(there, there, self.x_send.at[i, k], self.x_recv.at[i, k], ring.across)

    def own_copy(self, i):
        rows = self.weights[i].shape[0]
        there = self.fulls[i].at[pl.ds(pl.multiple_of(self.ring.index * rows, 16), rows), :]
        return send(self.weights[i], there, self.own.at[0, i], self.own.at[1, i], self.ring.sibling)

    def has_part(self, i):
        return self.weights[i].shape[self.axes[i]] // 2 > 2 * self.widths[i]

    def start(self):
        for i in range(len(self.weights)):
            for d in range(2):
                self.ring_copy(i, d, 0, True).start()
        for i in range(len(self.weights)):
            self.own_copy(i).start()

    def step(self, k):
        last = self.ring.n - 2
        for i in range(len(self.weights)):
            for d in range(2):
                self.ring_copy(i, d, k, False).wait_recv()

                @pl.when(k < last)
                def _():
                    self.ring_copy(i, d, k + 1, False).start()

                if d == 0 and self.has_part(i):
                    self.x_copy(i, k).start()
                self.core_copy(i, d, k).start()

            if self.has_part(i):
                @pl.when(k >= LAG)
                def _():
                    self.pass_on(i, k - LAG)

    def pass_on(self, i, k):
        self.x_copy(i, k).wait_recv()
        self.core_copy(i, 2, k).start()

    def finish(self):
        last = self.ring.n - 2
        for k in range(max(0, last + 1 - LAG), last + 1):
            for i in range(len(self.weights)):
                if self.has_part(i):
                    self.pass_on(i, k)

        def settle(k, carry):
            for i in range(len(self.weights)):
                for d in range(2):
                    self.ring_copy(i, d, k, False).wait_send()
                    self.core_copy(i, d, k).wait()
                if self.has_part(i):
                    self.x_copy(i, k).wait_send()
                    self.core_copy(i, 2, k).wait()
            return carry

        lax.fori_loop(0, self.ring.n - 1, settle, 0)
        for i in range(len(self.weights)):
            self.own_copy(i).wait()

    @staticmethod
    def scratch(count, n):
        dma = pltpu.SemaphoreType.DMA
        return [
            dma((2, count)), dma((count, 2, n - 1)), dma((count, 2, n - 1)),
            dma((count, 3, n - 1)), dma((count, 3, n - 1)), dma((count, n - 1)), dma((count, n - 1)),
        ]


def gather_kernel(n, count, widths, *refs):
    ring = Ring(n)
    gather = Gather(ring, refs[:count], refs[count : 2 * count], widths, refs[2 * count :])
    ring.meet()
    gather.start()

    def one(k, carry):
        gather.step(k)
        return carry

    lax.fori_loop(0, n - 1, one, 0)
    gather.finish()


def share(shape):
    rows, columns = shape
    axis, unit = (0, 16) if rows % 64 == 0 else (1, LANE)
    units = (rows, columns)[axis] // 2 // unit
    return axis, -(-units // 3) * unit


def gather_all(weights, n, collective):
    count = len(weights)
    widths = [share(w.shape) for w in weights]
    anywhere = pl.BlockSpec(memory_space=pl.ANY)
    return pl.pallas_call(
        functools.partial(gather_kernel, n, count, widths),
        out_shape=[jax.ShapeDtypeStruct((n * w.shape[0], w.shape[1]), w.dtype) for w in weights],
        in_specs=[anywhere] * count,
        out_specs=[anywhere] * count,
        scratch_shapes=Gather.scratch(count, n),
        compiler_params=pltpu.CompilerParams(collective_id=collective, has_side_effects=True),
    )(*weights)


class Reduce:
    def __init__(self, ring, grads, totals, others, shapes, scratch):
        self.ring, self.grads, self.totals, self.others, self.shapes = ring, grads, totals, others, shapes
        count = len(grads)
        pairs = 2 * count
        self.slots = [scratch[2 * i : 2 * i + 2] for i in range(count)]
        scratch = scratch[pairs:]
        self.mine = [scratch[2 * i : 2 * i + 2] for i in range(count)]
        scratch = scratch[pairs:]
        self.twin = [scratch[2 * i : 2 * i + 2] for i in range(count)]
        scratch = scratch[pairs:]
        self.plane = [scratch[2 * i : 2 * i + 2] for i in range(count)]
        scratch = scratch[pairs:]
        (self.load, self.ring_send, self.ring_recv, self.core_send, self.core_recv,
         self.end_send, self.end_recv, self.keep) = scratch

    def owner(self, d, j):
        ring = self.ring
        return ring_index(ring.place + (j + 1 if d else -j - 1), ring.n)

    def window(self, i, d, core):
        rows, columns = self.shapes[i]
        w = columns // 4
        return core * 2 * w + d * w, w

    def rows(self, i, index):
        rows = self.shapes[i][0]
        return pl.ds(pl.multiple_of(index * rows, 16), rows)

    def core_copy(self, i, d, j):
        ring = self.ring
        start, w = self.window(i, d, 1 - ring.core)
        rows = self.rows(i, self.owner(d, j))
        return send(
            self.grads[i].at[rows, cols(start, w)], self.others[i].at[rows, d * w : (d + 1) * w],
            self.core_send.at[i, d, j], self.core_recv.at[i, d, j], ring.sibling,
        )

    def loads(self, i, d, j):
        start, w = self.window(i, d, self.ring.core)
        rows = self.rows(i, self.owner(d, j))
        return (
            pltpu.make_async_copy(self.grads[i].at[rows, cols(start, w)], self.mine[i][d], self.load.at[i, d, 0]),
            pltpu.make_async_copy(self.others[i].at[rows, d * w : (d + 1) * w], self.twin[i][d], self.load.at[i, d, 1]),
        )

    def ring_copy(self, i, d, j):
        ring = self.ring
        return send(
            self.slots[i][d].at[j], self.slots[i][d].at[j + 1],
            self.ring_send.at[i, d, j], self.ring_recv.at[i, d, j + 1], ring.left if d else ring.right,
        )

    def arrived(self, i, d, j):
        ring = self.ring
        return send(
            self.slots[i][d].at[j], self.slots[i][d].at[j],
            self.ring_send.at[i, d, j], self.ring_recv.at[i, d, j], ring.left if d else ring.right,
        )

    def across_copy(self, i, d):
        return send(
            self.slots[i][d].at[self.ring.n - 1], self.plane[i][d],
            self.end_send.at[i, d, 0], self.end_recv.at[i, d, 0], self.ring.across,
        )

    def final_copies(self, i, d):
        start, w = self.window(i, d, self.ring.core)
        there = self.totals[i].at[:, cols(start, w)]
        return (
            send(self.mine[i][d], there, self.end_send.at[i, d, 1], self.end_recv.at[i, d, 1], self.ring.sibling),
            pltpu.make_async_copy(self.mine[i][d], there, self.keep.at[i, d]),
        )

    def each(self):
        return [(i, d) for i in range(len(self.grads)) for d in range(2)]

    def start(self):
        def give(j, carry):
            for i, d in self.each():
                self.core_copy(i, d, j).start()
            return carry

        lax.fori_loop(0, self.ring.n, give, 0)
        for i, d in self.each():
            self.fetch(i, d, 0)

    def fetch(self, i, d, j):
        own, other = self.loads(i, d, j)
        own.start()
        self.core_copy(i, d, j).wait_recv()
        other.start()

    def item(self, j):
        last = self.ring.n - 1
        for i, d in self.each():
            for copy in self.loads(i, d, j):
                copy.wait()
            slot = self.slots[i][d]
            both = self.mine[i][d][...].astype(F32) + self.twin[i][d][...].astype(F32)

            @pl.when(j == 0)
            def _():
                slot[j] = both.astype(BF16)

            @pl.when(j > 0)
            def _():
                self.arrived(i, d, j).wait_recv()
                slot[j] = (slot[j].astype(F32) + both).astype(BF16)

            @pl.when(j < last)
            def _():
                self.ring_copy(i, d, j).start()
                self.fetch(i, d, j + 1)

    def finish(self):
        last = self.ring.n - 1
        for i, d in self.each():
            self.across_copy(i, d).start()
        for i, d in self.each():
            self.across_copy(i, d).wait()
            both = self.slots[i][d][last].astype(F32) + self.plane[i][d][...].astype(F32)
            self.mine[i][d][...] = both.astype(BF16)
            for copy in self.final_copies(i, d):
                copy.start()
        for i, d in self.each():
            for copy in self.final_copies(i, d):
                copy.wait()

        def settle(j, carry):
            for i, d in self.each():
                self.core_copy(i, d, j).wait_send()

                @pl.when(j < last)
                def _():
                    self.ring_copy(i, d, j).wait_send()

            return carry

        lax.fori_loop(0, self.ring.n, settle, 0)

    @staticmethod
    def scratch(shapes, n):
        dma = pltpu.SemaphoreType.DMA
        count = len(shapes)
        blocks = [(rows, columns // 4) for rows, columns in shapes for _ in range(2)]
        return (
            [pltpu.VMEM((n,) + b, BF16) for b in blocks]
            + [pltpu.VMEM(b, BF16) for b in blocks] * 3
            + [
                dma((count, 2, 2)), dma((count, 2, n)), dma((count, 2, n)), dma((count, 2, n)), dma((count, 2, n)),
                dma((count, 2, 2)), dma((count, 2, 2)), dma((count, 2)),
            ]
        )


def reduce_kernel(n, shapes, *refs):
    count = len(shapes)
    ring = Ring(n)
    reduce = Reduce(ring, refs[:count], refs[count : 2 * count], refs[2 * count : 3 * count], shapes, refs[3 * count :])
    ring.meet()
    reduce.start()

    def one(j, carry):
        reduce.item(j)
        return carry

    lax.fori_loop(0, n, one, 0)
    reduce.finish()


def reduce_all(grads, n, collective):
    count = len(grads)
    shapes = [(g.shape[0] // n, g.shape[1]) for g in grads]
    anywhere = pl.BlockSpec(memory_space=pl.ANY)
    results = pl.pallas_call(
        functools.partial(reduce_kernel, n, shapes),
        out_shape=[jax.ShapeDtypeStruct(s, BF16) for s in shapes]
        + [jax.ShapeDtypeStruct((n * rows, columns // 2), BF16) for rows, columns in shapes],
        in_specs=[anywhere] * count,
        out_specs=[anywhere] * (2 * count),
        scratch_shapes=Reduce.scratch(shapes, n),
        compiler_params=pltpu.CompilerParams(
            collective_id=collective, has_side_effects=True, vmem_limit_bytes=60 * 1024 * 1024
        ),
    )(*grads)
    return results[:count]


def rms_norm(values, gains):
    return values * lax.rsqrt(jnp.mean(values * values, axis=-1, keepdims=True) + EPSILON) * gains


def swiglu(gate_up):
    middle_col = gate_up.shape[1] // 2
    return jax.nn.silu(gate_up[:, :middle_col]) * gate_up[:, middle_col:]


def project(operand, weight):
    return jnp.dot(operand, weight, preferred_element_type=F32)


def project_back(upstream, weight):
    return lax.dot_general(
        upstream, weight, (((1,), (1,)), ((), ())), preferred_element_type=F32
    )


def weight_grad(operand, upstream):
    return lax.dot_general(
        operand, upstream, (((0,), (0,)), ((), ())), preferred_element_type=F32
    ).astype(BF16)


def body(
    layer_input,
    first_gain,
    qkv_weight,
    conv_kernel,
    head_mixing,
    group_gain,
    out_weight,
    second_gain,
    inner_weight,
    down_weight,
    doc_lengths,
    cotangent,
):
    n = lax.axis_size("fsdp")
    (qkv_weight,) = gather_all([qkv_weight], n, 0)
    out_weight, inner_weight, down_weight = gather_all([out_weight, inner_weight, down_weight], n, 1)
    inputs = layer_input.astype(jnp.float32)
    normed_value, first_pull = jax.vjp(rms_norm, inputs, first_gain)
    normed = normed_value.astype(jnp.bfloat16)
    projected = project(normed, qkv_weight).astype(jnp.bfloat16)
    grouped, attended, soft = attend_forward(
        projected, conv_kernel, head_mixing, doc_lengths, group_gain
    )
    middle = inputs + project(grouped, out_weight)
    second_value, second_pull = jax.vjp(rms_norm, middle, second_gain)
    second = second_value.astype(jnp.bfloat16)
    gate_up = project(second, inner_weight)
    hidden_value, swiglu_pull = jax.vjp(swiglu, gate_up)
    hidden = hidden_value.astype(jnp.bfloat16)
    layer_output = (middle + project(hidden, down_weight)).astype(jnp.bfloat16)
    upstream = cotangent.astype(jnp.float32)
    grad_down = weight_grad(hidden, cotangent)
    d_hidden = project_back(cotangent, down_weight)
    d_gate_up = swiglu_pull(d_hidden)[0].astype(jnp.bfloat16)
    grad_inner = weight_grad(second, d_gate_up)
    d_second = project_back(d_gate_up, inner_weight)
    d_middle, grad_second = second_pull(d_second)
    d_middle = upstream + d_middle
    d_branch = d_middle.astype(jnp.bfloat16)
    grad_proj = weight_grad(grouped, d_branch)
    d_grouped = project_back(d_branch, out_weight)
    d_query, d_keys, d_values, grad_group, grad_kernel, grad_mixing = attend_backward(
        projected, conv_kernel, head_mixing, doc_lengths, group_gain, attended, d_grouped, soft
    )
    d_projected = jnp.concatenate([d_query, d_keys, d_values], axis=1)
    grad_qkv = weight_grad(normed, d_projected)
    d_normed = project_back(d_projected, qkv_weight)
    d_inputs, grad_first = first_pull(d_normed)
    grad_input = d_middle + d_inputs
    small = lax.psum(
        (grad_first, grad_kernel, grad_mixing, grad_group, grad_second), ("rep", "fsdp")
    )
    shards = reduce_all([grad_down, grad_inner, grad_proj, grad_qkv], n, 2)
    shards = [shards[i].astype(F32) for i in (3, 2, 1, 0)]
    return (
        layer_output,
        grad_input,
        small[0],
        shards[0],
        small[1],
        small[2],
        small[3],
        shards[1],
        small[4],
        shards[2],
        shards[3],
    )


def solution(mesh):
    placed = (
        P(("rep", "fsdp"), None),
        P(),
        P("fsdp", None),
        P(),
        P(),
        P(),
        P("fsdp", None),
        P(),
        P("fsdp", None),
        P("fsdp", None),
        P(("rep", "fsdp"), None),
        P(("rep", "fsdp"), None),
    )
    return jax.shard_map(
        body,
        mesh=mesh,
        in_specs=placed,
        out_specs=(
            P(("rep", "fsdp"), None),
            P(("rep", "fsdp"), None),
            P(),
            P("fsdp", None),
            P(),
            P(),
            P(),
            P("fsdp", None),
            P(),
            P("fsdp", None),
            P("fsdp", None),
        ),
        check_vma=False,
    )
```

```python
import functools, math
import jax, jax.numpy as jnp
from jax import lax
from jax.experimental import pallas as pl
from jax.experimental.pallas import tpu as pltpu
from jax.sharding import PartitionSpec as P

HEADS = 16
HEAD_DIM = 96
CQ = 6
CK = 11
EPSILON = 1e-05
LANE = 128
QUAD = 4
LAG = 1
LEAD = 3
SCALE = 1.0 / math.sqrt(HEAD_DIM)
F32 = jnp.float32
BF16 = jnp.bfloat16


def row_sets(seq):
    return [
        (r, min(r + LANE, 3 * LANE), max(0, r - 2 * LANE)) for r in range(0, seq, LANE)
    ]


def nt(a, b):
    return lax.dot_general(a, b, (((1,), (1,)), ((), ())), preferred_element_type=F32)


def nn(a, b):
    return jnp.dot(a, b, preferred_element_type=F32)


def fill_masks(docs_ref, masks, seq):
    ends = []
    total = jnp.int32(0)
    for d in range(docs_ref.shape[1] - 1):
        total = total + docs_ref[0, d]
        ends.append(total)
    for r0, width, c0 in row_sets(seq):
        rows = r0 + lax.broadcasted_iota(jnp.int32, (LANE, 1), 0)
        cols = c0 + lax.broadcasted_iota(jnp.int32, (1, width), 1)
        row_doc = sum((rows >= e).astype(jnp.int32) for e in ends)
        col_doc = sum((cols >= e).astype(jnp.int32) for e in ends)
        same = row_doc == col_doc
        for a in range(CQ):
            masks[a, r0 : r0 + LANE, :width] = jnp.where(
                same & (rows - cols >= a), 1.0, 0.0
            ).astype(BF16)


def circulant_masks():
    gap = lax.broadcasted_iota(jnp.int32, (LANE, LANE), 1) - lax.broadcasted_iota(
        jnp.int32, (LANE, LANE), 0
    )
    half = CK // 2
    return (jnp.abs(gap) <= half, gap <= half - LANE, gap >= LANE - half)


def circulant(taps):
    wide = jnp.broadcast_to(taps, (LANE, LANE))
    return pltpu.roll(wide, 0, axis=1, stride=1, stride_axis=0)


def fill_toeplitz(taps_ref, head, band, blocks):
    near, after, before = circulant_masks()
    for a in range(CQ):
        whole = circulant(taps_ref[head, a : a + 1, :])
        parts = {
            0: jnp.where(near, whole, 0.0).astype(BF16),
            1: jnp.where(after, whole, 0.0).astype(BF16),
            -1: jnp.where(before, whole, 0.0).astype(BF16),
        }
        for r in range(blocks):
            for c in range(blocks):
                part = parts.get(c - r)
                if part is not None:
                    yield a, r, c, part


def fill_forward_band(taps_ref, head, band):
    for a, r, c, part in fill_toeplitz(taps_ref, head, band, 3):
        at = (r * CQ + a) * LANE
        band[at : at + LANE, c * LANE : (c + 1) * LANE] = part


def fill_backward_band(taps_ref, head, band):
    for a, r, c, part in fill_toeplitz(taps_ref, head, band, 3):
        at = (c * CQ + a) * LANE
        band[r * LANE : (r + 1) * LANE, at : at + LANE] = part


def shifted_rows(query):
    wide = query.astype(F32)
    return [query] + [pltpu.roll(wide, a, axis=0).astype(BF16) for a in range(1, CQ)]


def masked_scores(shifted, keys, masks, r0, width, c0):
    left = jnp.concatenate([shifted[a, r0 : r0 + LANE] for a in range(CQ)], axis=0)
    scores = nt(left, keys[c0 : c0 + width]).astype(BF16)
    return left, [
        scores[a * LANE : (a + 1) * LANE] * masks[a, r0 : r0 + LANE, :width]
        for a in range(CQ)
    ]


def by_window(parts, width):
    return jnp.concatenate(
        [
            parts[a][:, b * LANE : (b + 1) * LANE]
            for b in range(width // LANE)
            for a in range(CQ)
        ],
        axis=1,
    )


def forward_kernel(
    n, first_widths, rest_widths, docs_ref, mix_ref, taps_ref, gain_ref, input_ref, first_gain_ref, second_gain_ref, *refs
):
    refs = list(refs)

    def take(size):
        taken = refs[:size]
        del refs[:size]
        return taken

    first_count, rest_count = len(first_widths), len(rest_widths)
    first_weights, rest_weights = take(first_count), take(rest_count)
    grouped_ref, attended_ref, soft_ref, normed_ref, middle_ref, second_ref, projected = take(7)
    first_fulls, rest_fulls = take(first_count), take(rest_count)
    masks, band, qs, ks, vs, shifted, outs = take(7)
    blocks, block_weight, every, out_weight, block_in, block_out, out_in = take(7)
    ring = Ring(n)
    sems = len(Gather.scratch(first_count, n))
    first = Gather(ring, first_weights, first_fulls, first_widths, take(sems))
    rest = Gather(ring, rest_weights, rest_fulls, rest_widths, take(sems))
    seq = input_ref.shape[0]
    quad = pl.program_id(0)
    quads = HEADS // QUAD
    size = QUAD * HEAD_DIM
    count = 3 * quads

    def block_copy(t):
        slot = lax.rem(t, 2)
        return pltpu.make_async_copy(first_fulls[0].at[:, cols(t * size, size)], block_weight.at[slot], block_in.at[slot])

    def block_save(t):
        return pltpu.make_async_copy(blocks.at[t], projected.at[:, cols(t * size, size)], block_out.at[t])

    out_copy = pltpu.make_async_copy(first_fulls[1], out_weight, out_in)

    @pl.when(quad == 0)
    def _():
        ring.meet()
        first.start()
        fill_masks(docs_ref, masks, seq)
        band[...] = jnp.zeros_like(band)
        values = input_ref[...].astype(F32)
        scale = lax.rsqrt(jnp.mean(values * values, axis=1, keepdims=True) + EPSILON)
        normed_ref[...] = (values * scale * first_gain_ref[...]).astype(BF16)

        def one(k, carry):
            first.step(k)
            pl.when(k == n - 3)(rest.start)
            return carry

        lax.fori_loop(0, n - 1, one, 0)
        first.finish()
        block_copy(0).start()
        out_copy.start()

        def project_block(t, carry):
            pl.when(t < count - 1)(lambda: block_copy(t + 1).start())
            block_copy(t).wait()
            blocks[t] = nn(normed_ref[...], block_weight[lax.rem(t, 2)]).astype(BF16)
            block_save(t).start()
            return carry

        lax.fori_loop(0, count, project_block, 0)

    for h in range(QUAD):
        at = slice(h * HEAD_DIM, (h + 1) * HEAD_DIM)
        qs[h] = blocks[quad, :, at]
        ks[h] = blocks[quads + quad, :, at]
        vs[h] = blocks[2 * quads + quad, :, at]

    sets = row_sets(seq)

    def pair(p, carry):
        group = quad * 2 + p
        for r in range(2):
            h = 2 * p + r
            fill_forward_band(taps_ref, quad * QUAD + h, band)
            for a, rows in enumerate(shifted_rows(qs[h])):
                shifted[a] = rows
            keys = ks[h]
            lefts = []
            for r0, width, c0 in sets:
                _, parts = masked_scores(shifted, keys, masks, r0, width, c0)
                lefts.append((width, by_window(parts, width)))
            convs = []
            i = 0
            while i < len(sets):
                width = sets[i][1]
                run = 1
                while i + run < len(sets) and sets[i + run][1] == width:
                    run += 1
                left = jnp.concatenate([lefts[i + m][1] for m in range(run)], axis=0)
                conv = nn(left, band[: width * CQ, :width])
                convs += [conv[m * LANE : (m + 1) * LANE] for m in range(run)]
                i += run
            for (r0, width, c0), conv in zip(sets, convs):
                logits = jnp.where(
                    masks[0, r0 : r0 + LANE, :width].astype(F32) > 0, conv, -1e30
                )
                weights = jnp.exp(logits - jnp.max(logits, axis=1, keepdims=True))
                soft = weights * (1.0 / jnp.sum(weights, axis=1, keepdims=True))
                soft_ref[h, r0 : r0 + LANE, :width] = soft.astype(BF16)
        for r in range(2):
            h = 2 * p + r
            values = vs[h]
            for r0, width, c0 in sets:
                mixed = (
                    mix_ref[group, 2 * r] * soft_ref[2 * p, r0 : r0 + LANE, :width].astype(F32)
                    + mix_ref[group, 2 * r + 1] * soft_ref[2 * p + 1, r0 : r0 + LANE, :width].astype(F32)
                ).astype(BF16)
                outs[h, r0 : r0 + LANE] = nn(mixed, values[c0 : c0 + width])
        for k in in_turn(group, HEADS // 2, n - 1):
            pl.when(k < n - 1)(functools.partial(rest.step, k))
        return carry

    lax.fori_loop(0, 2, pair, 0)
    wholes, grouped = [], []
    for h in range(QUAD):
        attended = outs[h]
        centred = attended - jnp.mean(attended, axis=1, keepdims=True)
        var = jnp.mean(centred * centred, axis=1, keepdims=True)
        wholes.append(attended)
        grouped.append(centred * lax.rsqrt(var + EPSILON))
    attended_ref[...] = jnp.concatenate(wholes, axis=1)
    every[quad] = (jnp.concatenate(grouped, axis=1) * gain_ref[...]).astype(BF16)
    grouped_ref[...] = every[quad]

    @pl.when(quad == quads - 1)
    def _():
        out_copy.wait()
        branch = nn(jnp.concatenate([every[i] for i in range(quads)], axis=1), out_weight[...])
        middle = input_ref[...].astype(F32) + branch
        scale = lax.rsqrt(jnp.mean(middle * middle, axis=1, keepdims=True) + EPSILON)
        middle_ref[...] = middle
        second_ref[...] = (middle * scale * second_gain_ref[...]).astype(BF16)

        def saved(t, carry):
            block_save(t).wait()
            return carry

        lax.fori_loop(0, count, saved, 0)
        rest.finish()


def pad_taps(kernel):
    padded = jnp.pad(kernel * SCALE, ((0, 0), (0, 2), (0, LANE - CK)))
    return jnp.roll(padded, -(CK // 2), axis=2)


def in_turn(turn, turns, steps):
    each = -(-steps // turns)
    return [turn * each + t for t in range(each)]


def attend_forward(layer_input, conv_kernel, head_mixing, docs, gains, first, rest, n, collective):
    seq, width = layer_input.shape
    block = QUAD * HEAD_DIM
    quads = HEADS // QUAD
    first_widths, rest_widths = [share(w.shape) for w in first], [share(w.shape) for w in rest]
    whole = pl.BlockSpec(memory_space=pltpu.VMEM)
    smem = pl.BlockSpec(memory_space=pltpu.SMEM)
    anywhere = pl.BlockSpec(memory_space=pl.ANY)
    columns = pl.BlockSpec((seq, block), lambda i: (0, i))
    dma = pltpu.SemaphoreType.DMA
    first_gain, group_gain, second_gain = [g.reshape(1, width) for g in gains]
    results = pl.pallas_call(
        functools.partial(forward_kernel, n, first_widths, rest_widths),
        grid=(quads,),
        out_shape=[
            jax.ShapeDtypeStruct((seq, width), BF16),
            jax.ShapeDtypeStruct((seq, width), F32),
            jax.ShapeDtypeStruct((HEADS, seq, 3 * LANE), BF16),
            jax.ShapeDtypeStruct((seq, width), BF16),
            jax.ShapeDtypeStruct((seq, width), F32),
            jax.ShapeDtypeStruct((seq, width), BF16),
            jax.ShapeDtypeStruct((seq, 3 * width), BF16),
        ]
        + [jax.ShapeDtypeStruct((n * w.shape[0], w.shape[1]), w.dtype) for w in first + rest],
        in_specs=[smem, smem, whole, pl.BlockSpec((1, block), lambda i: (0, i)), whole, whole, whole]
        + [anywhere] * len(first + rest),
        out_specs=[
            columns, columns,
            pl.BlockSpec((QUAD, seq, 3 * LANE), lambda i: (i, 0, 0)),
            whole, whole, whole,
        ]
        + [anywhere] * (1 + len(first + rest)),
        scratch_shapes=[
            pltpu.VMEM((CQ, seq, 3 * LANE), BF16),
            pltpu.VMEM((3 * LANE * CQ, 3 * LANE), BF16),
            pltpu.VMEM((QUAD, seq, HEAD_DIM), BF16),
            pltpu.VMEM((QUAD, seq, HEAD_DIM), BF16),
            pltpu.VMEM((QUAD, seq, HEAD_DIM), BF16),
            pltpu.VMEM((CQ, seq, HEAD_DIM), BF16),
            pltpu.VMEM((QUAD, seq, HEAD_DIM), F32),
            pltpu.VMEM((3 * quads, seq, block), BF16),
            pltpu.VMEM((2, width, block), BF16),
            pltpu.VMEM((quads, seq, block), BF16),
            pltpu.VMEM((width, width), BF16),
            dma((2,)), dma((3 * quads,)), dma,
        ]
        + Gather.scratch(len(first), n)
        + Gather.scratch(len(rest), n),
        compiler_params=pltpu.CompilerParams(
            collective_id=collective, has_side_effects=True, vmem_limit_bytes=60 * 1024 * 1024
        ),
    )(
        docs, head_mixing.reshape(HEADS // 2, 4), pad_taps(conv_kernel), group_gain, layer_input, first_gain, second_gain,
        *first, *rest,
    )
    return results[:7], results[7 : 7 + len(first)], results[7 + len(first) :]


def backward_kernel(
    n, specs, docs_ref, mix_ref, taps_ref, gain_ref, q_ref, k_ref, v_ref, attended_ref, d_grouped_ref, soft_ref, *refs
):
    count = len(specs)
    grads, refs = refs[:count], refs[count:]
    d_projected, grad_gain_ref, grad_taps_ref, grad_mix_ref = refs[:4]
    sums, others, refs = refs[4 : 4 + count], refs[4 + count : 4 + 2 * count], refs[4 + 2 * count :]
    masks, band, qs, ks, vs, ds, shifted, d_heads, d_rows, d_cols, diagonal, leaving, leave_sem = refs[:13]
    reduce = Reduce(Ring(n), grads, sums, others, specs, refs[13:])
    seq = q_ref.shape[0]
    quad = pl.program_id(0)

    @pl.when(quad == 0)
    def _():
        reduce.clear()
        reduce.ring.meet()
        reduce.start()

    @pl.when(quad == 0)
    def _():
        fill_masks(docs_ref, masks, seq)
        band[...] = jnp.zeros_like(band)

    gains = []
    for h in range(QUAD):
        at = slice(h * HEAD_DIM, (h + 1) * HEAD_DIM)
        qs[h] = q_ref[:, at]
        ks[h] = k_ref[:, at]
        vs[h] = v_ref[:, at]
        attended = attended_ref[:, at]
        d_grouped = d_grouped_ref[:, at]
        centred = attended - jnp.mean(attended, axis=1, keepdims=True)
        var = jnp.mean(centred * centred, axis=1, keepdims=True)
        scale = lax.rsqrt(var + EPSILON)
        unit = centred * scale
        gains.append(jnp.sum(d_grouped * unit, axis=0, keepdims=True))
        w = d_grouped * gain_ref[:, at]
        d_attended = scale * (
            w
            - jnp.mean(w, axis=1, keepdims=True)
            - unit * jnp.mean(w * unit, axis=1, keepdims=True)
        )
        ds[h] = d_attended.astype(BF16)
    grad_gain_ref[...] = jnp.concatenate(gains, axis=1)
    grad_taps_ref[...] = jnp.zeros_like(grad_taps_ref)
    grad_mix_ref[...] = jnp.zeros_like(grad_mix_ref)

    sets = row_sets(seq)
    up = lax.broadcasted_iota(jnp.int32, (LANE, LANE), 0)
    across = lax.broadcasted_iota(jnp.int32, (LANE, LANE), 1)
    flip = jnp.where(up + across == LANE - 1, 1.0, 0.0).astype(BF16)
    gap = up + across - (LANE - 1)
    keeps = {0: jnp.abs(gap) <= CK // 2, 1: gap <= CK // 2 - LANE, -1: gap >= LANE - CK // 2}

    def pair(p, carry):
        group = quad * 2 + p
        mix = [[mix_ref[group, 2 * r + s] for s in range(2)] for r in range(2)]
        upstream_t = [ds[2 * p + r].T for r in range(2)]
        grad_mix = [[jnp.zeros((1, 1), F32) for _ in range(2)] for _ in range(2)]
        for r in range(2):
            d_cols[r] = jnp.zeros_like(d_cols[r])
        for r0, width, c0 in sets:
            rows = slice(r0, r0 + LANE)
            soft = [soft_ref[2 * p + s, rows, :width].astype(F32) for s in range(2)]
            d_prob, sums = [], []
            for r in range(2):
                dp = nt(ds[2 * p + r, rows], vs[2 * p + r, c0 : c0 + width])
                d_prob.append(dp)
                sums.append([jnp.sum(dp * soft[s], axis=1, keepdims=True) for s in range(2)])
                for s in range(2):
                    grad_mix[r][s] += jnp.sum(sums[r][s], axis=0, keepdims=True)
                mixed = (mix[r][0] * soft[0] + mix[r][1] * soft[1]).astype(BF16)
                d_cols[r, :, c0 : c0 + width] += nn(upstream_t[r][:, r0 : r0 + LANE], mixed)
            for s in range(2):
                d_soft = mix[0][s] * d_prob[0] + mix[1][s] * d_prob[1]
                inner = mix[0][s] * sums[0][s] + mix[1][s] * sums[1][s]
                d_conv = soft[s] * (d_soft - inner)
                d_rows[s, rows, :width] = d_conv.astype(BF16)
        lane = lax.broadcasted_iota(jnp.int32, (1, LANE), 1)
        line = jnp.zeros((1, LANE), F32)
        for r in range(2):
            for s in range(2):
                line = line + jnp.where(lane == 2 * r + s, grad_mix[r][s], 0.0)
        grad_mix_ref[0, pl.ds(p, 1), :] = line
        for r in range(2):
            d_heads[2, 2 * p + r] = d_cols[r].T

        for r in range(2):
            h = 2 * p + r
            fill_backward_band(taps_ref, quad * QUAD + h, band)
            for a, moved in enumerate(shifted_rows(qs[h])):
                shifted[a] = moved
            keys = ks[h]
            d_cols[0] = jnp.zeros_like(d_cols[0])
            diagonal[...] = jnp.zeros_like(diagonal)
            d_query = []
            for r0, width, c0 in sets:
                rows = slice(r0, r0 + LANE)
                left, parts = masked_scores(shifted, keys, masks, r0, width, c0)
                d_conv = d_rows[r, rows, :width]
                blocks = width // LANE
                flipped = jnp.concatenate(
                    [
                        nt(flip, d_conv[:, b * LANE : (b + 1) * LANE]).astype(BF16)
                        for b in range(blocks)
                    ],
                    axis=0,
                )
                taken = nn(flipped, by_window(parts, width))
                for a in range(CQ):
                    total = diagonal[a]
                    for jb in range(blocks):
                        for qb in range(blocks):
                            if abs(jb - qb) > 1:
                                continue
                            at = (qb * CQ + a) * LANE
                            one = taken[jb * LANE : (jb + 1) * LANE, at : at + LANE]
                            total = total + jnp.where(keeps[qb - jb], one, 0.0)
                    diagonal[a] = total
                spread = nn(d_conv, band[:width, : width * CQ]).astype(BF16)
                stacked = jnp.concatenate(
                    [
                        jnp.concatenate(
                            [
                                spread[:, (b * CQ + a) * LANE : (b * CQ + a + 1) * LANE]
                                for b in range(blocks)
                            ],
                            axis=1,
                        )
                        * masks[a, rows, :width]
                        for a in range(CQ)
                    ],
                    axis=0,
                )
                d_query.append(nn(stacked, keys[c0 : c0 + width]))
                d_cols[0, :, c0 : c0 + width] += nn(left.T, stacked)
            total = None
            for a in range(CQ):
                whole = jnp.concatenate([d[a * LANE : (a + 1) * LANE] for d in d_query], axis=0)
                if a:
                    whole = pltpu.roll(whole, seq - a, axis=0)
                total = whole if total is None else total + whole
            d_heads[0, h] = total
            d_heads[1, h] = d_cols[0].T
            for a in range(CQ):
                aligned = pltpu.roll(diagonal[a], 0, axis=1, stride=1, stride_axis=0)
                grad_taps_ref[h, a : a + 1, :] = jnp.sum(aligned, axis=0, keepdims=True)
            work = reduce.each()
            middle = len(work) // 2
            for j in in_turn(group, HEADS // 2, n):
                pl.when(j < n)(functools.partial(reduce.item, j, work[middle:] if r else work[:middle]))
        return carry

    lax.fori_loop(0, 2, pair, 0)
    quads = HEADS // QUAD
    block = QUAD * HEAD_DIM

    def leave(part):
        there = d_projected.at[:, cols((part * quads + quad) * block, block)]
        return pltpu.make_async_copy(leaving.at[part], there, leave_sem.at[part])

    for part in range(3):
        pl.when(quad > 0)(leave(part).wait)
        leaving[part] = jnp.concatenate([d_heads[part, h] for h in range(QUAD)], axis=1).astype(BF16)
        leave(part).start()

    @pl.when(quad == quads - 1)
    def _():
        for part in range(3):
            leave(part).wait()

    @pl.when(quad == pl.num_programs(0) - 1)
    def _():
        reduce.finish()


def attend_backward(projected, conv_kernel, head_mixing, docs, gain, attended, d_grouped, soft, grads, n, collective):
    seq = projected.shape[0]
    width = projected.shape[1] // 3
    block = QUAD * HEAD_DIM
    quads = HEADS // QUAD
    count = len(grads)
    specs = Reduce.specs_of(grads, n, True)
    anywhere = pl.BlockSpec(memory_space=pl.ANY)
    whole = pl.BlockSpec(memory_space=pltpu.VMEM)
    smem = pl.BlockSpec(memory_space=pltpu.SMEM)

    def columns(first):
        return pl.BlockSpec((seq, block), lambda i: (0, first * quads + i))

    results = pl.pallas_call(
        functools.partial(backward_kernel, n, specs),
        grid=(quads,),
        out_shape=[
            jax.ShapeDtypeStruct((seq, 3 * width), BF16),
            jax.ShapeDtypeStruct((1, width), F32),
            jax.ShapeDtypeStruct((HEADS, 8, LANE), F32),
            jax.ShapeDtypeStruct((quads, 8, LANE), F32),
        ]
        + Reduce.results(specs, n),
        in_specs=[
            smem, smem, whole,
            pl.BlockSpec((1, block), lambda i: (0, i)),
            columns(0), columns(1), columns(2), columns(0), columns(0),
            pl.BlockSpec((QUAD, seq, 3 * LANE), lambda i: (i, 0, 0)),
        ]
        + [anywhere] * count,
        out_specs=[
            anywhere,
            pl.BlockSpec((1, block), lambda i: (0, i)),
            pl.BlockSpec((QUAD, 8, LANE), lambda i: (i, 0, 0)),
            pl.BlockSpec((1, 8, LANE), lambda i: (i, 0, 0)),
        ]
        + [anywhere] * (2 * count),
        scratch_shapes=[
            pltpu.VMEM((CQ, seq, 3 * LANE), BF16),
            pltpu.VMEM((3 * LANE, 3 * LANE * CQ), BF16),
            pltpu.VMEM((QUAD, seq, HEAD_DIM), BF16),
            pltpu.VMEM((QUAD, seq, HEAD_DIM), BF16),
            pltpu.VMEM((QUAD, seq, HEAD_DIM), BF16),
            pltpu.VMEM((QUAD, seq, HEAD_DIM), BF16),
            pltpu.VMEM((CQ, seq, HEAD_DIM), BF16),
            pltpu.VMEM((3, QUAD, seq, HEAD_DIM), F32),
            pltpu.VMEM((2, seq, 3 * LANE), BF16),
            pltpu.VMEM((2, HEAD_DIM, seq), F32),
            pltpu.VMEM((CQ, LANE, LANE), F32),
            pltpu.VMEM((3, seq, block), BF16),
            pltpu.SemaphoreType.DMA((3,)),
        ]
        + Reduce.scratch(specs, n),
        compiler_params=pltpu.CompilerParams(
            collective_id=collective, has_side_effects=True, vmem_limit_bytes=62 * 1024 * 1024
        ),
    )(
        docs, head_mixing.reshape(HEADS // 2, 4), pad_taps(conv_kernel[:, :, ::-1]), gain.reshape(1, width),
        projected, projected, projected, attended, d_grouped, soft, *grads,
    )
    d_projected, grad_gain, grad_taps, grad_mix = results[:4]
    return (
        d_projected, grad_gain, grad_taps.reshape(-1, LANE), grad_mix.reshape(-1, LANE),
    ), list(results[4 : 4 + count]), specs


MESH = pl.DeviceIdType.MESH


def ring_index(place, n):
    place = lax.rem(place + 2 * n, n)
    return jnp.where(place < n // 2, 2 * place, 2 * (n - 1 - place) + 1)


def ring_place(index, n):
    half = lax.div(index, 2)
    return jnp.where(lax.rem(index, 2) == 0, half, n - 1 - half)


class Ring:
    def __init__(self, n):
        self.n = n
        rep = lax.axis_index("rep")
        self.x, self.core = lax.div(rep, 2), lax.rem(rep, 2)
        index = lax.axis_index("fsdp")
        self.index = index
        self.place = ring_place(index, n)
        self.right = (rep, ring_index(self.place + 1, n))
        self.left = (rep, ring_index(self.place - 1, n))
        self.sibling = (self.x * 2 + 1 - self.core, index)
        self.across = ((1 - self.x) * 2 + self.core, index)

    def meet(self):
        barrier = pltpu.get_barrier_semaphore()
        for other in (self.right, self.left, self.sibling, self.across):
            pl.semaphore_signal(barrier, inc=1, device_id=other, device_id_type=MESH)
        pl.semaphore_wait(barrier, 4)


def send(src, dst, send_sem, recv_sem, device):
    return pltpu.make_async_remote_copy(
        src_ref=src, dst_ref=dst, send_sem=send_sem, recv_sem=recv_sem,
        device_id=device, device_id_type=MESH,
    )


def cols(start, size):
    return pl.ds(pl.multiple_of(start, LANE), size)


class Gather:
    def __init__(self, ring, weights, fulls, widths, sems):
        self.ring, self.weights, self.fulls = ring, weights, fulls
        self.axes, self.widths = zip(*widths)
        (self.own, self.ring_send, self.ring_recv, self.core_send, self.core_recv, self.x_send, self.x_recv) = sems

    def windows(self, i):
        ring = self.ring
        half = self.weights[i].shape[self.axes[i]] // 2
        w = self.widths[i]
        base = ring.core * half
        part = half - 2 * w
        first = base + jnp.where(ring.x == 0, 0, half - w)
        second = base + jnp.where(ring.x == 0, w, half - 2 * w)
        give = base + jnp.where(ring.x == 0, 0, half - part)
        take = base + jnp.where(ring.x == 0, half - part, 0)
        return w, part, first, second, give, take

    def block(self, i, index, start, width):
        rows = self.weights[i].shape[0]
        if self.axes[i] == 0:
            return self.fulls[i].at[pl.ds(pl.multiple_of(index * rows + start, 16), width), :]
        return self.fulls[i].at[pl.ds(pl.multiple_of(index * rows, 16), rows), cols(start, width)]

    def piece(self, i, start, width):
        if self.axes[i] == 0:
            return self.weights[i].at[pl.ds(pl.multiple_of(start, 16), width), :]
        return self.weights[i].at[:, cols(start, width)]

    def ring_copy(self, i, d, k, source):
        ring = self.ring
        w, _, first, second, _, _ = self.windows(i)
        start = second if d else first
        index = ring_index(ring.place + (k if d else -k), ring.n)
        there = self.block(i, index, start, w)
        src = self.piece(i, start, w) if source else there
        return send(src, there, self.ring_send.at[i, d, k], self.ring_recv.at[i, d, k], ring.left if d else ring.right)

    def core_copy(self, i, d, k):
        ring = self.ring
        w, part, first, second, _, take = self.windows(i)
        start, width = ((first, w), (second, w), (take, part))[d]
        index = ring_index(ring.place + (k + 1 if d == 1 else -k - 1), ring.n)
        there = self.block(i, index, start, width)
        return send(there, there, self.core_send.at[i, d, k], self.core_recv.at[i, d, k], ring.sibling)

    def x_copy(self, i, k):
        ring = self.ring
        _, part, _, _, give, _ = self.windows(i)
        there = self.block(i, ring_index(ring.place - k - 1, ring.n), give, part)
        return send(there, there, self.x_send.at[i, k], self.x_recv.at[i, k], ring.across)

    def own_copy(self, i):
        rows = self.weights[i].shape[0]
        there = self.fulls[i].at[pl.ds(pl.multiple_of(self.ring.index * rows, 16), rows), :]
        return send(self.weights[i], there, self.own.at[0, i], self.own.at[1, i], self.ring.sibling)

    def has_part(self, i):
        return self.weights[i].shape[self.axes[i]] // 2 > 2 * self.widths[i]

    def start(self):
        for i in range(len(self.weights)):
            for d in range(2):
                self.ring_copy(i, d, 0, True).start()
        for i in range(len(self.weights)):
            self.own_copy(i).start()

    def step(self, k):
        last = self.ring.n - 2
        for i in range(len(self.weights)):
            for d in range(2):
                self.ring_copy(i, d, k, False).wait_recv()

                @pl.when(k < last)
                def _():
                    self.ring_copy(i, d, k + 1, False).start()

                if d == 0 and self.has_part(i):
                    self.x_copy(i, k).start()
                self.core_copy(i, d, k).start()

            if self.has_part(i):
                @pl.when(k >= LAG)
                def _():
                    self.pass_on(i, k - LAG)

    def pass_on(self, i, k):
        self.x_copy(i, k).wait_recv()
        self.core_copy(i, 2, k).start()

    def finish(self):
        last = self.ring.n - 2
        for k in range(max(0, last + 1 - LAG), last + 1):
            for i in range(len(self.weights)):
                if self.has_part(i):
                    self.pass_on(i, k)

        def settle(k, carry):
            for i in range(len(self.weights)):
                for d in range(2):
                    self.ring_copy(i, d, k, False).wait_send()
                    self.core_copy(i, d, k).wait()
                if self.has_part(i):
                    self.x_copy(i, k).wait_send()
                    self.core_copy(i, 2, k).wait()
            return carry

        lax.fori_loop(0, self.ring.n - 1, settle, 0)
        for i in range(len(self.weights)):
            self.own_copy(i).wait()

    @staticmethod
    def scratch(count, n):
        dma = pltpu.SemaphoreType.DMA
        return [
            dma((2, count)), dma((count, 2, n - 1)), dma((count, 2, n - 1)),
            dma((count, 3, n - 1)), dma((count, 3, n - 1)), dma((count, n - 1)), dma((count, n - 1)),
        ]


def share(shape):
    rows, columns = shape
    axis, unit = (0, 16) if rows % 64 == 0 else (1, LANE)
    units = (rows, columns)[axis] // 2 // unit
    return axis, -(-units // 3) * unit


def carried(columns, shared):
    half = columns // 2
    units = half // LANE
    if not shared or units < 3:
        return half // 2, 0
    lanes = -(-units // 3) * LANE
    return lanes, half - 2 * lanes


class Reduce:
    def __init__(self, ring, grads, sums, others, specs, scratch):
        self.ring, self.grads, self.sums, self.others, self.specs = ring, grads, sums, others, specs
        count = len(grads)
        self.slots, self.mine, self.twin, self.x_slots, self.x_out = [], [], [], [], []
        scratch = list(scratch)
        for spec in specs:
            part = carried(spec[1], spec[2])[1]
            take = [scratch.pop(0) for _ in range(10 if part else 6)]
            self.slots.append(take[:2])
            self.mine.append(take[2:4] + take[6:7])
            self.twin.append(take[4:6] + take[7:8])
            self.x_slots.append(take[8] if part else None)
            self.x_out.append(take[9] if part else None)
        (self.load, self.ring_send, self.ring_recv, self.core_send, self.core_recv,
         self.x_send, self.x_recv, self.keep) = scratch

    def owner(self, kind, j):
        ring = self.ring
        return ring_index(ring.place + (j + 1 if kind == 1 else -j - 1), ring.n)

    def span(self, i, kind):
        columns, shared = self.specs[i][1:]
        w, part = carried(columns, shared)
        half = columns // 2
        lower, upper = ((0, half - w), (w, half - 2 * w), (half - part, 0))[kind]
        return jnp.where(self.ring.x == 0, lower, upper), part if kind == 2 else w

    def rows(self, i, index):
        rows = self.specs[i][0]
        return pl.ds(pl.multiple_of(index * rows, 16), rows)

    def kinds(self, i):
        return 3 if self.x_slots[i] is not None else 2

    def core_copy(self, i, kind, j):
        ring = self.ring
        start, width = self.span(i, kind)
        rows = self.rows(i, self.owner(kind, j))
        half = self.specs[i][1] // 2
        return send(
            self.grads[i].at[rows, cols((1 - ring.core) * half + start, width)], self.others[i].at[rows, cols(start, width)],
            self.core_send.at[i, kind, j], self.core_recv.at[i, kind, j], ring.sibling,
        )

    def loads(self, i, kind, j):
        start, width = self.span(i, kind)
        rows = self.rows(i, self.owner(kind, j))
        base = self.ring.core * (self.specs[i][1] // 2)
        return (
            pltpu.make_async_copy(
                self.grads[i].at[rows, cols(base + start, width)], self.mine[i][kind], self.load.at[i, kind, 0]
            ),
            pltpu.make_async_copy(self.others[i].at[rows, cols(start, width)], self.twin[i][kind], self.load.at[i, kind, 1]),
        )

    def fetch(self, i, kind, j):
        own, other = self.loads(i, kind, j)
        own.start()
        self.core_copy(i, kind, j).wait_recv()
        other.start()

    def ring_copy(self, i, d, j):
        ring = self.ring
        return send(
            self.slots[i][d].at[j], self.slots[i][d].at[j + 1],
            self.ring_send.at[i, d, j], self.ring_recv.at[i, d, j + 1], ring.left if d else ring.right,
        )

    def gap(self, i):
        w, part = carried(*self.specs[i][1:])
        x = self.ring.x
        return w - part, jnp.where(x == 0, part, 0), jnp.where(x == 0, w - part, 0), part

    def x_copy(self, i, j):
        _, _, at, part = self.gap(i)
        return send(
            self.x_out[i].at[lax.rem(j, 2)], self.x_slots[i].at[j, :, cols(at, part)],
            self.x_send.at[i, j], self.x_recv.at[i, j], self.ring.across,
        )

    def give(self, i, j):
        j = jnp.int32(j)
        for copy in self.loads(i, 2, j):
            copy.wait()

        @pl.when(j >= 2)
        def _():
            self.x_copy(i, j - 2).wait_send()

        self.x_out[i][lax.rem(j, 2)] = (self.mine[i][2][...].astype(F32) + self.twin[i][2][...].astype(F32)).astype(BF16)
        self.x_copy(i, j).start()
        self.hand_next(i, 2, j)

        @pl.when(j < self.ring.n - 1)
        def _():
            self.fetch(i, 2, j + 1)

    def each(self):
        return [(i, d) for i in range(len(self.grads)) for d in (1, 0)]

    def clear(self):
        for i in range(len(self.grads)):
            if self.kinds(i) == 3:
                width, at, _, _ = self.gap(i)
                if width:
                    rows = self.specs[i][0]
                    self.x_slots[i][:, :, cols(at, width)] = jnp.zeros((self.ring.n, rows, width), BF16)

    def hand_over(self):
        for j in range(min(LEAD, self.ring.n)):
            for i in range(len(self.grads)):
                for kind in reversed(range(self.kinds(i))):
                    self.core_copy(i, kind, j).start()

    def hand_next(self, i, kind, j):
        pl.when(j + LEAD < self.ring.n)(lambda: self.core_copy(i, kind, j + LEAD).start())

    def fetch_first(self):
        for i in range(len(self.grads)):
            for kind in reversed(range(self.kinds(i))):
                self.fetch(i, kind, 0)

    def give_all(self, j):
        for i in range(len(self.grads)):
            if self.kinds(i) == 3:
                self.give(i, j)

    def opening(self):
        return [
            self.hand_over, self.fetch_first,
            functools.partial(self.give_all, 0), functools.partial(self.give_all, 1),
        ]

    def start(self):
        for step in self.opening():
            step()

    def item(self, j, work):
        last = self.ring.n - 1
        for i, d in work:
            if d == 0 and self.kinds(i) == 3:
                pl.when(j < last - 1)(functools.partial(self.give, i, j + 2))
            for copy in self.loads(i, d, j):
                copy.wait()
            slot = self.slots[i][d]
            both = self.mine[i][d][...].astype(F32) + self.twin[i][d][...].astype(F32)
            if d == 0 and self.kinds(i) == 3:
                self.x_copy(i, j).wait_recv()
                both = both + self.x_slots[i][j].astype(F32)

            @pl.when(j == 0)
            def _():
                slot[j] = both.astype(BF16)

            @pl.when(j > 0)
            def _():
                self.ring_copy(i, d, j - 1).wait_recv()
                slot[j] = (slot[j].astype(F32) + both).astype(BF16)

            @pl.when(j < last)
            def _():
                self.ring_copy(i, d, j).start()
                self.fetch(i, d, j + 1)

            self.hand_next(i, d, j)

            @pl.when(j == last)
            def _():
                self.keep_copy(i, d).start()

    def keep_copy(self, i, d):
        w = carried(*self.specs[i][1:])[0]
        at = jnp.where(self.ring.x == 0, d * w, (1 - d) * w)
        return pltpu.make_async_copy(self.slots[i][d].at[self.ring.n - 1], self.sums[i].at[:, cols(at, w)], self.keep.at[i, d])

    def finish(self):
        last = self.ring.n - 1
        for i, d in self.each():
            self.keep_copy(i, d).wait()

        def settle(j, carry):
            for i in range(len(self.grads)):
                for kind in range(self.kinds(i)):
                    self.core_copy(i, kind, j).wait_send()
                for d in range(2):
                    pl.when(j < last)(lambda i=i, d=d: self.ring_copy(i, d, j).wait_send())
                if self.kinds(i) == 3:
                    pl.when(j >= last - 1)(lambda i=i: self.x_copy(i, j).wait_send())
            return carry

        lax.fori_loop(0, self.ring.n, settle, 0)

    @staticmethod
    def specs_of(grads, n, shared):
        return [(g.shape[0] // n, g.shape[1], shared) for g in grads]

    @staticmethod
    def results(specs, n):
        return [
            jax.ShapeDtypeStruct((rows, 2 * carried(columns, shared)[0]), BF16) for rows, columns, shared in specs
        ] + [jax.ShapeDtypeStruct((n * rows, columns // 2), BF16) for rows, columns, _ in specs]

    @staticmethod
    def scratch(specs, n):
        dma = pltpu.SemaphoreType.DMA
        count = len(specs)
        buffers = []
        for rows, columns, shared in specs:
            w, part = carried(columns, shared)
            buffers += [pltpu.VMEM((n, rows, w), BF16)] * 2 + [pltpu.VMEM((rows, w), BF16)] * 4
            if part:
                buffers += [pltpu.VMEM((rows, part), BF16)] * 2
                buffers += [pltpu.VMEM((n, rows, w), BF16), pltpu.VMEM((2, rows, part), BF16)]
        return buffers + [
            dma((count, 3, 2)), dma((count, 2, n)), dma((count, 2, n)), dma((count, 3, n)), dma((count, 3, n)),
            dma((count, n)), dma((count, n)), dma((count, 2)),
        ]


class FinalSum:
    def __init__(self, ring, sums, totals, specs, scratch):
        self.ring, self.sums, self.totals, self.specs = ring, sums, totals, specs
        scratch = list(scratch)
        self.mine, self.plane, self.own = [], [], []
        for spec in specs:
            self.mine.append(scratch.pop(0))
            self.plane.append(scratch.pop(0))
            self.own.append(scratch.pop(0) if carried(spec[1], spec[2])[1] else None)
        self.local, self.remote_send, self.remote_recv = scratch

    def spans(self, i):
        columns, shared = self.specs[i][1:]
        w, part = carried(columns, shared)
        half, wide = columns // 2, 2 * w - part
        base = self.ring.core * half
        low = self.ring.x == 0
        return (
            (jnp.where(low, part, 0), base + part, wide),
            (jnp.where(low, 0, wide), base + jnp.where(low, 0, half - part), part),
            (0, base + jnp.where(low, half - part, 0), part),
        )

    def remote(self, i, at, src, dst, device):
        return send(src, dst, self.remote_send.at[i, at], self.remote_recv.at[i, at], device)

    def copy(self, i, name):
        ring, sums, totals = self.ring, self.sums[i], self.totals[i]
        (a, a_out, wide), (b, b_out, part), (_, c_out, _) = self.spans(i)
        local = {"load": 0, "save": 1, "load done": 2, "save done": 3}
        remote = {"across": 0, "sibling": 1, "done across": 2, "done sibling": 3, "pass on": 4}
        if name in ("load", "save", "across", "sibling"):
            src, dst, mid = sums.at[:, cols(a, wide)], totals.at[:, cols(a_out, wide)], self.mine[i]
        elif name == "pass on":
            src = dst = mid = totals.at[:, cols(c_out, part)]
        else:
            src, dst, mid = sums.at[:, cols(b, part)], totals.at[:, cols(b_out, part)], self.own[i]
        if name in local:
            ends = (src, mid) if name.startswith("load") else (mid, dst)
            return pltpu.make_async_copy(*ends, self.local.at[i, local[name]])
        ends = {"across": (src, self.plane[i]), "sibling": (mid, dst)}.get(name, (src, dst))
        device = ring.across if "across" in name else ring.sibling
        at = remote[name]
        return send(*ends, self.remote_send.at[i, at], self.remote_recv.at[i, at], device)

    def shares(self, i):
        return carried(*self.specs[i][1:])[1] > 0

    def start(self):
        for i in range(len(self.specs)):
            for name in ("across", "load"):
                self.copy(i, name).start()
            if self.shares(i):
                for name in ("done across", "load done", "done sibling"):
                    self.copy(i, name).start()

    def add(self, i):
        self.copy(i, "load").wait()
        self.copy(i, "across").wait_recv()
        self.mine[i][...] = (self.mine[i][...].astype(F32) + self.plane[i][...].astype(F32)).astype(BF16)
        self.copy(i, "sibling").start()
        self.copy(i, "save").start()
        if self.shares(i):
            self.copy(i, "load done").wait()
            self.copy(i, "save done").start()
            self.copy(i, "done across").wait_recv()
            self.copy(i, "pass on").start()

    def finish(self):
        for i in range(len(self.specs)):
            self.copy(i, "across").wait_send()
            self.copy(i, "sibling").wait()
            self.copy(i, "save").wait()
            if self.shares(i):
                self.copy(i, "done across").wait_send()
                for name in ("done sibling", "save done", "pass on"):
                    self.copy(i, name).wait()

    @staticmethod
    def scratch(specs):
        dma = pltpu.SemaphoreType.DMA
        count = len(specs)
        buffers = []
        for rows, columns, shared in specs:
            w, part = carried(columns, shared)
            buffers += [pltpu.VMEM((rows, 2 * w - part), BF16)] * 2
            if part:
                buffers += [pltpu.VMEM((rows, part), BF16)]
        return buffers + [dma((count, 4)), dma((count, 5)), dma((count, 5))]


class SmallSum:
    def __init__(self, ring, given, total, scratch):
        self.ring, self.given, self.total = ring, given, total
        self.mine, self.twin, self.plane, self.slots, self.pair, self.ring_send, self.ring_recv = scratch

    def copy(self, src, dst, at, device):
        return send(src, dst, self.pair.at[0, at], self.pair.at[1, at], device)

    def start(self):
        ring = self.ring
        copy = self.copy(self.given, self.twin, 0, ring.sibling)
        copy.start()
        copy.wait()
        self.mine[...] = self.given[...] + self.twin[...]
        copy = self.copy(self.mine, self.plane, 1, ring.across)
        copy.start()
        copy.wait()
        self.slots[0] = self.mine[...] + self.plane[...]

    def ring_copy(self, j):
        return send(
            self.slots.at[j], self.slots.at[j + 1], self.ring_send.at[j], self.ring_recv.at[j + 1], self.ring.right
        )

    def item(self, j):
        @pl.when(j > 0)
        def _():
            self.ring_copy(j - 1).wait_recv()

        @pl.when(j < self.ring.n - 1)
        def _():
            self.ring_copy(j).start()

    def finish(self):
        ring = self.ring
        total = jnp.zeros(self.total.shape, F32)
        for place in range(ring.n):
            total = total + self.slots[lax.rem(ring.place - place + ring.n, ring.n)]
        self.total[...] = total

        def settle(j, carry):
            self.ring_copy(j).wait_send()
            return carry

        lax.fori_loop(0, ring.n - 1, settle, 0)

    @staticmethod
    def scratch(rows, n):
        dma = pltpu.SemaphoreType.DMA
        block = pltpu.VMEM((rows, LANE), F32)
        return [block, block, block, pltpu.VMEM((n, rows, LANE), F32), dma((2, 2)), dma((n,)), dma((n,))]


SMALL_SCRATCH = 7


NORM_ROUNDS = 3


def pack(given, at, value):
    if value.shape[0] == 1:
        for r in range(value.shape[1] // LANE):
            given[at + r : at + r + 1, :] = value[:, r * LANE : (r + 1) * LANE]
        return at + value.shape[1] // LANE
    given[at : at + value.shape[0], :] = value
    return at + value.shape[0]


def last_kernel(n, specs, early_specs, chunk, small_count, *refs):
    count, early = len(specs), len(early_specs)
    ring = Ring(n)
    refs = list(refs)

    def take(size):
        taken = refs[:size]
        del refs[:size]
        return taken

    small_refs = take(small_count)
    input_ref, gain_ref, d_middle_ref, d_projected, weight = take(5)
    grads, early_sums = take(count), take(early)
    grad_input_ref, total_ref = take(2)
    totals, early_totals, sums, others = take(count), take(early), take(count), take(count)
    given, d_normed, in_left, in_right, in_sem = take(5)
    small = SmallSum(ring, given, total_ref, take(SMALL_SCRATCH))
    last_sum = FinalSum(ring, sums, totals, specs, take(len(FinalSum.scratch(specs))))
    early_sum = FinalSum(ring, early_sums, early_totals, early_specs, take(len(FinalSum.scratch(early_specs))))
    reduce = Reduce(ring, grads, sums, others, specs, refs)
    chunks = d_projected.shape[1] // chunk
    turns = -(-chunks // NORM_ROUNDS)

    def arrive(t, slot):
        at = cols(t * chunk, chunk)
        return (
            pltpu.make_async_copy(d_projected.at[:, at], in_left.at[slot], in_sem.at[slot, 0]),
            pltpu.make_async_copy(weight.at[:, at], in_right.at[slot], in_sem.at[slot, 1]),
        )

    for copy in arrive(0, 0):
        copy.start()
    reduce.clear()
    ring.meet()
    d_normed[...] = jnp.zeros_like(d_normed)
    given[...] = jnp.zeros_like(given)
    reduce.start()

    def turn(t):
        slot = lax.rem(t, 2)
        for copy in arrive(t, slot):
            copy.wait()

        @pl.when(t < chunks - 1)
        def _():
            for copy in arrive(t + 1, 1 - slot):
                copy.start()

        d_normed[...] += nt(in_left[slot], in_right[slot])

    def first(j, carry):
        reduce.item(j, reduce.each())
        for k in range(turns):
            t = j * turns + k
            pl.when(t < chunks)(functools.partial(turn, t))
        return carry

    lax.fori_loop(0, NORM_ROUNDS, first, 0)
    values = input_ref[...].astype(F32)
    scale = lax.rsqrt(jnp.mean(values * values, axis=1, keepdims=True) + EPSILON)
    upstream = d_normed[...]
    grad_gain = jnp.sum(upstream * (values * scale), axis=0, keepdims=True)
    at = pack(given, 0, grad_gain)
    for ref in small_refs:
        at = pack(given, at, ref[...])
    scaled = upstream * gain_ref[...]
    inner = jnp.mean(scaled * values, axis=1, keepdims=True)
    grad_input_ref[...] = d_middle_ref[...] + scale * scaled - values * (scale * scale * scale * inner)
    small.start()
    early_sum.start()
    rounds = n - NORM_ROUNDS
    hops = -(-n // rounds)

    def rest(j, carry):
        reduce.item(j, reduce.each())
        for hop in range(hops):
            at = (j - NORM_ROUNDS) * hops + hop
            pl.when(at < n)(functools.partial(small.item, at))
        for i in range(early):
            pl.when(j == n - early + i)(functools.partial(early_sum.add, i))
        return carry

    lax.fori_loop(NORM_ROUNDS, n, rest, 0)
    reduce.finish()
    last_sum.start()
    small.finish()
    for i in range(count):
        last_sum.add(i)
    early_sum.finish()
    last_sum.finish()


def last_step(
    d_projected, qkv_weight, layer_input, first_gain, d_middle, grads, smalls, early_sums, early_specs, n, collective
):
    count, early = len(grads), len(early_specs)
    seq, width = layer_input.shape
    chunk = 512
    specs = Reduce.specs_of(grads, n, False)
    sizes = [v.size // LANE for v in [first_gain] + smalls]
    rows = -(-sum(sizes) // 8) * 8
    anywhere = pl.BlockSpec(memory_space=pl.ANY)
    whole = pl.BlockSpec(memory_space=pltpu.VMEM)
    results = pl.pallas_call(
        functools.partial(last_kernel, n, specs, early_specs, chunk, len(smalls)),
        out_shape=[jax.ShapeDtypeStruct((seq, width), F32), jax.ShapeDtypeStruct((rows, LANE), F32)]
        + [jax.ShapeDtypeStruct(spec[:2], BF16) for spec in specs + early_specs]
        + Reduce.results(specs, n),
        in_specs=[whole] * (len(smalls) + 3) + [anywhere] * (2 + count + early),
        out_specs=[whole] * 2 + [anywhere] * (3 * count + early),
        scratch_shapes=[
            pltpu.VMEM((rows, LANE), F32),
            pltpu.VMEM((seq, width), F32),
            pltpu.VMEM((2, seq, chunk), BF16),
            pltpu.VMEM((2, width, chunk), BF16),
            pltpu.SemaphoreType.DMA((2, 2)),
        ]
        + SmallSum.scratch(rows, n)
        + FinalSum.scratch(specs)
        + FinalSum.scratch(early_specs)
        + Reduce.scratch(specs, n),
        compiler_params=pltpu.CompilerParams(
            collective_id=collective, has_side_effects=True, vmem_limit_bytes=60 * 1024 * 1024
        ),
    )(*smalls, layer_input, first_gain.reshape(1, width), d_middle, d_projected, qkv_weight, *grads, *early_sums)
    out, at = [], 0
    for size in sizes:
        out.append(results[1][at : at + size])
        at += size
    return results[0], results[2 : 2 + count + early], out


TILES = 8
EARLY_TILES = 3


def mlp_kernel(n, specs, tile, *refs):
    refs = list(refs)

    def take(size):
        taken = refs[:size]
        del refs[:size]
        return taken

    second_ref, upstream_ref, middle, inner, down = take(5)
    out_ref, d_second_ref = take(2)
    (early, late, grad_down), sums, others = take(3), take(1), take(1)
    turned, out_sum, in_gate, in_up, in_down, to_gate, to_up, to_down = take(8)
    middle_sem, in_sem, to_sem = take(3)
    reduce = Reduce(Ring(n), [early], sums, others, specs, refs)
    hidden_size = down.shape[0]
    tiles = hidden_size // tile
    begun = EARLY_TILES
    each = -(-n // (tiles - begun - 1))
    due = -(-each // 2)

    def arrive(t, slot):
        at = pl.multiple_of(t * tile, tile)
        return (
            pltpu.make_async_copy(inner.at[:, pl.ds(at, tile)], in_gate.at[slot], in_sem.at[slot, 0]),
            pltpu.make_async_copy(
                inner.at[:, pl.ds(pl.multiple_of(hidden_size + at, tile), tile)], in_up.at[slot], in_sem.at[slot, 1]
            ),
            pltpu.make_async_copy(down.at[pl.ds(at, tile), :], in_down.at[slot], in_sem.at[slot, 2]),
        )

    def leave(grad, t, slot, first, count):
        at = pl.multiple_of((t - first) * tile, tile)
        return (
            pltpu.make_async_copy(to_gate.at[slot], grad.at[:, pl.ds(at, tile)], to_sem.at[slot, 0]),
            pltpu.make_async_copy(
                to_up.at[slot], grad.at[:, pl.ds(pl.multiple_of(count * tile + at, tile), tile)], to_sem.at[slot, 1]
            ),
            pltpu.make_async_copy(
                to_down.at[slot], grad_down.at[pl.ds(pl.multiple_of(t * tile, tile), tile), :], to_sem.at[slot, 2]
            ),
        )

    def leave_early(t):
        return leave(early, t, lax.rem(t, 2), 0, begun)

    def leave_late(t):
        return leave(late, t, lax.rem(t, 2), begun, tiles - begun)

    first = pltpu.make_async_copy(middle, out_sum, middle_sem)
    first.start()
    for copy in arrive(0, 0):
        copy.start()
    reduce.clear()
    reduce.ring.meet()
    turned[...] = second_ref[...].T
    d_second_ref[...] = jnp.zeros_like(d_second_ref)
    first.wait()

    def serve(t, point):
        @pl.when(t == begun)
        def _():
            if point == 0:
                for back in (2, 1):
                    for copy in leave_early(t - back):
                        copy.wait()
            reduce.opening()[point]()

        for step in range(due):
            if point // 2 * due + step < each:
                j = (t - begun - 1) * each + point // 2 * due + step
                pl.when((t > begun) & (j < n))(functools.partial(reduce.item, j, [(0, 1 - point % 2)]))

    def one(t, carry):
        slot = lax.rem(t, 2)
        for copy in arrive(t, slot):
            copy.wait()

        @pl.when(t < tiles - 1)
        def _():
            for copy in arrive(t + 1, 1 - slot):
                copy.start()

        second, upstream = second_ref[...], upstream_ref[...]
        gate = nn(second, in_gate[slot])
        up = nn(second, in_up[slot])
        sigmoid = jax.nn.sigmoid(gate)
        silu = gate * sigmoid
        hidden = (silu * up).astype(BF16)
        serve(t, 0)
        d_hidden = nt(upstream, in_down[slot])
        out_sum[...] += nn(hidden, in_down[slot])

        @pl.when((t >= 2) & (t < begun))
        def _():
            for copy in leave_early(t - 2):
                copy.wait()

        @pl.when(t >= begun + 2)
        def _():
            for copy in leave_late(t - 2):
                copy.wait()

        to_down[slot] = nn(hidden.T, upstream).astype(BF16)
        d_gate = (d_hidden * up * sigmoid * (1.0 + gate * (1.0 - sigmoid))).astype(BF16)
        d_up = (d_hidden * silu).astype(BF16)
        serve(t, 1)
        d_second_ref[...] += nt(d_gate, in_gate[slot])
        to_gate[slot] = nn(turned[...], d_gate).astype(BF16)
        serve(t, 2)
        d_second_ref[...] += nt(d_up, in_up[slot])
        to_up[slot] = nn(turned[...], d_up).astype(BF16)
        serve(t, 3)

        @pl.when(t < begun)
        def _():
            for copy in leave_early(t):
                copy.start()

        @pl.when(t >= begun)
        def _():
            for copy in leave_late(t):
                copy.start()

        return carry

    lax.fori_loop(0, tiles, one, 0)
    out_ref[...] = out_sum[...].astype(BF16)
    for t in (tiles - 2, tiles - 1):
        for copy in leave_late(t):
            copy.wait()
    reduce.finish()


def feed_forward(second, upstream, middle, inner, down, n, collective):
    seq, width = second.shape
    hidden_size = down.shape[0]
    tile = hidden_size // TILES
    early = EARLY_TILES * tile
    specs = [(width // n, 2 * early, True)]
    whole = pl.BlockSpec(memory_space=pltpu.VMEM)
    anywhere = pl.BlockSpec(memory_space=pl.ANY)
    dma = pltpu.SemaphoreType.DMA
    results = pl.pallas_call(
        functools.partial(mlp_kernel, n, specs, tile),
        out_shape=[
            jax.ShapeDtypeStruct((seq, width), BF16),
            jax.ShapeDtypeStruct((seq, width), F32),
        ]
        + [
            jax.ShapeDtypeStruct((width, 2 * early), BF16),
            jax.ShapeDtypeStruct((width, 2 * (hidden_size - early)), BF16),
            jax.ShapeDtypeStruct((hidden_size, width), BF16),
        ]
        + Reduce.results(specs, n),
        in_specs=[whole, whole, anywhere, anywhere, anywhere],
        out_specs=[whole, whole] + [anywhere] * 5,
        scratch_shapes=[
            pltpu.VMEM((width, seq), BF16),
            pltpu.VMEM((seq, width), F32),
            pltpu.VMEM((2, width, tile), BF16),
            pltpu.VMEM((2, width, tile), BF16),
            pltpu.VMEM((2, tile, width), BF16),
            pltpu.VMEM((2, width, tile), BF16),
            pltpu.VMEM((2, width, tile), BF16),
            pltpu.VMEM((2, tile, width), BF16),
            dma, dma((2, 3)), dma((2, 3)),
        ]
        + Reduce.scratch(specs, n),
        compiler_params=pltpu.CompilerParams(
            collective_id=collective, has_side_effects=True, vmem_limit_bytes=62 * 1024 * 1024
        ),
    )(second, upstream, middle, inner, down)
    out, d_second, _, late, grad_down, sums, _ = results
    return out, d_second, late, grad_down, [sums], specs


def rms_norm(values, gains):
    return values * lax.rsqrt(jnp.mean(values * values, axis=-1, keepdims=True) + EPSILON) * gains


def swiglu(gate_up):
    middle_col = gate_up.shape[1] // 2
    return jax.nn.silu(gate_up[:, :middle_col]) * gate_up[:, middle_col:]


def project(operand, weight):
    return jnp.dot(operand, weight, preferred_element_type=F32)


def project_back(upstream, weight):
    return lax.dot_general(
        upstream, weight, (((1,), (1,)), ((), ())), preferred_element_type=F32
    )


def weight_grad(operand, upstream):
    return lax.dot_general(
        operand, upstream, (((0,), (0,)), ((), ())), preferred_element_type=F32
    ).astype(BF16)


def body(
    layer_input,
    first_gain,
    qkv_weight,
    conv_kernel,
    head_mixing,
    group_gain,
    out_weight,
    second_gain,
    inner_weight,
    down_weight,
    doc_lengths,
    cotangent,
):
    n = lax.axis_size("fsdp")
    kept, (qkv_weight, out_weight), (inner_weight, down_weight) = attend_forward(
        layer_input, conv_kernel, head_mixing, doc_lengths, (first_gain, group_gain, second_gain),
        [qkv_weight, out_weight], [inner_weight, down_weight], n, 0,
    )
    grouped, attended, soft, normed, middle, second, projected = kept
    second_pull = jax.vjp(rms_norm, middle, second_gain)[1]
    layer_output, d_second, late_inner, grad_down, early_sums, early_specs = feed_forward(
        second, cotangent, middle, inner_weight, down_weight, n, 2
    )
    d_middle, grad_second = second_pull(d_second)
    d_middle = cotangent.astype(F32) + d_middle
    d_branch = d_middle.astype(jnp.bfloat16)
    grad_proj = weight_grad(grouped, d_branch)
    d_grouped = project_back(d_branch, out_weight)
    (d_projected, grad_group, grad_kernel, grad_mixing), sums, specs = attend_backward(
        projected, conv_kernel, head_mixing, doc_lengths, group_gain, attended, d_grouped, soft,
        [late_inner, grad_down, grad_proj], n, 3,
    )
    grad_qkv = weight_grad(normed, d_projected)
    grad_input, shards, small = last_step(
        d_projected, qkv_weight, layer_input, first_gain, d_middle, [grad_qkv],
        [grad_group, grad_second.reshape(1, -1), grad_kernel, grad_mixing], early_sums + sums, early_specs + specs, n, 4,
    )
    grad_first, grad_group, grad_second = [g.reshape(-1) for g in small[:3]]
    grad_kernel = jnp.roll(small[3].reshape(HEADS, 8, LANE), CK // 2 + 1, axis=2)[:, :CQ, :CK][:, :, ::-1] * SCALE
    grad_mixing = small[4].reshape(-1, 8, LANE)[:, :2, :4].reshape(HEADS // 2, 2, 2)
    early_half, late_half = shards[1].shape[1] // 2, shards[2].shape[1] // 2
    grad_inner = jnp.concatenate(
        [shards[1][:, :early_half], shards[2][:, :late_half], shards[1][:, early_half:], shards[2][:, late_half:]], axis=1
    )
    shards = [g.astype(F32) for g in (shards[0], shards[4], grad_inner, shards[3])]
    return (
        layer_output, grad_input, grad_first, shards[0], grad_kernel, grad_mixing, grad_group, shards[1], grad_second,
        shards[2], shards[3],
    )


def solution(mesh):
    placed = (
        P(("rep", "fsdp"), None),
        P(),
        P("fsdp", None),
        P(),
        P(),
        P(),
        P("fsdp", None),
        P(),
        P("fsdp", None),
        P("fsdp", None),
        P(("rep", "fsdp"), None),
        P(("rep", "fsdp"), None),
    )
    return jax.shard_map(
        body,
        mesh=mesh,
        in_specs=placed,
        out_specs=(
            P(("rep", "fsdp"), None),
            P(("rep", "fsdp"), None),
            P(),
            P("fsdp", None),
            P(),
            P(),
            P(),
            P("fsdp", None),
            P(),
            P("fsdp", None),
            P("fsdp", None),
        ),
        check_vma=False,
    )
```

```python
import functools, math
import jax, jax.numpy as jnp
from jax import lax
from jax.experimental import pallas as pl
from jax.experimental.pallas import tpu as pltpu
from jax.sharding import PartitionSpec as P

HEADS = 16
HEAD_DIM = 96
CQ = 6
CK = 11
EPSILON = 1e-05
LANE = 128
QUAD = 4
LAG = 1
LEAD = 3
SCALE = 1.0 / math.sqrt(HEAD_DIM)
F32 = jnp.float32
BF16 = jnp.bfloat16


def row_sets(seq):
    return [
        (r, min(r + LANE, 3 * LANE), max(0, r - 2 * LANE)) for r in range(0, seq, LANE)
    ]


def nt(a, b):
    return lax.dot_general(a, b, (((1,), (1,)), ((), ())), preferred_element_type=F32)


def nn(a, b):
    return jnp.dot(a, b, preferred_element_type=F32)


def fill_masks(docs_ref, masks, seq):
    ends = []
    total = jnp.int32(0)
    for d in range(docs_ref.shape[1] - 1):
        total = total + docs_ref[0, d]
        ends.append(total)
    for r0, width, c0 in row_sets(seq):
        rows = r0 + lax.broadcasted_iota(jnp.int32, (LANE, 1), 0)
        cols = c0 + lax.broadcasted_iota(jnp.int32, (1, width), 1)
        row_doc = sum((rows >= e).astype(jnp.int32) for e in ends)
        col_doc = sum((cols >= e).astype(jnp.int32) for e in ends)
        same = row_doc == col_doc
        for a in range(CQ):
            masks[a, r0 : r0 + LANE, :width] = jnp.where(
                same & (rows - cols >= a), 1.0, 0.0
            ).astype(BF16)


def circulant_masks():
    gap = lax.broadcasted_iota(jnp.int32, (LANE, LANE), 1) - lax.broadcasted_iota(
        jnp.int32, (LANE, LANE), 0
    )
    half = CK // 2
    return (jnp.abs(gap) <= half, gap <= half - LANE, gap >= LANE - half)


def circulant(taps):
    wide = jnp.broadcast_to(taps, (LANE, LANE))
    return pltpu.roll(wide, 0, axis=1, stride=1, stride_axis=0)


def fill_toeplitz(taps_ref, head, band, blocks):
    near, after, before = circulant_masks()
    for a in range(CQ):
        whole = circulant(taps_ref[head, a : a + 1, :])
        parts = {
            0: jnp.where(near, whole, 0.0).astype(BF16),
            1: jnp.where(after, whole, 0.0).astype(BF16),
            -1: jnp.where(before, whole, 0.0).astype(BF16),
        }
        for r in range(blocks):
            for c in range(blocks):
                part = parts.get(c - r)
                if part is not None:
                    yield a, r, c, part


def fill_forward_band(taps_ref, head, band):
    for a, r, c, part in fill_toeplitz(taps_ref, head, band, 3):
        at = (r * CQ + a) * LANE
        band[at : at + LANE, c * LANE : (c + 1) * LANE] = part


def fill_backward_band(taps_ref, head, band):
    for a, r, c, part in fill_toeplitz(taps_ref, head, band, 3):
        at = (c * CQ + a) * LANE
        band[r * LANE : (r + 1) * LANE, at : at + LANE] = part


def shifted_rows(query):
    wide = query.astype(F32)
    return [query] + [pltpu.roll(wide, a, axis=0).astype(BF16) for a in range(1, CQ)]


def masked_scores(shifted, keys, masks, r0, width, c0):
    left = jnp.concatenate([shifted[a, r0 : r0 + LANE] for a in range(CQ)], axis=0)
    scores = nt(left, keys[c0 : c0 + width]).astype(BF16)
    return left, [
        scores[a * LANE : (a + 1) * LANE] * masks[a, r0 : r0 + LANE, :width]
        for a in range(CQ)
    ]


def by_window(parts, width):
    return jnp.concatenate(
        [
            parts[a][:, b * LANE : (b + 1) * LANE]
            for b in range(width // LANE)
            for a in range(CQ)
        ],
        axis=1,
    )


def forward_kernel(
    n, first_widths, rest_widths, docs_ref, mix_ref, taps_ref, gain_ref, input_ref, gains_ref, *refs
):
    refs = list(refs)

    def take(size):
        taken = refs[:size]
        del refs[:size]
        return taken

    first_count, rest_count = len(first_widths), len(rest_widths)
    first_weights, rest_weights = take(first_count), take(rest_count)
    grouped_ref, attended_ref, soft_ref, normed_ref, middle_ref, second_ref, projected = take(7)
    first_fulls, rest_fulls = take(first_count), take(rest_count)
    masks, band, qs, ks, vs, shifted, outs = take(7)
    blocks, block_weight, every, out_weight, block_in, block_out, out_in = take(7)
    ring = Ring(n)
    sems = len(Gather.scratch(first_count, n))
    first = Gather(ring, first_weights, first_fulls, first_widths, take(sems))
    rest = Gather(ring, rest_weights, rest_fulls, rest_widths, take(sems))
    seq = input_ref.shape[0]
    quad = pl.program_id(0)
    quads = HEADS // QUAD
    size = QUAD * HEAD_DIM
    count = 3 * quads

    def block_copy(t):
        slot = lax.rem(t, 2)
        return pltpu.make_async_copy(first_fulls[0].at[:, cols(t * size, size)], block_weight.at[slot], block_in.at[slot])

    def block_save(t):
        return pltpu.make_async_copy(blocks.at[t], projected.at[:, cols(t * size, size)], block_out.at[t])

    out_copy = pltpu.make_async_copy(first_fulls[1], out_weight, out_in)

    @pl.when(quad == 0)
    def _():
        ring.meet()
        first.start()
        fill_masks(docs_ref, masks, seq)
        band[...] = jnp.zeros_like(band)
        values = input_ref[...].astype(F32)
        scale = lax.rsqrt(jnp.mean(values * values, axis=1, keepdims=True) + EPSILON)
        normed_ref[...] = (values * scale * gains_ref[0:1, :]).astype(BF16)

        def one(k, carry):
            first.step(k)
            pl.when(k == n - 3)(rest.start)
            return carry

        lax.fori_loop(0, n - 1, one, 0)
        first.finish()
        block_copy(0).start()
        out_copy.start()

        def project_block(t, carry):
            pl.when(t < count - 1)(lambda: block_copy(t + 1).start())
            block_copy(t).wait()
            blocks[t] = nn(normed_ref[...], block_weight[lax.rem(t, 2)]).astype(BF16)
            block_save(t).start()
            return carry

        lax.fori_loop(0, count, project_block, 0)

    for h in range(QUAD):
        at = slice(h * HEAD_DIM, (h + 1) * HEAD_DIM)
        qs[h] = blocks[quad, :, at]
        ks[h] = blocks[quads + quad, :, at]
        vs[h] = blocks[2 * quads + quad, :, at]

    sets = row_sets(seq)

    def pair(p, carry):
        group = quad * 2 + p
        for r in range(2):
            h = 2 * p + r
            fill_forward_band(taps_ref, quad * QUAD + h, band)
            for a, rows in enumerate(shifted_rows(qs[h])):
                shifted[a] = rows
            keys = ks[h]
            lefts = []
            for r0, width, c0 in sets:
                _, parts = masked_scores(shifted, keys, masks, r0, width, c0)
                lefts.append((width, by_window(parts, width)))
            convs = []
            i = 0
            while i < len(sets):
                width = sets[i][1]
                run = 1
                while i + run < len(sets) and sets[i + run][1] == width:
                    run += 1
                left = jnp.concatenate([lefts[i + m][1] for m in range(run)], axis=0)
                conv = nn(left, band[: width * CQ, :width])
                convs += [conv[m * LANE : (m + 1) * LANE] for m in range(run)]
                i += run
            for (r0, width, c0), conv in zip(sets, convs):
                logits = jnp.where(
                    masks[0, r0 : r0 + LANE, :width].astype(F32) > 0, conv, -1e30
                )
                weights = jnp.exp(logits - jnp.max(logits, axis=1, keepdims=True))
                soft = weights * (1.0 / jnp.sum(weights, axis=1, keepdims=True))
                soft_ref[h, r0 : r0 + LANE, :width] = soft.astype(BF16)
        for r in range(2):
            h = 2 * p + r
            values = vs[h]
            for r0, width, c0 in sets:
                mixed = (
                    mix_ref[group, r, 0] * soft_ref[2 * p, r0 : r0 + LANE, :width].astype(F32)
                    + mix_ref[group, r, 1] * soft_ref[2 * p + 1, r0 : r0 + LANE, :width].astype(F32)
                ).astype(BF16)
                outs[h, r0 : r0 + LANE] = nn(mixed, values[c0 : c0 + width])
        for k in in_turn(group, HEADS // 2, n - 1):
            pl.when(k < n - 1)(functools.partial(rest.step, k))
        return carry

    lax.fori_loop(0, 2, pair, 0)
    wholes, grouped = [], []
    for h in range(QUAD):
        attended = outs[h]
        centred = attended - jnp.mean(attended, axis=1, keepdims=True)
        var = jnp.mean(centred * centred, axis=1, keepdims=True)
        wholes.append(attended)
        grouped.append(centred * lax.rsqrt(var + EPSILON))
    attended_ref[...] = jnp.concatenate(wholes, axis=1)
    every[quad] = (jnp.concatenate(grouped, axis=1) * gain_ref[1:2, :]).astype(BF16)
    grouped_ref[...] = every[quad]

    @pl.when(quad == quads - 1)
    def _():
        out_copy.wait()
        branch = nn(jnp.concatenate([every[i] for i in range(quads)], axis=1), out_weight[...])
        middle = input_ref[...].astype(F32) + branch
        scale = lax.rsqrt(jnp.mean(middle * middle, axis=1, keepdims=True) + EPSILON)
        middle_ref[...] = middle
        second_ref[...] = (middle * scale * gains_ref[2:3, :]).astype(BF16)

        def saved(t, carry):
            block_save(t).wait()
            return carry

        lax.fori_loop(0, count, saved, 0)
        rest.finish()


def pad_taps(kernel):
    padded = jnp.pad(kernel * SCALE, ((0, 0), (0, 2), (0, LANE - CK)))
    return jnp.roll(padded, -(CK // 2), axis=2)


def in_turn(turn, turns, steps):
    each = -(-steps // turns)
    return [turn * each + t for t in range(each)]


def attend_forward(layer_input, conv_kernel, head_mixing, docs, gains, first, rest, n, collective):
    seq, width = layer_input.shape
    block = QUAD * HEAD_DIM
    quads = HEADS // QUAD
    first_widths, rest_widths = [share(w.shape) for w in first], [share(w.shape) for w in rest]
    whole = pl.BlockSpec(memory_space=pltpu.VMEM)
    smem = pl.BlockSpec(memory_space=pltpu.SMEM)
    anywhere = pl.BlockSpec(memory_space=pl.ANY)
    columns = pl.BlockSpec((seq, block), lambda i: (0, i))
    dma = pltpu.SemaphoreType.DMA
    gains = jnp.stack(gains)
    results = pl.pallas_call(
        functools.partial(forward_kernel, n, first_widths, rest_widths),
        grid=(quads,),
        out_shape=[
            jax.ShapeDtypeStruct((seq, width), BF16),
            jax.ShapeDtypeStruct((seq, width), F32),
            jax.ShapeDtypeStruct((HEADS, seq, 3 * LANE), BF16),
            jax.ShapeDtypeStruct((seq, width), BF16),
            jax.ShapeDtypeStruct((seq, width), F32),
            jax.ShapeDtypeStruct((seq, width), BF16),
            jax.ShapeDtypeStruct((seq, 3 * width), BF16),
        ]
        + [jax.ShapeDtypeStruct((n * w.shape[0], w.shape[1]), w.dtype) for w in first + rest],
        in_specs=[smem, smem, whole, pl.BlockSpec((3, block), lambda i: (0, i)), whole, whole]
        + [anywhere] * len(first + rest),
        out_specs=[
            columns, columns,
            pl.BlockSpec((QUAD, seq, 3 * LANE), lambda i: (i, 0, 0)),
            whole, whole, whole,
        ]
        + [anywhere] * (1 + len(first + rest)),
        scratch_shapes=[
            pltpu.VMEM((CQ, seq, 3 * LANE), BF16),
            pltpu.VMEM((3 * LANE * CQ, 3 * LANE), BF16),
            pltpu.VMEM((QUAD, seq, HEAD_DIM), BF16),
            pltpu.VMEM((QUAD, seq, HEAD_DIM), BF16),
            pltpu.VMEM((QUAD, seq, HEAD_DIM), BF16),
            pltpu.VMEM((CQ, seq, HEAD_DIM), BF16),
            pltpu.VMEM((QUAD, seq, HEAD_DIM), F32),
            pltpu.VMEM((3 * quads, seq, block), BF16),
            pltpu.VMEM((2, width, block), BF16),
            pltpu.VMEM((quads, seq, block), BF16),
            pltpu.VMEM((width, width), BF16),
            dma((2,)), dma((3 * quads,)), dma,
        ]
        + Gather.scratch(len(first), n)
        + Gather.scratch(len(rest), n),
        compiler_params=pltpu.CompilerParams(
            collective_id=collective, has_side_effects=True, vmem_limit_bytes=60 * 1024 * 1024
        ),
    )(
        docs, head_mixing, pad_taps(conv_kernel), gains, layer_input, gains,
        *first, *rest,
    )
    return results[:7], results[7 : 7 + len(first)], results[7 + len(first) :]


def backward_kernel(
    n, specs, done_specs, docs_ref, mix_ref, taps_ref, gain_ref, q_ref, k_ref, v_ref, attended_ref, d_grouped_ref, soft_ref, *refs
):
    count, done = len(specs), len(done_specs)
    grads, done_sums, refs = refs[:count], refs[count : count + done], refs[count + done :]
    d_projected, grad_gain_ref, grad_taps_ref, grad_mix_ref = refs[:4]
    sums, others, refs = refs[4 : 4 + count], refs[4 + count : 4 + 2 * count], refs[4 + 2 * count :]
    done_totals, refs = refs[:done], refs[done:]
    final_size = len(FinalSum.scratch(done_specs))
    masks, band, qs, ks, vs, ds, shifted, d_heads, d_rows, d_cols, near_keys, leaving, leave_sem = refs[:13]
    reduce = Reduce(Ring(n), grads, sums, others, specs, refs[13 + final_size :])
    final = FinalSum(reduce.ring, done_sums, done_totals, done_specs, refs[13 : 13 + final_size])
    seq = q_ref.shape[0]
    quad = pl.program_id(0)

    @pl.when(quad == 0)
    def _():
        reduce.clear()
        reduce.ring.meet()
        reduce.start()
        for i in range(done):
            final.start(i)

    @pl.when(quad == 0)
    def _():
        fill_masks(docs_ref, masks, seq)
        band[...] = jnp.zeros_like(band)

    gains = []
    for h in range(QUAD):
        at = slice(h * HEAD_DIM, (h + 1) * HEAD_DIM)
        qs[h] = q_ref[:, at]
        ks[h] = k_ref[:, at]
        vs[h] = v_ref[:, at]
        attended = attended_ref[:, at]
        d_grouped = d_grouped_ref[:, at]
        centred = attended - jnp.mean(attended, axis=1, keepdims=True)
        var = jnp.mean(centred * centred, axis=1, keepdims=True)
        scale = lax.rsqrt(var + EPSILON)
        unit = centred * scale
        gains.append(jnp.sum(d_grouped * unit, axis=0, keepdims=True))
        w = d_grouped * gain_ref[:, at]
        d_attended = scale * (
            w
            - jnp.mean(w, axis=1, keepdims=True)
            - unit * jnp.mean(w * unit, axis=1, keepdims=True)
        )
        ds[h] = d_attended.astype(BF16)
    grad_gain_ref[...] = jnp.concatenate(gains, axis=1)
    grad_taps_ref[...] = jnp.zeros_like(grad_taps_ref)
    grad_mix_ref[...] = jnp.zeros_like(grad_mix_ref)

    sets = row_sets(seq)
    up = lax.broadcasted_iota(jnp.int32, (LANE, LANE), 0)
    across = lax.broadcasted_iota(jnp.int32, (LANE, LANE), 1)
    flip = jnp.where(up + across == LANE - 1, 1.0, 0.0).astype(BF16)
    gap = up + across - (LANE - 1)
    keeps = {0: jnp.abs(gap) <= CK // 2, 1: gap <= CK // 2 - LANE, -1: gap >= LANE - CK // 2}

    def pair(p, carry):
        group = quad * 2 + p
        mix = [[mix_ref[group, r, s] for s in range(2)] for r in range(2)]
        upstream_t = [ds[2 * p + r].T for r in range(2)]
        grad_mix = [[jnp.zeros((1, 1), F32) for _ in range(2)] for _ in range(2)]
        for r in range(2):
            d_cols[r] = jnp.zeros_like(d_cols[r])
        for r0, width, c0 in sets:
            rows = slice(r0, r0 + LANE)
            soft = [soft_ref[2 * p + s, rows, :width].astype(F32) for s in range(2)]
            d_prob, sums = [], []
            for r in range(2):
                dp = nt(ds[2 * p + r, rows], vs[2 * p + r, c0 : c0 + width])
                d_prob.append(dp)
                sums.append([jnp.sum(dp * soft[s], axis=1, keepdims=True) for s in range(2)])
                for s in range(2):
                    grad_mix[r][s] += jnp.sum(sums[r][s], axis=0, keepdims=True)
                mixed = (mix[r][0] * soft[0] + mix[r][1] * soft[1]).astype(BF16)
                d_cols[r, :, c0 : c0 + width] += nn(upstream_t[r][:, r0 : r0 + LANE], mixed)
            for s in range(2):
                d_soft = mix[0][s] * d_prob[0] + mix[1][s] * d_prob[1]
                inner = mix[0][s] * sums[0][s] + mix[1][s] * sums[1][s]
                d_conv = soft[s] * (d_soft - inner)
                d_rows[s, rows, :width] = d_conv.astype(BF16)
        lane = lax.broadcasted_iota(jnp.int32, (1, LANE), 1)
        line = jnp.zeros((1, LANE), F32)
        for r in range(2):
            for s in range(2):
                line = line + jnp.where(lane == 2 * r + s, grad_mix[r][s], 0.0)
        grad_mix_ref[0, pl.ds(p, 1), :] = line
        for r in range(2):
            d_heads[2, 2 * p + r] = d_cols[r].T

        for r in range(2):
            h = 2 * p + r
            fill_backward_band(taps_ref, quad * QUAD + h, band)
            for a, moved in enumerate(shifted_rows(qs[h])):
                shifted[a] = moved
            keys = ks[h]
            d_cols[0] = jnp.zeros_like(d_cols[0])
            d_query = []
            below = jnp.zeros((8, LANE * CQ), F32)
            above = jnp.zeros((8, LANE * CQ), F32)
            mirrored = []
            for r0, width, c0 in sets:
                rows = slice(r0, r0 + LANE)
                left, parts = masked_scores(shifted, keys, masks, r0, width, c0)
                d_conv = d_rows[r, rows, :width]
                blocks = width // LANE
                flipped = [
                    nt(flip, d_conv[:, b * LANE : (b + 1) * LANE]).astype(BF16) for b in range(blocks)
                ]
                start = len(mirrored) * LANE
                mirrored += flipped
                for b in range(blocks):
                    near_keys[start + b * LANE : start + (b + 1) * LANE, :] = jnp.concatenate(
                        [parts[a][:, b * LANE : (b + 1) * LANE] for a in range(CQ)], axis=1
                    )
                if blocks > 1:
                    end = start + blocks * LANE
                    below = below + nn(
                        jnp.concatenate([f[:8] for f in flipped[:-1]], axis=1), near_keys[start + LANE : end, :]
                    )
                    above = above + nn(
                        jnp.concatenate([f[LANE - 8 :] for f in flipped[1:]], axis=1), near_keys[start : end - LANE, :]
                    )
                spread = nn(d_conv, band[:width, : width * CQ]).astype(BF16)
                stacked = jnp.concatenate(
                    [
                        jnp.concatenate(
                            [
                                spread[:, (b * CQ + a) * LANE : (b * CQ + a + 1) * LANE]
                                for b in range(blocks)
                            ],
                            axis=1,
                        )
                        * masks[a, rows, :width]
                        for a in range(CQ)
                    ],
                    axis=0,
                )
                d_query.append(nn(stacked, keys[c0 : c0 + width]))
                d_cols[0, :, c0 : c0 + width] += nn(left.T, stacked)
            total = None
            for a in range(CQ):
                whole = jnp.concatenate([d[a * LANE : (a + 1) * LANE] for d in d_query], axis=0)
                if a:
                    whole = pltpu.roll(whole, seq - a, axis=0)
                total = whole if total is None else total + whole
            d_heads[0, h] = total
            d_heads[1, h] = d_cols[0].T
            band_sum = nn(jnp.concatenate(mirrored, axis=1), near_keys[: len(mirrored) * LANE, :])
            for a in range(CQ):
                at = slice(a * LANE, (a + 1) * LANE)
                whole = jnp.where(keeps[0], band_sum[:, at], 0.0)
                whole = jnp.concatenate(
                    [
                        whole[:8] + jnp.where(keeps[1][:8], below[:, at], 0.0),
                        whole[8 : LANE - 8],
                        whole[LANE - 8 :] + jnp.where(keeps[-1][LANE - 8 :], above[:, at], 0.0),
                    ],
                    axis=0,
                )
                aligned = pltpu.roll(whole, 0, axis=1, stride=1, stride_axis=0)
                grad_taps_ref[h, a : a + 1, :] = jnp.sum(aligned, axis=0, keepdims=True)
            work = reduce.each()
            middle = len(work) // 2
            for j in in_turn(group, HEADS // 2, n):
                pl.when(j < n)(functools.partial(reduce.item, j, work[middle:] if r else work[:middle]))
        return carry

    lax.fori_loop(0, 2, pair, 0)
    quads = HEADS // QUAD
    block = QUAD * HEAD_DIM

    def leave(part):
        there = d_projected.at[:, cols((part * quads + quad) * block, block)]
        return pltpu.make_async_copy(leaving.at[part], there, leave_sem.at[part])

    for part in range(3):
        pl.when(quad > 0)(leave(part).wait)
        leaving[part] = jnp.concatenate([d_heads[part, h] for h in range(QUAD)], axis=1).astype(BF16)
        leave(part).start()

    @pl.when(quad == quads - 1)
    def _():
        for part in range(3):
            leave(part).wait()
        for i in range(done):
            final.add(i)

    @pl.when(quad == pl.num_programs(0) - 1)
    def _():
        reduce.finish()
        final.finish()


def attend_backward(projected, conv_kernel, head_mixing, docs, gain, attended, d_grouped, soft, grads, done_sums, done_specs, n, collective):
    seq = projected.shape[0]
    width = projected.shape[1] // 3
    block = QUAD * HEAD_DIM
    quads = HEADS // QUAD
    count = len(grads)
    specs = Reduce.specs_of(grads, n, (LESS, THIRD, THIRD))
    anywhere = pl.BlockSpec(memory_space=pl.ANY)
    whole = pl.BlockSpec(memory_space=pltpu.VMEM)
    smem = pl.BlockSpec(memory_space=pltpu.SMEM)

    def columns(first):
        return pl.BlockSpec((seq, block), lambda i: (0, first * quads + i))

    results = pl.pallas_call(
        functools.partial(backward_kernel, n, specs, done_specs),
        grid=(quads,),
        out_shape=[
            jax.ShapeDtypeStruct((seq, 3 * width), BF16),
            jax.ShapeDtypeStruct((1, width), F32),
            jax.ShapeDtypeStruct((HEADS, 8, LANE), F32),
            jax.ShapeDtypeStruct((quads, 8, LANE), F32),
        ]
        + Reduce.results(specs, n)
        + [jax.ShapeDtypeStruct(spec[:2], BF16) for spec in done_specs],
        in_specs=[
            smem, smem, whole,
            pl.BlockSpec((1, block), lambda i: (0, i)),
            columns(0), columns(1), columns(2), columns(0), columns(0),
            pl.BlockSpec((QUAD, seq, 3 * LANE), lambda i: (i, 0, 0)),
        ]
        + [anywhere] * (count + len(done_specs)),
        out_specs=[
            anywhere,
            pl.BlockSpec((1, block), lambda i: (0, i)),
            pl.BlockSpec((QUAD, 8, LANE), lambda i: (i, 0, 0)),
            pl.BlockSpec((1, 8, LANE), lambda i: (i, 0, 0)),
        ]
        + [anywhere] * (2 * count + len(done_specs)),
        scratch_shapes=[
            pltpu.VMEM((CQ, seq, 3 * LANE), BF16),
            pltpu.VMEM((3 * LANE, 3 * LANE * CQ), BF16),
            pltpu.VMEM((QUAD, seq, HEAD_DIM), BF16),
            pltpu.VMEM((QUAD, seq, HEAD_DIM), BF16),
            pltpu.VMEM((QUAD, seq, HEAD_DIM), BF16),
            pltpu.VMEM((QUAD, seq, HEAD_DIM), BF16),
            pltpu.VMEM((CQ, seq, HEAD_DIM), BF16),
            pltpu.VMEM((3, QUAD, seq, HEAD_DIM), F32),
            pltpu.VMEM((2, seq, 3 * LANE), BF16),
            pltpu.VMEM((2, HEAD_DIM, seq), F32),
            pltpu.VMEM((sum(w for _, w, _ in row_sets(seq)), LANE * CQ), BF16),
            pltpu.VMEM((3, seq, block), BF16),
            pltpu.SemaphoreType.DMA((3,)),
        ]
        + FinalSum.scratch(done_specs)
        + Reduce.scratch(specs, n),
        compiler_params=pltpu.CompilerParams(
            collective_id=collective, has_side_effects=True, vmem_limit_bytes=62 * 1024 * 1024
        ),
    )(
        docs, head_mixing, pad_taps(conv_kernel[:, :, ::-1]), gain.reshape(1, width),
        projected, projected, projected, attended, d_grouped, soft, *grads, *done_sums,
    )
    d_projected, grad_gain, grad_taps, grad_mix = results[:4]
    return (
        d_projected, grad_gain, grad_taps, grad_mix,
    ), list(results[4 : 4 + count]), specs, results[4 + 2 * count :]


MESH = pl.DeviceIdType.MESH


def ring_index(place, n):
    place = lax.rem(place + 2 * n, n)
    return jnp.where(place < n // 2, 2 * place, 2 * (n - 1 - place) + 1)


def ring_place(index, n):
    half = lax.div(index, 2)
    return jnp.where(lax.rem(index, 2) == 0, half, n - 1 - half)


class Ring:
    def __init__(self, n):
        self.n = n
        rep = lax.axis_index("rep")
        self.x, self.core = lax.div(rep, 2), lax.rem(rep, 2)
        index = lax.axis_index("fsdp")
        self.index = index
        self.place = ring_place(index, n)
        self.right = (rep, ring_index(self.place + 1, n))
        self.left = (rep, ring_index(self.place - 1, n))
        self.sibling = (self.x * 2 + 1 - self.core, index)
        self.across = ((1 - self.x) * 2 + self.core, index)

    def meet(self):
        barrier = pltpu.get_barrier_semaphore()
        for other in (self.right, self.left, self.sibling, self.across):
            pl.semaphore_signal(barrier, inc=1, device_id=other, device_id_type=MESH)
        pl.semaphore_wait(barrier, 4)


def send(src, dst, send_sem, recv_sem, device):
    return pltpu.make_async_remote_copy(
        src_ref=src, dst_ref=dst, send_sem=send_sem, recv_sem=recv_sem,
        device_id=device, device_id_type=MESH,
    )


def cols(start, size):
    return pl.ds(pl.multiple_of(start, LANE), size)


class Gather:
    def __init__(self, ring, weights, fulls, widths, sems):
        self.ring, self.weights, self.fulls = ring, weights, fulls
        self.axes, self.widths = zip(*widths)
        (self.own, self.ring_send, self.ring_recv, self.core_send, self.core_recv, self.x_send, self.x_recv) = sems

    def windows(self, i):
        ring = self.ring
        half = self.weights[i].shape[self.axes[i]] // 2
        w = self.widths[i]
        base = ring.core * half
        part = half - 2 * w
        first = base + jnp.where(ring.x == 0, 0, half - w)
        second = base + jnp.where(ring.x == 0, w, half - 2 * w)
        give = base + jnp.where(ring.x == 0, 0, half - part)
        take = base + jnp.where(ring.x == 0, half - part, 0)
        return w, part, first, second, give, take

    def block(self, i, index, start, width):
        rows = self.weights[i].shape[0]
        if self.axes[i] == 0:
            return self.fulls[i].at[pl.ds(pl.multiple_of(index * rows + start, 16), width), :]
        return self.fulls[i].at[pl.ds(pl.multiple_of(index * rows, 16), rows), cols(start, width)]

    def piece(self, i, start, width):
        if self.axes[i] == 0:
            return self.weights[i].at[pl.ds(pl.multiple_of(start, 16), width), :]
        return self.weights[i].at[:, cols(start, width)]

    def ring_copy(self, i, d, k, source):
        ring = self.ring
        w, _, first, second, _, _ = self.windows(i)
        start = second if d else first
        index = ring_index(ring.place + (k if d else -k), ring.n)
        there = self.block(i, index, start, w)
        src = self.piece(i, start, w) if source else there
        return send(src, there, self.ring_send.at[i, d, k], self.ring_recv.at[i, d, k], ring.left if d else ring.right)

    def core_copy(self, i, d, k):
        ring = self.ring
        w, part, first, second, _, take = self.windows(i)
        start, width = ((first, w), (second, w), (take, part))[d]
        index = ring_index(ring.place + (k + 1 if d == 1 else -k - 1), ring.n)
        there = self.block(i, index, start, width)
        return send(there, there, self.core_send.at[i, d, k], self.core_recv.at[i, d, k], ring.sibling)

    def x_copy(self, i, k):
        ring = self.ring
        _, part, _, _, give, _ = self.windows(i)
        there = self.block(i, ring_index(ring.place - k - 1, ring.n), give, part)
        return send(there, there, self.x_send.at[i, k], self.x_recv.at[i, k], ring.across)

    def own_copy(self, i):
        rows = self.weights[i].shape[0]
        there = self.fulls[i].at[pl.ds(pl.multiple_of(self.ring.index * rows, 16), rows), :]
        return send(self.weights[i], there, self.own.at[0, i], self.own.at[1, i], self.ring.sibling)

    def has_part(self, i):
        return self.weights[i].shape[self.axes[i]] // 2 > 2 * self.widths[i]

    def start(self):
        for i in range(len(self.weights)):
            for d in range(2):
                self.ring_copy(i, d, 0, True).start()
        for i in range(len(self.weights)):
            self.own_copy(i).start()

    def step(self, k):
        last = self.ring.n - 2
        for i in range(len(self.weights)):
            for d in range(2):
                self.ring_copy(i, d, k, False).wait_recv()

                @pl.when(k < last)
                def _():
                    self.ring_copy(i, d, k + 1, False).start()

                if d == 0 and self.has_part(i):
                    self.x_copy(i, k).start()
                self.core_copy(i, d, k).start()

            if self.has_part(i):
                @pl.when(k >= LAG)
                def _():
                    self.pass_on(i, k - LAG)

    def pass_on(self, i, k):
        self.x_copy(i, k).wait_recv()
        self.core_copy(i, 2, k).start()

    def finish(self):
        last = self.ring.n - 2
        for k in range(max(0, last + 1 - LAG), last + 1):
            for i in range(len(self.weights)):
                if self.has_part(i):
                    self.pass_on(i, k)

        def settle(k, carry):
            for i in range(len(self.weights)):
                for d in range(2):
                    self.ring_copy(i, d, k, False).wait_send()
                    self.core_copy(i, d, k).wait()
                if self.has_part(i):
                    self.x_copy(i, k).wait_send()
                    self.core_copy(i, 2, k).wait()
            return carry

        lax.fori_loop(0, self.ring.n - 1, settle, 0)
        for i in range(len(self.weights)):
            self.own_copy(i).wait()

    @staticmethod
    def scratch(count, n):
        dma = pltpu.SemaphoreType.DMA
        return [
            dma((2, count)), dma((count, 2, n - 1)), dma((count, 2, n - 1)),
            dma((count, 3, n - 1)), dma((count, 3, n - 1)), dma((count, n - 1)), dma((count, n - 1)),
        ]


def share(shape):
    rows, columns = shape
    axis, unit = (0, 16) if rows % 64 == 0 else (1, LANE)
    units = (rows, columns)[axis] // 2 // unit
    return axis, -(-units // 3) * unit


THIRD = (1, 3)
LESS = (7, 18)


def carried(columns, portion):
    half = columns // 2
    lanes = -(-(half // LANE) * portion[0] // portion[1]) * LANE
    if 2 * lanes >= half:
        return half // 2, 0
    return lanes, half - 2 * lanes


class Reduce:
    def __init__(self, ring, grads, sums, others, specs, scratch):
        self.ring, self.grads, self.sums, self.others, self.specs = ring, grads, sums, others, specs
        count = len(grads)
        self.slots, self.mine, self.twin, self.x_slots, self.x_out = [], [], [], [], []
        scratch = list(scratch)
        for spec in specs:
            part = carried(spec[1], spec[2])[1]
            take = [scratch.pop(0) for _ in range(10 if part else 6)]
            self.slots.append(take[:2])
            self.mine.append(take[2:4] + take[6:7])
            self.twin.append(take[4:6] + take[7:8])
            self.x_slots.append(take[8] if part else None)
            self.x_out.append(take[9] if part else None)
        (self.load, self.ring_send, self.ring_recv, self.core_send, self.core_recv,
         self.x_send, self.x_recv, self.keep) = scratch

    def owner(self, kind, j):
        ring = self.ring
        return ring_index(ring.place + (j + 1 if kind == 1 else -j - 1), ring.n)

    def span(self, i, kind):
        columns, shared = self.specs[i][1:]
        w, part = carried(columns, shared)
        half = columns // 2
        lower, upper = ((0, half - w), (w, half - 2 * w), (half - part, 0))[kind]
        return jnp.where(self.ring.x == 0, lower, upper), part if kind == 2 else w

    def rows(self, i, index):
        rows = self.specs[i][0]
        return pl.ds(pl.multiple_of(index * rows, 16), rows)

    def kinds(self, i):
        return 3 if self.x_slots[i] is not None else 2

    def core_copy(self, i, kind, j):
        ring = self.ring
        start, width = self.span(i, kind)
        rows = self.rows(i, self.owner(kind, j))
        half = self.specs[i][1] // 2
        return send(
            self.grads[i].at[rows, cols((1 - ring.core) * half + start, width)], self.others[i].at[rows, cols(start, width)],
            self.core_send.at[i, kind, j], self.core_recv.at[i, kind, j], ring.sibling,
        )

    def loads(self, i, kind, j):
        start, width = self.span(i, kind)
        rows = self.rows(i, self.owner(kind, j))
        base = self.ring.core * (self.specs[i][1] // 2)
        return (
            pltpu.make_async_copy(
                self.grads[i].at[rows, cols(base + start, width)], self.mine[i][kind], self.load.at[i, kind, 0]
            ),
            pltpu.make_async_copy(self.others[i].at[rows, cols(start, width)], self.twin[i][kind], self.load.at[i, kind, 1]),
        )

    def fetch(self, i, kind, j):
        own, other = self.loads(i, kind, j)
        own.start()
        self.core_copy(i, kind, j).wait_recv()
        other.start()

    def ring_copy(self, i, d, j):
        ring = self.ring
        return send(
            self.slots[i][d].at[j], self.slots[i][d].at[j + 1],
            self.ring_send.at[i, d, j], self.ring_recv.at[i, d, j + 1], ring.left if d else ring.right,
        )

    def gap(self, i):
        w, part = carried(*self.specs[i][1:])
        x = self.ring.x
        return w - part, jnp.where(x == 0, part, 0), jnp.where(x == 0, w - part, 0), part

    def x_copy(self, i, j):
        _, _, at, part = self.gap(i)
        return send(
            self.x_out[i].at[lax.rem(j, 2)], self.x_slots[i].at[j, :, cols(at, part)],
            self.x_send.at[i, j], self.x_recv.at[i, j], self.ring.across,
        )

    def give(self, i, j):
        j = jnp.int32(j)
        for copy in self.loads(i, 2, j):
            copy.wait()

        @pl.when(j >= 2)
        def _():
            self.x_copy(i, j - 2).wait_send()

        self.x_out[i][lax.rem(j, 2)] = (self.mine[i][2][...].astype(F32) + self.twin[i][2][...].astype(F32)).astype(BF16)
        self.x_copy(i, j).start()
        self.hand_next(i, 2, j)

        @pl.when(j < self.ring.n - 1)
        def _():
            self.fetch(i, 2, j + 1)

    def each(self):
        return [(i, d) for i in range(len(self.grads)) for d in (1, 0)]

    def clear(self):
        for i in range(len(self.grads)):
            if self.kinds(i) == 3:
                width, at, _, _ = self.gap(i)
                if width:
                    rows = self.specs[i][0]
                    self.x_slots[i][:, :, cols(at, width)] = jnp.zeros((self.ring.n, rows, width), BF16)

    def hand_over(self):
        for j in range(min(LEAD, self.ring.n)):
            for i in range(len(self.grads)):
                for kind in reversed(range(self.kinds(i))):
                    self.core_copy(i, kind, j).start()

    def hand_next(self, i, kind, j):
        pl.when(j + LEAD < self.ring.n)(lambda: self.core_copy(i, kind, j + LEAD).start())

    def fetch_first(self):
        for i in range(len(self.grads)):
            for kind in reversed(range(self.kinds(i))):
                self.fetch(i, kind, 0)

    def give_all(self, j):
        for i in range(len(self.grads)):
            if self.kinds(i) == 3:
                self.give(i, j)

    def opening(self):
        return [
            self.hand_over, self.fetch_first,
            functools.partial(self.give_all, 0), functools.partial(self.give_all, 1),
        ]

    def start(self):
        for step in self.opening():
            step()

    def item(self, j, work):
        last = self.ring.n - 1
        for i, d in work:
            if d == 0 and self.kinds(i) == 3:
                pl.when(j < last - 1)(functools.partial(self.give, i, j + 2))
            for copy in self.loads(i, d, j):
                copy.wait()
            slot = self.slots[i][d]
            both = self.mine[i][d][...].astype(F32) + self.twin[i][d][...].astype(F32)
            if d == 0 and self.kinds(i) == 3:
                self.x_copy(i, j).wait_recv()
                both = both + self.x_slots[i][j].astype(F32)

            @pl.when(j == 0)
            def _():
                slot[j] = both.astype(BF16)

            @pl.when(j > 0)
            def _():
                self.ring_copy(i, d, j - 1).wait_recv()
                slot[j] = (slot[j].astype(F32) + both).astype(BF16)

            @pl.when(j < last)
            def _():
                self.ring_copy(i, d, j).start()
                self.fetch(i, d, j + 1)

            self.hand_next(i, d, j)

            @pl.when(j == last)
            def _():
                self.keep_copy(i, d).start()

    def keep_copy(self, i, d):
        w = carried(*self.specs[i][1:])[0]
        at = jnp.where(self.ring.x == 0, d * w, (1 - d) * w)
        return pltpu.make_async_copy(self.slots[i][d].at[self.ring.n - 1], self.sums[i].at[:, cols(at, w)], self.keep.at[i, d])

    def finish(self):
        last = self.ring.n - 1
        for i, d in self.each():
            self.keep_copy(i, d).wait()

        def settle(j, carry):
            for i in range(len(self.grads)):
                for kind in range(self.kinds(i)):
                    self.core_copy(i, kind, j).wait_send()
                for d in range(2):
                    pl.when(j < last)(lambda i=i, d=d: self.ring_copy(i, d, j).wait_send())
                if self.kinds(i) == 3:
                    pl.when(j >= last - 1)(lambda i=i: self.x_copy(i, j).wait_send())
            return carry

        lax.fori_loop(0, self.ring.n, settle, 0)

    @staticmethod
    def specs_of(grads, n, portions):
        return [(g.shape[0] // n, g.shape[1], portion) for g, portion in zip(grads, portions)]

    @staticmethod
    def results(specs, n):
        return [
            jax.ShapeDtypeStruct((rows, 2 * carried(columns, shared)[0]), BF16) for rows, columns, shared in specs
        ] + [jax.ShapeDtypeStruct((n * rows, columns // 2), BF16) for rows, columns, _ in specs]

    @staticmethod
    def scratch(specs, n):
        dma = pltpu.SemaphoreType.DMA
        count = len(specs)
        buffers = []
        for rows, columns, shared in specs:
            w, part = carried(columns, shared)
            buffers += [pltpu.VMEM((n, rows, w), BF16)] * 2 + [pltpu.VMEM((rows, w), BF16)] * 4
            if part:
                buffers += [pltpu.VMEM((rows, part), BF16)] * 2
                buffers += [pltpu.VMEM((n, rows, w), BF16), pltpu.VMEM((2, rows, part), BF16)]
        return buffers + [
            dma((count, 3, 2)), dma((count, 2, n)), dma((count, 2, n)), dma((count, 3, n)), dma((count, 3, n)),
            dma((count, n)), dma((count, n)), dma((count, 2)),
        ]


class FinalSum:
    def __init__(self, ring, sums, totals, specs, scratch):
        self.ring, self.sums, self.totals, self.specs = ring, sums, totals, specs
        scratch = list(scratch)
        self.mine, self.plane, self.own = [], [], []
        for spec in specs:
            self.mine.append(scratch.pop(0))
            self.plane.append(scratch.pop(0))
            self.own.append(scratch.pop(0) if carried(spec[1], spec[2])[1] else None)
        self.local, self.remote_send, self.remote_recv = scratch

    def spans(self, i):
        columns, shared = self.specs[i][1:]
        w, part = carried(columns, shared)
        half, wide = columns // 2, 2 * w - part
        base = self.ring.core * half
        low = self.ring.x == 0
        return (
            (jnp.where(low, part, 0), base + part, wide),
            (jnp.where(low, 0, wide), base + jnp.where(low, 0, half - part), part),
            (0, base + jnp.where(low, half - part, 0), part),
        )

    def remote(self, i, at, src, dst, device):
        return send(src, dst, self.remote_send.at[i, at], self.remote_recv.at[i, at], device)

    def copy(self, i, name):
        ring, sums, totals = self.ring, self.sums[i], self.totals[i]
        (a, a_out, wide), (b, b_out, part), (_, c_out, _) = self.spans(i)
        local = {"load": 0, "save": 1, "load done": 2, "save done": 3}
        remote = {"across": 0, "sibling": 1, "done across": 2, "done sibling": 3, "pass on": 4}
        if name in ("load", "save", "across", "sibling"):
            src, dst, mid = sums.at[:, cols(a, wide)], totals.at[:, cols(a_out, wide)], self.mine[i]
        elif name == "pass on":
            src = dst = mid = totals.at[:, cols(c_out, part)]
        else:
            src, dst, mid = sums.at[:, cols(b, part)], totals.at[:, cols(b_out, part)], self.own[i]
        if name in local:
            ends = (src, mid) if name.startswith("load") else (mid, dst)
            return pltpu.make_async_copy(*ends, self.local.at[i, local[name]])
        ends = {"across": (src, self.plane[i]), "sibling": (mid, dst)}.get(name, (src, dst))
        device = ring.across if "across" in name else ring.sibling
        at = remote[name]
        return send(*ends, self.remote_send.at[i, at], self.remote_recv.at[i, at], device)

    def shares(self, i):
        return carried(*self.specs[i][1:])[1] > 0

    def start(self, i):
        for name in ("across", "load"):
            self.copy(i, name).start()
        if self.shares(i):
            for name in ("done across", "load done", "done sibling"):
                self.copy(i, name).start()

    def add(self, i):
        self.copy(i, "load").wait()
        self.copy(i, "across").wait_recv()
        self.mine[i][...] = (self.mine[i][...].astype(F32) + self.plane[i][...].astype(F32)).astype(BF16)
        self.copy(i, "sibling").start()
        self.copy(i, "save").start()
        if self.shares(i):
            self.copy(i, "load done").wait()
            self.copy(i, "save done").start()
            self.copy(i, "done across").wait_recv()
            self.copy(i, "pass on").start()

    def finish(self):
        for i in range(len(self.specs)):
            self.copy(i, "across").wait_send()
            self.copy(i, "sibling").wait()
            self.copy(i, "save").wait()
            if self.shares(i):
                self.copy(i, "done across").wait_send()
                for name in ("done sibling", "save done", "pass on"):
                    self.copy(i, name).wait()

    @staticmethod
    def scratch(specs):
        dma = pltpu.SemaphoreType.DMA
        count = len(specs)
        buffers = []
        for rows, columns, shared in specs:
            w, part = carried(columns, shared)
            buffers += [pltpu.VMEM((rows, 2 * w - part), BF16)] * 2
            if part:
                buffers += [pltpu.VMEM((rows, part), BF16)]
        return buffers + [dma((count, 4)), dma((count, 5)), dma((count, 5))]


class SmallSum:
    def __init__(self, ring, given, total, scratch):
        self.ring, self.given, self.total = ring, given, total
        self.mine, self.twin, self.plane, self.slots, self.pair, self.ring_send, self.ring_recv = scratch

    def copy(self, src, dst, at, device):
        return send(src, dst, self.pair.at[0, at], self.pair.at[1, at], device)

    def to_core(self):
        return self.copy(self.given, self.twin, 0, self.ring.sibling)

    def to_plane(self):
        return self.copy(self.mine, self.plane, 1, self.ring.across)

    def add_core(self):
        self.to_core().wait()
        self.mine[...] = self.given[...] + self.twin[...]
        self.to_plane().start()

    def add_plane(self):
        self.to_plane().wait()
        self.slots[0] = self.mine[...] + self.plane[...]

    def ring_copy(self, j):
        return send(
            self.slots.at[j], self.slots.at[j + 1], self.ring_send.at[j], self.ring_recv.at[j + 1], self.ring.right
        )

    def item(self, j):
        @pl.when(j > 0)
        def _():
            self.ring_copy(j - 1).wait_recv()

        @pl.when(j < self.ring.n - 1)
        def _():
            self.ring_copy(j).start()

    def finish(self):
        ring = self.ring
        total = jnp.zeros(self.total.shape, F32)
        for place in range(ring.n):
            total = total + self.slots[lax.rem(ring.place - place + ring.n, ring.n)]
        self.total[...] = total

        def settle(j, carry):
            self.ring_copy(j).wait_send()
            return carry

        lax.fori_loop(0, ring.n - 1, settle, 0)

    @staticmethod
    def scratch(rows, n):
        dma = pltpu.SemaphoreType.DMA
        block = pltpu.VMEM((rows, LANE), F32)
        return [block, block, block, pltpu.VMEM((n, rows, LANE), F32), dma((2, 2)), dma((n,)), dma((n,))]


SMALL_SCRATCH = 7


def pack(given, at, row):
    for r in range(row.shape[1] // LANE):
        given[at + r : at + r + 1, :] = row[:, r * LANE : (r + 1) * LANE]
    return at + row.shape[1] // LANE


SPOTS = 8


def pack_taps(given, at, taps_ref, mix_ref):
    rows = taps_ref.shape[1]
    for first in range(0, HEADS, SPOTS):
        together = taps_ref[first]
        for h in range(1, SPOTS):
            together = together + pltpu.roll(taps_ref[first + h], h * (LANE // SPOTS), axis=1)
        given[at : at + rows, :] = together
        at += rows
    together = mix_ref[0]
    for quad in range(1, mix_ref.shape[0]):
        together = together + pltpu.roll(mix_ref[quad], 2 * quad, axis=0)
    given[at : at + rows, :] = together


def unpack_taps(summed):
    rows = 8
    taps = jnp.roll(summed[: HEADS // SPOTS * rows], CK // 2 + 1, axis=1).reshape(-1, rows, SPOTS, LANE // SPOTS)
    taps = taps.transpose(0, 2, 1, 3).reshape(HEADS, rows, LANE // SPOTS)[:, :CQ, :CK]
    mixing = summed[HEADS // SPOTS * rows :][: HEADS // 2, :4]
    return taps[:, :, ::-1] * SCALE, mixing.reshape(HEADS // 2, 2, 2)


def last_kernel(n, specs, early_specs, chunk, small_count, *refs):
    count, early = len(specs), len(early_specs)
    ring = Ring(n)
    refs = list(refs)

    def take(size):
        taken = refs[:size]
        del refs[:size]
        return taken

    small_refs = take(small_count)
    input_ref, gain_ref, d_middle_ref, d_projected, weight = take(5)
    grads, early_sums = take(count), take(early)
    grad_input_ref, total_ref = take(2)
    totals, early_totals, sums, others = take(count), take(early), take(count), take(count)
    given, d_normed, in_left, in_right, in_sem = take(5)
    small = SmallSum(ring, given, total_ref, take(SMALL_SCRATCH))
    last_sum = FinalSum(ring, sums, totals, specs, take(len(FinalSum.scratch(specs))))
    early_sum = FinalSum(ring, early_sums, early_totals, early_specs, take(len(FinalSum.scratch(early_specs))))
    reduce = Reduce(ring, grads, sums, others, specs, refs)
    chunks = d_projected.shape[1] // chunk

    def arrive(t, slot):
        at = cols(t * chunk, chunk)
        return (
            pltpu.make_async_copy(d_projected.at[:, at], in_left.at[slot], in_sem.at[slot, 0]),
            pltpu.make_async_copy(weight.at[:, at], in_right.at[slot], in_sem.at[slot, 1]),
        )

    for copy in arrive(0, 0):
        copy.start()
    reduce.clear()
    ring.meet()

    def turn(t, carry):
        slot = lax.rem(t, 2)
        for copy in arrive(t, slot):
            copy.wait()

        @pl.when(t < chunks - 1)
        def _():
            for copy in arrive(t + 1, 1 - slot):
                copy.start()

        d_normed[...] += nt(in_left[slot], in_right[slot])
        return carry

    reduce.hand_over()
    d_normed[...] = jnp.zeros_like(d_normed)
    given[...] = jnp.zeros_like(given)
    lax.fori_loop(0, chunks // 3, turn, 0)
    for step in reduce.opening()[1:]:
        step()
    reduce.item(jnp.int32(0), reduce.each())
    lax.fori_loop(chunks // 3, chunks, turn, 0)
    values = input_ref[...].astype(F32)
    scale = lax.rsqrt(jnp.mean(values * values, axis=1, keepdims=True) + EPSILON)
    upstream = d_normed[...]
    grad_gain = jnp.sum(upstream * (values * scale), axis=0, keepdims=True)
    at = 0
    for row in [grad_gain] + [ref[...] for ref in small_refs[:2]]:
        at = pack(given, at, row)
    pack_taps(given, at, small_refs[2], small_refs[3])
    small.to_core().start()
    scaled = upstream * gain_ref[...]
    inner = jnp.mean(scaled * values, axis=1, keepdims=True)
    grad_input_ref[...] = d_middle_ref[...] + scale * scaled - values * (scale * scale * scale * inner)
    reduce.item(jnp.int32(1), reduce.each())
    small.add_core()
    reduce.item(jnp.int32(2), reduce.each())
    small.add_plane()
    hops = -(-n // (n - 4))

    def rest(j, carry):
        for hop in range(hops):
            at = (j - 3) * hops + hop
            pl.when(at < n)(functools.partial(small.item, at))
        for i in range(early):
            pl.when(j == 3 + i)(functools.partial(early_sum.start, i))
        reduce.item(j, reduce.each())
        for i in range(early):
            pl.when(j == n - early + i)(functools.partial(early_sum.add, i))
        return carry

    lax.fori_loop(3, n, rest, 0)
    reduce.finish()
    for i in range(count):
        last_sum.start(i)
    small.finish()
    for i in range(count):
        last_sum.add(i)
    early_sum.finish()
    last_sum.finish()


def last_step(
    d_projected, qkv_weight, layer_input, first_gain, d_middle, grads, smalls, early_sums, early_specs, n, collective
):
    count, early = len(grads), len(early_specs)
    seq, width = layer_input.shape
    chunk = 512
    specs = Reduce.specs_of(grads, n, (LESS,))
    sizes = [width // LANE] * 3 + [(HEADS // SPOTS + 1) * 8]
    rows = -(-sum(sizes) // 8) * 8
    anywhere = pl.BlockSpec(memory_space=pl.ANY)
    whole = pl.BlockSpec(memory_space=pltpu.VMEM)
    results = pl.pallas_call(
        functools.partial(last_kernel, n, specs, early_specs, chunk, len(smalls)),
        out_shape=[jax.ShapeDtypeStruct((seq, width), F32), jax.ShapeDtypeStruct((rows, LANE), F32)]
        + [jax.ShapeDtypeStruct(spec[:2], BF16) for spec in specs + early_specs]
        + Reduce.results(specs, n),
        in_specs=[whole] * (len(smalls) + 3) + [anywhere] * (2 + count + early),
        out_specs=[whole] * 2 + [anywhere] * (3 * count + early),
        scratch_shapes=[
            pltpu.VMEM((rows, LANE), F32),
            pltpu.VMEM((seq, width), F32),
            pltpu.VMEM((2, seq, chunk), BF16),
            pltpu.VMEM((2, width, chunk), BF16),
            pltpu.SemaphoreType.DMA((2, 2)),
        ]
        + SmallSum.scratch(rows, n)
        + FinalSum.scratch(specs)
        + FinalSum.scratch(early_specs)
        + Reduce.scratch(specs, n),
        compiler_params=pltpu.CompilerParams(
            collective_id=collective, has_side_effects=True, vmem_limit_bytes=60 * 1024 * 1024
        ),
    )(*smalls, layer_input, first_gain.reshape(1, width), d_middle, d_projected, qkv_weight, *grads, *early_sums)
    out, at = [], 0
    for size in sizes:
        out.append(results[1][at : at + size])
        at += size
    return results[0], results[2 : 2 + count + early], out


TILES = 8
EARLY_TILES = 3
LATE_TILES = 3


def mlp_kernel(n, specs, tile, *refs):
    refs = list(refs)

    def take(size):
        taken = refs[:size]
        del refs[:size]
        return taken

    second_ref, upstream_ref, middle, inner, down, coming = take(6)
    out_ref, d_second_ref = take(2)
    (early, late, grad_down), sums, others, (came,) = take(3), take(1), take(1), take(1)
    turned, out_sum, in_gate, in_up, in_down, to_gate, to_up, to_down = take(8)
    middle_sem, in_sem, to_sem = take(3)
    ring = Ring(n)
    gather = Gather(ring, [coming], [came], [share(coming.shape)], take(len(Gather.scratch(1, n))))
    reduce = Reduce(ring, [early], sums, others, specs, refs)
    hidden_size = down.shape[0]
    tiles = hidden_size // tile
    begun = EARLY_TILES
    each = -(-n // (tiles - begun - 1))
    due = -(-each // 2)

    split = tiles - LATE_TILES

    def arrive(t, slot, weight, first, count):
        at = pl.multiple_of((t - first) * tile, tile)
        return (
            pltpu.make_async_copy(weight.at[:, pl.ds(at, tile)], in_gate.at[slot], in_sem.at[slot, 0]),
            pltpu.make_async_copy(
                weight.at[:, pl.ds(pl.multiple_of(count * tile + at, tile), tile)], in_up.at[slot], in_sem.at[slot, 1]
            ),
            pltpu.make_async_copy(
                down.at[pl.ds(pl.multiple_of(t * tile, tile), tile), :], in_down.at[slot], in_sem.at[slot, 2]
            ),
        )

    def arrivals(t, act):
        slot = lax.rem(t, 2)

        @pl.when(t < split)
        def _():
            for copy in arrive(t, slot, inner, 0, split):
                act(copy)

        @pl.when((t >= split) & (t < tiles))
        def _():
            for copy in arrive(t, slot, came, split, LATE_TILES):
                act(copy)

    def leave(grad, t, slot, first, count):
        at = pl.multiple_of((t - first) * tile, tile)
        return (
            pltpu.make_async_copy(to_gate.at[slot], grad.at[:, pl.ds(at, tile)], to_sem.at[slot, 0]),
            pltpu.make_async_copy(
                to_up.at[slot], grad.at[:, pl.ds(pl.multiple_of(count * tile + at, tile), tile)], to_sem.at[slot, 1]
            ),
            pltpu.make_async_copy(
                to_down.at[slot], grad_down.at[pl.ds(pl.multiple_of(t * tile, tile), tile), :], to_sem.at[slot, 2]
            ),
        )

    def leave_early(t):
        return leave(early, t, lax.rem(t, 2), 0, begun)

    def leave_late(t):
        return leave(late, t, lax.rem(t, 2), begun, tiles - begun)

    first = pltpu.make_async_copy(middle, out_sum, middle_sem)
    first.start()
    arrivals(jnp.int32(0), lambda copy: copy.start())
    reduce.clear()
    ring.meet()
    gather.start()
    turned[...] = second_ref[...].T
    d_second_ref[...] = jnp.zeros_like(d_second_ref)
    first.wait()

    def serve(t, point):
        turns = 2 * (split - 1) - 1
        if point % 2:
            turn = 2 * t + point // 2
            for k in in_turn(turn, turns, n - 1):
                pl.when((turn < turns) & (k < n - 1))(functools.partial(gather.step, k))
            pl.when(turn == turns)(gather.finish)

        @pl.when(t == begun)
        def _():
            if point == 0:
                for back in (2, 1):
                    for copy in leave_early(t - back):
                        copy.wait()
            reduce.opening()[point]()

        for step in range(due):
            if point // 2 * due + step < each:
                j = (t - begun - 1) * each + point // 2 * due + step
                pl.when((t > begun) & (j < n))(functools.partial(reduce.item, j, [(0, 1 - point % 2)]))

    def one(t, carry):
        slot = lax.rem(t, 2)
        arrivals(t, lambda copy: copy.wait())
        arrivals(t + 1, lambda copy: copy.start())
        second, upstream = second_ref[...], upstream_ref[...]
        gate = nn(second, in_gate[slot])
        up = nn(second, in_up[slot])
        sigmoid = jax.nn.sigmoid(gate)
        silu = gate * sigmoid
        hidden = (silu * up).astype(BF16)
        serve(t, 0)
        d_hidden = nt(upstream, in_down[slot])
        out_sum[...] += nn(hidden, in_down[slot])

        @pl.when((t >= 2) & (t < begun))
        def _():
            for copy in leave_early(t - 2):
                copy.wait()

        @pl.when(t >= begun + 2)
        def _():
            for copy in leave_late(t - 2):
                copy.wait()

        to_down[slot] = nn(hidden.T, upstream).astype(BF16)
        d_gate = (d_hidden * up * sigmoid * (1.0 + gate * (1.0 - sigmoid))).astype(BF16)
        d_up = (d_hidden * silu).astype(BF16)
        serve(t, 1)
        d_second_ref[...] += nt(d_gate, in_gate[slot])
        to_gate[slot] = nn(turned[...], d_gate).astype(BF16)
        serve(t, 2)
        d_second_ref[...] += nt(d_up, in_up[slot])
        to_up[slot] = nn(turned[...], d_up).astype(BF16)
        serve(t, 3)

        @pl.when(t < begun)
        def _():
            for copy in leave_early(t):
                copy.start()

        @pl.when(t >= begun)
        def _():
            for copy in leave_late(t):
                copy.start()

        return carry

    lax.fori_loop(0, tiles, one, 0)
    out_ref[...] = out_sum[...].astype(BF16)
    for t in (tiles - 2, tiles - 1):
        for copy in leave_late(t):
            copy.wait()
    reduce.finish()


def feed_forward(second, upstream, middle, inner, down, coming, n, collective):
    seq, width = second.shape
    hidden_size = down.shape[0]
    tile = hidden_size // TILES
    early = EARLY_TILES * tile
    specs = [(width // n, 2 * early, THIRD)]
    whole = pl.BlockSpec(memory_space=pltpu.VMEM)
    anywhere = pl.BlockSpec(memory_space=pl.ANY)
    dma = pltpu.SemaphoreType.DMA
    results = pl.pallas_call(
        functools.partial(mlp_kernel, n, specs, tile),
        out_shape=[
            jax.ShapeDtypeStruct((seq, width), BF16),
            jax.ShapeDtypeStruct((seq, width), F32),
        ]
        + [
            jax.ShapeDtypeStruct((width, 2 * early), BF16),
            jax.ShapeDtypeStruct((width, 2 * (hidden_size - early)), BF16),
            jax.ShapeDtypeStruct((hidden_size, width), BF16),
        ]
        + Reduce.results(specs, n)
        + [jax.ShapeDtypeStruct((n * coming.shape[0], coming.shape[1]), BF16)],
        in_specs=[whole, whole] + [anywhere] * 4,
        out_specs=[whole, whole] + [anywhere] * 6,
        scratch_shapes=[
            pltpu.VMEM((width, seq), BF16),
            pltpu.VMEM((seq, width), F32),
            pltpu.VMEM((2, width, tile), BF16),
            pltpu.VMEM((2, width, tile), BF16),
            pltpu.VMEM((2, tile, width), BF16),
            pltpu.VMEM((2, width, tile), BF16),
            pltpu.VMEM((2, width, tile), BF16),
            pltpu.VMEM((2, tile, width), BF16),
            dma, dma((2, 3)), dma((2, 3)),
        ]
        + Gather.scratch(1, n)
        + Reduce.scratch(specs, n),
        compiler_params=pltpu.CompilerParams(
            collective_id=collective, has_side_effects=True, vmem_limit_bytes=62 * 1024 * 1024
        ),
    )(second, upstream, middle, inner, down, coming)
    out, d_second, _, late, grad_down, sums, _, _ = results
    return out, d_second, late, grad_down, [sums], specs


def rms_norm(values, gains):
    return values * lax.rsqrt(jnp.mean(values * values, axis=-1, keepdims=True) + EPSILON) * gains


def swiglu(gate_up):
    middle_col = gate_up.shape[1] // 2
    return jax.nn.silu(gate_up[:, :middle_col]) * gate_up[:, middle_col:]


def project(operand, weight):
    return jnp.dot(operand, weight, preferred_element_type=F32)


def project_back(upstream, weight):
    return lax.dot_general(
        upstream, weight, (((1,), (1,)), ((), ())), preferred_element_type=F32
    )


def weight_grad(operand, upstream):
    return lax.dot_general(
        operand, upstream, (((0,), (0,)), ((), ())), preferred_element_type=F32
    ).astype(BF16)


def body(
    layer_input,
    first_gain,
    qkv_weight,
    conv_kernel,
    head_mixing,
    group_gain,
    out_weight,
    second_gain,
    inner_weight,
    down_weight,
    doc_lengths,
    cotangent,
):
    n = lax.axis_size("fsdp")
    hidden_size = inner_weight.shape[1] // 2
    cut = hidden_size // TILES * (TILES - LATE_TILES)
    gates, ups = inner_weight[:, :hidden_size], inner_weight[:, hidden_size:]
    inner_first = jnp.concatenate([gates[:, :cut], ups[:, :cut]], axis=1)
    inner_last = jnp.concatenate([gates[:, cut:], ups[:, cut:]], axis=1)
    kept, (qkv_weight, out_weight), (inner_first, down_weight) = attend_forward(
        layer_input, conv_kernel, head_mixing, doc_lengths, (first_gain, group_gain, second_gain),
        [qkv_weight, out_weight], [inner_first, down_weight], n, 0,
    )
    grouped, attended, soft, normed, middle, second, projected = kept
    second_pull = jax.vjp(rms_norm, middle, second_gain)[1]
    layer_output, d_second, late_inner, grad_down, early_sums, early_specs = feed_forward(
        second, cotangent, middle, inner_first, down_weight, inner_last, n, 2
    )
    d_middle, grad_second = second_pull(d_second)
    d_middle = cotangent.astype(F32) + d_middle
    d_branch = d_middle.astype(jnp.bfloat16)
    grad_proj = weight_grad(grouped, d_branch)
    d_grouped = project_back(d_branch, out_weight)
    (d_projected, grad_group, grad_kernel, grad_mixing), sums, specs, (early_inner,) = attend_backward(
        projected, conv_kernel, head_mixing, doc_lengths, group_gain, attended, d_grouped, soft,
        [late_inner, grad_down, grad_proj], early_sums, early_specs, n, 3,
    )
    grad_qkv = weight_grad(normed, d_projected)
    grad_input, shards, small = last_step(
        d_projected, qkv_weight, layer_input, first_gain, d_middle, [grad_qkv],
        [grad_group, grad_second.reshape(1, -1), grad_kernel, grad_mixing], sums, specs, n, 4,
    )
    grad_first, grad_group, grad_second = [g.reshape(-1) for g in small[:3]]
    grad_kernel, grad_mixing = unpack_taps(small[3])
    grad_qkv, late_inner, grad_down, grad_proj = shards
    cut, late_cut = early_inner.shape[1] // 2, late_inner.shape[1] // 2
    grad_inner = jnp.concatenate(
        [early_inner[:, :cut], late_inner[:, :late_cut], early_inner[:, cut:], late_inner[:, late_cut:]], axis=1
    )
    shards = [g.astype(F32) for g in (grad_qkv, grad_proj, grad_inner, grad_down)]
    return (
        layer_output, grad_input, grad_first, shards[0], grad_kernel, grad_mixing, grad_group, shards[1], grad_second,
        shards[2], shards[3],
    )


def solution(mesh):
    placed = (
        P(("rep", "fsdp"), None),
        P(),
        P("fsdp", None),
        P(),
        P(),
        P(),
        P("fsdp", None),
        P(),
        P("fsdp", None),
        P("fsdp", None),
        P(("rep", "fsdp"), None),
        P(("rep", "fsdp"), None),
    )
    return jax.shard_map(
        body,
        mesh=mesh,
        in_specs=placed,
        out_specs=(
            P(("rep", "fsdp"), None),
            P(("rep", "fsdp"), None),
            P(),
            P("fsdp", None),
            P(),
            P(),
            P(),
            P("fsdp", None),
            P(),
            P("fsdp", None),
            P("fsdp", None),
        ),
        check_vma=False,
    )
```

```python
import functools, math
import jax, jax.numpy as jnp
from jax import lax
from jax.experimental import pallas as pl
from jax.experimental.pallas import tpu as pltpu
from jax.sharding import PartitionSpec as P

HEADS = 16
HEAD_DIM = 96
CQ = 6
CK = 11
EPSILON = 1e-05
LANE = 128
QUAD = 4
LAG = 1
LEAD = 3
SCALE = 1.0 / math.sqrt(HEAD_DIM)
F32 = jnp.float32
BF16 = jnp.bfloat16


def row_sets(seq):
    return [
        (r, min(r + LANE, 3 * LANE), max(0, r - 2 * LANE)) for r in range(0, seq, LANE)
    ]


def nt(a, b):
    return lax.dot_general(a, b, (((1,), (1,)), ((), ())), preferred_element_type=F32)


def nn(a, b):
    return jnp.dot(a, b, preferred_element_type=F32)


def fill_masks(docs_ref, masks, seq):
    ends = []
    total = jnp.int32(0)
    for d in range(docs_ref.shape[1] - 1):
        total = total + docs_ref[0, d]
        ends.append(total)
    for r0, width, c0 in row_sets(seq):
        rows = r0 + lax.broadcasted_iota(jnp.int32, (LANE, 1), 0)
        cols = c0 + lax.broadcasted_iota(jnp.int32, (1, width), 1)
        row_doc = sum((rows >= e).astype(jnp.int32) for e in ends)
        col_doc = sum((cols >= e).astype(jnp.int32) for e in ends)
        same = row_doc == col_doc
        for a in range(CQ):
            masks[a, r0 : r0 + LANE, :width] = jnp.where(
                same & (rows - cols >= a), 1.0, 0.0
            ).astype(BF16)


def circulant_masks():
    gap = lax.broadcasted_iota(jnp.int32, (LANE, LANE), 1) - lax.broadcasted_iota(
        jnp.int32, (LANE, LANE), 0
    )
    half = CK // 2
    return (jnp.abs(gap) <= half, gap <= half - LANE, gap >= LANE - half)


def circulant(taps):
    wide = jnp.broadcast_to(taps, (LANE, LANE))
    return pltpu.roll(wide, 0, axis=1, stride=1, stride_axis=0)


def fill_toeplitz(taps_ref, head, band, blocks):
    near, after, before = circulant_masks()
    for a in range(CQ):
        whole = circulant(taps_ref[head, a : a + 1, :])
        parts = {
            0: jnp.where(near, whole, 0.0).astype(BF16),
            1: jnp.where(after, whole, 0.0).astype(BF16),
            -1: jnp.where(before, whole, 0.0).astype(BF16),
        }
        for r in range(blocks):
            for c in range(blocks):
                part = parts.get(c - r)
                if part is not None:
                    yield a, r, c, part


def fill_forward_band(taps_ref, head, band):
    for a, r, c, part in fill_toeplitz(taps_ref, head, band, 3):
        at = (r * CQ + a) * LANE
        band[at : at + LANE, c * LANE : (c + 1) * LANE] = part


def fill_backward_band(taps_ref, head, band):
    near, after, before = circulant_masks()
    for a in range(CQ):
        whole = circulant(taps_ref[head, a : a + 1, :])
        for at, keep in enumerate((after, near, before)):
            band[at * LANE : (at + 1) * LANE, a * LANE : (a + 1) * LANE] = jnp.where(keep, whole, 0.0).astype(BF16)


def shifted_rows(query):
    wide = query.astype(F32)
    return [query] + [pltpu.roll(wide, a, axis=0).astype(BF16) for a in range(1, CQ)]


def masked_scores(shifted, keys, masks, r0, width, c0):
    left = jnp.concatenate([shifted[a, r0 : r0 + LANE] for a in range(CQ)], axis=0)
    scores = nt(left, keys[c0 : c0 + width]).astype(BF16)
    return left, [
        scores[a * LANE : (a + 1) * LANE] * masks[a, r0 : r0 + LANE, :width]
        for a in range(CQ)
    ]


def by_window(parts, width):
    return jnp.concatenate(
        [
            parts[a][:, b * LANE : (b + 1) * LANE]
            for b in range(width // LANE)
            for a in range(CQ)
        ],
        axis=1,
    )


def forward_kernel(
    n, first_widths, rest_widths, docs_ref, mix_ref, taps_ref, gain_ref, input_ref, gains_ref, *refs
):
    refs = list(refs)

    def take(size):
        taken = refs[:size]
        del refs[:size]
        return taken

    first_count, rest_count = len(first_widths), len(rest_widths)
    first_weights, rest_weights = take(first_count), take(rest_count)
    grouped_ref, attended_ref, soft_ref, normed_ref, middle_ref, second_ref, projected = take(7)
    first_fulls, rest_fulls = take(first_count), take(rest_count)
    masks, band, qs, ks, vs, shifted, outs = take(7)
    blocks, block_weight, every, out_weight, block_in, block_out, out_in = take(7)
    ring = Ring(n)
    sems = len(Gather.scratch(first_count, n))
    first = Gather(ring, first_weights, first_fulls, first_widths, take(sems))
    rest = Gather(ring, rest_weights, rest_fulls, rest_widths, take(sems))
    seq = input_ref.shape[0]
    quad = pl.program_id(0)
    quads = HEADS // QUAD
    size = QUAD * HEAD_DIM
    count = 3 * quads

    def block_copy(t):
        slot = lax.rem(t, 2)
        return pltpu.make_async_copy(first_fulls[0].at[:, cols(t * size, size)], block_weight.at[slot], block_in.at[slot])

    def block_save(t):
        return pltpu.make_async_copy(blocks.at[t], projected.at[:, cols(t * size, size)], block_out.at[t])

    out_copy = pltpu.make_async_copy(first_fulls[1], out_weight, out_in)

    def serve(turn):
        for k in in_turn(turn, 2 + HEADS // 2, n - 2):
            pl.when(k < n - 2)(functools.partial(rest.step, k + 1))

    @pl.when(quad == 0)
    def _():
        ring.meet()
        first.start()
        fill_masks(docs_ref, masks, seq)
        band[...] = jnp.zeros_like(band)
        values = input_ref[...].astype(F32)
        scale = lax.rsqrt(jnp.mean(values * values, axis=1, keepdims=True) + EPSILON)
        normed_ref[...] = (values * scale * gains_ref[0:1, :]).astype(BF16)

        def one(k, carry):
            first.step(k)
            pl.when(k == n // 2 - 2)(rest.start)
            pl.when(k == n - 3)(lambda: rest.step(jnp.int32(0)))
            return carry

        lax.fori_loop(0, n - 1, one, 0)
        first.finish()
        serve(jnp.int32(0))
        block_copy(0).start()
        out_copy.start()

        def project_block(t, carry):
            pl.when(t < count - 1)(lambda: block_copy(t + 1).start())
            block_copy(t).wait()
            blocks[t] = nn(normed_ref[...], block_weight[lax.rem(t, 2)]).astype(BF16)
            block_save(t).start()
            return carry

        lax.fori_loop(0, count, project_block, 0)
        serve(jnp.int32(1))

    for h in range(QUAD):
        at = slice(h * HEAD_DIM, (h + 1) * HEAD_DIM)
        qs[h] = blocks[quad, :, at]
        ks[h] = blocks[quads + quad, :, at]
        vs[h] = blocks[2 * quads + quad, :, at]

    sets = row_sets(seq)

    def pair(p, carry):
        group = quad * 2 + p
        for r in range(2):
            h = 2 * p + r
            fill_forward_band(taps_ref, quad * QUAD + h, band)
            for a, rows in enumerate(shifted_rows(qs[h])):
                shifted[a] = rows
            keys = ks[h]
            lefts = []
            for r0, width, c0 in sets:
                _, parts = masked_scores(shifted, keys, masks, r0, width, c0)
                lefts.append((width, by_window(parts, width)))
            convs = []
            i = 0
            while i < len(sets):
                width = sets[i][1]
                run = 1
                while i + run < len(sets) and sets[i + run][1] == width:
                    run += 1
                left = jnp.concatenate([lefts[i + m][1] for m in range(run)], axis=0)
                conv = nn(left, band[: width * CQ, :width])
                convs += [conv[m * LANE : (m + 1) * LANE] for m in range(run)]
                i += run
            for (r0, width, c0), conv in zip(sets, convs):
                logits = jnp.where(
                    masks[0, r0 : r0 + LANE, :width].astype(F32) > 0, conv, -1e30
                )
                weights = jnp.exp(logits - jnp.max(logits, axis=1, keepdims=True))
                soft = weights * (1.0 / jnp.sum(weights, axis=1, keepdims=True))
                soft_ref[h, r0 : r0 + LANE, :width] = soft.astype(BF16)
        for r in range(2):
            h = 2 * p + r
            values = vs[h]
            for r0, width, c0 in sets:
                mixed = (
                    mix_ref[group, r, 0] * soft_ref[2 * p, r0 : r0 + LANE, :width].astype(F32)
                    + mix_ref[group, r, 1] * soft_ref[2 * p + 1, r0 : r0 + LANE, :width].astype(F32)
                ).astype(BF16)
                outs[h, r0 : r0 + LANE] = nn(mixed, values[c0 : c0 + width])
        serve(2 + group)
        return carry

    lax.fori_loop(0, 2, pair, 0)
    wholes, grouped = [], []
    for h in range(QUAD):
        attended = outs[h]
        centred = attended - jnp.mean(attended, axis=1, keepdims=True)
        var = jnp.mean(centred * centred, axis=1, keepdims=True)
        wholes.append(attended)
        grouped.append(centred * lax.rsqrt(var + EPSILON))
    attended_ref[...] = jnp.concatenate(wholes, axis=1)
    every[quad] = (jnp.concatenate(grouped, axis=1) * gain_ref[1:2, :]).astype(BF16)
    grouped_ref[...] = every[quad]

    @pl.when(quad == quads - 1)
    def _():
        out_copy.wait()
        branch = nn(jnp.concatenate([every[i] for i in range(quads)], axis=1), out_weight[...])
        middle = input_ref[...].astype(F32) + branch
        scale = lax.rsqrt(jnp.mean(middle * middle, axis=1, keepdims=True) + EPSILON)
        middle_ref[...] = middle
        second_ref[...] = (middle * scale * gains_ref[2:3, :]).astype(BF16)

        def saved(t, carry):
            block_save(t).wait()
            return carry

        lax.fori_loop(0, count, saved, 0)
        rest.finish()


def pad_taps(kernel):
    padded = jnp.pad(kernel * SCALE, ((0, 0), (0, 2), (0, LANE - CK)))
    return jnp.roll(padded, -(CK // 2), axis=2)


def in_turn(turn, turns, steps):
    each = -(-steps // turns)
    return [turn * each + t for t in range(each)]


def attend_forward(layer_input, conv_kernel, head_mixing, docs, gains, first, rest, n, collective):
    seq, width = layer_input.shape
    block = QUAD * HEAD_DIM
    quads = HEADS // QUAD
    first_widths, rest_widths = [share(w.shape) for w in first], [share(w.shape) for w in rest]
    whole = pl.BlockSpec(memory_space=pltpu.VMEM)
    smem = pl.BlockSpec(memory_space=pltpu.SMEM)
    anywhere = pl.BlockSpec(memory_space=pl.ANY)
    columns = pl.BlockSpec((seq, block), lambda i: (0, i))
    dma = pltpu.SemaphoreType.DMA
    gains = jnp.stack(gains)
    results = pl.pallas_call(
        functools.partial(forward_kernel, n, first_widths, rest_widths),
        grid=(quads,),
        out_shape=[
            jax.ShapeDtypeStruct((seq, width), BF16),
            jax.ShapeDtypeStruct((seq, width), F32),
            jax.ShapeDtypeStruct((HEADS, seq, 3 * LANE), BF16),
            jax.ShapeDtypeStruct((seq, width), BF16),
            jax.ShapeDtypeStruct((seq, width), F32),
            jax.ShapeDtypeStruct((seq, width), BF16),
            jax.ShapeDtypeStruct((seq, 3 * width), BF16),
        ]
        + [jax.ShapeDtypeStruct((n * w.shape[0], w.shape[1]), w.dtype) for w in first + rest],
        in_specs=[smem, smem, whole, pl.BlockSpec((3, block), lambda i: (0, i)), whole, whole]
        + [anywhere] * len(first + rest),
        out_specs=[
            columns, columns,
            pl.BlockSpec((QUAD, seq, 3 * LANE), lambda i: (i, 0, 0)),
            whole, whole, whole,
        ]
        + [anywhere] * (1 + len(first + rest)),
        scratch_shapes=[
            pltpu.VMEM((CQ, seq, 3 * LANE), BF16),
            pltpu.VMEM((3 * LANE * CQ, 3 * LANE), BF16),
            pltpu.VMEM((QUAD, seq, HEAD_DIM), BF16),
            pltpu.VMEM((QUAD, seq, HEAD_DIM), BF16),
            pltpu.VMEM((QUAD, seq, HEAD_DIM), BF16),
            pltpu.VMEM((CQ, seq, HEAD_DIM), BF16),
            pltpu.VMEM((QUAD, seq, HEAD_DIM), F32),
            pltpu.VMEM((3 * quads, seq, block), BF16),
            pltpu.VMEM((2, width, block), BF16),
            pltpu.VMEM((quads, seq, block), BF16),
            pltpu.VMEM((width, width), BF16),
            dma((2,)), dma((3 * quads,)), dma,
        ]
        + Gather.scratch(len(first), n)
        + Gather.scratch(len(rest), n),
        compiler_params=pltpu.CompilerParams(
            collective_id=collective, has_side_effects=True, vmem_limit_bytes=60 * 1024 * 1024
        ),
    )(
        docs, head_mixing, pad_taps(conv_kernel), gains, layer_input, gains,
        *first, *rest,
    )
    return results[:7], results[7 : 7 + len(first)], results[7 + len(first) :]


def backward_kernel(
    n, specs, done_specs, docs_ref, mix_ref, taps_ref, gain_ref, q_ref, k_ref, v_ref, attended_ref, d_grouped_ref, soft_ref, *refs
):
    count, done = len(specs), len(done_specs)
    grads, done_sums, refs = refs[:count], refs[count : count + done], refs[count + done :]
    d_projected, grad_gain_ref, grad_taps_ref, grad_mix_ref = refs[:4]
    sums, others, refs = refs[4 : 4 + count], refs[4 + count : 4 + 2 * count], refs[4 + 2 * count :]
    done_totals, refs = refs[:done], refs[done:]
    final_size = len(FinalSum.scratch(done_specs))
    masks, band, qs, ks, vs, ds, shifted, d_heads, d_rows, d_cols, near_keys, leaving, leave_sem = refs[:13]
    reduce = Reduce(Ring(n), grads, sums, others, specs, refs[13 + final_size :])
    final = FinalSum(reduce.ring, done_sums, done_totals, done_specs, refs[13 : 13 + final_size])
    seq = q_ref.shape[0]
    quad = pl.program_id(0)

    @pl.when(quad == 0)
    def _():
        reduce.clear()
        reduce.ring.meet()
        reduce.start()
        for i in range(done):
            final.start(i)

    @pl.when(quad == 0)
    def _():
        fill_masks(docs_ref, masks, seq)

    gains = []
    for h in range(QUAD):
        at = slice(h * HEAD_DIM, (h + 1) * HEAD_DIM)
        qs[h] = q_ref[:, at]
        ks[h] = k_ref[:, at]
        vs[h] = v_ref[:, at]
        attended = attended_ref[:, at]
        d_grouped = d_grouped_ref[:, at]
        centred = attended - jnp.mean(attended, axis=1, keepdims=True)
        var = jnp.mean(centred * centred, axis=1, keepdims=True)
        scale = lax.rsqrt(var + EPSILON)
        unit = centred * scale
        gains.append(jnp.sum(d_grouped * unit, axis=0, keepdims=True))
        w = d_grouped * gain_ref[:, at]
        d_attended = scale * (
            w
            - jnp.mean(w, axis=1, keepdims=True)
            - unit * jnp.mean(w * unit, axis=1, keepdims=True)
        )
        ds[h] = d_attended.astype(BF16)
    grad_gain_ref[...] = jnp.concatenate(gains, axis=1)
    grad_taps_ref[...] = jnp.zeros_like(grad_taps_ref)
    grad_mix_ref[...] = jnp.zeros_like(grad_mix_ref)

    sets = row_sets(seq)
    up = lax.broadcasted_iota(jnp.int32, (LANE, LANE), 0)
    across = lax.broadcasted_iota(jnp.int32, (LANE, LANE), 1)
    flip = jnp.where(up + across == LANE - 1, 1.0, 0.0).astype(BF16)
    gap = up + across - (LANE - 1)
    keeps = {0: jnp.abs(gap) <= CK // 2, 1: gap <= CK // 2 - LANE, -1: gap >= LANE - CK // 2}

    def pair(p, carry):
        group = quad * 2 + p
        mix = [[mix_ref[group, r, s] for s in range(2)] for r in range(2)]
        upstream_t = [ds[2 * p + r].T for r in range(2)]
        grad_mix = [[jnp.zeros((1, 1), F32) for _ in range(2)] for _ in range(2)]
        for r in range(2):
            d_cols[r] = jnp.zeros_like(d_cols[r])
        for r0, width, c0 in sets:
            rows = slice(r0, r0 + LANE)
            soft = [soft_ref[2 * p + s, rows, :width].astype(F32) for s in range(2)]
            d_prob, sums = [], []
            for r in range(2):
                dp = nt(ds[2 * p + r, rows], vs[2 * p + r, c0 : c0 + width])
                d_prob.append(dp)
                sums.append([jnp.sum(dp * soft[s], axis=1, keepdims=True) for s in range(2)])
                for s in range(2):
                    grad_mix[r][s] += jnp.sum(sums[r][s], axis=0, keepdims=True)
                mixed = (mix[r][0] * soft[0] + mix[r][1] * soft[1]).astype(BF16)
                d_cols[r, :, c0 : c0 + width] += nn(upstream_t[r][:, r0 : r0 + LANE], mixed)
            for s in range(2):
                d_soft = mix[0][s] * d_prob[0] + mix[1][s] * d_prob[1]
                inner = mix[0][s] * sums[0][s] + mix[1][s] * sums[1][s]
                d_conv = soft[s] * (d_soft - inner)
                d_rows[s, rows, :width] = d_conv.astype(BF16)
        lane = lax.broadcasted_iota(jnp.int32, (1, LANE), 1)
        line = jnp.zeros((1, LANE), F32)
        for r in range(2):
            for s in range(2):
                line = line + jnp.where(lane == 2 * r + s, grad_mix[r][s], 0.0)
        grad_mix_ref[0, pl.ds(p, 1), :] = line
        for r in range(2):
            d_heads[2, 2 * p + r] = d_cols[r].T

        for r in range(2):
            h = 2 * p + r
            fill_backward_band(taps_ref, quad * QUAD + h, band)
            for a, moved in enumerate(shifted_rows(qs[h])):
                shifted[a] = moved
            keys = ks[h]
            d_cols[0] = jnp.zeros_like(d_cols[0])
            d_query = []
            below = jnp.zeros((8, LANE * CQ), F32)
            above = jnp.zeros((8, LANE * CQ), F32)
            mirrored = []
            for r0, width, c0 in sets:
                rows = slice(r0, r0 + LANE)
                left, parts = masked_scores(shifted, keys, masks, r0, width, c0)
                d_conv = d_rows[r, rows, :width]
                blocks = width // LANE
                flipped = [
                    nt(flip, d_conv[:, b * LANE : (b + 1) * LANE]).astype(BF16) for b in range(blocks)
                ]
                start = len(mirrored) * LANE
                mirrored += flipped
                for b in range(blocks):
                    near_keys[start + b * LANE : start + (b + 1) * LANE, :] = jnp.concatenate(
                        [parts[a][:, b * LANE : (b + 1) * LANE] for a in range(CQ)], axis=1
                    )
                if blocks > 1:
                    end = start + blocks * LANE
                    below = below + nn(
                        jnp.concatenate([f[:8] for f in flipped[:-1]], axis=1), near_keys[start + LANE : end, :]
                    )
                    above = above + nn(
                        jnp.concatenate([f[LANE - 8 :] for f in flipped[1:]], axis=1), near_keys[start : end - LANE, :]
                    )
                spread = []
                for b in range(blocks):
                    low, high = max(b - 1, 0), min(b + 1, blocks - 1)
                    spread.append(
                        nn(
                            d_conv[:, low * LANE : (high + 1) * LANE],
                            band[(low - b + 1) * LANE : (high - b + 2) * LANE, :],
                        ).astype(BF16)
                    )
                stacked = jnp.concatenate(
                    [
                        jnp.concatenate(
                            [
                                spread[b][:, a * LANE : (a + 1) * LANE]
                                for b in range(blocks)
                            ],
                            axis=1,
                        )
                        * masks[a, rows, :width]
                        for a in range(CQ)
                    ],
                    axis=0,
                )
                d_query.append(nn(stacked, keys[c0 : c0 + width]))
                d_cols[0, :, c0 : c0 + width] += nn(left.T, stacked)
            total = None
            for a in range(CQ):
                whole = jnp.concatenate([d[a * LANE : (a + 1) * LANE] for d in d_query], axis=0)
                if a:
                    whole = pltpu.roll(whole, seq - a, axis=0)
                total = whole if total is None else total + whole
            d_heads[0, h] = total
            d_heads[1, h] = d_cols[0].T
            band_sum = nn(jnp.concatenate(mirrored, axis=1), near_keys[: len(mirrored) * LANE, :])
            for a in range(CQ):
                at = slice(a * LANE, (a + 1) * LANE)
                whole = jnp.where(keeps[0], band_sum[:, at], 0.0)
                whole = jnp.concatenate(
                    [
                        whole[:8] + jnp.where(keeps[1][:8], below[:, at], 0.0),
                        whole[8 : LANE - 8],
                        whole[LANE - 8 :] + jnp.where(keeps[-1][LANE - 8 :], above[:, at], 0.0),
                    ],
                    axis=0,
                )
                aligned = pltpu.roll(whole, 0, axis=1, stride=1, stride_axis=0)
                grad_taps_ref[h, a : a + 1, :] = jnp.sum(aligned, axis=0, keepdims=True)
            work = reduce.each()
            middle = len(work) // 2
            for j in in_turn(group, HEADS // 2, n):
                pl.when(j < n)(functools.partial(reduce.item, j, work[middle:] if r else work[:middle]))
        return carry

    lax.fori_loop(0, 2, pair, 0)
    quads = HEADS // QUAD
    block = QUAD * HEAD_DIM

    def leave(part):
        there = d_projected.at[:, cols((part * quads + quad) * block, block)]
        return pltpu.make_async_copy(leaving.at[part], there, leave_sem.at[part])

    for part in range(3):
        pl.when(quad > 0)(leave(part).wait)
        leaving[part] = jnp.concatenate([d_heads[part, h] for h in range(QUAD)], axis=1).astype(BF16)
        leave(part).start()

    @pl.when(quad == quads - 1)
    def _():
        for part in range(3):
            leave(part).wait()
        for i in range(done):
            final.add(i)

    @pl.when(quad == pl.num_programs(0) - 1)
    def _():
        reduce.finish()
        final.finish()


def attend_backward(projected, conv_kernel, head_mixing, docs, gain, attended, d_grouped, soft, grads, done_sums, done_specs, n, collective):
    seq = projected.shape[0]
    width = projected.shape[1] // 3
    block = QUAD * HEAD_DIM
    quads = HEADS // QUAD
    count = len(grads)
    specs = Reduce.specs_of(grads, n, (THIRD, THIRD))
    anywhere = pl.BlockSpec(memory_space=pl.ANY)
    whole = pl.BlockSpec(memory_space=pltpu.VMEM)
    smem = pl.BlockSpec(memory_space=pltpu.SMEM)

    def columns(first):
        return pl.BlockSpec((seq, block), lambda i: (0, first * quads + i))

    results = pl.pallas_call(
        functools.partial(backward_kernel, n, specs, done_specs),
        grid=(quads,),
        out_shape=[
            jax.ShapeDtypeStruct((seq, 3 * width), BF16),
            jax.ShapeDtypeStruct((1, width), F32),
            jax.ShapeDtypeStruct((HEADS, 8, LANE), F32),
            jax.ShapeDtypeStruct((quads, 8, LANE), F32),
        ]
        + Reduce.results(specs, n)
        + [jax.ShapeDtypeStruct(spec[:2], BF16) for spec in done_specs],
        in_specs=[
            smem, smem, whole,
            pl.BlockSpec((1, block), lambda i: (0, i)),
            columns(0), columns(1), columns(2), columns(0), columns(0),
            pl.BlockSpec((QUAD, seq, 3 * LANE), lambda i: (i, 0, 0)),
        ]
        + [anywhere] * (count + len(done_specs)),
        out_specs=[
            anywhere,
            pl.BlockSpec((1, block), lambda i: (0, i)),
            pl.BlockSpec((QUAD, 8, LANE), lambda i: (i, 0, 0)),
            pl.BlockSpec((1, 8, LANE), lambda i: (i, 0, 0)),
        ]
        + [anywhere] * (2 * count + len(done_specs)),
        scratch_shapes=[
            pltpu.VMEM((CQ, seq, 3 * LANE), BF16),
            pltpu.VMEM((3 * LANE, LANE * CQ), BF16),
            pltpu.VMEM((QUAD, seq, HEAD_DIM), BF16),
            pltpu.VMEM((QUAD, seq, HEAD_DIM), BF16),
            pltpu.VMEM((QUAD, seq, HEAD_DIM), BF16),
            pltpu.VMEM((QUAD, seq, HEAD_DIM), BF16),
            pltpu.VMEM((CQ, seq, HEAD_DIM), BF16),
            pltpu.VMEM((3, QUAD, seq, HEAD_DIM), F32),
            pltpu.VMEM((2, seq, 3 * LANE), BF16),
            pltpu.VMEM((2, HEAD_DIM, seq), F32),
            pltpu.VMEM((sum(w for _, w, _ in row_sets(seq)), LANE * CQ), BF16),
            pltpu.VMEM((3, seq, block), BF16),
            pltpu.SemaphoreType.DMA((3,)),
        ]
        + FinalSum.scratch(done_specs)
        + Reduce.scratch(specs, n),
        compiler_params=pltpu.CompilerParams(
            collective_id=collective, has_side_effects=True, vmem_limit_bytes=62 * 1024 * 1024
        ),
    )(
        docs, head_mixing, pad_taps(conv_kernel[:, :, ::-1]), gain.reshape(1, width),
        projected, projected, projected, attended, d_grouped, soft, *grads, *done_sums,
    )
    d_projected, grad_gain, grad_taps, grad_mix = results[:4]
    return (
        d_projected, grad_gain, grad_taps, grad_mix,
    ), list(results[4 : 4 + count]), specs, results[4 + 2 * count :]


MESH = pl.DeviceIdType.MESH


def ring_index(place, n):
    place = lax.rem(place + 2 * n, n)
    return jnp.where(place < n // 2, 2 * place, 2 * (n - 1 - place) + 1)


def ring_place(index, n):
    half = lax.div(index, 2)
    return jnp.where(lax.rem(index, 2) == 0, half, n - 1 - half)


class Ring:
    def __init__(self, n):
        self.n = n
        rep = lax.axis_index("rep")
        self.x, self.core = lax.div(rep, 2), lax.rem(rep, 2)
        index = lax.axis_index("fsdp")
        self.index = index
        self.place = ring_place(index, n)
        self.right = (rep, ring_index(self.place + 1, n))
        self.left = (rep, ring_index(self.place - 1, n))
        self.sibling = (self.x * 2 + 1 - self.core, index)
        self.across = ((1 - self.x) * 2 + self.core, index)

    def meet(self):
        barrier = pltpu.get_barrier_semaphore()
        for other in (self.right, self.left, self.sibling, self.across):
            pl.semaphore_signal(barrier, inc=1, device_id=other, device_id_type=MESH)
        pl.semaphore_wait(barrier, 4)


def send(src, dst, send_sem, recv_sem, device):
    return pltpu.make_async_remote_copy(
        src_ref=src, dst_ref=dst, send_sem=send_sem, recv_sem=recv_sem,
        device_id=device, device_id_type=MESH,
    )


def cols(start, size):
    return pl.ds(pl.multiple_of(start, LANE), size)


class Gather:
    def __init__(self, ring, weights, fulls, widths, sems):
        self.ring, self.weights, self.fulls = ring, weights, fulls
        self.axes, self.widths = zip(*widths)
        (self.own, self.ring_send, self.ring_recv, self.core_send, self.core_recv, self.x_send, self.x_recv) = sems

    def windows(self, i):
        ring = self.ring
        half = self.weights[i].shape[self.axes[i]] // 2
        w = self.widths[i]
        base = ring.core * half
        part = half - 2 * w
        first = base + jnp.where(ring.x == 0, 0, half - w)
        second = base + jnp.where(ring.x == 0, w, half - 2 * w)
        give = base + jnp.where(ring.x == 0, 0, half - part)
        take = base + jnp.where(ring.x == 0, half - part, 0)
        return w, part, first, second, give, take

    def block(self, i, index, start, width):
        rows = self.weights[i].shape[0]
        if self.axes[i] == 0:
            return self.fulls[i].at[pl.ds(pl.multiple_of(index * rows + start, 16), width), :]
        return self.fulls[i].at[pl.ds(pl.multiple_of(index * rows, 16), rows), cols(start, width)]

    def piece(self, i, start, width):
        if self.axes[i] == 0:
            return self.weights[i].at[pl.ds(pl.multiple_of(start, 16), width), :]
        return self.weights[i].at[:, cols(start, width)]

    def ring_copy(self, i, d, k, source):
        ring = self.ring
        w, _, first, second, _, _ = self.windows(i)
        start = second if d else first
        index = ring_index(ring.place + (k if d else -k), ring.n)
        there = self.block(i, index, start, w)
        src = self.piece(i, start, w) if source else there
        return send(src, there, self.ring_send.at[i, d, k], self.ring_recv.at[i, d, k], ring.left if d else ring.right)

    def core_copy(self, i, d, k):
        ring = self.ring
        w, part, first, second, _, take = self.windows(i)
        start, width = ((first, w), (second, w), (take, part))[d]
        index = ring_index(ring.place + (k + 1 if d == 1 else -k - 1), ring.n)
        there = self.block(i, index, start, width)
        return send(there, there, self.core_send.at[i, d, k], self.core_recv.at[i, d, k], ring.sibling)

    def x_copy(self, i, k):
        ring = self.ring
        _, part, _, _, give, _ = self.windows(i)
        there = self.block(i, ring_index(ring.place - k - 1, ring.n), give, part)
        return send(there, there, self.x_send.at[i, k], self.x_recv.at[i, k], ring.across)

    def own_copy(self, i):
        rows = self.weights[i].shape[0]
        there = self.fulls[i].at[pl.ds(pl.multiple_of(self.ring.index * rows, 16), rows), :]
        return send(self.weights[i], there, self.own.at[0, i], self.own.at[1, i], self.ring.sibling)

    def has_part(self, i):
        return self.weights[i].shape[self.axes[i]] // 2 > 2 * self.widths[i]

    def start(self):
        for i in range(len(self.weights)):
            for d in range(2):
                self.ring_copy(i, d, 0, True).start()
        for i in range(len(self.weights)):
            self.own_copy(i).start()

    def step(self, k):
        last = self.ring.n - 2
        for i in range(len(self.weights)):
            for d in range(2):
                self.ring_copy(i, d, k, False).wait_recv()

                @pl.when(k < last)
                def _():
                    self.ring_copy(i, d, k + 1, False).start()

                if d == 0 and self.has_part(i):
                    self.x_copy(i, k).start()
                self.core_copy(i, d, k).start()

            if self.has_part(i):
                @pl.when(k >= LAG)
                def _():
                    self.pass_on(i, k - LAG)

    def pass_on(self, i, k):
        self.x_copy(i, k).wait_recv()
        self.core_copy(i, 2, k).start()

    def finish(self):
        last = self.ring.n - 2
        for k in range(max(0, last + 1 - LAG), last + 1):
            for i in range(len(self.weights)):
                if self.has_part(i):
                    self.pass_on(i, k)

        def settle(k, carry):
            for i in range(len(self.weights)):
                for d in range(2):
                    self.ring_copy(i, d, k, False).wait_send()
                    self.core_copy(i, d, k).wait()
                if self.has_part(i):
                    self.x_copy(i, k).wait_send()
                    self.core_copy(i, 2, k).wait()
            return carry

        lax.fori_loop(0, self.ring.n - 1, settle, 0)
        for i in range(len(self.weights)):
            self.own_copy(i).wait()

    @staticmethod
    def scratch(count, n):
        dma = pltpu.SemaphoreType.DMA
        return [
            dma((2, count)), dma((count, 2, n - 1)), dma((count, 2, n - 1)),
            dma((count, 3, n - 1)), dma((count, 3, n - 1)), dma((count, n - 1)), dma((count, n - 1)),
        ]


def share(shape):
    rows, columns = shape
    axis, unit = (0, 16) if rows % 64 == 0 else (1, LANE)
    units = (rows, columns)[axis] // 2 // unit
    return axis, -(-units // 3) * unit


THIRD = (1, 3)
LESS = (7, 18)


def carried(columns, portion):
    half = columns // 2
    lanes = -(-(half // LANE) * portion[0] // portion[1]) * LANE
    if 2 * lanes >= half:
        return half // 2, 0
    return lanes, half - 2 * lanes


class Reduce:
    def __init__(self, ring, grads, sums, others, specs, scratch):
        self.ring, self.grads, self.sums, self.others, self.specs = ring, grads, sums, others, specs
        count = len(grads)
        self.slots, self.mine, self.twin, self.x_slots, self.x_out = [], [], [], [], []
        scratch = list(scratch)
        for spec in specs:
            part = carried(spec[1], spec[2])[1]
            take = [scratch.pop(0) for _ in range(10 if part else 6)]
            self.slots.append(take[:2])
            self.mine.append(take[2:4] + take[6:7])
            self.twin.append(take[4:6] + take[7:8])
            self.x_slots.append(take[8] if part else None)
            self.x_out.append(take[9] if part else None)
        (self.load, self.ring_send, self.ring_recv, self.core_send, self.core_recv,
         self.x_send, self.x_recv, self.keep) = scratch

    def owner(self, kind, j):
        ring = self.ring
        return ring_index(ring.place + (j + 1 if kind == 1 else -j - 1), ring.n)

    def span(self, i, kind):
        columns, shared = self.specs[i][1:]
        w, part = carried(columns, shared)
        half = columns // 2
        lower, upper = ((0, half - w), (w, half - 2 * w), (half - part, 0))[kind]
        return jnp.where(self.ring.x == 0, lower, upper), part if kind == 2 else w

    def rows(self, i, index):
        rows = self.specs[i][0]
        return pl.ds(pl.multiple_of(index * rows, 16), rows)

    def kinds(self, i):
        return 3 if self.x_slots[i] is not None else 2

    def core_copy(self, i, kind, j):
        ring = self.ring
        start, width = self.span(i, kind)
        rows = self.rows(i, self.owner(kind, j))
        half = self.specs[i][1] // 2
        return send(
            self.grads[i].at[rows, cols((1 - ring.core) * half + start, width)], self.others[i].at[rows, cols(start, width)],
            self.core_send.at[i, kind, j], self.core_recv.at[i, kind, j], ring.sibling,
        )

    def loads(self, i, kind, j):
        start, width = self.span(i, kind)
        rows = self.rows(i, self.owner(kind, j))
        base = self.ring.core * (self.specs[i][1] // 2)
        return (
            pltpu.make_async_copy(
                self.grads[i].at[rows, cols(base + start, width)], self.mine[i][kind], self.load.at[i, kind, 0]
            ),
            pltpu.make_async_copy(self.others[i].at[rows, cols(start, width)], self.twin[i][kind], self.load.at[i, kind, 1]),
        )

    def fetch(self, i, kind, j):
        own, other = self.loads(i, kind, j)
        own.start()
        self.core_copy(i, kind, j).wait_recv()
        other.start()

    def ring_copy(self, i, d, j):
        ring = self.ring
        return send(
            self.slots[i][d].at[j], self.slots[i][d].at[j + 1],
            self.ring_send.at[i, d, j], self.ring_recv.at[i, d, j + 1], ring.left if d else ring.right,
        )

    def gap(self, i):
        w, part = carried(*self.specs[i][1:])
        x = self.ring.x
        return w - part, jnp.where(x == 0, part, 0), jnp.where(x == 0, w - part, 0), part

    def x_copy(self, i, j):
        _, _, at, part = self.gap(i)
        return send(
            self.x_out[i].at[lax.rem(j, 2)], self.x_slots[i].at[j, :, cols(at, part)],
            self.x_send.at[i, j], self.x_recv.at[i, j], self.ring.across,
        )

    def give(self, i, j):
        j = jnp.int32(j)
        for copy in self.loads(i, 2, j):
            copy.wait()

        @pl.when(j >= 2)
        def _():
            self.x_copy(i, j - 2).wait_send()

        self.x_out[i][lax.rem(j, 2)] = (self.mine[i][2][...].astype(F32) + self.twin[i][2][...].astype(F32)).astype(BF16)
        self.x_copy(i, j).start()
        self.hand_next(i, 2, j)

        @pl.when(j < self.ring.n - 1)
        def _():
            self.fetch(i, 2, j + 1)

    def each(self):
        return [(i, d) for i in range(len(self.grads)) for d in (1, 0)]

    def clear(self):
        for i in range(len(self.grads)):
            if self.kinds(i) == 3:
                width, at, _, _ = self.gap(i)
                if width:
                    rows = self.specs[i][0]
                    self.x_slots[i][:, :, cols(at, width)] = jnp.zeros((self.ring.n, rows, width), BF16)

    def hand_over(self):
        for j in range(min(LEAD, self.ring.n)):
            for i in range(len(self.grads)):
                for kind in reversed(range(self.kinds(i))):
                    self.core_copy(i, kind, j).start()

    def hand_next(self, i, kind, j):
        pl.when(j + LEAD < self.ring.n)(lambda: self.core_copy(i, kind, j + LEAD).start())

    def fetch_first(self):
        for i in range(len(self.grads)):
            for kind in reversed(range(self.kinds(i))):
                self.fetch(i, kind, 0)

    def give_all(self, j):
        for i in range(len(self.grads)):
            if self.kinds(i) == 3:
                self.give(i, j)

    def opening(self):
        return [
            self.hand_over, self.fetch_first,
            functools.partial(self.give_all, 0), functools.partial(self.give_all, 1),
        ]

    def start(self):
        for step in self.opening():
            step()

    def item(self, j, work):
        last = self.ring.n - 1
        for i, d in work:
            if d == 0 and self.kinds(i) == 3:
                pl.when(j < last - 1)(functools.partial(self.give, i, j + 2))
            for copy in self.loads(i, d, j):
                copy.wait()
            slot = self.slots[i][d]
            both = self.mine[i][d][...].astype(F32) + self.twin[i][d][...].astype(F32)
            if d == 0 and self.kinds(i) == 3:
                self.x_copy(i, j).wait_recv()
                both = both + self.x_slots[i][j].astype(F32)

            @pl.when(j == 0)
            def _():
                slot[j] = both.astype(BF16)

            @pl.when(j > 0)
            def _():
                self.ring_copy(i, d, j - 1).wait_recv()
                slot[j] = (slot[j].astype(F32) + both).astype(BF16)

            @pl.when(j < last)
            def _():
                self.ring_copy(i, d, j).start()
                self.fetch(i, d, j + 1)

            self.hand_next(i, d, j)

            @pl.when(j == last)
            def _():
                self.keep_copy(i, d).start()

    def keep_copy(self, i, d):
        w = carried(*self.specs[i][1:])[0]
        at = jnp.where(self.ring.x == 0, d * w, (1 - d) * w)
        return pltpu.make_async_copy(self.slots[i][d].at[self.ring.n - 1], self.sums[i].at[:, cols(at, w)], self.keep.at[i, d])

    def finish(self):
        last = self.ring.n - 1
        for i, d in self.each():
            self.keep_copy(i, d).wait()

        def settle(j, carry):
            for i in range(len(self.grads)):
                for kind in range(self.kinds(i)):
                    self.core_copy(i, kind, j).wait_send()
                for d in range(2):
                    pl.when(j < last)(lambda i=i, d=d: self.ring_copy(i, d, j).wait_send())
                if self.kinds(i) == 3:
                    pl.when(j >= last - 1)(lambda i=i: self.x_copy(i, j).wait_send())
            return carry

        lax.fori_loop(0, self.ring.n, settle, 0)

    @staticmethod
    def specs_of(grads, n, portions):
        return [(g.shape[0] // n, g.shape[1], portion) for g, portion in zip(grads, portions)]

    @staticmethod
    def results(specs, n):
        return [
            jax.ShapeDtypeStruct((rows, 2 * carried(columns, shared)[0]), BF16) for rows, columns, shared in specs
        ] + [jax.ShapeDtypeStruct((n * rows, columns // 2), BF16) for rows, columns, _ in specs]

    @staticmethod
    def scratch(specs, n):
        dma = pltpu.SemaphoreType.DMA
        count = len(specs)
        buffers = []
        for rows, columns, shared in specs:
            w, part = carried(columns, shared)
            buffers += [pltpu.VMEM((n, rows, w), BF16)] * 2 + [pltpu.VMEM((rows, w), BF16)] * 4
            if part:
                buffers += [pltpu.VMEM((rows, part), BF16)] * 2
                buffers += [pltpu.VMEM((n, rows, w), BF16), pltpu.VMEM((2, rows, part), BF16)]
        return buffers + [
            dma((count, 3, 2)), dma((count, 2, n)), dma((count, 2, n)), dma((count, 3, n)), dma((count, 3, n)),
            dma((count, n)), dma((count, n)), dma((count, 2)),
        ]


class FinalSum:
    def __init__(self, ring, sums, totals, specs, scratch):
        self.ring, self.sums, self.totals, self.specs = ring, sums, totals, specs
        scratch = list(scratch)
        self.mine, self.plane, self.own = [], [], []
        for spec in specs:
            self.mine.append(scratch.pop(0))
            self.plane.append(scratch.pop(0))
            self.own.append(scratch.pop(0) if carried(spec[1], spec[2])[1] else None)
        self.local, self.remote_send, self.remote_recv = scratch

    def spans(self, i):
        columns, shared = self.specs[i][1:]
        w, part = carried(columns, shared)
        half, wide = columns // 2, 2 * w - part
        base = self.ring.core * half
        low = self.ring.x == 0
        return (
            (jnp.where(low, part, 0), base + part, wide),
            (jnp.where(low, 0, wide), base + jnp.where(low, 0, half - part), part),
            (0, base + jnp.where(low, half - part, 0), part),
        )

    def remote(self, i, at, src, dst, device):
        return send(src, dst, self.remote_send.at[i, at], self.remote_recv.at[i, at], device)

    def copy(self, i, name):
        ring, sums, totals = self.ring, self.sums[i], self.totals[i]
        (a, a_out, wide), (b, b_out, part), (_, c_out, _) = self.spans(i)
        local = {"load": 0, "save": 1, "load done": 2, "save done": 3}
        remote = {"across": 0, "sibling": 1, "done across": 2, "done sibling": 3, "pass on": 4}
        if name in ("load", "save", "across", "sibling"):
            src, dst, mid = sums.at[:, cols(a, wide)], totals.at[:, cols(a_out, wide)], self.mine[i]
        elif name == "pass on":
            src = dst = mid = totals.at[:, cols(c_out, part)]
        else:
            src, dst, mid = sums.at[:, cols(b, part)], totals.at[:, cols(b_out, part)], self.own[i]
        if name in local:
            ends = (src, mid) if name.startswith("load") else (mid, dst)
            return pltpu.make_async_copy(*ends, self.local.at[i, local[name]])
        ends = {"across": (src, self.plane[i]), "sibling": (mid, dst)}.get(name, (src, dst))
        device = ring.across if "across" in name else ring.sibling
        at = remote[name]
        return send(*ends, self.remote_send.at[i, at], self.remote_recv.at[i, at], device)

    def shares(self, i):
        return carried(*self.specs[i][1:])[1] > 0

    def start(self, i):
        for name in ("across", "load"):
            self.copy(i, name).start()
        if self.shares(i):
            for name in ("done across", "load done", "done sibling"):
                self.copy(i, name).start()

    def add(self, i):
        self.copy(i, "load").wait()
        self.copy(i, "across").wait_recv()
        self.mine[i][...] = (self.mine[i][...].astype(F32) + self.plane[i][...].astype(F32)).astype(BF16)
        self.copy(i, "sibling").start()
        self.copy(i, "save").start()
        if self.shares(i):
            self.copy(i, "load done").wait()
            self.copy(i, "save done").start()
            self.copy(i, "done across").wait_recv()
            self.copy(i, "pass on").start()

    def finish(self):
        for i in range(len(self.specs)):
            self.copy(i, "across").wait_send()
            self.copy(i, "sibling").wait()
            self.copy(i, "save").wait()
            if self.shares(i):
                self.copy(i, "done across").wait_send()
                for name in ("done sibling", "save done", "pass on"):
                    self.copy(i, name).wait()

    @staticmethod
    def scratch(specs):
        dma = pltpu.SemaphoreType.DMA
        count = len(specs)
        buffers = []
        for rows, columns, shared in specs:
            w, part = carried(columns, shared)
            buffers += [pltpu.VMEM((rows, 2 * w - part), BF16)] * 2
            if part:
                buffers += [pltpu.VMEM((rows, part), BF16)]
        return buffers + [dma((count, 4)), dma((count, 5)), dma((count, 5))]


class SmallSum:
    def __init__(self, ring, given, total, scratch):
        self.ring, self.given, self.total = ring, given, total
        self.mine, self.twin, self.plane, self.slots, self.pair, self.ring_send, self.ring_recv = scratch

    def copy(self, src, dst, at, device):
        return send(src, dst, self.pair.at[0, at], self.pair.at[1, at], device)

    def to_core(self):
        return self.copy(self.given, self.twin, 0, self.ring.sibling)

    def to_plane(self):
        return self.copy(self.mine, self.plane, 1, self.ring.across)

    def add_core(self):
        self.to_core().wait()
        self.mine[...] = self.given[...] + self.twin[...]
        self.to_plane().start()

    def add_plane(self):
        self.to_plane().wait()
        self.slots[0] = self.mine[...] + self.plane[...]

    def ring_copy(self, j):
        return send(
            self.slots.at[j], self.slots.at[j + 1], self.ring_send.at[j], self.ring_recv.at[j + 1], self.ring.right
        )

    def item(self, j):
        @pl.when(j > 0)
        def _():
            self.ring_copy(j - 1).wait_recv()

        @pl.when(j < self.ring.n - 1)
        def _():
            self.ring_copy(j).start()

    def finish(self):
        ring = self.ring
        total = jnp.zeros(self.total.shape, F32)
        for place in range(ring.n):
            total = total + self.slots[lax.rem(ring.place - place + ring.n, ring.n)]
        self.total[...] = total

        def settle(j, carry):
            self.ring_copy(j).wait_send()
            return carry

        lax.fori_loop(0, ring.n - 1, settle, 0)

    @staticmethod
    def scratch(rows, n):
        dma = pltpu.SemaphoreType.DMA
        block = pltpu.VMEM((rows, LANE), F32)
        return [block, block, block, pltpu.VMEM((n, rows, LANE), F32), dma((2, 2)), dma((n,)), dma((n,))]


SMALL_SCRATCH = 7


def pack(given, at, row):
    for r in range(row.shape[1] // LANE):
        given[at + r : at + r + 1, :] = row[:, r * LANE : (r + 1) * LANE]
    return at + row.shape[1] // LANE


SPOTS = 8


def pack_taps(given, at, taps_ref, mix_ref):
    rows = taps_ref.shape[1]
    for first in range(0, HEADS, SPOTS):
        together = taps_ref[first]
        for h in range(1, SPOTS):
            together = together + pltpu.roll(taps_ref[first + h], h * (LANE // SPOTS), axis=1)
        given[at : at + rows, :] = together
        at += rows
    together = mix_ref[0]
    for quad in range(1, mix_ref.shape[0]):
        together = together + pltpu.roll(mix_ref[quad], 2 * quad, axis=0)
    given[at : at + rows, :] = together


def unpack_taps(summed):
    rows = 8
    taps = jnp.roll(summed[: HEADS // SPOTS * rows], CK // 2 + 1, axis=1).reshape(-1, rows, SPOTS, LANE // SPOTS)
    taps = taps.transpose(0, 2, 1, 3).reshape(HEADS, rows, LANE // SPOTS)[:, :CQ, :CK]
    mixing = summed[HEADS // SPOTS * rows :][: HEADS // 2, :4]
    return taps[:, :, ::-1] * SCALE, mixing.reshape(HEADS // 2, 2, 2)


def last_kernel(n, specs, early_specs, chunk, small_count, *refs):
    count, early = len(specs), len(early_specs)
    ring = Ring(n)
    refs = list(refs)

    def take(size):
        taken = refs[:size]
        del refs[:size]
        return taken

    small_refs = take(small_count)
    input_ref, gain_ref, d_middle_ref, d_projected, weight = take(5)
    grads, early_sums = take(count), take(early)
    grad_input_ref, total_ref = take(2)
    totals, early_totals, sums, others = take(count), take(early), take(count), take(count)
    given, d_normed, in_left, in_right, in_sem = take(5)
    small = SmallSum(ring, given, total_ref, take(SMALL_SCRATCH))
    last_sum = FinalSum(ring, sums, totals, specs, take(len(FinalSum.scratch(specs))))
    early_sum = FinalSum(ring, early_sums, early_totals, early_specs, take(len(FinalSum.scratch(early_specs))))
    reduce = Reduce(ring, grads, sums, others, specs, refs)
    chunks = d_projected.shape[1] // chunk

    def arrive(t, slot):
        at = cols(t * chunk, chunk)
        return (
            pltpu.make_async_copy(d_projected.at[:, at], in_left.at[slot], in_sem.at[slot, 0]),
            pltpu.make_async_copy(weight.at[:, at], in_right.at[slot], in_sem.at[slot, 1]),
        )

    for copy in arrive(0, 0):
        copy.start()
    reduce.clear()
    ring.meet()

    def turn(t, carry):
        slot = lax.rem(t, 2)
        for copy in arrive(t, slot):
            copy.wait()

        @pl.when(t < chunks - 1)
        def _():
            for copy in arrive(t + 1, 1 - slot):
                copy.start()

        d_normed[...] += nt(in_left[slot], in_right[slot])
        return carry

    reduce.hand_over()
    d_normed[...] = jnp.zeros_like(d_normed)
    given[...] = jnp.zeros_like(given)
    lax.fori_loop(0, chunks // 3, turn, 0)
    for step in reduce.opening()[1:]:
        step()
    reduce.item(jnp.int32(0), reduce.each())
    lax.fori_loop(chunks // 3, chunks, turn, 0)
    values = input_ref[...].astype(F32)
    scale = lax.rsqrt(jnp.mean(values * values, axis=1, keepdims=True) + EPSILON)
    upstream = d_normed[...]
    grad_gain = jnp.sum(upstream * (values * scale), axis=0, keepdims=True)
    at = 0
    for row in [grad_gain] + [ref[...] for ref in small_refs[:2]]:
        at = pack(given, at, row)
    pack_taps(given, at, small_refs[2], small_refs[3])
    small.to_core().start()
    scaled = upstream * gain_ref[...]
    inner = jnp.mean(scaled * values, axis=1, keepdims=True)
    grad_input_ref[...] = d_middle_ref[...] + scale * scaled - values * (scale * scale * scale * inner)
    reduce.item(jnp.int32(1), reduce.each())
    small.add_core()
    reduce.item(jnp.int32(2), reduce.each())
    small.add_plane()
    hops = -(-n // (n - 4))

    def rest(j, carry):
        for hop in range(hops):
            at = (j - 3) * hops + hop
            pl.when(at < n)(functools.partial(small.item, at))
        for i in range(early):
            pl.when(j == 3 + i)(functools.partial(early_sum.start, i))
        reduce.item(j, reduce.each())
        for i in range(early):
            pl.when(j == n - early + i)(functools.partial(early_sum.add, i))
        return carry

    lax.fori_loop(3, n, rest, 0)
    reduce.finish()
    for i in range(count):
        last_sum.start(i)
    small.finish()
    for i in range(count):
        last_sum.add(i)
    early_sum.finish()
    last_sum.finish()


def last_step(
    d_projected, qkv_weight, layer_input, first_gain, d_middle, grads, smalls, early_sums, early_specs, n, collective
):
    count, early = len(grads), len(early_specs)
    seq, width = layer_input.shape
    chunk = 512
    specs = Reduce.specs_of(grads, n, (LESS, THIRD))
    sizes = [width // LANE] * 3 + [(HEADS // SPOTS + 1) * 8]
    rows = -(-sum(sizes) // 8) * 8
    anywhere = pl.BlockSpec(memory_space=pl.ANY)
    whole = pl.BlockSpec(memory_space=pltpu.VMEM)
    results = pl.pallas_call(
        functools.partial(last_kernel, n, specs, early_specs, chunk, len(smalls)),
        out_shape=[jax.ShapeDtypeStruct((seq, width), F32), jax.ShapeDtypeStruct((rows, LANE), F32)]
        + [jax.ShapeDtypeStruct(spec[:2], BF16) for spec in specs + early_specs]
        + Reduce.results(specs, n),
        in_specs=[whole] * (len(smalls) + 3) + [anywhere] * (2 + count + early),
        out_specs=[whole] * 2 + [anywhere] * (3 * count + early),
        scratch_shapes=[
            pltpu.VMEM((rows, LANE), F32),
            pltpu.VMEM((seq, width), F32),
            pltpu.VMEM((2, seq, chunk), BF16),
            pltpu.VMEM((2, width, chunk), BF16),
            pltpu.SemaphoreType.DMA((2, 2)),
        ]
        + SmallSum.scratch(rows, n)
        + FinalSum.scratch(specs)
        + FinalSum.scratch(early_specs)
        + Reduce.scratch(specs, n),
        compiler_params=pltpu.CompilerParams(
            collective_id=collective, has_side_effects=True, vmem_limit_bytes=60 * 1024 * 1024
        ),
    )(*smalls, layer_input, first_gain.reshape(1, width), d_middle, d_projected, qkv_weight, *grads, *early_sums)
    out, at = [], 0
    for size in sizes:
        out.append(results[1][at : at + size])
        at += size
    return results[0], results[2 : 2 + count + early], out


TILES = 8
EARLY_TILES = 3
LATE_TILES = 3


def mlp_kernel(n, specs, tile, *refs):
    refs = list(refs)

    def take(size):
        taken = refs[:size]
        del refs[:size]
        return taken

    second_ref, upstream_ref, middle, inner, down, coming = take(6)
    out_ref, d_second_ref = take(2)
    (early, late, grad_down), sums, others, (came,) = take(3), take(1), take(1), take(1)
    turned, out_sum, in_gate, in_up, in_down, to_gate, to_up, to_down = take(8)
    middle_sem, in_sem, to_sem = take(3)
    ring = Ring(n)
    gather = Gather(ring, [coming], [came], [share(coming.shape)], take(len(Gather.scratch(1, n))))
    reduce = Reduce(ring, [early], sums, others, specs, refs)
    hidden_size = down.shape[0]
    tiles = hidden_size // tile
    begun = EARLY_TILES
    each = -(-n // (tiles - begun - 1))
    due = -(-each // 2)

    split = tiles - LATE_TILES

    def arrive(t, slot, weight, first, count):
        at = pl.multiple_of((t - first) * tile, tile)
        return (
            pltpu.make_async_copy(weight.at[:, pl.ds(at, tile)], in_gate.at[slot], in_sem.at[slot, 0]),
            pltpu.make_async_copy(
                weight.at[:, pl.ds(pl.multiple_of(count * tile + at, tile), tile)], in_up.at[slot], in_sem.at[slot, 1]
            ),
            pltpu.make_async_copy(
                down.at[pl.ds(pl.multiple_of(t * tile, tile), tile), :], in_down.at[slot], in_sem.at[slot, 2]
            ),
        )

    def arrivals(t, act):
        slot = lax.rem(t, 2)

        @pl.when(t < split)
        def _():
            for copy in arrive(t, slot, inner, 0, split):
                act(copy)

        @pl.when((t >= split) & (t < tiles))
        def _():
            for copy in arrive(t, slot, came, split, LATE_TILES):
                act(copy)

    def leave(grad, t, slot, first, count):
        at = pl.multiple_of((t - first) * tile, tile)
        return (
            pltpu.make_async_copy(to_gate.at[slot], grad.at[:, pl.ds(at, tile)], to_sem.at[slot, 0]),
            pltpu.make_async_copy(
                to_up.at[slot], grad.at[:, pl.ds(pl.multiple_of(count * tile + at, tile), tile)], to_sem.at[slot, 1]
            ),
            pltpu.make_async_copy(
                to_down.at[slot], grad_down.at[pl.ds(pl.multiple_of(t * tile, tile), tile), :], to_sem.at[slot, 2]
            ),
        )

    def leave_early(t):
        return leave(early, t, lax.rem(t, 2), 0, begun)

    def leave_late(t):
        return leave(late, t, lax.rem(t, 2), begun, tiles - begun)

    first = pltpu.make_async_copy(middle, out_sum, middle_sem)
    first.start()
    arrivals(jnp.int32(0), lambda copy: copy.start())
    reduce.clear()
    ring.meet()
    gather.start()
    turned[...] = second_ref[...].T
    d_second_ref[...] = jnp.zeros_like(d_second_ref)
    first.wait()

    def serve(t, point):
        turns = 2 * (split - 1) - 1
        if point % 2:
            turn = 2 * t + point // 2
            for k in in_turn(turn, turns, n - 1):
                pl.when((turn < turns) & (k < n - 1))(functools.partial(gather.step, k))
            pl.when(turn == turns)(gather.finish)

        @pl.when(t == begun)
        def _():
            if point == 0:
                for back in (2, 1):
                    for copy in leave_early(t - back):
                        copy.wait()
            reduce.opening()[point]()

        for step in range(due):
            if point // 2 * due + step < each:
                j = (t - begun - 1) * each + point // 2 * due + step
                pl.when((t > begun) & (j < n))(functools.partial(reduce.item, j, [(0, 1 - point % 2)]))

    def one(t, carry):
        slot = lax.rem(t, 2)
        arrivals(t, lambda copy: copy.wait())
        arrivals(t + 1, lambda copy: copy.start())
        second, upstream = second_ref[...], upstream_ref[...]
        gate = nn(second, in_gate[slot])
        up = nn(second, in_up[slot])
        sigmoid = jax.nn.sigmoid(gate)
        silu = gate * sigmoid
        hidden = (silu * up).astype(BF16)
        serve(t, 0)
        d_hidden = nt(upstream, in_down[slot])
        out_sum[...] += nn(hidden, in_down[slot])

        @pl.when((t >= 2) & (t < begun))
        def _():
            for copy in leave_early(t - 2):
                copy.wait()

        @pl.when(t >= begun + 2)
        def _():
            for copy in leave_late(t - 2):
                copy.wait()

        to_down[slot] = nn(hidden.T, upstream).astype(BF16)
        d_gate = (d_hidden * up * sigmoid * (1.0 + gate * (1.0 - sigmoid))).astype(BF16)
        d_up = (d_hidden * silu).astype(BF16)
        serve(t, 1)
        d_second_ref[...] += nt(d_gate, in_gate[slot])
        to_gate[slot] = nn(turned[...], d_gate).astype(BF16)
        serve(t, 2)
        d_second_ref[...] += nt(d_up, in_up[slot])
        to_up[slot] = nn(turned[...], d_up).astype(BF16)
        serve(t, 3)

        @pl.when(t < begun)
        def _():
            for copy in leave_early(t):
                copy.start()

        @pl.when(t >= begun)
        def _():
            for copy in leave_late(t):
                copy.start()

        return carry

    lax.fori_loop(0, tiles, one, 0)
    out_ref[...] = out_sum[...].astype(BF16)
    for t in (tiles - 2, tiles - 1):
        for copy in leave_late(t):
            copy.wait()
    reduce.finish()


def feed_forward(second, upstream, middle, inner, down, coming, n, collective):
    seq, width = second.shape
    hidden_size = down.shape[0]
    tile = hidden_size // TILES
    early = EARLY_TILES * tile
    specs = [(width // n, 2 * early, THIRD)]
    whole = pl.BlockSpec(memory_space=pltpu.VMEM)
    anywhere = pl.BlockSpec(memory_space=pl.ANY)
    dma = pltpu.SemaphoreType.DMA
    results = pl.pallas_call(
        functools.partial(mlp_kernel, n, specs, tile),
        out_shape=[
            jax.ShapeDtypeStruct((seq, width), BF16),
            jax.ShapeDtypeStruct((seq, width), F32),
        ]
        + [
            jax.ShapeDtypeStruct((width, 2 * early), BF16),
            jax.ShapeDtypeStruct((width, 2 * (hidden_size - early)), BF16),
            jax.ShapeDtypeStruct((hidden_size, width), BF16),
        ]
        + Reduce.results(specs, n)
        + [jax.ShapeDtypeStruct((n * coming.shape[0], coming.shape[1]), BF16)],
        in_specs=[whole, whole] + [anywhere] * 4,
        out_specs=[whole, whole] + [anywhere] * 6,
        scratch_shapes=[
            pltpu.VMEM((width, seq), BF16),
            pltpu.VMEM((seq, width), F32),
            pltpu.VMEM((2, width, tile), BF16),
            pltpu.VMEM((2, width, tile), BF16),
            pltpu.VMEM((2, tile, width), BF16),
            pltpu.VMEM((2, width, tile), BF16),
            pltpu.VMEM((2, width, tile), BF16),
            pltpu.VMEM((2, tile, width), BF16),
            dma, dma((2, 3)), dma((2, 3)),
        ]
        + Gather.scratch(1, n)
        + Reduce.scratch(specs, n),
        compiler_params=pltpu.CompilerParams(
            collective_id=collective, has_side_effects=True, vmem_limit_bytes=62 * 1024 * 1024
        ),
    )(second, upstream, middle, inner, down, coming)
    out, d_second, _, late, grad_down, sums, _, _ = results
    return out, d_second, late, grad_down, [sums], specs


def rms_norm(values, gains):
    return values * lax.rsqrt(jnp.mean(values * values, axis=-1, keepdims=True) + EPSILON) * gains


def swiglu(gate_up):
    middle_col = gate_up.shape[1] // 2
    return jax.nn.silu(gate_up[:, :middle_col]) * gate_up[:, middle_col:]


def project(operand, weight):
    return jnp.dot(operand, weight, preferred_element_type=F32)


def project_back(upstream, weight):
    return lax.dot_general(
        upstream, weight, (((1,), (1,)), ((), ())), preferred_element_type=F32
    )


def weight_grad(operand, upstream):
    return lax.dot_general(
        operand, upstream, (((0,), (0,)), ((), ())), preferred_element_type=F32
    ).astype(BF16)


def body(
    layer_input,
    first_gain,
    qkv_weight,
    conv_kernel,
    head_mixing,
    group_gain,
    out_weight,
    second_gain,
    inner_weight,
    down_weight,
    doc_lengths,
    cotangent,
):
    n = lax.axis_size("fsdp")
    hidden_size = inner_weight.shape[1] // 2
    cut = hidden_size // TILES * (TILES - LATE_TILES)
    gates, ups = inner_weight[:, :hidden_size], inner_weight[:, hidden_size:]
    inner_first = jnp.concatenate([gates[:, :cut], ups[:, :cut]], axis=1)
    inner_last = jnp.concatenate([gates[:, cut:], ups[:, cut:]], axis=1)
    kept, (qkv_weight, out_weight), (inner_first, down_weight) = attend_forward(
        layer_input, conv_kernel, head_mixing, doc_lengths, (first_gain, group_gain, second_gain),
        [qkv_weight, out_weight], [inner_first, down_weight], n, 0,
    )
    grouped, attended, soft, normed, middle, second, projected = kept
    second_pull = jax.vjp(rms_norm, middle, second_gain)[1]
    layer_output, d_second, late_inner, grad_down, early_sums, early_specs = feed_forward(
        second, cotangent, middle, inner_first, down_weight, inner_last, n, 2
    )
    d_middle, grad_second = second_pull(d_second)
    d_middle = cotangent.astype(F32) + d_middle
    d_branch = d_middle.astype(jnp.bfloat16)
    d_grouped = project_back(d_branch, out_weight)
    (d_projected, grad_group, grad_kernel, grad_mixing), sums, specs, (early_inner,) = attend_backward(
        projected, conv_kernel, head_mixing, doc_lengths, group_gain, attended, d_grouped, soft,
        [late_inner, grad_down], early_sums, early_specs, n, 3,
    )
    grad_qkv = weight_grad(normed, d_projected)
    grad_proj = weight_grad(grouped, d_branch)
    grad_input, shards, small = last_step(
        d_projected, qkv_weight, layer_input, first_gain, d_middle, [grad_qkv, grad_proj],
        [grad_group, grad_second.reshape(1, -1), grad_kernel, grad_mixing], sums, specs, n, 4,
    )
    grad_first, grad_group, grad_second = [g.reshape(-1) for g in small[:3]]
    grad_kernel, grad_mixing = unpack_taps(small[3])
    grad_qkv, grad_proj, late_inner, grad_down = shards
    cut, late_cut = early_inner.shape[1] // 2, late_inner.shape[1] // 2
    grad_inner = jnp.concatenate(
        [early_inner[:, :cut], late_inner[:, :late_cut], early_inner[:, cut:], late_inner[:, late_cut:]], axis=1
    )
    shards = [g.astype(F32) for g in (grad_qkv, grad_proj, grad_inner, grad_down)]
    return (
        layer_output, grad_input, grad_first, shards[0], grad_kernel, grad_mixing, grad_group, shards[1], grad_second,
        shards[2], shards[3],
    )


def solution(mesh):
    placed = (
        P(("rep", "fsdp"), None),
        P(),
        P("fsdp", None),
        P(),
        P(),
        P(),
        P("fsdp", None),
        P(),
        P("fsdp", None),
        P("fsdp", None),
        P(("rep", "fsdp"), None),
        P(("rep", "fsdp"), None),
    )
    return jax.shard_map(
        body,
        mesh=mesh,
        in_specs=placed,
        out_specs=(
            P(("rep", "fsdp"), None),
            P(("rep", "fsdp"), None),
            P(),
            P("fsdp", None),
            P(),
            P(),
            P(),
            P("fsdp", None),
            P(),
            P("fsdp", None),
            P("fsdp", None),
        ),
        check_vma=False,
    )
```

```python
import functools, math
import jax, jax.numpy as jnp
from jax import lax
from jax.experimental import pallas as pl
from jax.experimental.pallas import tpu as pltpu
from jax.sharding import PartitionSpec as P

HEADS = 16
HEAD_DIM = 96
CQ = 6
CK = 11
EPSILON = 1e-05
LANE = 128
QUAD = 4
LAG = 1
LEAD = 3
REST_AHEAD = 2
SCALE = 1.0 / math.sqrt(HEAD_DIM)
F32 = jnp.float32
BF16 = jnp.bfloat16


def row_sets(seq):
    return [
        (r, min(r + LANE, 3 * LANE), max(0, r - 2 * LANE)) for r in range(0, seq, LANE)
    ]


def nt(a, b):
    return lax.dot_general(a, b, (((1,), (1,)), ((), ())), preferred_element_type=F32)


def nn(a, b):
    return jnp.dot(a, b, preferred_element_type=F32)


def fill_masks(docs_ref, masks, seq):
    ends = []
    total = jnp.int32(0)
    for d in range(docs_ref.shape[1] - 1):
        total = total + docs_ref[0, d]
        ends.append(total)
    for r0, width, c0 in row_sets(seq):
        rows = r0 + lax.broadcasted_iota(jnp.int32, (LANE, 1), 0)
        cols = c0 + lax.broadcasted_iota(jnp.int32, (1, width), 1)
        row_doc = sum((rows >= e).astype(jnp.int32) for e in ends)
        col_doc = sum((cols >= e).astype(jnp.int32) for e in ends)
        same = row_doc == col_doc
        for a in range(CQ):
            masks[a, r0 : r0 + LANE, :width] = jnp.where(
                same & (rows - cols >= a), 1.0, 0.0
            ).astype(BF16)


def circulant_masks():
    gap = lax.broadcasted_iota(jnp.int32, (LANE, LANE), 1) - lax.broadcasted_iota(
        jnp.int32, (LANE, LANE), 0
    )
    half = CK // 2
    return (jnp.abs(gap) <= half, gap <= half - LANE, gap >= LANE - half)


def circulant(taps):
    wide = jnp.broadcast_to(taps, (LANE, LANE))
    return pltpu.roll(wide, 0, axis=1, stride=1, stride_axis=0)


def fill_toeplitz(taps_ref, head, band, blocks):
    near, after, before = circulant_masks()
    for a in range(CQ):
        whole = circulant(taps_ref[head, a : a + 1, :])
        parts = {
            0: jnp.where(near, whole, 0.0).astype(BF16),
            1: jnp.where(after, whole, 0.0).astype(BF16),
            -1: jnp.where(before, whole, 0.0).astype(BF16),
        }
        for r in range(blocks):
            for c in range(blocks):
                part = parts.get(c - r)
                if part is not None:
                    yield a, r, c, part


def fill_forward_band(taps_ref, head, band):
    for a, r, c, part in fill_toeplitz(taps_ref, head, band, 3):
        at = (r * CQ + a) * LANE
        band[at : at + LANE, c * LANE : (c + 1) * LANE] = part


def fill_backward_band(taps_ref, head, band):
    near, after, before = circulant_masks()
    for a in range(CQ):
        whole = circulant(taps_ref[head, a : a + 1, :])
        for at, keep in enumerate((after, near, before)):
            band[at * LANE : (at + 1) * LANE, a * LANE : (a + 1) * LANE] = jnp.where(keep, whole, 0.0).astype(BF16)


def shifted_rows(query):
    wide = query.astype(F32)
    return [query] + [pltpu.roll(wide, a, axis=0).astype(BF16) for a in range(1, CQ)]


def masked_scores(shifted, keys, masks, r0, width, c0):
    left = jnp.concatenate([shifted[a, r0 : r0 + LANE] for a in range(CQ)], axis=0)
    scores = nt(left, keys[c0 : c0 + width]).astype(BF16)
    return left, [
        scores[a * LANE : (a + 1) * LANE] * masks[a, r0 : r0 + LANE, :width]
        for a in range(CQ)
    ]


def by_window(parts, width):
    return jnp.concatenate(
        [
            parts[a][:, b * LANE : (b + 1) * LANE]
            for b in range(width // LANE)
            for a in range(CQ)
        ],
        axis=1,
    )


def forward_kernel(
    n, first_widths, rest_widths, docs_ref, mix_ref, taps_ref, gain_ref, input_ref, gains_ref, *refs
):
    refs = list(refs)

    def take(size):
        taken = refs[:size]
        del refs[:size]
        return taken

    first_count, rest_count = len(first_widths), len(rest_widths)
    first_weights, rest_weights = take(first_count), take(rest_count)
    grouped_ref, attended_ref, soft_ref, normed_ref, middle_ref, second_ref, projected = take(7)
    first_fulls, rest_fulls = take(first_count), take(rest_count)
    masks, band, qs, ks, vs, shifted, outs = take(7)
    blocks, block_weight, every, out_weight, block_in, block_out, out_in = take(7)
    ring = Ring(n)
    sems = len(Gather.scratch(first_count, n))
    first = Gather(ring, first_weights, first_fulls, first_widths, take(sems))
    rest = Gather(ring, rest_weights, rest_fulls, rest_widths, take(sems))
    seq = input_ref.shape[0]
    quad = pl.program_id(0)
    quads = HEADS // QUAD
    size = QUAD * HEAD_DIM
    count = 3 * quads

    def block_copy(t):
        slot = lax.rem(t, 2)
        return pltpu.make_async_copy(first_fulls[0].at[:, cols(t * size, size)], block_weight.at[slot], block_in.at[slot])

    def block_save(t):
        return pltpu.make_async_copy(blocks.at[t], projected.at[:, cols(t * size, size)], block_out.at[t])

    out_copy = pltpu.make_async_copy(first_fulls[1], out_weight, out_in)

    def serve(turn):
        for k in in_turn(turn, 2 + HEADS // 2, n - 1):
            pl.when(k < n - 1)(functools.partial(rest.step, k))

    @pl.when(quad == 0)
    def _():
        ring.meet()
        first.start()
        fill_masks(docs_ref, masks, seq)
        band[...] = jnp.zeros_like(band)
        values = input_ref[...].astype(F32)
        scale = lax.rsqrt(jnp.mean(values * values, axis=1, keepdims=True) + EPSILON)
        normed_ref[...] = (values * scale * gains_ref[0:1, :]).astype(BF16)

        def one(k, carry):
            first.step(k)
            pl.when(k == n - REST_AHEAD)(rest.start)
            return carry

        lax.fori_loop(0, n - 1, one, 0)
        first.finish()
        serve(jnp.int32(0))
        block_copy(0).start()
        out_copy.start()

        def project_block(t, carry):
            pl.when(t < count - 1)(lambda: block_copy(t + 1).start())
            block_copy(t).wait()
            blocks[t] = nn(normed_ref[...], block_weight[lax.rem(t, 2)]).astype(BF16)
            block_save(t).start()
            return carry

        lax.fori_loop(0, count, project_block, 0)
        serve(jnp.int32(1))

    for h in range(QUAD):
        at = slice(h * HEAD_DIM, (h + 1) * HEAD_DIM)
        qs[h] = blocks[quad, :, at]
        ks[h] = blocks[quads + quad, :, at]
        vs[h] = blocks[2 * quads + quad, :, at]

    sets = row_sets(seq)

    def pair(p, carry):
        group = quad * 2 + p
        for r in range(2):
            h = 2 * p + r
            fill_forward_band(taps_ref, quad * QUAD + h, band)
            for a, rows in enumerate(shifted_rows(qs[h])):
                shifted[a] = rows
            keys = ks[h]
            lefts = []
            for r0, width, c0 in sets:
                _, parts = masked_scores(shifted, keys, masks, r0, width, c0)
                lefts.append((width, by_window(parts, width)))
            convs = []
            i = 0
            while i < len(sets):
                width = sets[i][1]
                run = 1
                while i + run < len(sets) and sets[i + run][1] == width:
                    run += 1
                left = jnp.concatenate([lefts[i + m][1] for m in range(run)], axis=0)
                conv = nn(left, band[: width * CQ, :width])
                convs += [conv[m * LANE : (m + 1) * LANE] for m in range(run)]
                i += run
            for (r0, width, c0), conv in zip(sets, convs):
                logits = jnp.where(
                    masks[0, r0 : r0 + LANE, :width].astype(F32) > 0, conv, -1e30
                )
                weights = jnp.exp(logits - jnp.max(logits, axis=1, keepdims=True))
                soft = weights * (1.0 / jnp.sum(weights, axis=1, keepdims=True))
                soft_ref[h, r0 : r0 + LANE, :width] = soft.astype(BF16)
        for r in range(2):
            h = 2 * p + r
            values = vs[h]
            for r0, width, c0 in sets:
                mixed = (
                    mix_ref[group, r, 0] * soft_ref[2 * p, r0 : r0 + LANE, :width].astype(F32)
                    + mix_ref[group, r, 1] * soft_ref[2 * p + 1, r0 : r0 + LANE, :width].astype(F32)
                ).astype(BF16)
                outs[h, r0 : r0 + LANE] = nn(mixed, values[c0 : c0 + width])
        serve(2 + group)
        return carry

    lax.fori_loop(0, 2, pair, 0)
    wholes, grouped = [], []
    for h in range(QUAD):
        attended = outs[h]
        centred = attended - jnp.mean(attended, axis=1, keepdims=True)
        var = jnp.mean(centred * centred, axis=1, keepdims=True)
        wholes.append(attended)
        grouped.append(centred * lax.rsqrt(var + EPSILON))
    attended_ref[...] = jnp.concatenate(wholes, axis=1)
    every[quad] = (jnp.concatenate(grouped, axis=1) * gain_ref[1:2, :]).astype(BF16)
    grouped_ref[...] = every[quad]

    @pl.when(quad == quads - 1)
    def _():
        out_copy.wait()
        branch = nn(jnp.concatenate([every[i] for i in range(quads)], axis=1), out_weight[...])
        middle = input_ref[...].astype(F32) + branch
        scale = lax.rsqrt(jnp.mean(middle * middle, axis=1, keepdims=True) + EPSILON)
        middle_ref[...] = middle
        second_ref[...] = (middle * scale * gains_ref[2:3, :]).astype(BF16)

        def saved(t, carry):
            block_save(t).wait()
            return carry

        lax.fori_loop(0, count, saved, 0)
        rest.finish()


def pad_taps(kernel):
    padded = jnp.pad(kernel * SCALE, ((0, 0), (0, 2), (0, LANE - CK)))
    return jnp.roll(padded, -(CK // 2), axis=2)


def in_turn(turn, turns, steps):
    each = -(-steps // turns)
    return [turn * each + t for t in range(each)]


def attend_forward(layer_input, conv_kernel, head_mixing, docs, gains, first, rest, n, collective):
    seq, width = layer_input.shape
    block = QUAD * HEAD_DIM
    quads = HEADS // QUAD
    first_widths, rest_widths = [share(w.shape) for w in first], [share(w.shape) for w in rest]
    whole = pl.BlockSpec(memory_space=pltpu.VMEM)
    smem = pl.BlockSpec(memory_space=pltpu.SMEM)
    anywhere = pl.BlockSpec(memory_space=pl.ANY)
    columns = pl.BlockSpec((seq, block), lambda i: (0, i))
    dma = pltpu.SemaphoreType.DMA
    gains = jnp.stack(gains)
    results = pl.pallas_call(
        functools.partial(forward_kernel, n, first_widths, rest_widths),
        grid=(quads,),
        out_shape=[
            jax.ShapeDtypeStruct((seq, width), BF16),
            jax.ShapeDtypeStruct((seq, width), F32),
            jax.ShapeDtypeStruct((HEADS, seq, 3 * LANE), BF16),
            jax.ShapeDtypeStruct((seq, width), BF16),
            jax.ShapeDtypeStruct((seq, width), F32),
            jax.ShapeDtypeStruct((seq, width), BF16),
            jax.ShapeDtypeStruct((seq, 3 * width), BF16),
        ]
        + [jax.ShapeDtypeStruct((n * w.shape[0], w.shape[1]), w.dtype) for w in first + rest],
        in_specs=[smem, smem, whole, pl.BlockSpec((3, block), lambda i: (0, i)), whole, whole]
        + [anywhere] * len(first + rest),
        out_specs=[
            columns, columns,
            pl.BlockSpec((QUAD, seq, 3 * LANE), lambda i: (i, 0, 0)),
            whole, whole, whole,
        ]
        + [anywhere] * (1 + len(first + rest)),
        scratch_shapes=[
            pltpu.VMEM((CQ, seq, 3 * LANE), BF16),
            pltpu.VMEM((3 * LANE * CQ, 3 * LANE), BF16),
            pltpu.VMEM((QUAD, seq, HEAD_DIM), BF16),
            pltpu.VMEM((QUAD, seq, HEAD_DIM), BF16),
            pltpu.VMEM((QUAD, seq, HEAD_DIM), BF16),
            pltpu.VMEM((CQ, seq, HEAD_DIM), BF16),
            pltpu.VMEM((QUAD, seq, HEAD_DIM), F32),
            pltpu.VMEM((3 * quads, seq, block), BF16),
            pltpu.VMEM((2, width, block), BF16),
            pltpu.VMEM((quads, seq, block), BF16),
            pltpu.VMEM((width, width), BF16),
            dma((2,)), dma((3 * quads,)), dma,
        ]
        + Gather.scratch(len(first), n)
        + Gather.scratch(len(rest), n),
        compiler_params=pltpu.CompilerParams(
            collective_id=collective, has_side_effects=True, vmem_limit_bytes=60 * 1024 * 1024
        ),
    )(
        docs, head_mixing, pad_taps(conv_kernel), gains, layer_input, gains,
        *first, *rest,
    )
    return results[:7], results[7 : 7 + len(first)], results[7 + len(first) :]


def backward_kernel(
    n, specs, done_specs, docs_ref, mix_ref, taps_ref, gain_ref, q_ref, k_ref, v_ref, attended_ref, d_grouped_ref, soft_ref, *refs
):
    count, done = len(specs), len(done_specs)
    grads, done_sums, refs = refs[:count], refs[count : count + done], refs[count + done :]
    d_projected, grad_gain_ref, grad_taps_ref, grad_mix_ref = refs[:4]
    sums, others, refs = refs[4 : 4 + count], refs[4 + count : 4 + 2 * count], refs[4 + 2 * count :]
    done_totals, refs = refs[:done], refs[done:]
    final_size = len(FinalSum.scratch(done_specs))
    masks, band, qs, ks, vs, ds, shifted, d_heads, d_rows, d_cols, near_keys, leaving, leave_sem = refs[:13]
    reduce = Reduce(Ring(n), grads, sums, others, specs, refs[13 + final_size :])
    final = FinalSum(reduce.ring, done_sums, done_totals, done_specs, refs[13 : 13 + final_size])
    seq = q_ref.shape[0]
    quad = pl.program_id(0)

    @pl.when(quad == 0)
    def _():
        reduce.clear()
        reduce.ring.meet()
        reduce.hand_over()

    @pl.when(quad == 0)
    def _():
        fill_masks(docs_ref, masks, seq)

    gains = []
    for h in range(QUAD):
        at = slice(h * HEAD_DIM, (h + 1) * HEAD_DIM)
        qs[h] = q_ref[:, at]
        ks[h] = k_ref[:, at]
        vs[h] = v_ref[:, at]
        attended = attended_ref[:, at]
        d_grouped = d_grouped_ref[:, at]
        centred = attended - jnp.mean(attended, axis=1, keepdims=True)
        var = jnp.mean(centred * centred, axis=1, keepdims=True)
        scale = lax.rsqrt(var + EPSILON)
        unit = centred * scale
        gains.append(jnp.sum(d_grouped * unit, axis=0, keepdims=True))
        w = d_grouped * gain_ref[:, at]
        d_attended = scale * (
            w
            - jnp.mean(w, axis=1, keepdims=True)
            - unit * jnp.mean(w * unit, axis=1, keepdims=True)
        )
        ds[h] = d_attended.astype(BF16)
    grad_gain_ref[...] = jnp.concatenate(gains, axis=1)
    grad_taps_ref[...] = jnp.zeros_like(grad_taps_ref)
    grad_mix_ref[...] = jnp.zeros_like(grad_mix_ref)

    @pl.when(quad == 0)
    def _():
        for step in reduce.opening()[1:]:
            step()

    @pl.when(quad == 1)
    def _():
        for i in range(done):
            final.start(i)

    sets = row_sets(seq)
    up = lax.broadcasted_iota(jnp.int32, (LANE, LANE), 0)
    across = lax.broadcasted_iota(jnp.int32, (LANE, LANE), 1)
    flip = jnp.where(up + across == LANE - 1, 1.0, 0.0).astype(BF16)
    gap = up + across - (LANE - 1)
    keeps = {0: jnp.abs(gap) <= CK // 2, 1: gap <= CK // 2 - LANE, -1: gap >= LANE - CK // 2}

    def pair(p, carry):
        group = quad * 2 + p
        mix = [[mix_ref[group, r, s] for s in range(2)] for r in range(2)]
        upstream_t = [ds[2 * p + r].T for r in range(2)]
        grad_mix = [[jnp.zeros((1, 1), F32) for _ in range(2)] for _ in range(2)]
        for r in range(2):
            d_cols[r] = jnp.zeros_like(d_cols[r])
        for r0, width, c0 in sets:
            rows = slice(r0, r0 + LANE)
            soft = [soft_ref[2 * p + s, rows, :width].astype(F32) for s in range(2)]
            d_prob, sums = [], []
            for r in range(2):
                dp = nt(ds[2 * p + r, rows], vs[2 * p + r, c0 : c0 + width])
                d_prob.append(dp)
                sums.append([jnp.sum(dp * soft[s], axis=1, keepdims=True) for s in range(2)])
                for s in range(2):
                    grad_mix[r][s] += jnp.sum(sums[r][s], axis=0, keepdims=True)
                mixed = (mix[r][0] * soft[0] + mix[r][1] * soft[1]).astype(BF16)
                d_cols[r, :, c0 : c0 + width] += nn(upstream_t[r][:, r0 : r0 + LANE], mixed)
            for s in range(2):
                d_soft = mix[0][s] * d_prob[0] + mix[1][s] * d_prob[1]
                inner = mix[0][s] * sums[0][s] + mix[1][s] * sums[1][s]
                d_conv = soft[s] * (d_soft - inner)
                d_rows[s, rows, :width] = d_conv.astype(BF16)
        lane = lax.broadcasted_iota(jnp.int32, (1, LANE), 1)
        line = jnp.zeros((1, LANE), F32)
        for r in range(2):
            for s in range(2):
                line = line + jnp.where(lane == 2 * r + s, grad_mix[r][s], 0.0)
        grad_mix_ref[0, pl.ds(p, 1), :] = line
        for r in range(2):
            d_heads[2, 2 * p + r] = d_cols[r].T

        for r in range(2):
            h = 2 * p + r
            fill_backward_band(taps_ref, quad * QUAD + h, band)
            for a, moved in enumerate(shifted_rows(qs[h])):
                shifted[a] = moved
            keys = ks[h]
            d_cols[0] = jnp.zeros_like(d_cols[0])
            d_query = []
            below = jnp.zeros((8, LANE * CQ), F32)
            above = jnp.zeros((8, LANE * CQ), F32)
            mirrored = []
            for r0, width, c0 in sets:
                rows = slice(r0, r0 + LANE)
                left, parts = masked_scores(shifted, keys, masks, r0, width, c0)
                d_conv = d_rows[r, rows, :width]
                blocks = width // LANE
                flipped = [
                    nt(flip, d_conv[:, b * LANE : (b + 1) * LANE]).astype(BF16) for b in range(blocks)
                ]
                start = len(mirrored) * LANE
                mirrored += flipped
                for b in range(blocks):
                    near_keys[start + b * LANE : start + (b + 1) * LANE, :] = jnp.concatenate(
                        [parts[a][:, b * LANE : (b + 1) * LANE] for a in range(CQ)], axis=1
                    )
                if blocks > 1:
                    end = start + blocks * LANE
                    below = below + nn(
                        jnp.concatenate([f[:8] for f in flipped[:-1]], axis=1), near_keys[start + LANE : end, :]
                    )
                    above = above + nn(
                        jnp.concatenate([f[LANE - 8 :] for f in flipped[1:]], axis=1), near_keys[start : end - LANE, :]
                    )
                spread = []
                for b in range(blocks):
                    low, high = max(b - 1, 0), min(b + 1, blocks - 1)
                    spread.append(
                        nn(
                            d_conv[:, low * LANE : (high + 1) * LANE],
                            band[(low - b + 1) * LANE : (high - b + 2) * LANE, :],
                        ).astype(BF16)
                    )
                stacked = jnp.concatenate(
                    [
                        jnp.concatenate(
                            [
                                spread[b][:, a * LANE : (a + 1) * LANE]
                                for b in range(blocks)
                            ],
                            axis=1,
                        )
                        * masks[a, rows, :width]
                        for a in range(CQ)
                    ],
                    axis=0,
                )
                d_query.append(nn(stacked, keys[c0 : c0 + width]))
                d_cols[0, :, c0 : c0 + width] += nn(left.T, stacked)
            total = None
            for a in range(CQ):
                whole = jnp.concatenate([d[a * LANE : (a + 1) * LANE] for d in d_query], axis=0)
                if a:
                    whole = pltpu.roll(whole, seq - a, axis=0)
                total = whole if total is None else total + whole
            d_heads[0, h] = total
            d_heads[1, h] = d_cols[0].T
            band_sum = nn(jnp.concatenate(mirrored, axis=1), near_keys[: len(mirrored) * LANE, :])
            for a in range(CQ):
                at = slice(a * LANE, (a + 1) * LANE)
                whole = jnp.where(keeps[0], band_sum[:, at], 0.0)
                whole = jnp.concatenate(
                    [
                        whole[:8] + jnp.where(keeps[1][:8], below[:, at], 0.0),
                        whole[8 : LANE - 8],
                        whole[LANE - 8 :] + jnp.where(keeps[-1][LANE - 8 :], above[:, at], 0.0),
                    ],
                    axis=0,
                )
                aligned = pltpu.roll(whole, 0, axis=1, stride=1, stride_axis=0)
                grad_taps_ref[h, a : a + 1, :] = jnp.sum(aligned, axis=0, keepdims=True)
            work = reduce.each()
            middle = len(work) // 2
            for j in in_turn(group, HEADS // 2, n):
                pl.when(j < n)(functools.partial(reduce.item, j, work[middle:] if r else work[:middle]))
        return carry

    lax.fori_loop(0, 2, pair, 0)
    quads = HEADS // QUAD
    block = QUAD * HEAD_DIM

    def leave(part):
        there = d_projected.at[:, cols((part * quads + quad) * block, block)]
        return pltpu.make_async_copy(leaving.at[part], there, leave_sem.at[part])

    for part in range(3):
        pl.when(quad > 0)(leave(part).wait)
        leaving[part] = jnp.concatenate([d_heads[part, h] for h in range(QUAD)], axis=1).astype(BF16)
        leave(part).start()

    @pl.when(quad == quads - 1)
    def _():
        for part in range(3):
            leave(part).wait()
        for i in range(done):
            final.add(i)

    @pl.when(quad == pl.num_programs(0) - 1)
    def _():
        reduce.finish()
        final.finish()


def attend_backward(projected, conv_kernel, head_mixing, docs, gain, attended, d_grouped, soft, grads, done_sums, done_specs, n, collective):
    seq = projected.shape[0]
    width = projected.shape[1] // 3
    block = QUAD * HEAD_DIM
    quads = HEADS // QUAD
    count = len(grads)
    specs = Reduce.specs_of(grads, n, (THIRD, THIRD))
    anywhere = pl.BlockSpec(memory_space=pl.ANY)
    whole = pl.BlockSpec(memory_space=pltpu.VMEM)
    smem = pl.BlockSpec(memory_space=pltpu.SMEM)

    def columns(first):
        return pl.BlockSpec((seq, block), lambda i: (0, first * quads + i))

    results = pl.pallas_call(
        functools.partial(backward_kernel, n, specs, done_specs),
        grid=(quads,),
        out_shape=[
            jax.ShapeDtypeStruct((seq, 3 * width), BF16),
            jax.ShapeDtypeStruct((1, width), F32),
            jax.ShapeDtypeStruct((HEADS, 8, LANE), F32),
            jax.ShapeDtypeStruct((quads, 8, LANE), F32),
        ]
        + Reduce.results(specs, n)
        + [jax.ShapeDtypeStruct(spec[:2], BF16) for spec in done_specs],
        in_specs=[
            smem, smem, whole,
            pl.BlockSpec((1, block), lambda i: (0, i)),
            columns(0), columns(1), columns(2), columns(0), columns(0),
            pl.BlockSpec((QUAD, seq, 3 * LANE), lambda i: (i, 0, 0)),
        ]
        + [anywhere] * (count + len(done_specs)),
        out_specs=[
            anywhere,
            pl.BlockSpec((1, block), lambda i: (0, i)),
            pl.BlockSpec((QUAD, 8, LANE), lambda i: (i, 0, 0)),
            pl.BlockSpec((1, 8, LANE), lambda i: (i, 0, 0)),
        ]
        + [anywhere] * (2 * count + len(done_specs)),
        scratch_shapes=[
            pltpu.VMEM((CQ, seq, 3 * LANE), BF16),
            pltpu.VMEM((3 * LANE, LANE * CQ), BF16),
            pltpu.VMEM((QUAD, seq, HEAD_DIM), BF16),
            pltpu.VMEM((QUAD, seq, HEAD_DIM), BF16),
            pltpu.VMEM((QUAD, seq, HEAD_DIM), BF16),
            pltpu.VMEM((QUAD, seq, HEAD_DIM), BF16),
            pltpu.VMEM((CQ, seq, HEAD_DIM), BF16),
            pltpu.VMEM((3, QUAD, seq, HEAD_DIM), F32),
            pltpu.VMEM((2, seq, 3 * LANE), BF16),
            pltpu.VMEM((2, HEAD_DIM, seq), F32),
            pltpu.VMEM((sum(w for _, w, _ in row_sets(seq)), LANE * CQ), BF16),
            pltpu.VMEM((3, seq, block), BF16),
            pltpu.SemaphoreType.DMA((3,)),
        ]
        + FinalSum.scratch(done_specs)
        + Reduce.scratch(specs, n),
        compiler_params=pltpu.CompilerParams(
            collective_id=collective, has_side_effects=True, vmem_limit_bytes=62 * 1024 * 1024
        ),
    )(
        docs, head_mixing, pad_taps(conv_kernel[:, :, ::-1]), gain.reshape(1, width),
        projected, projected, projected, attended, d_grouped, soft, *grads, *done_sums,
    )
    d_projected, grad_gain, grad_taps, grad_mix = results[:4]
    return (
        d_projected, grad_gain, grad_taps, grad_mix,
    ), list(results[4 : 4 + count]), specs, results[4 + 2 * count :]


MESH = pl.DeviceIdType.MESH


def ring_index(place, n):
    place = lax.rem(place + 2 * n, n)
    return jnp.where(place < n // 2, 2 * place, 2 * (n - 1 - place) + 1)


def ring_place(index, n):
    half = lax.div(index, 2)
    return jnp.where(lax.rem(index, 2) == 0, half, n - 1 - half)


class Ring:
    def __init__(self, n):
        self.n = n
        rep = lax.axis_index("rep")
        self.x, self.core = lax.div(rep, 2), lax.rem(rep, 2)
        index = lax.axis_index("fsdp")
        self.index = index
        self.place = ring_place(index, n)
        self.right = (rep, ring_index(self.place + 1, n))
        self.left = (rep, ring_index(self.place - 1, n))
        self.sibling = (self.x * 2 + 1 - self.core, index)
        self.across = ((1 - self.x) * 2 + self.core, index)

    def meet(self):
        barrier = pltpu.get_barrier_semaphore()
        for other in (self.right, self.left, self.sibling, self.across):
            pl.semaphore_signal(barrier, inc=1, device_id=other, device_id_type=MESH)
        pl.semaphore_wait(barrier, 4)


def send(src, dst, send_sem, recv_sem, device):
    return pltpu.make_async_remote_copy(
        src_ref=src, dst_ref=dst, send_sem=send_sem, recv_sem=recv_sem,
        device_id=device, device_id_type=MESH,
    )


def cols(start, size):
    return pl.ds(pl.multiple_of(start, LANE), size)


class Gather:
    def __init__(self, ring, weights, fulls, widths, sems):
        self.ring, self.weights, self.fulls = ring, weights, fulls
        self.axes, self.widths = zip(*widths)
        (self.own, self.ring_send, self.ring_recv, self.core_send, self.core_recv, self.x_send, self.x_recv) = sems

    def windows(self, i):
        ring = self.ring
        half = self.weights[i].shape[self.axes[i]] // 2
        w = self.widths[i]
        base = ring.core * half
        part = half - 2 * w
        first = base + jnp.where(ring.x == 0, 0, half - w)
        second = base + jnp.where(ring.x == 0, w, half - 2 * w)
        give = base + jnp.where(ring.x == 0, 0, half - part)
        take = base + jnp.where(ring.x == 0, half - part, 0)
        return w, part, first, second, give, take

    def block(self, i, index, start, width):
        rows = self.weights[i].shape[0]
        if self.axes[i] == 0:
            return self.fulls[i].at[pl.ds(pl.multiple_of(index * rows + start, 16), width), :]
        return self.fulls[i].at[pl.ds(pl.multiple_of(index * rows, 16), rows), cols(start, width)]

    def piece(self, i, start, width):
        if self.axes[i] == 0:
            return self.weights[i].at[pl.ds(pl.multiple_of(start, 16), width), :]
        return self.weights[i].at[:, cols(start, width)]

    def ring_copy(self, i, d, k, source):
        ring = self.ring
        w, _, first, second, _, _ = self.windows(i)
        start = second if d else first
        index = ring_index(ring.place + (k if d else -k), ring.n)
        there = self.block(i, index, start, w)
        src = self.piece(i, start, w) if source else there
        return send(src, there, self.ring_send.at[i, d, k], self.ring_recv.at[i, d, k], ring.left if d else ring.right)

    def core_copy(self, i, d, k):
        ring = self.ring
        w, part, first, second, _, take = self.windows(i)
        start, width = ((first, w), (second, w), (take, part))[d]
        index = ring_index(ring.place + (k + 1 if d == 1 else -k - 1), ring.n)
        there = self.block(i, index, start, width)
        return send(there, there, self.core_send.at[i, d, k], self.core_recv.at[i, d, k], ring.sibling)

    def x_copy(self, i, k):
        ring = self.ring
        _, part, _, _, give, _ = self.windows(i)
        there = self.block(i, ring_index(ring.place - k - 1, ring.n), give, part)
        return send(there, there, self.x_send.at[i, k], self.x_recv.at[i, k], ring.across)

    def own_copy(self, i):
        rows = self.weights[i].shape[0]
        there = self.fulls[i].at[pl.ds(pl.multiple_of(self.ring.index * rows, 16), rows), :]
        return send(self.weights[i], there, self.own.at[0, i], self.own.at[1, i], self.ring.sibling)

    def has_part(self, i):
        return self.weights[i].shape[self.axes[i]] // 2 > 2 * self.widths[i]

    def start(self):
        for i in range(len(self.weights)):
            for d in range(2):
                self.ring_copy(i, d, 0, True).start()
        for i in range(len(self.weights)):
            self.own_copy(i).start()

    def step(self, k):
        last = self.ring.n - 2
        for i in range(len(self.weights)):
            for d in range(2):
                self.ring_copy(i, d, k, False).wait_recv()

                @pl.when(k < last)
                def _():
                    self.ring_copy(i, d, k + 1, False).start()

                if d == 0 and self.has_part(i):
                    self.x_copy(i, k).start()
                self.core_copy(i, d, k).start()

            if self.has_part(i):
                @pl.when(k >= LAG)
                def _():
                    self.pass_on(i, k - LAG)

    def pass_on(self, i, k):
        self.x_copy(i, k).wait_recv()
        self.core_copy(i, 2, k).start()

    def finish(self):
        last = self.ring.n - 2
        for k in range(max(0, last + 1 - LAG), last + 1):
            for i in range(len(self.weights)):
                if self.has_part(i):
                    self.pass_on(i, k)

        def settle(k, carry):
            for i in range(len(self.weights)):
                for d in range(2):
                    self.ring_copy(i, d, k, False).wait_send()
                    self.core_copy(i, d, k).wait()
                if self.has_part(i):
                    self.x_copy(i, k).wait_send()
                    self.core_copy(i, 2, k).wait()
            return carry

        lax.fori_loop(0, self.ring.n - 1, settle, 0)
        for i in range(len(self.weights)):
            self.own_copy(i).wait()

    @staticmethod
    def scratch(count, n):
        dma = pltpu.SemaphoreType.DMA
        return [
            dma((2, count)), dma((count, 2, n - 1)), dma((count, 2, n - 1)),
            dma((count, 3, n - 1)), dma((count, 3, n - 1)), dma((count, n - 1)), dma((count, n - 1)),
        ]


def share(shape):
    rows, columns = shape
    axis, unit = (0, 16) if rows % 64 == 0 else (1, LANE)
    units = (rows, columns)[axis] // 2 // unit
    return axis, -(-units // 3) * unit


THIRD = (1, 3)
LESS = (7, 18)
HALF = (1, 2)
LAST_PORTIONS = (LESS, THIRD)


def carried(columns, portion):
    half = columns // 2
    lanes = -(-(half // LANE) * portion[0] // portion[1]) * LANE
    if 2 * lanes >= half:
        return half // 2, 0
    return lanes, half - 2 * lanes


class Reduce:
    def __init__(self, ring, grads, sums, others, specs, scratch):
        self.ring, self.grads, self.sums, self.others, self.specs = ring, grads, sums, others, specs
        count = len(grads)
        self.slots, self.mine, self.twin, self.x_slots, self.x_out = [], [], [], [], []
        scratch = list(scratch)
        for spec in specs:
            part = carried(spec[1], spec[2])[1]
            take = [scratch.pop(0) for _ in range(10 if part else 6)]
            self.slots.append(take[:2])
            self.mine.append(take[2:4] + take[6:7])
            self.twin.append(take[4:6] + take[7:8])
            self.x_slots.append(take[8] if part else None)
            self.x_out.append(take[9] if part else None)
        (self.load, self.ring_send, self.ring_recv, self.core_send, self.core_recv,
         self.x_send, self.x_recv, self.keep) = scratch

    def owner(self, kind, j):
        ring = self.ring
        return ring_index(ring.place + (j + 1 if kind == 1 else -j - 1), ring.n)

    def span(self, i, kind):
        columns, shared = self.specs[i][1:]
        w, part = carried(columns, shared)
        half = columns // 2
        lower, upper = ((0, half - w), (w, half - 2 * w), (half - part, 0))[kind]
        return jnp.where(self.ring.x == 0, lower, upper), part if kind == 2 else w

    def rows(self, i, index):
        rows = self.specs[i][0]
        return pl.ds(pl.multiple_of(index * rows, 16), rows)

    def kinds(self, i):
        return 3 if self.x_slots[i] is not None else 2

    def core_copy(self, i, kind, j):
        ring = self.ring
        start, width = self.span(i, kind)
        rows = self.rows(i, self.owner(kind, j))
        half = self.specs[i][1] // 2
        return send(
            self.grads[i].at[rows, cols((1 - ring.core) * half + start, width)], self.others[i].at[rows, cols(start, width)],
            self.core_send.at[i, kind, j], self.core_recv.at[i, kind, j], ring.sibling,
        )

    def loads(self, i, kind, j):
        start, width = self.span(i, kind)
        rows = self.rows(i, self.owner(kind, j))
        base = self.ring.core * (self.specs[i][1] // 2)
        return (
            pltpu.make_async_copy(
                self.grads[i].at[rows, cols(base + start, width)], self.mine[i][kind], self.load.at[i, kind, 0]
            ),
            pltpu.make_async_copy(self.others[i].at[rows, cols(start, width)], self.twin[i][kind], self.load.at[i, kind, 1]),
        )

    def fetch(self, i, kind, j):
        own, other = self.loads(i, kind, j)
        own.start()
        self.core_copy(i, kind, j).wait_recv()
        other.start()

    def ring_copy(self, i, d, j):
        ring = self.ring
        return send(
            self.slots[i][d].at[j], self.slots[i][d].at[j + 1],
            self.ring_send.at[i, d, j], self.ring_recv.at[i, d, j + 1], ring.left if d else ring.right,
        )

    def gap(self, i):
        w, part = carried(*self.specs[i][1:])
        x = self.ring.x
        return w - part, jnp.where(x == 0, part, 0), jnp.where(x == 0, w - part, 0), part

    def x_copy(self, i, j):
        _, _, at, part = self.gap(i)
        return send(
            self.x_out[i].at[lax.rem(j, 2)], self.x_slots[i].at[j, :, cols(at, part)],
            self.x_send.at[i, j], self.x_recv.at[i, j], self.ring.across,
        )

    def give(self, i, j):
        j = jnp.int32(j)
        for copy in self.loads(i, 2, j):
            copy.wait()

        @pl.when(j >= 2)
        def _():
            self.x_copy(i, j - 2).wait_send()

        self.x_out[i][lax.rem(j, 2)] = (self.mine[i][2][...].astype(F32) + self.twin[i][2][...].astype(F32)).astype(BF16)
        self.x_copy(i, j).start()
        self.hand_next(i, 2, j)

        @pl.when(j < self.ring.n - 1)
        def _():
            self.fetch(i, 2, j + 1)

    def each(self):
        return [(i, d) for i in range(len(self.grads)) for d in (1, 0)]

    def clear(self):
        for i in range(len(self.grads)):
            if self.kinds(i) == 3:
                width, at, _, _ = self.gap(i)
                if width:
                    rows = self.specs[i][0]
                    self.x_slots[i][:, :, cols(at, width)] = jnp.zeros((self.ring.n, rows, width), BF16)

    def hand_over(self):
        for j in range(min(LEAD, self.ring.n)):
            for i in range(len(self.grads)):
                for kind in reversed(range(self.kinds(i))):
                    self.core_copy(i, kind, j).start()

    def hand_next(self, i, kind, j):
        pl.when(j + LEAD < self.ring.n)(lambda: self.core_copy(i, kind, j + LEAD).start())

    def fetch_first(self):
        for i in range(len(self.grads)):
            for kind in reversed(range(self.kinds(i))):
                self.fetch(i, kind, 0)

    def give_all(self, j):
        for i in range(len(self.grads)):
            if self.kinds(i) == 3:
                self.give(i, j)

    def opening(self):
        return [
            self.hand_over, self.fetch_first,
            functools.partial(self.give_all, 0), functools.partial(self.give_all, 1),
        ]

    def start(self):
        for step in self.opening():
            step()

    def item(self, j, work):
        last = self.ring.n - 1
        for i, d in work:
            if d == 0 and self.kinds(i) == 3:
                pl.when(j < last - 1)(functools.partial(self.give, i, j + 2))
            for copy in self.loads(i, d, j):
                copy.wait()
            slot = self.slots[i][d]
            both = self.mine[i][d][...].astype(F32) + self.twin[i][d][...].astype(F32)
            if d == 0 and self.kinds(i) == 3:
                self.x_copy(i, j).wait_recv()
                both = both + self.x_slots[i][j].astype(F32)

            @pl.when(j == 0)
            def _():
                slot[j] = both.astype(BF16)

            @pl.when(j > 0)
            def _():
                self.ring_copy(i, d, j - 1).wait_recv()
                slot[j] = (slot[j].astype(F32) + both).astype(BF16)

            @pl.when(j < last)
            def _():
                self.ring_copy(i, d, j).start()
                self.fetch(i, d, j + 1)

            self.hand_next(i, d, j)

            @pl.when(j == last)
            def _():
                self.keep_copy(i, d).start()

    def keep_copy(self, i, d):
        w = carried(*self.specs[i][1:])[0]
        at = jnp.where(self.ring.x == 0, d * w, (1 - d) * w)
        return pltpu.make_async_copy(self.slots[i][d].at[self.ring.n - 1], self.sums[i].at[:, cols(at, w)], self.keep.at[i, d])

    def finish(self):
        last = self.ring.n - 1
        for i, d in self.each():
            self.keep_copy(i, d).wait()

        def settle(j, carry):
            for i in range(len(self.grads)):
                for kind in range(self.kinds(i)):
                    self.core_copy(i, kind, j).wait_send()
                for d in range(2):
                    pl.when(j < last)(lambda i=i, d=d: self.ring_copy(i, d, j).wait_send())
                if self.kinds(i) == 3:
                    pl.when(j >= last - 1)(lambda i=i: self.x_copy(i, j).wait_send())
            return carry

        lax.fori_loop(0, self.ring.n, settle, 0)

    @staticmethod
    def specs_of(grads, n, portions):
        return [(g.shape[0] // n, g.shape[1], portion) for g, portion in zip(grads, portions)]

    @staticmethod
    def results(specs, n):
        return [
            jax.ShapeDtypeStruct((rows, 2 * carried(columns, shared)[0]), BF16) for rows, columns, shared in specs
        ] + [jax.ShapeDtypeStruct((n * rows, columns // 2), BF16) for rows, columns, _ in specs]

    @staticmethod
    def scratch(specs, n):
        dma = pltpu.SemaphoreType.DMA
        count = len(specs)
        buffers = []
        for rows, columns, shared in specs:
            w, part = carried(columns, shared)
            buffers += [pltpu.VMEM((n, rows, w), BF16)] * 2 + [pltpu.VMEM((rows, w), BF16)] * 4
            if part:
                buffers += [pltpu.VMEM((rows, part), BF16)] * 2
                buffers += [pltpu.VMEM((n, rows, w), BF16), pltpu.VMEM((2, rows, part), BF16)]
        return buffers + [
            dma((count, 3, 2)), dma((count, 2, n)), dma((count, 2, n)), dma((count, 3, n)), dma((count, 3, n)),
            dma((count, n)), dma((count, n)), dma((count, 2)),
        ]


class FinalSum:
    def __init__(self, ring, sums, totals, specs, scratch):
        self.ring, self.sums, self.totals, self.specs = ring, sums, totals, specs
        scratch = list(scratch)
        self.mine, self.plane, self.own = [], [], []
        for spec in specs:
            self.mine.append(scratch.pop(0))
            self.plane.append(scratch.pop(0))
            self.own.append(scratch.pop(0) if carried(spec[1], spec[2])[1] else None)
        self.local, self.remote_send, self.remote_recv = scratch

    def spans(self, i):
        columns, shared = self.specs[i][1:]
        w, part = carried(columns, shared)
        half, wide = columns // 2, 2 * w - part
        base = self.ring.core * half
        low = self.ring.x == 0
        return (
            (jnp.where(low, part, 0), base + part, wide),
            (jnp.where(low, 0, wide), base + jnp.where(low, 0, half - part), part),
            (0, base + jnp.where(low, half - part, 0), part),
        )

    def remote(self, i, at, src, dst, device):
        return send(src, dst, self.remote_send.at[i, at], self.remote_recv.at[i, at], device)

    def copy(self, i, name):
        ring, sums, totals = self.ring, self.sums[i], self.totals[i]
        (a, a_out, wide), (b, b_out, part), (_, c_out, _) = self.spans(i)
        local = {"load": 0, "save": 1, "load done": 2, "save done": 3}
        remote = {"across": 0, "sibling": 1, "done across": 2, "done sibling": 3, "pass on": 4}
        if name in ("load", "save", "across", "sibling"):
            src, dst, mid = sums.at[:, cols(a, wide)], totals.at[:, cols(a_out, wide)], self.mine[i]
        elif name == "pass on":
            src = dst = mid = totals.at[:, cols(c_out, part)]
        else:
            src, dst, mid = sums.at[:, cols(b, part)], totals.at[:, cols(b_out, part)], self.own[i]
        if name in local:
            ends = (src, mid) if name.startswith("load") else (mid, dst)
            return pltpu.make_async_copy(*ends, self.local.at[i, local[name]])
        ends = {"across": (src, self.plane[i]), "sibling": (mid, dst)}.get(name, (src, dst))
        device = ring.across if "across" in name else ring.sibling
        at = remote[name]
        return send(*ends, self.remote_send.at[i, at], self.remote_recv.at[i, at], device)

    def shares(self, i):
        return carried(*self.specs[i][1:])[1] > 0

    def start(self, i):
        for name in ("across", "load"):
            self.copy(i, name).start()
        if self.shares(i):
            for name in ("done across", "load done", "done sibling"):
                self.copy(i, name).start()

    def add(self, i):
        self.copy(i, "load").wait()
        self.copy(i, "across").wait_recv()
        self.mine[i][...] = (self.mine[i][...].astype(F32) + self.plane[i][...].astype(F32)).astype(BF16)
        self.copy(i, "sibling").start()
        self.copy(i, "save").start()
        if self.shares(i):
            self.copy(i, "load done").wait()
            self.copy(i, "save done").start()
            self.copy(i, "done across").wait_recv()
            self.copy(i, "pass on").start()

    def finish(self):
        for i in range(len(self.specs)):
            self.copy(i, "across").wait_send()
            self.copy(i, "sibling").wait()
            self.copy(i, "save").wait()
            if self.shares(i):
                self.copy(i, "done across").wait_send()
                for name in ("done sibling", "save done", "pass on"):
                    self.copy(i, name).wait()

    @staticmethod
    def scratch(specs):
        dma = pltpu.SemaphoreType.DMA
        count = len(specs)
        buffers = []
        for rows, columns, shared in specs:
            w, part = carried(columns, shared)
            buffers += [pltpu.VMEM((rows, 2 * w - part), BF16)] * 2
            if part:
                buffers += [pltpu.VMEM((rows, part), BF16)]
        return buffers + [dma((count, 4)), dma((count, 5)), dma((count, 5))]


class SmallSum:
    def __init__(self, ring, given, total, scratch):
        self.ring, self.given, self.total = ring, given, total
        self.mine, self.twin, self.plane, self.slots, self.pair, self.ring_send, self.ring_recv = scratch

    def copy(self, src, dst, at, device):
        return send(src, dst, self.pair.at[0, at], self.pair.at[1, at], device)

    def to_core(self):
        return self.copy(self.given, self.twin, 0, self.ring.sibling)

    def to_plane(self):
        return self.copy(self.mine, self.plane, 1, self.ring.across)

    def add_core(self):
        self.to_core().wait()
        self.mine[...] = self.given[...] + self.twin[...]
        self.to_plane().start()

    def add_plane(self):
        self.to_plane().wait()
        self.slots[0] = self.mine[...] + self.plane[...]

    def ring_copy(self, j):
        return send(
            self.slots.at[j], self.slots.at[j + 1], self.ring_send.at[j], self.ring_recv.at[j + 1], self.ring.right
        )

    def item(self, j):
        @pl.when(j > 0)
        def _():
            self.ring_copy(j - 1).wait_recv()

        @pl.when(j < self.ring.n - 1)
        def _():
            self.ring_copy(j).start()

    def finish(self):
        ring = self.ring
        total = jnp.zeros(self.total.shape, F32)
        for place in range(ring.n):
            total = total + self.slots[lax.rem(ring.place - place + ring.n, ring.n)]
        self.total[...] = total

        def settle(j, carry):
            self.ring_copy(j).wait_send()
            return carry

        lax.fori_loop(0, ring.n - 1, settle, 0)

    @staticmethod
    def scratch(rows, n):
        dma = pltpu.SemaphoreType.DMA
        block = pltpu.VMEM((rows, LANE), F32)
        return [block, block, block, pltpu.VMEM((n, rows, LANE), F32), dma((2, 2)), dma((n,)), dma((n,))]


SMALL_SCRATCH = 7


def pack(given, at, row):
    for r in range(row.shape[1] // LANE):
        given[at + r : at + r + 1, :] = row[:, r * LANE : (r + 1) * LANE]
    return at + row.shape[1] // LANE


SPOTS = 8


def pack_taps(given, at, taps_ref, mix_ref):
    rows = taps_ref.shape[1]
    for first in range(0, HEADS, SPOTS):
        together = taps_ref[first]
        for h in range(1, SPOTS):
            together = together + pltpu.roll(taps_ref[first + h], h * (LANE // SPOTS), axis=1)
        given[at : at + rows, :] = together
        at += rows
    together = mix_ref[0]
    for quad in range(1, mix_ref.shape[0]):
        together = together + pltpu.roll(mix_ref[quad], 2 * quad, axis=0)
    given[at : at + rows, :] = together


def unpack_taps(summed):
    rows = 8
    taps = jnp.roll(summed[: HEADS // SPOTS * rows], CK // 2 + 1, axis=1).reshape(-1, rows, SPOTS, LANE // SPOTS)
    taps = taps.transpose(0, 2, 1, 3).reshape(HEADS, rows, LANE // SPOTS)[:, :CQ, :CK]
    mixing = summed[HEADS // SPOTS * rows :][: HEADS // 2, :4]
    return taps[:, :, ::-1] * SCALE, mixing.reshape(HEADS // 2, 2, 2)


def last_kernel(n, specs, early_specs, chunk, small_count, *refs):
    count, early = len(specs), len(early_specs)
    ring = Ring(n)
    refs = list(refs)

    def take(size):
        taken = refs[:size]
        del refs[:size]
        return taken

    small_refs = take(small_count)
    input_ref, gain_ref, d_middle_ref, d_projected, weight = take(5)
    grads, early_sums = take(count), take(early)
    grad_input_ref, total_ref = take(2)
    totals, early_totals, sums, others = take(count), take(early), take(count), take(count)
    given, d_normed, in_left, in_right, in_sem = take(5)
    small = SmallSum(ring, given, total_ref, take(SMALL_SCRATCH))
    last_sum = FinalSum(ring, sums, totals, specs, take(len(FinalSum.scratch(specs))))
    early_sum = FinalSum(ring, early_sums, early_totals, early_specs, take(len(FinalSum.scratch(early_specs))))
    reduce = Reduce(ring, grads, sums, others, specs, refs)
    chunks = d_projected.shape[1] // chunk

    def arrive(t, slot):
        at = cols(t * chunk, chunk)
        return (
            pltpu.make_async_copy(d_projected.at[:, at], in_left.at[slot], in_sem.at[slot, 0]),
            pltpu.make_async_copy(weight.at[:, at], in_right.at[slot], in_sem.at[slot, 1]),
        )

    for copy in arrive(0, 0):
        copy.start()
    reduce.clear()
    ring.meet()

    def turn(t, carry):
        slot = lax.rem(t, 2)
        for copy in arrive(t, slot):
            copy.wait()

        @pl.when(t < chunks - 1)
        def _():
            for copy in arrive(t + 1, 1 - slot):
                copy.start()

        d_normed[...] += nt(in_left[slot], in_right[slot])
        return carry

    reduce.hand_over()
    d_normed[...] = jnp.zeros_like(d_normed)
    given[...] = jnp.zeros_like(given)
    lax.fori_loop(0, chunks // 3, turn, 0)
    for step in reduce.opening()[1:]:
        step()
    reduce.item(jnp.int32(0), reduce.each())
    lax.fori_loop(chunks // 3, chunks, turn, 0)
    values = input_ref[...].astype(F32)
    scale = lax.rsqrt(jnp.mean(values * values, axis=1, keepdims=True) + EPSILON)
    upstream = d_normed[...]
    grad_gain = jnp.sum(upstream * (values * scale), axis=0, keepdims=True)
    at = 0
    for row in [grad_gain] + [ref[...] for ref in small_refs[:2]]:
        at = pack(given, at, row)
    pack_taps(given, at, small_refs[2], small_refs[3])
    small.to_core().start()
    scaled = upstream * gain_ref[...]
    inner = jnp.mean(scaled * values, axis=1, keepdims=True)
    grad_input_ref[...] = d_middle_ref[...] + scale * scaled - values * (scale * scale * scale * inner)
    reduce.item(jnp.int32(1), reduce.each())
    small.add_core()
    reduce.item(jnp.int32(2), reduce.each())
    small.add_plane()
    hops = -(-n // (n - 4))

    def rest(j, carry):
        for hop in range(hops):
            at = (j - 3) * hops + hop
            pl.when(at < n)(functools.partial(small.item, at))
        for i in range(early):
            pl.when(j == 3 + i)(functools.partial(early_sum.start, i))
        reduce.item(j, reduce.each())
        for i in range(early):
            pl.when(j == n - early + i)(functools.partial(early_sum.add, i))
        return carry

    lax.fori_loop(3, n, rest, 0)
    reduce.finish()
    for i in range(count):
        last_sum.start(i)
    small.finish()
    for i in range(count):
        last_sum.add(i)
    early_sum.finish()
    last_sum.finish()


def last_step(
    d_projected, qkv_weight, layer_input, first_gain, d_middle, grads, smalls, early_sums, early_specs, n, collective
):
    count, early = len(grads), len(early_specs)
    seq, width = layer_input.shape
    chunk = 512
    specs = Reduce.specs_of(grads, n, LAST_PORTIONS)
    sizes = [width // LANE] * 3 + [(HEADS // SPOTS + 1) * 8]
    rows = -(-sum(sizes) // 8) * 8
    anywhere = pl.BlockSpec(memory_space=pl.ANY)
    whole = pl.BlockSpec(memory_space=pltpu.VMEM)
    results = pl.pallas_call(
        functools.partial(last_kernel, n, specs, early_specs, chunk, len(smalls)),
        out_shape=[jax.ShapeDtypeStruct((seq, width), F32), jax.ShapeDtypeStruct((rows, LANE), F32)]
        + [jax.ShapeDtypeStruct(spec[:2], BF16) for spec in specs + early_specs]
        + Reduce.results(specs, n),
        in_specs=[whole] * (len(smalls) + 3) + [anywhere] * (2 + count + early),
        out_specs=[whole] * 2 + [anywhere] * (3 * count + early),
        scratch_shapes=[
            pltpu.VMEM((rows, LANE), F32),
            pltpu.VMEM((seq, width), F32),
            pltpu.VMEM((2, seq, chunk), BF16),
            pltpu.VMEM((2, width, chunk), BF16),
            pltpu.SemaphoreType.DMA((2, 2)),
        ]
        + SmallSum.scratch(rows, n)
        + FinalSum.scratch(specs)
        + FinalSum.scratch(early_specs)
        + Reduce.scratch(specs, n),
        compiler_params=pltpu.CompilerParams(
            collective_id=collective, has_side_effects=True, vmem_limit_bytes=60 * 1024 * 1024
        ),
    )(*smalls, layer_input, first_gain.reshape(1, width), d_middle, d_projected, qkv_weight, *grads, *early_sums)
    out, at = [], 0
    for size in sizes:
        out.append(results[1][at : at + size])
        at += size
    return results[0], results[2 : 2 + count + early], out


TILES = 8
EARLY_TILES = 3
POINTS = 4
LATE_TILES = 3


def mlp_kernel(n, specs, tile, *refs):
    refs = list(refs)

    def take(size):
        taken = refs[:size]
        del refs[:size]
        return taken

    second_ref, upstream_ref, gain_ref, middle, out_weight, inner, down, coming = take(8)
    out_ref, d_middle_ref, d_grouped_ref, grad_gain_ref = take(4)
    (early, late, grad_down), sums, others, (came,) = take(3), take(1), take(1), take(1)
    turned, out_sum, d_second_ref, in_gate, in_up, in_down, to_gate, to_up, to_down = take(9)
    middle_sem, in_sem, to_sem, out_sem = take(4)
    ring = Ring(n)
    gather = Gather(ring, [coming], [came], [share(coming.shape)], take(len(Gather.scratch(1, n))))
    reduce = Reduce(ring, [early], sums, others, specs, refs)
    hidden_size = down.shape[0]
    tiles = hidden_size // tile
    begun = EARLY_TILES
    each = -(-n // (tiles - begun - 1))
    due = -(-each // 2)

    split = tiles - LATE_TILES

    def arrive(t, slot, weight, first, count):
        at = pl.multiple_of((t - first) * tile, tile)
        return (
            pltpu.make_async_copy(weight.at[:, pl.ds(at, tile)], in_gate.at[slot], in_sem.at[slot, 0]),
            pltpu.make_async_copy(
                weight.at[:, pl.ds(pl.multiple_of(count * tile + at, tile), tile)], in_up.at[slot], in_sem.at[slot, 1]
            ),
            pltpu.make_async_copy(
                down.at[pl.ds(pl.multiple_of(t * tile, tile), tile), :], in_down.at[slot], in_sem.at[slot, 2]
            ),
        )

    def arrivals(t, act):
        slot = lax.rem(t, 2)

        @pl.when(t < split)
        def _():
            for copy in arrive(t, slot, inner, 0, split):
                act(copy)

        @pl.when((t >= split) & (t < tiles))
        def _():
            for copy in arrive(t, slot, came, split, LATE_TILES):
                act(copy)

    def leave(grad, t, slot, first, count):
        at = pl.multiple_of((t - first) * tile, tile)
        return (
            pltpu.make_async_copy(to_gate.at[slot], grad.at[:, pl.ds(at, tile)], to_sem.at[slot, 0]),
            pltpu.make_async_copy(
                to_up.at[slot], grad.at[:, pl.ds(pl.multiple_of(count * tile + at, tile), tile)], to_sem.at[slot, 1]
            ),
            pltpu.make_async_copy(
                to_down.at[slot], grad_down.at[pl.ds(pl.multiple_of(t * tile, tile), tile), :], to_sem.at[slot, 2]
            ),
        )

    def leave_early(t):
        return leave(early, t, lax.rem(t, 2), 0, begun)

    def leave_late(t):
        return leave(late, t, lax.rem(t, 2), begun, tiles - begun)

    first = pltpu.make_async_copy(middle, out_sum, middle_sem)
    first.start()
    arrivals(jnp.int32(0), lambda copy: copy.start())
    reduce.clear()
    ring.meet()
    gather.start()
    turned[...] = second_ref[...].T
    d_second_ref[...] = jnp.zeros_like(d_second_ref)
    first.wait()

    def serve(t, point):
        ends = (split - 1) * POINTS + 1
        turns = 7
        for turn in range(turns):
            at = 2 + turn * (ends - 3) // (turns - 1)
            if at % POINTS == point:
                for k in in_turn(turn, turns, n - 1):
                    if k < n - 1:
                        pl.when(t == at // POINTS)(functools.partial(gather.step, jnp.int32(k)))
        if ends % POINTS == point:
            pl.when(t == ends // POINTS)(gather.finish)

        @pl.when(t == begun)
        def _():
            if point == 0:
                for back in (2, 1):
                    for copy in leave_early(t - back):
                        copy.wait()
            reduce.opening()[point]()

        for step in range(due):
            if point // 2 * due + step < each:
                j = (t - begun - 1) * each + point // 2 * due + step
                pl.when((t > begun) & (j < n))(functools.partial(reduce.item, j, [(0, 1 - point % 2)]))

    def one(t, carry):
        slot = lax.rem(t, 2)
        arrivals(t, lambda copy: copy.wait())
        second, upstream = second_ref[...], upstream_ref[...]
        gate = nn(second, in_gate[slot])
        up = nn(second, in_up[slot])
        sigmoid = jax.nn.sigmoid(gate)
        silu = gate * sigmoid
        hidden = (silu * up).astype(BF16)
        serve(t, 0)
        d_hidden = nt(upstream, in_down[slot])
        out_sum[...] += nn(hidden, in_down[slot])

        @pl.when((t >= 2) & (t < begun))
        def _():
            for copy in leave_early(t - 2):
                copy.wait()

        @pl.when(t >= begun + 2)
        def _():
            for copy in leave_late(t - 2):
                copy.wait()

        to_down[slot] = nn(hidden.T, upstream).astype(BF16)
        d_gate = (d_hidden * up * sigmoid * (1.0 + gate * (1.0 - sigmoid))).astype(BF16)
        d_up = (d_hidden * silu).astype(BF16)
        serve(t, 1)
        d_second_ref[...] += nt(d_gate, in_gate[slot])
        to_gate[slot] = nn(turned[...], d_gate).astype(BF16)
        serve(t, 2)
        arrivals(t + 1, lambda copy: copy.start())
        d_second_ref[...] += nt(d_up, in_up[slot])
        to_up[slot] = nn(turned[...], d_up).astype(BF16)
        serve(t, 3)

        @pl.when(t < begun)
        def _():
            for copy in leave_early(t):
                copy.start()

        @pl.when(t >= begun)
        def _():
            for copy in leave_late(t):
                copy.start()

        return carry

    def out_piece(c):
        into = (in_gate.at[0], in_up.at[0], in_gate.at[1])[c]
        return pltpu.make_async_copy(out_weight.at[:, c * tile : (c + 1) * tile], into, out_sem.at[c])

    lax.fori_loop(0, tiles, one, 0)
    pieces = out_weight.shape[1] // tile
    for c in range(pieces):
        out_piece(c).start()
    out_ref[...] = out_sum[...].astype(BF16)
    first.start()
    first.wait()
    values = out_sum[...]
    scale = lax.rsqrt(jnp.mean(values * values, axis=1, keepdims=True) + EPSILON)
    d_second = d_second_ref[...]
    grad_gain_ref[...] = jnp.sum(d_second * (values * scale), axis=0, keepdims=True)
    scaled = d_second * gain_ref[...]
    mean = jnp.mean(scaled * values, axis=1, keepdims=True)
    d_middle_ref[...] = (
        upstream_ref[...].astype(F32) + scale * scaled - values * (scale * scale * scale * mean)
    )
    for c in range(pieces):
        out_piece(c).wait()
        part = nt(
            d_middle_ref[:, c * tile : (c + 1) * tile].astype(BF16), (in_gate.at[0], in_up.at[0], in_gate.at[1])[c][...]
        )
        if c == 0:
            d_grouped_ref[...] = part
        else:
            d_grouped_ref[...] += part
    for t in (tiles - 2, tiles - 1):
        for copy in leave_late(t):
            copy.wait()
    reduce.finish()


def feed_forward(second, upstream, gain, middle, out_weight, inner, down, coming, n, collective):
    seq, width = second.shape
    hidden_size = down.shape[0]
    tile = hidden_size // TILES
    early = EARLY_TILES * tile
    specs = [(width // n, 2 * early, THIRD)]
    whole = pl.BlockSpec(memory_space=pltpu.VMEM)
    anywhere = pl.BlockSpec(memory_space=pl.ANY)
    dma = pltpu.SemaphoreType.DMA
    results = pl.pallas_call(
        functools.partial(mlp_kernel, n, specs, tile),
        out_shape=[
            jax.ShapeDtypeStruct((seq, width), BF16),
            jax.ShapeDtypeStruct((seq, width), F32),
            jax.ShapeDtypeStruct((seq, width), F32),
            jax.ShapeDtypeStruct((1, width), F32),
        ]
        + [
            jax.ShapeDtypeStruct((width, 2 * early), BF16),
            jax.ShapeDtypeStruct((width, 2 * (hidden_size - early)), BF16),
            jax.ShapeDtypeStruct((hidden_size, width), BF16),
        ]
        + Reduce.results(specs, n)
        + [jax.ShapeDtypeStruct((n * coming.shape[0], coming.shape[1]), BF16)],
        in_specs=[whole] * 3 + [anywhere] * 5,
        out_specs=[whole] * 4 + [anywhere] * 6,
        scratch_shapes=[
            pltpu.VMEM((width, seq), BF16),
            pltpu.VMEM((seq, width), F32),
            pltpu.VMEM((seq, width), F32),
            pltpu.VMEM((2, width, tile), BF16),
            pltpu.VMEM((2, width, tile), BF16),
            pltpu.VMEM((2, tile, width), BF16),
            pltpu.VMEM((2, width, tile), BF16),
            pltpu.VMEM((2, width, tile), BF16),
            pltpu.VMEM((2, tile, width), BF16),
            dma, dma((2, 3)), dma((2, 3)), dma((3,)),
        ]
        + Gather.scratch(1, n)
        + Reduce.scratch(specs, n),
        compiler_params=pltpu.CompilerParams(
            collective_id=collective, has_side_effects=True, vmem_limit_bytes=62 * 1024 * 1024
        ),
    )(second, upstream, gain.reshape(1, width), middle, out_weight, inner, down, coming)
    out, d_middle, d_grouped, grad_gain, _, late, grad_down, sums, _, _ = results
    return out, d_middle, d_grouped, grad_gain, late, grad_down, [sums], specs


def weight_grad(operand, upstream):
    return lax.dot_general(
        operand, upstream, (((0,), (0,)), ((), ())), preferred_element_type=F32
    ).astype(BF16)


def body(
    layer_input,
    first_gain,
    qkv_weight,
    conv_kernel,
    head_mixing,
    group_gain,
    out_weight,
    second_gain,
    inner_weight,
    down_weight,
    doc_lengths,
    cotangent,
):
    n = lax.axis_size("fsdp")
    hidden_size = inner_weight.shape[1] // 2
    cut = hidden_size // TILES * (TILES - LATE_TILES)
    gates, ups = inner_weight[:, :hidden_size], inner_weight[:, hidden_size:]
    inner_first = jnp.concatenate([gates[:, :cut], ups[:, :cut]], axis=1)
    inner_last = jnp.concatenate([gates[:, cut:], ups[:, cut:]], axis=1)
    kept, (qkv_weight, out_weight), (inner_first, down_weight) = attend_forward(
        layer_input, conv_kernel, head_mixing, doc_lengths, (first_gain, group_gain, second_gain),
        [qkv_weight, out_weight], [inner_first, down_weight], n, 0,
    )
    grouped, attended, soft, normed, middle, second, projected = kept
    layer_output, d_middle, d_grouped, grad_second, late_inner, grad_down, early_sums, early_specs = feed_forward(
        second, cotangent, second_gain, middle, out_weight, inner_first, down_weight, inner_last, n, 2
    )
    (d_projected, grad_group, grad_kernel, grad_mixing), sums, specs, (early_inner,) = attend_backward(
        projected, conv_kernel, head_mixing, doc_lengths, group_gain, attended, d_grouped, soft,
        [late_inner, grad_down], early_sums, early_specs, n, 3,
    )
    grad_qkv = weight_grad(normed, d_projected)
    grad_proj = weight_grad(grouped, d_middle.astype(BF16))
    grad_input, shards, small = last_step(
        d_projected, qkv_weight, layer_input, first_gain, d_middle, [grad_qkv, grad_proj],
        [grad_group, grad_second, grad_kernel, grad_mixing], sums, specs, n, 4,
    )
    grad_first, grad_group, grad_second = [g.reshape(-1) for g in small[:3]]
    grad_kernel, grad_mixing = unpack_taps(small[3])
    grad_qkv, grad_proj, late_inner, grad_down = shards
    cut, late_cut = early_inner.shape[1] // 2, late_inner.shape[1] // 2
    grad_inner = jnp.concatenate(
        [early_inner[:, :cut], late_inner[:, :late_cut], early_inner[:, cut:], late_inner[:, late_cut:]], axis=1
    )
    shards = [g.astype(F32) for g in (grad_qkv, grad_proj, grad_inner, grad_down)]
    return (
        layer_output, grad_input, grad_first, shards[0], grad_kernel, grad_mixing, grad_group, shards[1], grad_second,
        shards[2], shards[3],
    )


def solution(mesh):
    placed = (
        P(("rep", "fsdp"), None),
        P(),
        P("fsdp", None),
        P(),
        P(),
        P(),
        P("fsdp", None),
        P(),
        P("fsdp", None),
        P("fsdp", None),
        P(("rep", "fsdp"), None),
        P(("rep", "fsdp"), None),
    )
    return jax.shard_map(
        body,
        mesh=mesh,
        in_specs=placed,
        out_specs=(
            P(("rep", "fsdp"), None),
            P(("rep", "fsdp"), None),
            P(),
            P("fsdp", None),
            P(),
            P(),
            P(),
            P("fsdp", None),
            P(),
            P("fsdp", None),
            P("fsdp", None),
        ),
        check_vma=False,
    )
```

```python
import functools, math
import jax, jax.numpy as jnp
from jax import lax
from jax.experimental import pallas as pl
from jax.experimental.pallas import tpu as pltpu
from jax.sharding import PartitionSpec as P

HEADS = 16
HEAD_DIM = 96
CQ = 6
CK = 11
EPSILON = 1e-05
LANE = 128
QUAD = 4
LAG = 1
LEAD = 3
REST_AHEAD = 2
SCALE = 1.0 / math.sqrt(HEAD_DIM)
F32 = jnp.float32
BF16 = jnp.bfloat16


def row_sets(seq):
    return [
        (r, min(r + LANE, 3 * LANE), max(0, r - 2 * LANE)) for r in range(0, seq, LANE)
    ]


def nt(a, b):
    return lax.dot_general(a, b, (((1,), (1,)), ((), ())), preferred_element_type=F32)


def nn(a, b):
    return jnp.dot(a, b, preferred_element_type=F32)


def fill_masks(docs_ref, masks, seq):
    ends = []
    total = jnp.int32(0)
    for d in range(docs_ref.shape[1] - 1):
        total = total + docs_ref[0, d]
        ends.append(total)
    for r0, width, c0 in row_sets(seq):
        rows = r0 + lax.broadcasted_iota(jnp.int32, (LANE, 1), 0)
        cols = c0 + lax.broadcasted_iota(jnp.int32, (1, width), 1)
        row_doc = sum((rows >= e).astype(jnp.int32) for e in ends)
        col_doc = sum((cols >= e).astype(jnp.int32) for e in ends)
        same = row_doc == col_doc
        for a in range(CQ):
            masks[a, r0 : r0 + LANE, :width] = jnp.where(
                same & (rows - cols >= a), 1.0, 0.0
            ).astype(BF16)


def circulant_masks():
    gap = lax.broadcasted_iota(jnp.int32, (LANE, LANE), 1) - lax.broadcasted_iota(
        jnp.int32, (LANE, LANE), 0
    )
    half = CK // 2
    return (jnp.abs(gap) <= half, gap <= half - LANE, gap >= LANE - half)


def circulant(taps):
    wide = jnp.broadcast_to(taps, (LANE, LANE))
    return pltpu.roll(wide, 0, axis=1, stride=1, stride_axis=0)


def fill_toeplitz(taps_ref, head, band, blocks):
    near, after, before = circulant_masks()
    for a in range(CQ):
        whole = circulant(taps_ref[head, a : a + 1, :])
        parts = {
            0: jnp.where(near, whole, 0.0).astype(BF16),
            1: jnp.where(after, whole, 0.0).astype(BF16),
            -1: jnp.where(before, whole, 0.0).astype(BF16),
        }
        for r in range(blocks):
            for c in range(blocks):
                part = parts.get(c - r)
                if part is not None:
                    yield a, r, c, part


def fill_forward_band(taps_ref, head, band):
    for a, r, c, part in fill_toeplitz(taps_ref, head, band, 3):
        at = (r * CQ + a) * LANE
        band[at : at + LANE, c * LANE : (c + 1) * LANE] = part


def fill_backward_band(taps_ref, head, band):
    near, after, before = circulant_masks()
    for a in range(CQ):
        whole = circulant(taps_ref[head, a : a + 1, :])
        for at, keep in enumerate((after, near, before)):
            band[at * LANE : (at + 1) * LANE, a * LANE : (a + 1) * LANE] = jnp.where(keep, whole, 0.0).astype(BF16)


def shifted_rows(query):
    wide = query.astype(F32)
    return [query] + [pltpu.roll(wide, a, axis=0).astype(BF16) for a in range(1, CQ)]


def masked_scores(shifted, keys, masks, r0, width, c0):
    left = jnp.concatenate([shifted[a, r0 : r0 + LANE] for a in range(CQ)], axis=0)
    scores = nt(left, keys[c0 : c0 + width]).astype(BF16)
    return left, [
        scores[a * LANE : (a + 1) * LANE] * masks[a, r0 : r0 + LANE, :width]
        for a in range(CQ)
    ]


def by_window(parts, width):
    return jnp.concatenate(
        [
            parts[a][:, b * LANE : (b + 1) * LANE]
            for b in range(width // LANE)
            for a in range(CQ)
        ],
        axis=1,
    )


def forward_kernel(
    n, first_widths, cut, docs_ref, mix_ref, taps_ref, gain_ref, input_ref, gains_ref, *refs
):
    refs = list(refs)

    def take(size):
        taken = refs[:size]
        del refs[:size]
        return taken

    first_count = len(first_widths)
    first_weights, (inner, down) = take(first_count), take(2)
    grouped_ref, attended_ref, soft_ref, normed_ref, middle_ref, second_ref, projected = take(7)
    first_fulls, (inner_full, down_full) = take(first_count), take(2)
    masks, band, qs, ks, vs, shifted, outs = take(7)
    blocks, block_weight, every, out_weight, block_in, block_out, out_in = take(7)
    ring = Ring(n)
    sems = len(Gather.scratch(first_count, n))
    hidden_size = inner.shape[1] // 2
    rest_weights = [inner.at[:, :cut], inner.at[:, hidden_size : hidden_size + cut], down]
    rest_fulls = [inner_full.at[:, :cut], inner_full.at[:, cut:], down_full]
    rest_widths = [share((inner.shape[0], cut))] * 2 + [share(down.shape)]
    first = Gather(ring, first_weights, first_fulls, first_widths, take(sems))
    rest = Gather(ring, rest_weights, rest_fulls, rest_widths, take(sems))
    seq = input_ref.shape[0]
    quad = pl.program_id(0)
    quads = HEADS // QUAD
    size = QUAD * HEAD_DIM
    count = 3 * quads

    def block_copy(t):
        slot = lax.rem(t, 2)
        return pltpu.make_async_copy(first_fulls[0].at[:, cols(t * size, size)], block_weight.at[slot], block_in.at[slot])

    def block_save(t):
        return pltpu.make_async_copy(blocks.at[t], projected.at[:, cols(t * size, size)], block_out.at[t])

    out_copy = pltpu.make_async_copy(first_fulls[1], out_weight, out_in)

    def serve(turn):
        for k in in_turn(turn, 2 + HEADS // 2, n - 1):
            pl.when(k < n - 1)(functools.partial(rest.step, k))

    @pl.when(quad == 0)
    def _():
        ring.meet()
        first.start()
        fill_masks(docs_ref, masks, seq)
        band[...] = jnp.zeros_like(band)
        values = input_ref[...].astype(F32)
        scale = lax.rsqrt(jnp.mean(values * values, axis=1, keepdims=True) + EPSILON)
        normed_ref[...] = (values * scale * gains_ref[0:1, :]).astype(BF16)

        def one(k, carry):
            first.step(k)
            pl.when(k == n - REST_AHEAD)(rest.start)
            return carry

        lax.fori_loop(0, n - 1, one, 0)
        first.finish()
        serve(jnp.int32(0))
        block_copy(0).start()
        out_copy.start()

        def project_block(t, carry):
            pl.when(t < count - 1)(lambda: block_copy(t + 1).start())
            block_copy(t).wait()
            blocks[t] = nn(normed_ref[...], block_weight[lax.rem(t, 2)]).astype(BF16)
            block_save(t).start()
            return carry

        lax.fori_loop(0, count, project_block, 0)
        serve(jnp.int32(1))

    for h in range(QUAD):
        at = slice(h * HEAD_DIM, (h + 1) * HEAD_DIM)
        qs[h] = blocks[quad, :, at]
        ks[h] = blocks[quads + quad, :, at]
        vs[h] = blocks[2 * quads + quad, :, at]

    sets = row_sets(seq)

    def pair(p, carry):
        group = quad * 2 + p
        for r in range(2):
            h = 2 * p + r
            fill_forward_band(taps_ref, quad * QUAD + h, band)
            for a, rows in enumerate(shifted_rows(qs[h])):
                shifted[a] = rows
            keys = ks[h]
            lefts = []
            for r0, width, c0 in sets:
                _, parts = masked_scores(shifted, keys, masks, r0, width, c0)
                lefts.append((width, by_window(parts, width)))
            convs = []
            i = 0
            while i < len(sets):
                width = sets[i][1]
                run = 1
                while i + run < len(sets) and sets[i + run][1] == width:
                    run += 1
                left = jnp.concatenate([lefts[i + m][1] for m in range(run)], axis=0)
                conv = nn(left, band[: width * CQ, :width])
                convs += [conv[m * LANE : (m + 1) * LANE] for m in range(run)]
                i += run
            for (r0, width, c0), conv in zip(sets, convs):
                logits = jnp.where(
                    masks[0, r0 : r0 + LANE, :width].astype(F32) > 0, conv, -1e30
                )
                weights = jnp.exp(logits - jnp.max(logits, axis=1, keepdims=True))
                soft = weights * (1.0 / jnp.sum(weights, axis=1, keepdims=True))
                soft_ref[h, r0 : r0 + LANE, :width] = soft.astype(BF16)
        for r in range(2):
            h = 2 * p + r
            values = vs[h]
            for r0, width, c0 in sets:
                mixed = (
                    mix_ref[group, r, 0] * soft_ref[2 * p, r0 : r0 + LANE, :width].astype(F32)
                    + mix_ref[group, r, 1] * soft_ref[2 * p + 1, r0 : r0 + LANE, :width].astype(F32)
                ).astype(BF16)
                outs[h, r0 : r0 + LANE] = nn(mixed, values[c0 : c0 + width])
        serve(2 + group)
        return carry

    lax.fori_loop(0, 2, pair, 0)
    wholes, grouped = [], []
    for h in range(QUAD):
        attended = outs[h]
        centred = attended - jnp.mean(attended, axis=1, keepdims=True)
        var = jnp.mean(centred * centred, axis=1, keepdims=True)
        wholes.append(attended)
        grouped.append(centred * lax.rsqrt(var + EPSILON))
    attended_ref[...] = jnp.concatenate(wholes, axis=1)
    every[quad] = (jnp.concatenate(grouped, axis=1) * gain_ref[1:2, :]).astype(BF16)
    grouped_ref[...] = every[quad]

    @pl.when(quad == quads - 1)
    def _():
        out_copy.wait()
        branch = nn(jnp.concatenate([every[i] for i in range(quads)], axis=1), out_weight[...])
        middle = input_ref[...].astype(F32) + branch
        scale = lax.rsqrt(jnp.mean(middle * middle, axis=1, keepdims=True) + EPSILON)
        middle_ref[...] = middle
        second_ref[...] = (middle * scale * gains_ref[2:3, :]).astype(BF16)

        def saved(t, carry):
            block_save(t).wait()
            return carry

        lax.fori_loop(0, count, saved, 0)
        rest.finish()


def pad_taps(kernel):
    padded = jnp.pad(kernel * SCALE, ((0, 0), (0, 2), (0, LANE - CK)))
    return jnp.roll(padded, -(CK // 2), axis=2)


def in_turn(turn, turns, steps):
    each = -(-steps // turns)
    return [turn * each + t for t in range(each)]


def attend_forward(layer_input, conv_kernel, head_mixing, docs, gains, first, inner, down, n, collective):
    seq, width = layer_input.shape
    block = QUAD * HEAD_DIM
    quads = HEADS // QUAD
    first_widths = [share(w.shape) for w in first]
    cut = inner.shape[1] // 2 // TILES * (TILES - LATE_TILES)
    whole = pl.BlockSpec(memory_space=pltpu.VMEM)
    smem = pl.BlockSpec(memory_space=pltpu.SMEM)
    anywhere = pl.BlockSpec(memory_space=pl.ANY)
    columns = pl.BlockSpec((seq, block), lambda i: (0, i))
    dma = pltpu.SemaphoreType.DMA
    results = pl.pallas_call(
        functools.partial(forward_kernel, n, first_widths, cut),
        grid=(quads,),
        out_shape=[
            jax.ShapeDtypeStruct((seq, width), BF16),
            jax.ShapeDtypeStruct((seq, width), F32),
            jax.ShapeDtypeStruct((HEADS, seq, 3 * LANE), BF16),
            jax.ShapeDtypeStruct((seq, width), BF16),
            jax.ShapeDtypeStruct((seq, width), F32),
            jax.ShapeDtypeStruct((seq, width), BF16),
            jax.ShapeDtypeStruct((seq, 3 * width), BF16),
        ]
        + [jax.ShapeDtypeStruct((n * w.shape[0], w.shape[1]), w.dtype) for w in first]
        + [jax.ShapeDtypeStruct((width, 2 * cut), BF16), jax.ShapeDtypeStruct((n * down.shape[0], width), BF16)],
        in_specs=[smem, smem, whole, pl.BlockSpec((3, block), lambda i: (0, i)), whole, whole]
        + [anywhere] * (2 + len(first)),
        out_specs=[
            columns, columns,
            pl.BlockSpec((QUAD, seq, 3 * LANE), lambda i: (i, 0, 0)),
            whole, whole, whole,
        ]
        + [anywhere] * (3 + len(first)),
        scratch_shapes=[
            pltpu.VMEM((CQ, seq, 3 * LANE), BF16),
            pltpu.VMEM((3 * LANE * CQ, 3 * LANE), BF16),
            pltpu.VMEM((QUAD, seq, HEAD_DIM), BF16),
            pltpu.VMEM((QUAD, seq, HEAD_DIM), BF16),
            pltpu.VMEM((QUAD, seq, HEAD_DIM), BF16),
            pltpu.VMEM((CQ, seq, HEAD_DIM), BF16),
            pltpu.VMEM((QUAD, seq, HEAD_DIM), F32),
            pltpu.VMEM((3 * quads, seq, block), BF16),
            pltpu.VMEM((2, width, block), BF16),
            pltpu.VMEM((quads, seq, block), BF16),
            pltpu.VMEM((width, width), BF16),
            dma((2,)), dma((3 * quads,)), dma,
        ]
        + Gather.scratch(len(first), n)
        + Gather.scratch(3, n),
        compiler_params=pltpu.CompilerParams(
            collective_id=collective, has_side_effects=True, vmem_limit_bytes=60 * 1024 * 1024
        ),
    )(
        docs, head_mixing, pad_taps(conv_kernel), gains, layer_input, gains,
        *first, inner, down,
    )
    return results[:7], results[7 : 7 + len(first)], results[7 + len(first) :]


def backward_kernel(
    n, specs, done_specs, docs_ref, mix_ref, taps_ref, gain_ref, q_ref, k_ref, v_ref, attended_ref, d_grouped_ref, soft_ref, *refs
):
    count, done = len(specs), len(done_specs)
    grads, done_sums, refs = refs[:count], refs[count : count + done], refs[count + done :]
    d_projected, grad_gain_ref, grad_taps_ref, grad_mix_ref = refs[:4]
    sums, others, refs = refs[4 : 4 + count], refs[4 + count : 4 + 2 * count], refs[4 + 2 * count :]
    done_totals, refs = refs[:done], refs[done:]
    final_size = len(FinalSum.scratch(done_specs))
    masks, band, qs, ks, vs, ds, shifted, d_heads, d_rows, d_cols, near_keys, leaving, leave_sem = refs[:13]
    reduce = Reduce(Ring(n), grads, sums, others, specs, refs[13 + final_size :])
    final = FinalSum(reduce.ring, done_sums, done_totals, done_specs, refs[13 : 13 + final_size])
    seq = q_ref.shape[0]
    quad = pl.program_id(0)

    @pl.when(quad == 0)
    def _():
        reduce.clear()
        reduce.ring.meet()
        reduce.hand_over()

    @pl.when(quad == 0)
    def _():
        fill_masks(docs_ref, masks, seq)

    gains = []
    for h in range(QUAD):
        at = slice(h * HEAD_DIM, (h + 1) * HEAD_DIM)
        qs[h] = q_ref[:, at]
        ks[h] = k_ref[:, at]
        vs[h] = v_ref[:, at]
        attended = attended_ref[:, at]
        d_grouped = d_grouped_ref[:, at]
        centred = attended - jnp.mean(attended, axis=1, keepdims=True)
        var = jnp.mean(centred * centred, axis=1, keepdims=True)
        scale = lax.rsqrt(var + EPSILON)
        unit = centred * scale
        gains.append(jnp.sum(d_grouped * unit, axis=0, keepdims=True))
        w = d_grouped * gain_ref[1:2, at]
        d_attended = scale * (
            w
            - jnp.mean(w, axis=1, keepdims=True)
            - unit * jnp.mean(w * unit, axis=1, keepdims=True)
        )
        ds[h] = d_attended.astype(BF16)
    grad_gain_ref[...] = jnp.concatenate(gains, axis=1)
    grad_taps_ref[...] = jnp.zeros_like(grad_taps_ref)
    grad_mix_ref[...] = jnp.zeros_like(grad_mix_ref)

    @pl.when(quad == 0)
    def _():
        for step in reduce.opening()[1:]:
            step()

    @pl.when(quad == 1)
    def _():
        for i in range(done):
            final.start(i)

    sets = row_sets(seq)
    up = lax.broadcasted_iota(jnp.int32, (LANE, LANE), 0)
    across = lax.broadcasted_iota(jnp.int32, (LANE, LANE), 1)
    flip = jnp.where(up + across == LANE - 1, 1.0, 0.0).astype(BF16)
    gap = up + across - (LANE - 1)
    keeps = {0: jnp.abs(gap) <= CK // 2, 1: gap <= CK // 2 - LANE, -1: gap >= LANE - CK // 2}

    def pair(p, carry):
        group = quad * 2 + p
        mix = [[mix_ref[group, r, s] for s in range(2)] for r in range(2)]
        upstream_t = [ds[2 * p + r].T for r in range(2)]
        grad_mix = [[jnp.zeros((1, 1), F32) for _ in range(2)] for _ in range(2)]
        for r in range(2):
            d_cols[r] = jnp.zeros_like(d_cols[r])
        for r0, width, c0 in sets:
            rows = slice(r0, r0 + LANE)
            soft = [soft_ref[2 * p + s, rows, :width].astype(F32) for s in range(2)]
            d_prob, sums = [], []
            for r in range(2):
                dp = nt(ds[2 * p + r, rows], vs[2 * p + r, c0 : c0 + width])
                d_prob.append(dp)
                sums.append([jnp.sum(dp * soft[s], axis=1, keepdims=True) for s in range(2)])
                for s in range(2):
                    grad_mix[r][s] += jnp.sum(sums[r][s], axis=0, keepdims=True)
                mixed = (mix[r][0] * soft[0] + mix[r][1] * soft[1]).astype(BF16)
                d_cols[r, :, c0 : c0 + width] += nn(upstream_t[r][:, r0 : r0 + LANE], mixed)
            for s in range(2):
                d_soft = mix[0][s] * d_prob[0] + mix[1][s] * d_prob[1]
                inner = mix[0][s] * sums[0][s] + mix[1][s] * sums[1][s]
                d_conv = soft[s] * (d_soft - inner)
                d_rows[s, rows, :width] = d_conv.astype(BF16)
        lane = lax.broadcasted_iota(jnp.int32, (1, LANE), 1)
        line = jnp.zeros((1, LANE), F32)
        for r in range(2):
            for s in range(2):
                line = line + jnp.where(lane == 2 * r + s, grad_mix[r][s], 0.0)
        grad_mix_ref[0, pl.ds(p, 1), :] = line
        for r in range(2):
            d_heads[2, 2 * p + r] = d_cols[r].T

        for r in range(2):
            h = 2 * p + r
            fill_backward_band(taps_ref, quad * QUAD + h, band)
            for a, moved in enumerate(shifted_rows(qs[h])):
                shifted[a] = moved
            keys = ks[h]
            d_cols[0] = jnp.zeros_like(d_cols[0])
            d_query = []
            below = jnp.zeros((8, LANE * CQ), F32)
            above = jnp.zeros((8, LANE * CQ), F32)
            mirrored = []
            for r0, width, c0 in sets:
                rows = slice(r0, r0 + LANE)
                left, parts = masked_scores(shifted, keys, masks, r0, width, c0)
                d_conv = d_rows[r, rows, :width]
                blocks = width // LANE
                flipped = [
                    nt(flip, d_conv[:, b * LANE : (b + 1) * LANE]).astype(BF16) for b in range(blocks)
                ]
                start = len(mirrored) * LANE
                mirrored += flipped
                for b in range(blocks):
                    near_keys[start + b * LANE : start + (b + 1) * LANE, :] = jnp.concatenate(
                        [parts[a][:, b * LANE : (b + 1) * LANE] for a in range(CQ)], axis=1
                    )
                if blocks > 1:
                    end = start + blocks * LANE
                    below = below + nn(
                        jnp.concatenate([f[:8] for f in flipped[:-1]], axis=1), near_keys[start + LANE : end, :]
                    )
                    above = above + nn(
                        jnp.concatenate([f[LANE - 8 :] for f in flipped[1:]], axis=1), near_keys[start : end - LANE, :]
                    )
                spread = []
                for b in range(blocks):
                    low, high = max(b - 1, 0), min(b + 1, blocks - 1)
                    spread.append(
                        nn(
                            d_conv[:, low * LANE : (high + 1) * LANE],
                            band[(low - b + 1) * LANE : (high - b + 2) * LANE, :],
                        ).astype(BF16)
                    )
                stacked = jnp.concatenate(
                    [
                        jnp.concatenate(
                            [
                                spread[b][:, a * LANE : (a + 1) * LANE]
                                for b in range(blocks)
                            ],
                            axis=1,
                        )
                        * masks[a, rows, :width]
                        for a in range(CQ)
                    ],
                    axis=0,
                )
                d_query.append(nn(stacked, keys[c0 : c0 + width]))
                d_cols[0, :, c0 : c0 + width] += nn(left.T, stacked)
            total = None
            for a in range(CQ):
                whole = jnp.concatenate([d[a * LANE : (a + 1) * LANE] for d in d_query], axis=0)
                if a:
                    whole = pltpu.roll(whole, seq - a, axis=0)
                total = whole if total is None else total + whole
            d_heads[0, h] = total
            d_heads[1, h] = d_cols[0].T
            band_sum = nn(jnp.concatenate(mirrored, axis=1), near_keys[: len(mirrored) * LANE, :])
            for a in range(CQ):
                at = slice(a * LANE, (a + 1) * LANE)
                whole = jnp.where(keeps[0], band_sum[:, at], 0.0)
                whole = jnp.concatenate(
                    [
                        whole[:8] + jnp.where(keeps[1][:8], below[:, at], 0.0),
                        whole[8 : LANE - 8],
                        whole[LANE - 8 :] + jnp.where(keeps[-1][LANE - 8 :], above[:, at], 0.0),
                    ],
                    axis=0,
                )
                aligned = pltpu.roll(whole, 0, axis=1, stride=1, stride_axis=0)
                grad_taps_ref[h, a : a + 1, :] = jnp.sum(aligned, axis=0, keepdims=True)
            work = reduce.each()
            middle = len(work) // 2
            for j in in_turn(group, HEADS // 2, n):
                pl.when(j < n)(functools.partial(reduce.item, j, work[middle:] if r else work[:middle]))
        return carry

    lax.fori_loop(0, 2, pair, 0)
    quads = HEADS // QUAD
    block = QUAD * HEAD_DIM

    def leave(part):
        there = d_projected.at[:, cols((part * quads + quad) * block, block)]
        return pltpu.make_async_copy(leaving.at[part], there, leave_sem.at[part])

    for part in range(3):
        pl.when(quad > 0)(leave(part).wait)
        leaving[part] = jnp.concatenate([d_heads[part, h] for h in range(QUAD)], axis=1).astype(BF16)
        leave(part).start()

    @pl.when(quad == quads - 1)
    def _():
        for part in range(3):
            leave(part).wait()
        for i in range(done):
            final.add(i)

    @pl.when(quad == pl.num_programs(0) - 1)
    def _():
        reduce.finish()
        final.finish()


def attend_backward(projected, conv_kernel, head_mixing, docs, gains, attended, d_grouped, soft, grads, done_sums, done_specs, n, collective):
    seq = projected.shape[0]
    width = projected.shape[1] // 3
    block = QUAD * HEAD_DIM
    quads = HEADS // QUAD
    count = len(grads)
    specs = Reduce.specs_of(grads, n, (THIRD, THIRD))
    anywhere = pl.BlockSpec(memory_space=pl.ANY)
    whole = pl.BlockSpec(memory_space=pltpu.VMEM)
    smem = pl.BlockSpec(memory_space=pltpu.SMEM)

    def columns(first):
        return pl.BlockSpec((seq, block), lambda i: (0, first * quads + i))

    results = pl.pallas_call(
        functools.partial(backward_kernel, n, specs, done_specs),
        grid=(quads,),
        out_shape=[
            jax.ShapeDtypeStruct((seq, 3 * width), BF16),
            jax.ShapeDtypeStruct((1, width), F32),
            jax.ShapeDtypeStruct((HEADS, 8, LANE), F32),
            jax.ShapeDtypeStruct((quads, 8, LANE), F32),
        ]
        + Reduce.results(specs, n)
        + [jax.ShapeDtypeStruct(spec[:2], BF16) for spec in done_specs],
        in_specs=[
            smem, smem, whole,
            pl.BlockSpec((3, block), lambda i: (0, i)),
            columns(0), columns(1), columns(2), columns(0), columns(0),
            pl.BlockSpec((QUAD, seq, 3 * LANE), lambda i: (i, 0, 0)),
        ]
        + [anywhere] * (count + len(done_specs)),
        out_specs=[
            anywhere,
            pl.BlockSpec((1, block), lambda i: (0, i)),
            pl.BlockSpec((QUAD, 8, LANE), lambda i: (i, 0, 0)),
            pl.BlockSpec((1, 8, LANE), lambda i: (i, 0, 0)),
        ]
        + [anywhere] * (2 * count + len(done_specs)),
        scratch_shapes=[
            pltpu.VMEM((CQ, seq, 3 * LANE), BF16),
            pltpu.VMEM((3 * LANE, LANE * CQ), BF16),
            pltpu.VMEM((QUAD, seq, HEAD_DIM), BF16),
            pltpu.VMEM((QUAD, seq, HEAD_DIM), BF16),
            pltpu.VMEM((QUAD, seq, HEAD_DIM), BF16),
            pltpu.VMEM((QUAD, seq, HEAD_DIM), BF16),
            pltpu.VMEM((CQ, seq, HEAD_DIM), BF16),
            pltpu.VMEM((3, QUAD, seq, HEAD_DIM), F32),
            pltpu.VMEM((2, seq, 3 * LANE), BF16),
            pltpu.VMEM((2, HEAD_DIM, seq), F32),
            pltpu.VMEM((sum(w for _, w, _ in row_sets(seq)), LANE * CQ), BF16),
            pltpu.VMEM((3, seq, block), BF16),
            pltpu.SemaphoreType.DMA((3,)),
        ]
        + FinalSum.scratch(done_specs)
        + Reduce.scratch(specs, n),
        compiler_params=pltpu.CompilerParams(
            collective_id=collective, has_side_effects=True, vmem_limit_bytes=62 * 1024 * 1024
        ),
    )(
        docs, head_mixing, pad_taps(conv_kernel[:, :, ::-1]), gains,
        projected, projected, projected, attended, d_grouped, soft, *grads, *done_sums,
    )
    d_projected, grad_gain, grad_taps, grad_mix = results[:4]
    return (
        d_projected, grad_gain, grad_taps, grad_mix,
    ), list(results[4 : 4 + count]), specs, results[4 + 2 * count :]


MESH = pl.DeviceIdType.MESH


def ring_index(place, n):
    place = lax.rem(place + 2 * n, n)
    return jnp.where(place < n // 2, 2 * place, 2 * (n - 1 - place) + 1)


def ring_place(index, n):
    half = lax.div(index, 2)
    return jnp.where(lax.rem(index, 2) == 0, half, n - 1 - half)


class Ring:
    def __init__(self, n):
        self.n = n
        rep = lax.axis_index("rep")
        self.x, self.core = lax.div(rep, 2), lax.rem(rep, 2)
        index = lax.axis_index("fsdp")
        self.index = index
        self.place = ring_place(index, n)
        self.right = (rep, ring_index(self.place + 1, n))
        self.left = (rep, ring_index(self.place - 1, n))
        self.sibling = (self.x * 2 + 1 - self.core, index)
        self.across = ((1 - self.x) * 2 + self.core, index)

    def meet(self):
        barrier = pltpu.get_barrier_semaphore()
        for other in (self.right, self.left, self.sibling, self.across):
            pl.semaphore_signal(barrier, inc=1, device_id=other, device_id_type=MESH)
        pl.semaphore_wait(barrier, 4)


def send(src, dst, send_sem, recv_sem, device):
    return pltpu.make_async_remote_copy(
        src_ref=src, dst_ref=dst, send_sem=send_sem, recv_sem=recv_sem,
        device_id=device, device_id_type=MESH,
    )


def cols(start, size):
    return pl.ds(pl.multiple_of(start, LANE), size)


class Gather:
    def __init__(self, ring, weights, fulls, widths, sems):
        self.ring, self.weights, self.fulls = ring, weights, fulls
        self.axes, self.widths = zip(*widths)
        (self.own, self.ring_send, self.ring_recv, self.core_send, self.core_recv, self.x_send, self.x_recv) = sems

    def windows(self, i):
        ring = self.ring
        half = self.weights[i].shape[self.axes[i]] // 2
        w = self.widths[i]
        base = ring.core * half
        part = half - 2 * w
        first = base + jnp.where(ring.x == 0, 0, half - w)
        second = base + jnp.where(ring.x == 0, w, half - 2 * w)
        give = base + jnp.where(ring.x == 0, 0, half - part)
        take = base + jnp.where(ring.x == 0, half - part, 0)
        return w, part, first, second, give, take

    def block(self, i, index, start, width):
        rows = self.weights[i].shape[0]
        if self.axes[i] == 0:
            return self.fulls[i].at[pl.ds(pl.multiple_of(index * rows + start, 16), width), :]
        return self.fulls[i].at[pl.ds(pl.multiple_of(index * rows, 16), rows), cols(start, width)]

    def piece(self, i, start, width):
        if self.axes[i] == 0:
            return self.weights[i].at[pl.ds(pl.multiple_of(start, 16), width), :]
        return self.weights[i].at[:, cols(start, width)]

    def ring_copy(self, i, d, k, source):
        ring = self.ring
        w, _, first, second, _, _ = self.windows(i)
        start = second if d else first
        index = ring_index(ring.place + (k if d else -k), ring.n)
        there = self.block(i, index, start, w)
        src = self.piece(i, start, w) if source else there
        return send(src, there, self.ring_send.at[i, d, k], self.ring_recv.at[i, d, k], ring.left if d else ring.right)

    def core_copy(self, i, d, k):
        ring = self.ring
        w, part, first, second, _, take = self.windows(i)
        start, width = ((first, w), (second, w), (take, part))[d]
        index = ring_index(ring.place + (k + 1 if d == 1 else -k - 1), ring.n)
        there = self.block(i, index, start, width)
        return send(there, there, self.core_send.at[i, d, k], self.core_recv.at[i, d, k], ring.sibling)

    def x_copy(self, i, k):
        ring = self.ring
        _, part, _, _, give, _ = self.windows(i)
        there = self.block(i, ring_index(ring.place - k - 1, ring.n), give, part)
        return send(there, there, self.x_send.at[i, k], self.x_recv.at[i, k], ring.across)

    def own_copy(self, i):
        rows = self.weights[i].shape[0]
        there = self.fulls[i].at[pl.ds(pl.multiple_of(self.ring.index * rows, 16), rows), :]
        return send(self.weights[i], there, self.own.at[0, i], self.own.at[1, i], self.ring.sibling)

    def has_part(self, i):
        return self.weights[i].shape[self.axes[i]] // 2 > 2 * self.widths[i]

    def start(self):
        for i in range(len(self.weights)):
            for d in range(2):
                self.ring_copy(i, d, 0, True).start()
        for i in range(len(self.weights)):
            self.own_copy(i).start()

    def step(self, k):
        last = self.ring.n - 2
        for i in range(len(self.weights)):
            for d in range(2):
                self.ring_copy(i, d, k, False).wait_recv()

                @pl.when(k < last)
                def _():
                    self.ring_copy(i, d, k + 1, False).start()

                if d == 0 and self.has_part(i):
                    self.x_copy(i, k).start()
                self.core_copy(i, d, k).start()

            if self.has_part(i):
                @pl.when(k >= LAG)
                def _():
                    self.pass_on(i, k - LAG)

    def pass_on(self, i, k):
        self.x_copy(i, k).wait_recv()
        self.core_copy(i, 2, k).start()

    def finish(self):
        last = self.ring.n - 2
        for k in range(max(0, last + 1 - LAG), last + 1):
            for i in range(len(self.weights)):
                if self.has_part(i):
                    self.pass_on(i, k)

        def settle(k, carry):
            for i in range(len(self.weights)):
                for d in range(2):
                    self.ring_copy(i, d, k, False).wait_send()
                    self.core_copy(i, d, k).wait()
                if self.has_part(i):
                    self.x_copy(i, k).wait_send()
                    self.core_copy(i, 2, k).wait()
            return carry

        lax.fori_loop(0, self.ring.n - 1, settle, 0)
        for i in range(len(self.weights)):
            self.own_copy(i).wait()

    @staticmethod
    def scratch(count, n):
        dma = pltpu.SemaphoreType.DMA
        return [
            dma((2, count)), dma((count, 2, n - 1)), dma((count, 2, n - 1)),
            dma((count, 3, n - 1)), dma((count, 3, n - 1)), dma((count, n - 1)), dma((count, n - 1)),
        ]


def share(shape):
    rows, columns = shape
    axis, unit = (0, 16) if rows % 64 == 0 else (1, LANE)
    units = (rows, columns)[axis] // 2 // unit
    return axis, -(-units // 3) * unit


THIRD = (1, 3)
LESS = (7, 18)
HALF = (1, 2)
LAST_PORTIONS = (LESS, THIRD)


def carried(columns, portion):
    half = columns // 2
    lanes = -(-(half // LANE) * portion[0] // portion[1]) * LANE
    if 2 * lanes >= half:
        return half // 2, 0
    return lanes, half - 2 * lanes


class Reduce:
    def __init__(self, ring, grads, sums, others, specs, scratch):
        self.ring, self.grads, self.sums, self.others, self.specs = ring, grads, sums, others, specs
        count = len(grads)
        self.slots, self.mine, self.twin, self.x_slots, self.x_out = [], [], [], [], []
        scratch = list(scratch)
        for spec in specs:
            part = carried(spec[1], spec[2])[1]
            take = [scratch.pop(0) for _ in range(10 if part else 6)]
            self.slots.append(take[:2])
            self.mine.append(take[2:4] + take[6:7])
            self.twin.append(take[4:6] + take[7:8])
            self.x_slots.append(take[8] if part else None)
            self.x_out.append(take[9] if part else None)
        (self.load, self.ring_send, self.ring_recv, self.core_send, self.core_recv,
         self.x_send, self.x_recv, self.keep) = scratch

    def owner(self, kind, j):
        ring = self.ring
        return ring_index(ring.place + (j + 1 if kind == 1 else -j - 1), ring.n)

    def span(self, i, kind):
        columns, shared = self.specs[i][1:]
        w, part = carried(columns, shared)
        half = columns // 2
        lower, upper = ((0, half - w), (w, half - 2 * w), (half - part, 0))[kind]
        return jnp.where(self.ring.x == 0, lower, upper), part if kind == 2 else w

    def rows(self, i, index):
        rows = self.specs[i][0]
        return pl.ds(pl.multiple_of(index * rows, 16), rows)

    def kinds(self, i):
        return 3 if self.x_slots[i] is not None else 2

    def core_copy(self, i, kind, j):
        ring = self.ring
        start, width = self.span(i, kind)
        rows = self.rows(i, self.owner(kind, j))
        half = self.specs[i][1] // 2
        return send(
            self.grads[i].at[rows, cols((1 - ring.core) * half + start, width)], self.others[i].at[rows, cols(start, width)],
            self.core_send.at[i, kind, j], self.core_recv.at[i, kind, j], ring.sibling,
        )

    def loads(self, i, kind, j):
        start, width = self.span(i, kind)
        rows = self.rows(i, self.owner(kind, j))
        base = self.ring.core * (self.specs[i][1] // 2)
        return (
            pltpu.make_async_copy(
                self.grads[i].at[rows, cols(base + start, width)], self.mine[i][kind], self.load.at[i, kind, 0]
            ),
            pltpu.make_async_copy(self.others[i].at[rows, cols(start, width)], self.twin[i][kind], self.load.at[i, kind, 1]),
        )

    def fetch(self, i, kind, j):
        own, other = self.loads(i, kind, j)
        own.start()
        self.core_copy(i, kind, j).wait_recv()
        other.start()

    def ring_copy(self, i, d, j):
        ring = self.ring
        return send(
            self.slots[i][d].at[j], self.slots[i][d].at[j + 1],
            self.ring_send.at[i, d, j], self.ring_recv.at[i, d, j + 1], ring.left if d else ring.right,
        )

    def gap(self, i):
        w, part = carried(*self.specs[i][1:])
        x = self.ring.x
        return w - part, jnp.where(x == 0, part, 0), jnp.where(x == 0, w - part, 0), part

    def x_copy(self, i, j):
        _, _, at, part = self.gap(i)
        return send(
            self.x_out[i].at[lax.rem(j, 2)], self.x_slots[i].at[j, :, cols(at, part)],
            self.x_send.at[i, j], self.x_recv.at[i, j], self.ring.across,
        )

    def give(self, i, j):
        j = jnp.int32(j)
        for copy in self.loads(i, 2, j):
            copy.wait()

        @pl.when(j >= 2)
        def _():
            self.x_copy(i, j - 2).wait_send()

        self.x_out[i][lax.rem(j, 2)] = (self.mine[i][2][...].astype(F32) + self.twin[i][2][...].astype(F32)).astype(BF16)
        self.x_copy(i, j).start()
        self.hand_next(i, 2, j)

        @pl.when(j < self.ring.n - 1)
        def _():
            self.fetch(i, 2, j + 1)

    def each(self):
        return [(i, d) for i in range(len(self.grads)) for d in (1, 0)]

    def clear(self):
        for i in range(len(self.grads)):
            if self.kinds(i) == 3:
                width, at, _, _ = self.gap(i)
                if width:
                    rows = self.specs[i][0]
                    self.x_slots[i][:, :, cols(at, width)] = jnp.zeros((self.ring.n, rows, width), BF16)

    def all(self):
        return range(len(self.grads))

    def hand_over(self, which=None):
        for j in range(min(LEAD, self.ring.n)):
            for i in which or self.all():
                for kind in reversed(range(self.kinds(i))):
                    self.core_copy(i, kind, j).start()

    def hand_next(self, i, kind, j):
        pl.when(j + LEAD < self.ring.n)(lambda: self.core_copy(i, kind, j + LEAD).start())

    def fetch_first(self, which=None):
        for i in which or self.all():
            for kind in reversed(range(self.kinds(i))):
                self.fetch(i, kind, 0)

    def give_all(self, j, which=None):
        for i in which or self.all():
            if self.kinds(i) == 3:
                self.give(i, j)

    def opening(self, which=None):
        return [
            functools.partial(self.hand_over, which), functools.partial(self.fetch_first, which),
            functools.partial(self.give_all, 0, which), functools.partial(self.give_all, 1, which),
        ]

    def start(self):
        for step in self.opening():
            step()

    def item(self, j, work):
        last = self.ring.n - 1
        for i, d in work:
            if d == 0 and self.kinds(i) == 3:
                pl.when(j < last - 1)(functools.partial(self.give, i, j + 2))
            for copy in self.loads(i, d, j):
                copy.wait()
            slot = self.slots[i][d]
            both = self.mine[i][d][...].astype(F32) + self.twin[i][d][...].astype(F32)
            if d == 0 and self.kinds(i) == 3:
                self.x_copy(i, j).wait_recv()
                both = both + self.x_slots[i][j].astype(F32)

            @pl.when(j == 0)
            def _():
                slot[j] = both.astype(BF16)

            @pl.when(j > 0)
            def _():
                self.ring_copy(i, d, j - 1).wait_recv()
                slot[j] = (slot[j].astype(F32) + both).astype(BF16)

            @pl.when(j < last)
            def _():
                self.ring_copy(i, d, j).start()
                self.fetch(i, d, j + 1)

            self.hand_next(i, d, j)

            @pl.when(j == last)
            def _():
                self.keep_copy(i, d).start()

    def keep_copy(self, i, d):
        w = carried(*self.specs[i][1:])[0]
        at = jnp.where(self.ring.x == 0, d * w, (1 - d) * w)
        return pltpu.make_async_copy(self.slots[i][d].at[self.ring.n - 1], self.sums[i].at[:, cols(at, w)], self.keep.at[i, d])

    def finish(self):
        last = self.ring.n - 1
        for i, d in self.each():
            self.keep_copy(i, d).wait()

        def settle(j, carry):
            for i in range(len(self.grads)):
                for kind in range(self.kinds(i)):
                    self.core_copy(i, kind, j).wait_send()
                for d in range(2):
                    pl.when(j < last)(lambda i=i, d=d: self.ring_copy(i, d, j).wait_send())
                if self.kinds(i) == 3:
                    pl.when(j >= last - 1)(lambda i=i: self.x_copy(i, j).wait_send())
            return carry

        lax.fori_loop(0, self.ring.n, settle, 0)

    @staticmethod
    def specs_of(grads, n, portions):
        return [(g.shape[0] // n, g.shape[1], portion) for g, portion in zip(grads, portions)]

    @staticmethod
    def results(specs, n):
        return [
            jax.ShapeDtypeStruct((rows, 2 * carried(columns, shared)[0]), BF16) for rows, columns, shared in specs
        ] + [jax.ShapeDtypeStruct((n * rows, columns // 2), BF16) for rows, columns, _ in specs]

    @staticmethod
    def scratch(specs, n):
        dma = pltpu.SemaphoreType.DMA
        count = len(specs)
        buffers = []
        for rows, columns, shared in specs:
            w, part = carried(columns, shared)
            buffers += [pltpu.VMEM((n, rows, w), BF16)] * 2 + [pltpu.VMEM((rows, w), BF16)] * 4
            if part:
                buffers += [pltpu.VMEM((rows, part), BF16)] * 2
                buffers += [pltpu.VMEM((n, rows, w), BF16), pltpu.VMEM((2, rows, part), BF16)]
        return buffers + [
            dma((count, 3, 2)), dma((count, 2, n)), dma((count, 2, n)), dma((count, 3, n)), dma((count, 3, n)),
            dma((count, n)), dma((count, n)), dma((count, 2)),
        ]


class FinalSum:
    def __init__(self, ring, sums, totals, specs, scratch):
        self.ring, self.sums, self.totals, self.specs = ring, sums, totals, specs
        scratch = list(scratch)
        self.mine, self.plane, self.own = [], [], []
        for spec in specs:
            self.mine.append(scratch.pop(0))
            self.plane.append(scratch.pop(0))
            self.own.append(scratch.pop(0) if carried(spec[1], spec[2])[1] else None)
        self.local, self.remote_send, self.remote_recv = scratch

    def spans(self, i):
        columns, shared = self.specs[i][1:]
        w, part = carried(columns, shared)
        half, wide = columns // 2, 2 * w - part
        base = self.ring.core * half
        low = self.ring.x == 0
        return (
            (jnp.where(low, part, 0), base + part, wide),
            (jnp.where(low, 0, wide), base + jnp.where(low, 0, half - part), part),
            (0, base + jnp.where(low, half - part, 0), part),
        )

    def remote(self, i, at, src, dst, device):
        return send(src, dst, self.remote_send.at[i, at], self.remote_recv.at[i, at], device)

    def copy(self, i, name):
        ring, sums, totals = self.ring, self.sums[i], self.totals[i]
        (a, a_out, wide), (b, b_out, part), (_, c_out, _) = self.spans(i)
        local = {"load": 0, "save": 1, "load done": 2, "save done": 3}
        remote = {"across": 0, "sibling": 1, "done across": 2, "done sibling": 3, "pass on": 4}
        if name in ("load", "save", "across", "sibling"):
            src, dst, mid = sums.at[:, cols(a, wide)], totals.at[:, cols(a_out, wide)], self.mine[i]
        elif name == "pass on":
            src = dst = mid = totals.at[:, cols(c_out, part)]
        else:
            src, dst, mid = sums.at[:, cols(b, part)], totals.at[:, cols(b_out, part)], self.own[i]
        if name in local:
            ends = (src, mid) if name.startswith("load") else (mid, dst)
            return pltpu.make_async_copy(*ends, self.local.at[i, local[name]])
        ends = {"across": (src, self.plane[i]), "sibling": (mid, dst)}.get(name, (src, dst))
        device = ring.across if "across" in name else ring.sibling
        at = remote[name]
        return send(*ends, self.remote_send.at[i, at], self.remote_recv.at[i, at], device)

    def shares(self, i):
        return carried(*self.specs[i][1:])[1] > 0

    def start(self, i):
        for name in ("across", "load"):
            self.copy(i, name).start()
        if self.shares(i):
            for name in ("done across", "load done", "done sibling"):
                self.copy(i, name).start()

    def add(self, i):
        self.copy(i, "load").wait()
        self.copy(i, "across").wait_recv()
        self.mine[i][...] = (self.mine[i][...].astype(F32) + self.plane[i][...].astype(F32)).astype(BF16)
        self.copy(i, "sibling").start()
        self.copy(i, "save").start()
        if self.shares(i):
            self.copy(i, "load done").wait()
            self.copy(i, "save done").start()
            self.copy(i, "done across").wait_recv()
            self.copy(i, "pass on").start()

    def finish(self):
        for i in range(len(self.specs)):
            self.copy(i, "across").wait_send()
            self.copy(i, "sibling").wait()
            self.copy(i, "save").wait()
            if self.shares(i):
                self.copy(i, "done across").wait_send()
                for name in ("done sibling", "save done", "pass on"):
                    self.copy(i, name).wait()

    @staticmethod
    def scratch(specs):
        dma = pltpu.SemaphoreType.DMA
        count = len(specs)
        buffers = []
        for rows, columns, shared in specs:
            w, part = carried(columns, shared)
            buffers += [pltpu.VMEM((rows, 2 * w - part), BF16)] * 2
            if part:
                buffers += [pltpu.VMEM((rows, part), BF16)]
        return buffers + [dma((count, 4)), dma((count, 5)), dma((count, 5))]


class SmallSum:
    def __init__(self, ring, given, total, scratch):
        self.ring, self.given, self.total = ring, given, total
        self.mine, self.twin, self.plane, self.slots, self.pair, self.ring_send, self.ring_recv = scratch

    def copy(self, src, dst, at, device):
        return send(src, dst, self.pair.at[0, at], self.pair.at[1, at], device)

    def to_core(self):
        return self.copy(self.given, self.twin, 0, self.ring.sibling)

    def to_plane(self):
        return self.copy(self.mine, self.plane, 1, self.ring.across)

    def add_core(self):
        self.to_core().wait()
        self.mine[...] = self.given[...] + self.twin[...]
        self.to_plane().start()

    def add_plane(self):
        self.to_plane().wait()
        self.slots[0] = self.mine[...] + self.plane[...]

    def ring_copy(self, j):
        return send(
            self.slots.at[j], self.slots.at[j + 1], self.ring_send.at[j], self.ring_recv.at[j + 1], self.ring.right
        )

    def item(self, j):
        @pl.when(j > 0)
        def _():
            self.ring_copy(j - 1).wait_recv()

        @pl.when(j < self.ring.n - 1)
        def _():
            self.ring_copy(j).start()

    def finish(self):
        ring = self.ring
        total = jnp.zeros(self.total.shape, F32)
        for place in range(ring.n):
            total = total + self.slots[lax.rem(ring.place - place + ring.n, ring.n)]
        self.total[...] = total

        def settle(j, carry):
            self.ring_copy(j).wait_send()
            return carry

        lax.fori_loop(0, ring.n - 1, settle, 0)

    @staticmethod
    def scratch(rows, n):
        dma = pltpu.SemaphoreType.DMA
        block = pltpu.VMEM((rows, LANE), F32)
        return [block, block, block, pltpu.VMEM((n, rows, LANE), F32), dma((2, 2)), dma((n,)), dma((n,))]


SMALL_SCRATCH = 7


def pack(given, at, row):
    for r in range(row.shape[1] // LANE):
        given[at + r : at + r + 1, :] = row[:, r * LANE : (r + 1) * LANE]
    return at + row.shape[1] // LANE


SPOTS = 8


def pack_taps(given, at, taps_ref, mix_ref):
    rows = taps_ref.shape[1]
    for first in range(0, HEADS, SPOTS):
        together = taps_ref[first]
        for h in range(1, SPOTS):
            together = together + pltpu.roll(taps_ref[first + h], h * (LANE // SPOTS), axis=1)
        given[at : at + rows, :] = together
        at += rows
    together = mix_ref[0]
    for quad in range(1, mix_ref.shape[0]):
        together = together + pltpu.roll(mix_ref[quad], 2 * quad, axis=0)
    given[at : at + rows, :] = together


def unpack_taps(summed):
    rows = 8
    taps = jnp.roll(summed[: HEADS // SPOTS * rows], CK // 2 + 1, axis=1).reshape(-1, rows, SPOTS, LANE // SPOTS)
    taps = taps.transpose(0, 2, 1, 3).reshape(HEADS, rows, LANE // SPOTS)[:, :CQ, :CK]
    mixing = summed[HEADS // SPOTS * rows :][: HEADS // 2, :4]
    return taps[:, :, ::-1] * SCALE, mixing.reshape(HEADS // 2, 2, 2)


def last_kernel(n, specs, early_specs, chunk, small_count, *refs):
    count, early = len(specs), len(early_specs)
    ring = Ring(n)
    refs = list(refs)

    def take(size):
        taken = refs[:size]
        del refs[:size]
        return taken

    small_refs = take(small_count)
    input_ref, normed_ref, gain_ref, d_middle_ref, d_projected, weight = take(6)
    grads, early_sums = take(count - 1), take(early)
    grad_input_ref, total_ref, grad_qkv = take(3)
    totals, early_totals, sums, others = take(count), take(early), take(count), take(count)
    given, d_normed, in_left, in_right, turned, leaving, in_sem, leave_sem = take(8)
    small = SmallSum(ring, given, total_ref, take(SMALL_SCRATCH))
    last_sum = FinalSum(ring, sums, totals, specs, take(len(FinalSum.scratch(specs))))
    early_sum = FinalSum(ring, early_sums, early_totals, early_specs, take(len(FinalSum.scratch(early_specs))))
    reduce = Reduce(ring, [grad_qkv] + grads, sums, others, specs, refs)
    chunks = d_projected.shape[1] // chunk

    def arrive(t, slot):
        at = cols(t * chunk, chunk)
        return (
            pltpu.make_async_copy(d_projected.at[:, at], in_left.at[slot], in_sem.at[slot, 0]),
            pltpu.make_async_copy(weight.at[:, at], in_right.at[slot], in_sem.at[slot, 1]),
        )

    def leave(t):
        slot = lax.rem(t, 2)
        return pltpu.make_async_copy(leaving.at[slot], grad_qkv.at[:, cols(t * chunk, chunk)], leave_sem.at[slot])

    def turn(t, carry):
        slot = lax.rem(t, 2)
        for copy in arrive(t, slot):
            copy.wait()

        @pl.when(t < chunks - 1)
        def _():
            for copy in arrive(t + 1, 1 - slot):
                copy.start()

        pl.when(t >= 2)(lambda: leave(t - 2).wait())
        leaving[slot] = nn(turned[...], in_left[slot]).astype(BF16)
        leave(t).start()
        d_normed[...] += nt(in_left[slot], in_right[slot])
        return carry

    ahead = 3
    qkv, others_at = [0], list(range(1, count))
    behind = [(i, d) for i, d in reduce.each() if i > 0]

    for copy in arrive(0, 0):
        copy.start()
    reduce.clear()
    ring.meet()
    reduce.hand_over(others_at)
    d_normed[...] = jnp.zeros_like(d_normed)
    given[...] = jnp.zeros_like(given)
    turned[...] = normed_ref[...].T
    for step in reduce.opening(others_at)[1:]:
        step()
    for j in range(ahead):
        lax.fori_loop(j * chunks // ahead, (j + 1) * chunks // ahead, turn, 0)
        reduce.item(jnp.int32(j), behind)
    for t in (chunks - 2, chunks - 1):
        leave(jnp.int32(t)).wait()
    reduce.hand_over(qkv)
    values = input_ref[...].astype(F32)
    scale = lax.rsqrt(jnp.mean(values * values, axis=1, keepdims=True) + EPSILON)
    upstream = d_normed[...]
    grad_gain = jnp.sum(upstream * (values * scale), axis=0, keepdims=True)
    at = 0
    for row in [grad_gain] + [ref[...] for ref in small_refs[:2]]:
        at = pack(given, at, row)
    pack_taps(given, at, small_refs[2], small_refs[3])
    small.to_core().start()
    for step in reduce.opening(qkv)[1:]:
        step()

    def items(j):
        reduce.item(j, [(0, 1), (0, 0)])
        pl.when(j + ahead < n)(lambda: reduce.item(j + ahead, behind))

    items(jnp.int32(0))
    scaled = upstream * gain_ref[0:1, :]
    inner = jnp.mean(scaled * values, axis=1, keepdims=True)
    grad_input_ref[...] = d_middle_ref[...] + scale * scaled - values * (scale * scale * scale * inner)
    small.add_core()
    items(jnp.int32(1))
    small.add_plane()
    hops = -(-n // (n - 3))

    def rest(j, carry):
        for hop in range(hops):
            at = (j - 2) * hops + hop
            pl.when(at < n)(functools.partial(small.item, at))
        for i in range(early):
            pl.when(j == 2 + i)(functools.partial(early_sum.start, i))
        items(j)
        for i in range(early):
            pl.when(j == n - early + i)(functools.partial(early_sum.add, i))
        return carry

    lax.fori_loop(2, n, rest, 0)
    reduce.finish()
    for i in range(count):
        last_sum.start(i)
    small.finish()
    for i in range(count):
        last_sum.add(i)
    early_sum.finish()
    last_sum.finish()


def last_step(
    d_projected, qkv_weight, layer_input, normed, gains, d_middle, grads, smalls, early_sums, early_specs, n, collective
):
    count, early = 1 + len(grads), len(early_specs)
    seq, width = layer_input.shape
    chunk = 512
    grad_qkv = jax.ShapeDtypeStruct((width, d_projected.shape[1]), BF16)
    specs = Reduce.specs_of([grad_qkv] + grads, n, LAST_PORTIONS)
    sizes = [width // LANE] * 3 + [(HEADS // SPOTS + 1) * 8]
    rows = -(-sum(sizes) // 8) * 8
    anywhere = pl.BlockSpec(memory_space=pl.ANY)
    whole = pl.BlockSpec(memory_space=pltpu.VMEM)
    results = pl.pallas_call(
        functools.partial(last_kernel, n, specs, early_specs, chunk, len(smalls)),
        out_shape=[jax.ShapeDtypeStruct((seq, width), F32), jax.ShapeDtypeStruct((rows, LANE), F32), grad_qkv]
        + [jax.ShapeDtypeStruct(spec[:2], BF16) for spec in specs + early_specs]
        + Reduce.results(specs, n),
        in_specs=[whole] * (len(smalls) + 4) + [anywhere] * (1 + count + early),
        out_specs=[whole] * 2 + [anywhere] * (1 + 3 * count + early),
        scratch_shapes=[
            pltpu.VMEM((rows, LANE), F32),
            pltpu.VMEM((seq, width), F32),
            pltpu.VMEM((2, seq, chunk), BF16),
            pltpu.VMEM((2, width, chunk), BF16),
            pltpu.VMEM((width, seq), BF16),
            pltpu.VMEM((2, width, chunk), BF16),
            pltpu.SemaphoreType.DMA((2, 2)),
            pltpu.SemaphoreType.DMA((2,)),
        ]
        + SmallSum.scratch(rows, n)
        + FinalSum.scratch(specs)
        + FinalSum.scratch(early_specs)
        + Reduce.scratch(specs, n),
        compiler_params=pltpu.CompilerParams(
            collective_id=collective, has_side_effects=True, vmem_limit_bytes=60 * 1024 * 1024
        ),
    )(*smalls, layer_input, normed, gains, d_middle, d_projected, qkv_weight, *grads, *early_sums)
    out, at = [], 0
    for size in sizes:
        out.append(results[1][at : at + size])
        at += size
    return results[0], results[3 : 3 + count + early], out


TILES = 8
EARLY_TILES = 3
POINTS = 4
LATE_TILES = 3


def mlp_kernel(n, specs, tile, *refs):
    refs = list(refs)

    def take(size):
        taken = refs[:size]
        del refs[:size]
        return taken

    second_ref, upstream_ref, gain_ref, middle, out_weight, inner, down, coming = take(8)
    out_ref, d_middle_ref, d_grouped_ref, grad_gain_ref = take(4)
    (early, late, grad_down), sums, others, (came,) = take(3), take(1), take(1), take(1)
    turned, out_sum, d_second_ref, in_gate, in_up, in_down, to_gate, to_up, to_down = take(9)
    middle_sem, in_sem, to_sem, out_sem = take(4)
    ring = Ring(n)
    hidden_size = down.shape[0]
    cut = hidden_size - LATE_TILES * tile
    size = hidden_size - cut
    pieces = [coming.at[:, cut:hidden_size], coming.at[:, hidden_size + cut :]]
    gather = Gather(
        ring, pieces, [came.at[:, :size], came.at[:, size:]], [share((coming.shape[0], size))] * 2,
        take(len(Gather.scratch(2, n))),
    )
    reduce = Reduce(ring, [early], sums, others, specs, refs)
    tiles = hidden_size // tile
    begun = EARLY_TILES
    each = -(-n // (tiles - begun - 1))
    due = -(-each // 2)

    split = tiles - LATE_TILES

    def arrive(t, slot, weight, first, count):
        at = pl.multiple_of((t - first) * tile, tile)
        return (
            pltpu.make_async_copy(weight.at[:, pl.ds(at, tile)], in_gate.at[slot], in_sem.at[slot, 0]),
            pltpu.make_async_copy(
                weight.at[:, pl.ds(pl.multiple_of(count * tile + at, tile), tile)], in_up.at[slot], in_sem.at[slot, 1]
            ),
            pltpu.make_async_copy(
                down.at[pl.ds(pl.multiple_of(t * tile, tile), tile), :], in_down.at[slot], in_sem.at[slot, 2]
            ),
        )

    def arrivals(t, act):
        slot = lax.rem(t, 2)

        @pl.when(t < split)
        def _():
            for copy in arrive(t, slot, inner, 0, split):
                act(copy)

        @pl.when((t >= split) & (t < tiles))
        def _():
            for copy in arrive(t, slot, came, split, LATE_TILES):
                act(copy)

    def leave(grad, t, slot, first, count):
        at = pl.multiple_of((t - first) * tile, tile)
        return (
            pltpu.make_async_copy(to_gate.at[slot], grad.at[:, pl.ds(at, tile)], to_sem.at[slot, 0]),
            pltpu.make_async_copy(
                to_up.at[slot], grad.at[:, pl.ds(pl.multiple_of(count * tile + at, tile), tile)], to_sem.at[slot, 1]
            ),
            pltpu.make_async_copy(
                to_down.at[slot], grad_down.at[pl.ds(pl.multiple_of(t * tile, tile), tile), :], to_sem.at[slot, 2]
            ),
        )

    def leave_early(t):
        return leave(early, t, lax.rem(t, 2), 0, begun)

    def leave_late(t):
        return leave(late, t, lax.rem(t, 2), begun, tiles - begun)

    first = pltpu.make_async_copy(middle, out_sum, middle_sem.at[0])
    again = pltpu.make_async_copy(middle, d_middle_ref, middle_sem.at[1])
    first.start()
    again.start()
    arrivals(jnp.int32(0), lambda copy: copy.start())
    reduce.clear()
    ring.meet()
    gather.start()
    turned[...] = second_ref[...].T
    d_second_ref[...] = jnp.zeros_like(d_second_ref)
    first.wait()

    def serve(t, point):
        ends = (split - 1) * POINTS + 1
        turns = 7
        for turn in range(turns):
            at = 2 + turn * (ends - 3) // (turns - 1)
            if at % POINTS == point:
                for k in in_turn(turn, turns, n - 1):
                    if k < n - 1:
                        pl.when(t == at // POINTS)(functools.partial(gather.step, jnp.int32(k)))
        if ends % POINTS == point:
            pl.when(t == ends // POINTS)(gather.finish)

        @pl.when(t == begun)
        def _():
            if point == 0:
                for back in (2, 1):
                    for copy in leave_early(t - back):
                        copy.wait()
            reduce.opening()[point]()

        for step in range(due):
            if point // 2 * due + step < each:
                j = (t - begun - 1) * each + point // 2 * due + step
                pl.when((t > begun) & (j < n))(functools.partial(reduce.item, j, [(0, 1 - point % 2)]))

    def one(t, carry):
        slot = lax.rem(t, 2)
        arrivals(t, lambda copy: copy.wait())
        second, upstream = second_ref[...], upstream_ref[...]
        gate = nn(second, in_gate[slot])
        up = nn(second, in_up[slot])
        sigmoid = jax.nn.sigmoid(gate)
        silu = gate * sigmoid
        hidden = (silu * up).astype(BF16)
        serve(t, 0)
        d_hidden = nt(upstream, in_down[slot])
        out_sum[...] += nn(hidden, in_down[slot])

        @pl.when((t >= 2) & (t < begun))
        def _():
            for copy in leave_early(t - 2):
                copy.wait()

        @pl.when(t >= begun + 2)
        def _():
            for copy in leave_late(t - 2):
                copy.wait()

        to_down[slot] = nn(hidden.T, upstream).astype(BF16)
        d_gate = (d_hidden * up * sigmoid * (1.0 + gate * (1.0 - sigmoid))).astype(BF16)
        d_up = (d_hidden * silu).astype(BF16)
        serve(t, 1)
        d_second_ref[...] += nt(d_gate, in_gate[slot])
        to_gate[slot] = nn(turned[...], d_gate).astype(BF16)
        serve(t, 2)
        arrivals(t + 1, lambda copy: copy.start())
        d_second_ref[...] += nt(d_up, in_up[slot])
        to_up[slot] = nn(turned[...], d_up).astype(BF16)
        serve(t, 3)

        @pl.when(t < begun)
        def _():
            for copy in leave_early(t):
                copy.start()

        @pl.when(t >= begun)
        def _():
            for copy in leave_late(t):
                copy.start()

        return carry

    def out_piece(c):
        into = (in_gate.at[0], in_up.at[0], in_gate.at[1])[c]
        return pltpu.make_async_copy(out_weight.at[:, c * tile : (c + 1) * tile], into, out_sem.at[c])

    lax.fori_loop(0, tiles, one, 0)
    pieces = out_weight.shape[1] // tile
    for c in range(pieces):
        out_piece(c).start()
    out_ref[...] = out_sum[...].astype(BF16)
    again.wait()
    values = d_middle_ref[...]
    scale = lax.rsqrt(jnp.mean(values * values, axis=1, keepdims=True) + EPSILON)
    d_second = d_second_ref[...]
    grad_gain_ref[...] = jnp.sum(d_second * (values * scale), axis=0, keepdims=True)
    scaled = d_second * gain_ref[2:3, :]
    mean = jnp.mean(scaled * values, axis=1, keepdims=True)
    d_middle_ref[...] = (
        upstream_ref[...].astype(F32) + scale * scaled - values * (scale * scale * scale * mean)
    )
    for c in range(pieces):
        out_piece(c).wait()
        part = nt(
            d_middle_ref[:, c * tile : (c + 1) * tile].astype(BF16), (in_gate.at[0], in_up.at[0], in_gate.at[1])[c][...]
        )
        if c == 0:
            d_grouped_ref[...] = part
        else:
            d_grouped_ref[...] += part
    for t in (tiles - 2, tiles - 1):
        for copy in leave_late(t):
            copy.wait()
    reduce.finish()


def feed_forward(second, upstream, gains, middle, out_weight, inner, down, coming, n, collective):
    seq, width = second.shape
    hidden_size = down.shape[0]
    tile = hidden_size // TILES
    early = EARLY_TILES * tile
    specs = [(width // n, 2 * early, THIRD)]
    whole = pl.BlockSpec(memory_space=pltpu.VMEM)
    anywhere = pl.BlockSpec(memory_space=pl.ANY)
    dma = pltpu.SemaphoreType.DMA
    results = pl.pallas_call(
        functools.partial(mlp_kernel, n, specs, tile),
        out_shape=[
            jax.ShapeDtypeStruct((seq, width), BF16),
            jax.ShapeDtypeStruct((seq, width), F32),
            jax.ShapeDtypeStruct((seq, width), F32),
            jax.ShapeDtypeStruct((1, width), F32),
        ]
        + [
            jax.ShapeDtypeStruct((width, 2 * early), BF16),
            jax.ShapeDtypeStruct((width, 2 * (hidden_size - early)), BF16),
            jax.ShapeDtypeStruct((hidden_size, width), BF16),
        ]
        + Reduce.results(specs, n)
        + [jax.ShapeDtypeStruct((width, 2 * LATE_TILES * tile), BF16)],
        in_specs=[whole] * 3 + [anywhere] * 5,
        out_specs=[whole] * 4 + [anywhere] * 6,
        scratch_shapes=[
            pltpu.VMEM((width, seq), BF16),
            pltpu.VMEM((seq, width), F32),
            pltpu.VMEM((seq, width), F32),
            pltpu.VMEM((2, width, tile), BF16),
            pltpu.VMEM((2, width, tile), BF16),
            pltpu.VMEM((2, tile, width), BF16),
            pltpu.VMEM((2, width, tile), BF16),
            pltpu.VMEM((2, width, tile), BF16),
            pltpu.VMEM((2, tile, width), BF16),
            dma((2,)), dma((2, 3)), dma((2, 3)), dma((3,)),
        ]
        + Gather.scratch(2, n)
        + Reduce.scratch(specs, n),
        compiler_params=pltpu.CompilerParams(
            collective_id=collective, has_side_effects=True, vmem_limit_bytes=62 * 1024 * 1024
        ),
    )(second, upstream, gains, middle, out_weight, inner, down, coming)
    out, d_middle, d_grouped, grad_gain, _, late, grad_down, sums, _, _ = results
    return out, d_middle, d_grouped, grad_gain, late, grad_down, [sums], specs


def weight_grad(operand, upstream):
    return lax.dot_general(
        operand, upstream, (((0,), (0,)), ((), ())), preferred_element_type=F32
    ).astype(BF16)


def body(
    layer_input,
    first_gain,
    qkv_weight,
    conv_kernel,
    head_mixing,
    group_gain,
    out_weight,
    second_gain,
    inner_weight,
    down_weight,
    doc_lengths,
    cotangent,
):
    n = lax.axis_size("fsdp")
    gains = jnp.stack([first_gain, group_gain, second_gain])
    kept, (qkv_weight, out_weight), (inner_first, down_full) = attend_forward(
        layer_input, conv_kernel, head_mixing, doc_lengths, gains, [qkv_weight, out_weight], inner_weight, down_weight, n, 0,
    )
    grouped, attended, soft, normed, middle, second, projected = kept
    layer_output, d_middle, d_grouped, grad_second, late_inner, grad_down, early_sums, early_specs = feed_forward(
        second, cotangent, gains, middle, out_weight, inner_first, down_full, inner_weight, n, 2
    )
    (d_projected, grad_group, grad_kernel, grad_mixing), sums, specs, (early_inner,) = attend_backward(
        projected, conv_kernel, head_mixing, doc_lengths, gains, attended, d_grouped, soft,
        [late_inner, grad_down], early_sums, early_specs, n, 3,
    )
    grad_proj = weight_grad(grouped, d_middle.astype(BF16))
    grad_input, shards, small = last_step(
        d_projected, qkv_weight, layer_input, normed, gains, d_middle, [grad_proj],
        [grad_group, grad_second, grad_kernel, grad_mixing], sums, specs, n, 4,
    )
    grad_first, grad_group, grad_second = [g.reshape(-1) for g in small[:3]]
    grad_kernel, grad_mixing = unpack_taps(small[3])
    grad_qkv, grad_proj, late_inner, grad_down = shards
    cut, late_cut = early_inner.shape[1] // 2, late_inner.shape[1] // 2
    grad_inner = jnp.concatenate(
        [early_inner[:, :cut], late_inner[:, :late_cut], early_inner[:, cut:], late_inner[:, late_cut:]], axis=1
    )
    shards = [g.astype(F32) for g in (grad_qkv, grad_proj, grad_inner, grad_down)]
    return (
        layer_output, grad_input, grad_first, shards[0], grad_kernel, grad_mixing, grad_group, shards[1], grad_second,
        shards[2], shards[3],
    )


def solution(mesh):
    placed = (
        P(("rep", "fsdp"), None),
        P(),
        P("fsdp", None),
        P(),
        P(),
        P(),
        P("fsdp", None),
        P(),
        P("fsdp", None),
        P("fsdp", None),
        P(("rep", "fsdp"), None),
        P(("rep", "fsdp"), None),
    )
    return jax.shard_map(
        body,
        mesh=mesh,
        in_specs=placed,
        out_specs=(
            P(("rep", "fsdp"), None),
            P(("rep", "fsdp"), None),
            P(),
            P("fsdp", None),
            P(),
            P(),
            P(),
            P("fsdp", None),
            P(),
            P("fsdp", None),
            P("fsdp", None),
        ),
        check_vma=False,
    )
```

```python
import functools, math
import jax, jax.numpy as jnp
from jax import lax
from jax.experimental import pallas as pl
from jax.experimental.pallas import tpu as pltpu
from jax.sharding import PartitionSpec as P

HEADS = 16
HEAD_DIM = 96
CQ = 6
CK = 11
EPSILON = 1e-05
LANE = 128
QUAD = 4
LAG = 1
LEAD = 3
REST_AHEAD = 2
SCALE = 1.0 / math.sqrt(HEAD_DIM)
F32 = jnp.float32
BF16 = jnp.bfloat16


def row_sets(seq):
    return [
        (r, min(r + LANE, 3 * LANE), max(0, r - 2 * LANE)) for r in range(0, seq, LANE)
    ]


def nt(a, b):
    return lax.dot_general(a, b, (((1,), (1,)), ((), ())), preferred_element_type=F32)


def nn(a, b):
    return jnp.dot(a, b, preferred_element_type=F32)


def fill_masks(docs_ref, masks, seq):
    ends = []
    total = jnp.int32(0)
    for d in range(docs_ref.shape[1] - 1):
        total = total + docs_ref[0, d]
        ends.append(total)
    for r0, width, c0 in row_sets(seq):
        rows = r0 + lax.broadcasted_iota(jnp.int32, (LANE, 1), 0)
        cols = c0 + lax.broadcasted_iota(jnp.int32, (1, width), 1)
        row_doc = sum((rows >= e).astype(jnp.int32) for e in ends)
        col_doc = sum((cols >= e).astype(jnp.int32) for e in ends)
        same = row_doc == col_doc
        for a in range(CQ):
            masks[a, r0 : r0 + LANE, :width] = jnp.where(
                same & (rows - cols >= a), 1.0, 0.0
            ).astype(BF16)


def circulant_masks():
    gap = lax.broadcasted_iota(jnp.int32, (LANE, LANE), 1) - lax.broadcasted_iota(
        jnp.int32, (LANE, LANE), 0
    )
    half = CK // 2
    return (jnp.abs(gap) <= half, gap <= half - LANE, gap >= LANE - half)


def circulant(taps):
    wide = jnp.broadcast_to(taps, (LANE, LANE))
    return pltpu.roll(wide, 0, axis=1, stride=1, stride_axis=0)


def fill_toeplitz(taps_ref, head, band, blocks):
    near, after, before = circulant_masks()
    for a in range(CQ):
        whole = circulant(taps_ref[head, a : a + 1, :])
        parts = {
            0: jnp.where(near, whole, 0.0).astype(BF16),
            1: jnp.where(after, whole, 0.0).astype(BF16),
            -1: jnp.where(before, whole, 0.0).astype(BF16),
        }
        for r in range(blocks):
            for c in range(blocks):
                part = parts.get(c - r)
                if part is not None:
                    yield a, r, c, part


def fill_forward_band(taps_ref, head, band):
    for a, r, c, part in fill_toeplitz(taps_ref, head, band, 3):
        at = (r * CQ + a) * LANE
        band[at : at + LANE, c * LANE : (c + 1) * LANE] = part


def fill_backward_band(taps_ref, head, band):
    near, after, before = circulant_masks()
    for a in range(CQ):
        whole = circulant(taps_ref[head, a : a + 1, :])
        for at, keep in enumerate((after, near, before)):
            band[at * LANE : (at + 1) * LANE, a * LANE : (a + 1) * LANE] = jnp.where(keep, whole, 0.0).astype(BF16)


def shifted_rows(query):
    wide = query.astype(F32)
    return [query] + [pltpu.roll(wide, a, axis=0).astype(BF16) for a in range(1, CQ)]


def masked_scores(shifted, keys, masks, r0, width, c0):
    left = jnp.concatenate([shifted[a, r0 : r0 + LANE] for a in range(CQ)], axis=0)
    scores = nt(left, keys[c0 : c0 + width]).astype(BF16)
    return left, [
        scores[a * LANE : (a + 1) * LANE] * masks[a, r0 : r0 + LANE, :width]
        for a in range(CQ)
    ]


def by_window(parts, width):
    return jnp.concatenate(
        [
            parts[a][:, b * LANE : (b + 1) * LANE]
            for b in range(width // LANE)
            for a in range(CQ)
        ],
        axis=1,
    )


def forward_kernel(
    n, first_widths, cut, docs_ref, mix_ref, taps_ref, gain_ref, input_ref, gains_ref, *refs
):
    refs = list(refs)

    def take(size):
        taken = refs[:size]
        del refs[:size]
        return taken

    first_count = len(first_widths)
    first_weights, (inner, down) = take(first_count), take(2)
    grouped_ref, attended_ref, soft_ref, normed_ref, middle_ref, second_ref, projected = take(7)
    first_fulls, (inner_full, down_full) = take(first_count), take(2)
    masks, band, qs, ks, vs, shifted, outs = take(7)
    blocks, block_weight, every, out_weight, block_in, block_out, out_in = take(7)
    ring = Ring(n)
    sems = len(Gather.scratch(first_count, n))
    hidden_size = inner.shape[1] // 2
    rest_weights = [inner.at[:, :cut], inner.at[:, hidden_size : hidden_size + cut], down]
    rest_fulls = [inner_full.at[:, :cut], inner_full.at[:, cut:], down_full]
    rest_widths = [share((inner.shape[0], cut))] * 2 + [share(down.shape)]
    first = Gather(ring, first_weights, first_fulls, first_widths, take(sems))
    rest = Gather(ring, rest_weights, rest_fulls, rest_widths, take(sems))
    seq = input_ref.shape[0]
    quad = pl.program_id(0)
    quads = HEADS // QUAD
    size = QUAD * HEAD_DIM
    count = 3 * quads

    def block_copy(t):
        slot = lax.rem(t, 2)
        return pltpu.make_async_copy(first_fulls[0].at[:, cols(t * size, size)], block_weight.at[slot], block_in.at[slot])

    def block_save(t):
        return pltpu.make_async_copy(blocks.at[t], projected.at[:, cols(t * size, size)], block_out.at[t])

    out_copy = pltpu.make_async_copy(first_fulls[1], out_weight, out_in)

    def serve(turn):
        for k in in_turn(turn, 2 + HEADS // 2, n - 1):
            pl.when(k < n - 1)(functools.partial(rest.step, k))

    @pl.when(quad == 0)
    def _():
        ring.meet()
        first.start()
        fill_masks(docs_ref, masks, seq)
        band[...] = jnp.zeros_like(band)
        values = input_ref[...].astype(F32)
        scale = lax.rsqrt(jnp.mean(values * values, axis=1, keepdims=True) + EPSILON)
        normed_ref[...] = (values * scale * gains_ref[0:1, :]).astype(BF16)

        def one(k, carry):
            first.step(k)
            pl.when(k == n - REST_AHEAD)(rest.start)
            return carry

        lax.fori_loop(0, n - 1, one, 0)
        first.finish()
        serve(jnp.int32(0))
        block_copy(0).start()
        out_copy.start()

        def project_block(t, carry):
            pl.when(t < count - 1)(lambda: block_copy(t + 1).start())
            block_copy(t).wait()
            blocks[t] = nn(normed_ref[...], block_weight[lax.rem(t, 2)]).astype(BF16)
            block_save(t).start()
            return carry

        lax.fori_loop(0, count, project_block, 0)
        serve(jnp.int32(1))

    for h in range(QUAD):
        at = slice(h * HEAD_DIM, (h + 1) * HEAD_DIM)
        qs[h] = blocks[quad, :, at]
        ks[h] = blocks[quads + quad, :, at]
        vs[h] = blocks[2 * quads + quad, :, at]

    sets = row_sets(seq)

    def pair(p, carry):
        group = quad * 2 + p
        for r in range(2):
            h = 2 * p + r
            fill_forward_band(taps_ref, quad * QUAD + h, band)
            for a, rows in enumerate(shifted_rows(qs[h])):
                shifted[a] = rows
            keys = ks[h]
            lefts = []
            for r0, width, c0 in sets:
                _, parts = masked_scores(shifted, keys, masks, r0, width, c0)
                lefts.append((width, by_window(parts, width)))
            convs = []
            i = 0
            while i < len(sets):
                width = sets[i][1]
                run = 1
                while i + run < len(sets) and sets[i + run][1] == width:
                    run += 1
                left = jnp.concatenate([lefts[i + m][1] for m in range(run)], axis=0)
                conv = nn(left, band[: width * CQ, :width])
                convs += [conv[m * LANE : (m + 1) * LANE] for m in range(run)]
                i += run
            for (r0, width, c0), conv in zip(sets, convs):
                logits = jnp.where(
                    masks[0, r0 : r0 + LANE, :width].astype(F32) > 0, conv, -1e30
                )
                weights = jnp.exp(logits - jnp.max(logits, axis=1, keepdims=True))
                soft = weights * (1.0 / jnp.sum(weights, axis=1, keepdims=True))
                soft_ref[h, r0 : r0 + LANE, :width] = soft.astype(BF16)
        for r in range(2):
            h = 2 * p + r
            values = vs[h]
            for r0, width, c0 in sets:
                mixed = (
                    mix_ref[group, r, 0] * soft_ref[2 * p, r0 : r0 + LANE, :width].astype(F32)
                    + mix_ref[group, r, 1] * soft_ref[2 * p + 1, r0 : r0 + LANE, :width].astype(F32)
                ).astype(BF16)
                outs[h, r0 : r0 + LANE] = nn(mixed, values[c0 : c0 + width])
        serve(2 + group)
        return carry

    lax.fori_loop(0, 2, pair, 0)
    wholes, grouped = [], []
    for h in range(QUAD):
        attended = outs[h]
        centred = attended - jnp.mean(attended, axis=1, keepdims=True)
        var = jnp.mean(centred * centred, axis=1, keepdims=True)
        wholes.append(attended)
        grouped.append(centred * lax.rsqrt(var + EPSILON))
    attended_ref[...] = jnp.concatenate(wholes, axis=1)
    every[quad] = (jnp.concatenate(grouped, axis=1) * gain_ref[1:2, :]).astype(BF16)
    grouped_ref[...] = every[quad]

    @pl.when(quad == quads - 1)
    def _():
        out_copy.wait()
        branch = nn(jnp.concatenate([every[i] for i in range(quads)], axis=1), out_weight[...])
        middle = input_ref[...].astype(F32) + branch
        scale = lax.rsqrt(jnp.mean(middle * middle, axis=1, keepdims=True) + EPSILON)
        middle_ref[...] = middle
        second_ref[...] = (middle * scale * gains_ref[2:3, :]).astype(BF16)

        def saved(t, carry):
            block_save(t).wait()
            return carry

        lax.fori_loop(0, count, saved, 0)
        rest.finish()


def pad_taps(kernel):
    padded = jnp.pad(kernel * SCALE, ((0, 0), (0, 2), (0, LANE - CK)))
    return jnp.roll(padded, -(CK // 2), axis=2)


def in_turn(turn, turns, steps):
    each = -(-steps // turns)
    return [turn * each + t for t in range(each)]


def attend_forward(layer_input, conv_kernel, head_mixing, docs, gains, first, inner, down, n, collective):
    seq, width = layer_input.shape
    block = QUAD * HEAD_DIM
    quads = HEADS // QUAD
    first_widths = [share(w.shape) for w in first]
    cut = inner.shape[1] // 2 // TILES * (TILES - LATE_TILES)
    whole = pl.BlockSpec(memory_space=pltpu.VMEM)
    smem = pl.BlockSpec(memory_space=pltpu.SMEM)
    anywhere = pl.BlockSpec(memory_space=pl.ANY)
    columns = pl.BlockSpec((seq, block), lambda i: (0, i))
    dma = pltpu.SemaphoreType.DMA
    results = pl.pallas_call(
        functools.partial(forward_kernel, n, first_widths, cut),
        grid=(quads,),
        out_shape=[
            jax.ShapeDtypeStruct((seq, width), BF16),
            jax.ShapeDtypeStruct((seq, width), F32),
            jax.ShapeDtypeStruct((HEADS, seq, 3 * LANE), BF16),
            jax.ShapeDtypeStruct((seq, width), BF16),
            jax.ShapeDtypeStruct((seq, width), F32),
            jax.ShapeDtypeStruct((seq, width), BF16),
            jax.ShapeDtypeStruct((seq, 3 * width), BF16),
        ]
        + [jax.ShapeDtypeStruct((n * w.shape[0], w.shape[1]), w.dtype) for w in first]
        + [jax.ShapeDtypeStruct((width, 2 * cut), BF16), jax.ShapeDtypeStruct((n * down.shape[0], width), BF16)],
        in_specs=[smem, smem, whole, pl.BlockSpec((3, block), lambda i: (0, i)), whole, whole]
        + [anywhere] * (2 + len(first)),
        out_specs=[
            columns, columns,
            pl.BlockSpec((QUAD, seq, 3 * LANE), lambda i: (i, 0, 0)),
            whole, whole, whole,
        ]
        + [anywhere] * (3 + len(first)),
        scratch_shapes=[
            pltpu.VMEM((CQ, seq, 3 * LANE), BF16),
            pltpu.VMEM((3 * LANE * CQ, 3 * LANE), BF16),
            pltpu.VMEM((QUAD, seq, HEAD_DIM), BF16),
            pltpu.VMEM((QUAD, seq, HEAD_DIM), BF16),
            pltpu.VMEM((QUAD, seq, HEAD_DIM), BF16),
            pltpu.VMEM((CQ, seq, HEAD_DIM), BF16),
            pltpu.VMEM((QUAD, seq, HEAD_DIM), F32),
            pltpu.VMEM((3 * quads, seq, block), BF16),
            pltpu.VMEM((2, width, block), BF16),
            pltpu.VMEM((quads, seq, block), BF16),
            pltpu.VMEM((width, width), BF16),
            dma((2,)), dma((3 * quads,)), dma,
        ]
        + Gather.scratch(len(first), n)
        + Gather.scratch(3, n),
        compiler_params=pltpu.CompilerParams(
            collective_id=collective, has_side_effects=True, vmem_limit_bytes=60 * 1024 * 1024
        ),
    )(
        docs, head_mixing, pad_taps(conv_kernel), gains, layer_input, gains,
        *first, inner, down,
    )
    return results[:7], results[7 : 7 + len(first)], results[7 + len(first) :]


def backward_kernel(
    n, specs, done_specs, docs_ref, mix_ref, taps_ref, gain_ref, q_ref, k_ref, v_ref, attended_ref, d_grouped_ref, soft_ref, *refs
):
    count, done = len(specs), len(done_specs)
    grads, done_sums, refs = refs[:count], refs[count : count + done], refs[count + done :]
    d_projected, grad_gain_ref, grad_taps_ref, grad_mix_ref = refs[:4]
    sums, others, refs = refs[4 : 4 + count], refs[4 + count : 4 + 2 * count], refs[4 + 2 * count :]
    done_totals, refs = refs[:done], refs[done:]
    final_size = len(FinalSum.scratch(done_specs))
    masks, band, qs, ks, vs, ds, shifted, d_heads, d_rows, d_cols, near_keys, leaving, leave_sem = refs[:13]
    reduce = Reduce(Ring(n), grads, sums, others, specs, refs[13 + final_size :])
    final = FinalSum(reduce.ring, done_sums, done_totals, done_specs, refs[13 : 13 + final_size])
    seq = q_ref.shape[0]
    quad = pl.program_id(0)

    @pl.when(quad == 0)
    def _():
        reduce.clear()
        reduce.ring.meet()
        reduce.hand_over()

    @pl.when(quad == 0)
    def _():
        fill_masks(docs_ref, masks, seq)

    gains = []
    for h in range(QUAD):
        at = slice(h * HEAD_DIM, (h + 1) * HEAD_DIM)
        qs[h] = q_ref[:, at]
        ks[h] = k_ref[:, at]
        vs[h] = v_ref[:, at]
        attended = attended_ref[:, at]
        d_grouped = d_grouped_ref[:, at]
        centred = attended - jnp.mean(attended, axis=1, keepdims=True)
        var = jnp.mean(centred * centred, axis=1, keepdims=True)
        scale = lax.rsqrt(var + EPSILON)
        unit = centred * scale
        gains.append(jnp.sum(d_grouped * unit, axis=0, keepdims=True))
        w = d_grouped * gain_ref[1:2, at]
        d_attended = scale * (
            w
            - jnp.mean(w, axis=1, keepdims=True)
            - unit * jnp.mean(w * unit, axis=1, keepdims=True)
        )
        ds[h] = d_attended.astype(BF16)
    grad_gain_ref[...] = jnp.concatenate(gains, axis=1)
    grad_taps_ref[...] = jnp.zeros_like(grad_taps_ref)
    grad_mix_ref[...] = jnp.zeros_like(grad_mix_ref)

    @pl.when(quad == 0)
    def _():
        for step in reduce.opening()[1:]:
            step()

    @pl.when(quad == 1)
    def _():
        for i in range(done):
            final.start(i)

    sets = row_sets(seq)
    up = lax.broadcasted_iota(jnp.int32, (LANE, LANE), 0)
    across = lax.broadcasted_iota(jnp.int32, (LANE, LANE), 1)
    flip = jnp.where(up + across == LANE - 1, 1.0, 0.0).astype(BF16)
    gap = up + across - (LANE - 1)
    keeps = {0: jnp.abs(gap) <= CK // 2, 1: gap <= CK // 2 - LANE, -1: gap >= LANE - CK // 2}

    def pair(p, carry):
        group = quad * 2 + p
        mix = [[mix_ref[group, r, s] for s in range(2)] for r in range(2)]
        upstream_t = [ds[2 * p + r].T for r in range(2)]
        grad_mix = [[jnp.zeros((1, 1), F32) for _ in range(2)] for _ in range(2)]
        for r in range(2):
            d_cols[r] = jnp.zeros_like(d_cols[r])
        for r0, width, c0 in sets:
            rows = slice(r0, r0 + LANE)
            soft = [soft_ref[2 * p + s, rows, :width].astype(F32) for s in range(2)]
            d_prob, sums = [], []
            for r in range(2):
                dp = nt(ds[2 * p + r, rows], vs[2 * p + r, c0 : c0 + width])
                d_prob.append(dp)
                sums.append([jnp.sum(dp * soft[s], axis=1, keepdims=True) for s in range(2)])
                for s in range(2):
                    grad_mix[r][s] += jnp.sum(sums[r][s], axis=0, keepdims=True)
                mixed = (mix[r][0] * soft[0] + mix[r][1] * soft[1]).astype(BF16)
                d_cols[r, :, c0 : c0 + width] += nn(upstream_t[r][:, r0 : r0 + LANE], mixed)
            for s in range(2):
                d_soft = mix[0][s] * d_prob[0] + mix[1][s] * d_prob[1]
                inner = mix[0][s] * sums[0][s] + mix[1][s] * sums[1][s]
                d_conv = soft[s] * (d_soft - inner)
                d_rows[s, rows, :width] = d_conv.astype(BF16)
        lane = lax.broadcasted_iota(jnp.int32, (1, LANE), 1)
        line = jnp.zeros((1, LANE), F32)
        for r in range(2):
            for s in range(2):
                line = line + jnp.where(lane == 2 * r + s, grad_mix[r][s], 0.0)
        grad_mix_ref[0, pl.ds(p, 1), :] = line
        for r in range(2):
            d_heads[2, 2 * p + r] = d_cols[r].T

        for r in range(2):
            h = 2 * p + r
            fill_backward_band(taps_ref, quad * QUAD + h, band)
            for a, moved in enumerate(shifted_rows(qs[h])):
                shifted[a] = moved
            keys = ks[h]
            d_cols[0] = jnp.zeros_like(d_cols[0])
            d_query = []
            below = jnp.zeros((8, LANE * CQ), F32)
            above = jnp.zeros((8, LANE * CQ), F32)
            mirrored = []
            for r0, width, c0 in sets:
                rows = slice(r0, r0 + LANE)
                left, parts = masked_scores(shifted, keys, masks, r0, width, c0)
                d_conv = d_rows[r, rows, :width]
                blocks = width // LANE
                flipped = [
                    nt(flip, d_conv[:, b * LANE : (b + 1) * LANE]).astype(BF16) for b in range(blocks)
                ]
                start = len(mirrored) * LANE
                mirrored += flipped
                for b in range(blocks):
                    near_keys[start + b * LANE : start + (b + 1) * LANE, :] = jnp.concatenate(
                        [parts[a][:, b * LANE : (b + 1) * LANE] for a in range(CQ)], axis=1
                    )
                if blocks > 1:
                    end = start + blocks * LANE
                    below = below + nn(
                        jnp.concatenate([f[:8] for f in flipped[:-1]], axis=1), near_keys[start + LANE : end, :]
                    )
                    above = above + nn(
                        jnp.concatenate([f[LANE - 8 :] for f in flipped[1:]], axis=1), near_keys[start : end - LANE, :]
                    )
                spread = []
                for b in range(blocks):
                    low, high = max(b - 1, 0), min(b + 1, blocks - 1)
                    spread.append(
                        nn(
                            d_conv[:, low * LANE : (high + 1) * LANE],
                            band[(low - b + 1) * LANE : (high - b + 2) * LANE, :],
                        ).astype(BF16)
                    )
                stacked = jnp.concatenate(
                    [
                        jnp.concatenate(
                            [
                                spread[b][:, a * LANE : (a + 1) * LANE]
                                for b in range(blocks)
                            ],
                            axis=1,
                        )
                        * masks[a, rows, :width]
                        for a in range(CQ)
                    ],
                    axis=0,
                )
                d_query.append(nn(stacked, keys[c0 : c0 + width]))
                d_cols[0, :, c0 : c0 + width] += nn(left.T, stacked)
            total = None
            for a in range(CQ):
                whole = jnp.concatenate([d[a * LANE : (a + 1) * LANE] for d in d_query], axis=0)
                if a:
                    whole = pltpu.roll(whole, seq - a, axis=0)
                total = whole if total is None else total + whole
            d_heads[0, h] = total
            d_heads[1, h] = d_cols[0].T
            band_sum = nn(jnp.concatenate(mirrored, axis=1), near_keys[: len(mirrored) * LANE, :])
            for a in range(CQ):
                at = slice(a * LANE, (a + 1) * LANE)
                whole = jnp.where(keeps[0], band_sum[:, at], 0.0)
                whole = jnp.concatenate(
                    [
                        whole[:8] + jnp.where(keeps[1][:8], below[:, at], 0.0),
                        whole[8 : LANE - 8],
                        whole[LANE - 8 :] + jnp.where(keeps[-1][LANE - 8 :], above[:, at], 0.0),
                    ],
                    axis=0,
                )
                aligned = pltpu.roll(whole, 0, axis=1, stride=1, stride_axis=0)
                grad_taps_ref[h, a : a + 1, :] = jnp.sum(aligned, axis=0, keepdims=True)
            work = reduce.each()
            middle = len(work) // 2
            for j in in_turn(group, HEADS // 2, n):
                pl.when(j < n)(functools.partial(reduce.item, j, work[middle:] if r else work[:middle]))
        return carry

    lax.fori_loop(0, 2, pair, 0)
    quads = HEADS // QUAD
    block = QUAD * HEAD_DIM

    def leave(part):
        there = d_projected.at[:, cols((part * quads + quad) * block, block)]
        return pltpu.make_async_copy(leaving.at[part], there, leave_sem.at[part])

    for part in range(3):
        pl.when(quad > 0)(leave(part).wait)
        leaving[part] = jnp.concatenate([d_heads[part, h] for h in range(QUAD)], axis=1).astype(BF16)
        leave(part).start()

    @pl.when(quad == quads - 1)
    def _():
        for part in range(3):
            leave(part).wait()
        for i in range(done):
            final.add(i)

    @pl.when(quad == pl.num_programs(0) - 1)
    def _():
        reduce.finish()
        final.finish()


def attend_backward(projected, conv_kernel, head_mixing, docs, gains, attended, d_grouped, soft, grads, done_sums, done_specs, n, collective):
    seq = projected.shape[0]
    width = projected.shape[1] // 3
    block = QUAD * HEAD_DIM
    quads = HEADS // QUAD
    count = len(grads)
    specs = Reduce.specs_of(grads, n, (THIRD, THIRD))
    anywhere = pl.BlockSpec(memory_space=pl.ANY)
    whole = pl.BlockSpec(memory_space=pltpu.VMEM)
    smem = pl.BlockSpec(memory_space=pltpu.SMEM)

    def columns(first):
        return pl.BlockSpec((seq, block), lambda i: (0, first * quads + i))

    results = pl.pallas_call(
        functools.partial(backward_kernel, n, specs, done_specs),
        grid=(quads,),
        out_shape=[
            jax.ShapeDtypeStruct((seq, 3 * width), BF16),
            jax.ShapeDtypeStruct((1, width), F32),
            jax.ShapeDtypeStruct((HEADS, 8, LANE), F32),
            jax.ShapeDtypeStruct((quads, 8, LANE), F32),
        ]
        + Reduce.results(specs, n)
        + [jax.ShapeDtypeStruct(spec[:2], BF16) for spec in done_specs],
        in_specs=[
            smem, smem, whole,
            pl.BlockSpec((3, block), lambda i: (0, i)),
            columns(0), columns(1), columns(2), columns(0), columns(0),
            pl.BlockSpec((QUAD, seq, 3 * LANE), lambda i: (i, 0, 0)),
        ]
        + [anywhere] * (count + len(done_specs)),
        out_specs=[
            anywhere,
            pl.BlockSpec((1, block), lambda i: (0, i)),
            pl.BlockSpec((QUAD, 8, LANE), lambda i: (i, 0, 0)),
            pl.BlockSpec((1, 8, LANE), lambda i: (i, 0, 0)),
        ]
        + [anywhere] * (2 * count + len(done_specs)),
        scratch_shapes=[
            pltpu.VMEM((CQ, seq, 3 * LANE), BF16),
            pltpu.VMEM((3 * LANE, LANE * CQ), BF16),
            pltpu.VMEM((QUAD, seq, HEAD_DIM), BF16),
            pltpu.VMEM((QUAD, seq, HEAD_DIM), BF16),
            pltpu.VMEM((QUAD, seq, HEAD_DIM), BF16),
            pltpu.VMEM((QUAD, seq, HEAD_DIM), BF16),
            pltpu.VMEM((CQ, seq, HEAD_DIM), BF16),
            pltpu.VMEM((3, QUAD, seq, HEAD_DIM), F32),
            pltpu.VMEM((2, seq, 3 * LANE), BF16),
            pltpu.VMEM((2, HEAD_DIM, seq), F32),
            pltpu.VMEM((sum(w for _, w, _ in row_sets(seq)), LANE * CQ), BF16),
            pltpu.VMEM((3, seq, block), BF16),
            pltpu.SemaphoreType.DMA((3,)),
        ]
        + FinalSum.scratch(done_specs)
        + Reduce.scratch(specs, n),
        compiler_params=pltpu.CompilerParams(
            collective_id=collective, has_side_effects=True, vmem_limit_bytes=62 * 1024 * 1024
        ),
    )(
        docs, head_mixing, pad_taps(conv_kernel[:, :, ::-1]), gains,
        projected, projected, projected, attended, d_grouped, soft, *grads, *done_sums,
    )
    d_projected, grad_gain, grad_taps, grad_mix = results[:4]
    return (
        d_projected, grad_gain, grad_taps, grad_mix,
    ), list(results[4 : 4 + count]), specs, results[4 + 2 * count :]


MESH = pl.DeviceIdType.MESH


def ring_index(place, n):
    place = lax.rem(place + 2 * n, n)
    return jnp.where(place < n // 2, 2 * place, 2 * (n - 1 - place) + 1)


def ring_place(index, n):
    half = lax.div(index, 2)
    return jnp.where(lax.rem(index, 2) == 0, half, n - 1 - half)


class Ring:
    def __init__(self, n):
        self.n = n
        rep = lax.axis_index("rep")
        self.x, self.core = lax.div(rep, 2), lax.rem(rep, 2)
        index = lax.axis_index("fsdp")
        self.index = index
        self.place = ring_place(index, n)
        self.right = (rep, ring_index(self.place + 1, n))
        self.left = (rep, ring_index(self.place - 1, n))
        self.sibling = (self.x * 2 + 1 - self.core, index)
        self.across = ((1 - self.x) * 2 + self.core, index)

    def meet(self):
        barrier = pltpu.get_barrier_semaphore()
        for other in (self.right, self.left, self.sibling, self.across):
            pl.semaphore_signal(barrier, inc=1, device_id=other, device_id_type=MESH)
        pl.semaphore_wait(barrier, 4)


def send(src, dst, send_sem, recv_sem, device):
    return pltpu.make_async_remote_copy(
        src_ref=src, dst_ref=dst, send_sem=send_sem, recv_sem=recv_sem,
        device_id=device, device_id_type=MESH,
    )


def cols(start, size):
    return pl.ds(pl.multiple_of(start, LANE), size)


class Gather:
    def __init__(self, ring, weights, fulls, widths, sems):
        self.ring, self.weights, self.fulls = ring, weights, fulls
        self.axes, self.widths = zip(*widths)
        (self.own, self.ring_send, self.ring_recv, self.core_send, self.core_recv, self.x_send, self.x_recv) = sems

    def windows(self, i):
        ring = self.ring
        half = self.weights[i].shape[self.axes[i]] // 2
        w = self.widths[i]
        base = ring.core * half
        part = half - 2 * w
        first = base + jnp.where(ring.x == 0, 0, half - w)
        second = base + jnp.where(ring.x == 0, w, half - 2 * w)
        give = base + jnp.where(ring.x == 0, 0, half - part)
        take = base + jnp.where(ring.x == 0, half - part, 0)
        return w, part, first, second, give, take

    def block(self, i, index, start, width):
        rows = self.weights[i].shape[0]
        if self.axes[i] == 0:
            return self.fulls[i].at[pl.ds(pl.multiple_of(index * rows + start, 16), width), :]
        return self.fulls[i].at[pl.ds(pl.multiple_of(index * rows, 16), rows), cols(start, width)]

    def piece(self, i, start, width):
        if self.axes[i] == 0:
            return self.weights[i].at[pl.ds(pl.multiple_of(start, 16), width), :]
        return self.weights[i].at[:, cols(start, width)]

    def ring_copy(self, i, d, k, source):
        ring = self.ring
        w, _, first, second, _, _ = self.windows(i)
        start = second if d else first
        index = ring_index(ring.place + (k if d else -k), ring.n)
        there = self.block(i, index, start, w)
        src = self.piece(i, start, w) if source else there
        return send(src, there, self.ring_send.at[i, d, k], self.ring_recv.at[i, d, k], ring.left if d else ring.right)

    def core_copy(self, i, d, k):
        ring = self.ring
        w, part, first, second, _, take = self.windows(i)
        start, width = ((first, w), (second, w), (take, part))[d]
        index = ring_index(ring.place + (k + 1 if d == 1 else -k - 1), ring.n)
        there = self.block(i, index, start, width)
        return send(there, there, self.core_send.at[i, d, k], self.core_recv.at[i, d, k], ring.sibling)

    def x_copy(self, i, k):
        ring = self.ring
        _, part, _, _, give, _ = self.windows(i)
        there = self.block(i, ring_index(ring.place - k - 1, ring.n), give, part)
        return send(there, there, self.x_send.at[i, k], self.x_recv.at[i, k], ring.across)

    def own_copy(self, i):
        rows = self.weights[i].shape[0]
        there = self.fulls[i].at[pl.ds(pl.multiple_of(self.ring.index * rows, 16), rows), :]
        return send(self.weights[i], there, self.own.at[0, i], self.own.at[1, i], self.ring.sibling)

    def has_part(self, i):
        return self.weights[i].shape[self.axes[i]] // 2 > 2 * self.widths[i]

    def start(self):
        for i in range(len(self.weights)):
            for d in range(2):
                self.ring_copy(i, d, 0, True).start()
        for i in range(len(self.weights)):
            self.own_copy(i).start()

    def step(self, k):
        last = self.ring.n - 2
        for i in range(len(self.weights)):
            for d in range(2):
                self.ring_copy(i, d, k, False).wait_recv()

                @pl.when(k < last)
                def _():
                    self.ring_copy(i, d, k + 1, False).start()

                if d == 0 and self.has_part(i):
                    self.x_copy(i, k).start()
                self.core_copy(i, d, k).start()

            if self.has_part(i):
                @pl.when(k >= LAG)
                def _():
                    self.pass_on(i, k - LAG)

    def pass_on(self, i, k):
        self.x_copy(i, k).wait_recv()
        self.core_copy(i, 2, k).start()

    def finish(self):
        last = self.ring.n - 2
        for k in range(max(0, last + 1 - LAG), last + 1):
            for i in range(len(self.weights)):
                if self.has_part(i):
                    self.pass_on(i, k)

        def settle(k, carry):
            for i in range(len(self.weights)):
                for d in range(2):
                    self.ring_copy(i, d, k, False).wait_send()
                    self.core_copy(i, d, k).wait()
                if self.has_part(i):
                    self.x_copy(i, k).wait_send()
                    self.core_copy(i, 2, k).wait()
            return carry

        lax.fori_loop(0, self.ring.n - 1, settle, 0)
        for i in range(len(self.weights)):
            self.own_copy(i).wait()

    @staticmethod
    def scratch(count, n):
        dma = pltpu.SemaphoreType.DMA
        return [
            dma((2, count)), dma((count, 2, n - 1)), dma((count, 2, n - 1)),
            dma((count, 3, n - 1)), dma((count, 3, n - 1)), dma((count, n - 1)), dma((count, n - 1)),
        ]


def share(shape):
    rows, columns = shape
    axis, unit = (0, 16) if rows % 64 == 0 else (1, LANE)
    units = (rows, columns)[axis] // 2 // unit
    return axis, -(-units // 3) * unit


THIRD = (1, 3)
LESS = (7, 18)
HALF = (1, 2)
LAST_PORTIONS = (LESS, THIRD)


def carried(columns, portion):
    half = columns // 2
    lanes = -(-(half // LANE) * portion[0] // portion[1]) * LANE
    if 2 * lanes >= half:
        return half // 2, 0
    return lanes, half - 2 * lanes


class Reduce:
    def __init__(self, ring, grads, sums, others, specs, scratch):
        self.ring, self.grads, self.sums, self.others, self.specs = ring, grads, sums, others, specs
        count = len(grads)
        self.slots, self.mine, self.twin, self.x_slots, self.x_out = [], [], [], [], []
        scratch = list(scratch)
        for spec in specs:
            part = carried(spec[1], spec[2])[1]
            take = [scratch.pop(0) for _ in range(10 if part else 6)]
            self.slots.append(take[:2])
            self.mine.append(take[2:4] + take[6:7])
            self.twin.append(take[4:6] + take[7:8])
            self.x_slots.append(take[8] if part else None)
            self.x_out.append(take[9] if part else None)
        (self.load, self.ring_send, self.ring_recv, self.core_send, self.core_recv,
         self.x_send, self.x_recv, self.keep) = scratch

    def owner(self, kind, j):
        ring = self.ring
        return ring_index(ring.place + (j + 1 if kind == 1 else -j - 1), ring.n)

    def span(self, i, kind):
        columns, shared = self.specs[i][1:]
        w, part = carried(columns, shared)
        half = columns // 2
        lower, upper = ((0, half - w), (w, half - 2 * w), (half - part, 0))[kind]
        return jnp.where(self.ring.x == 0, lower, upper), part if kind == 2 else w

    def rows(self, i, index):
        rows = self.specs[i][0]
        return pl.ds(pl.multiple_of(index * rows, 16), rows)

    def kinds(self, i):
        return 3 if self.x_slots[i] is not None else 2

    def core_copy(self, i, kind, j):
        ring = self.ring
        start, width = self.span(i, kind)
        rows = self.rows(i, self.owner(kind, j))
        half = self.specs[i][1] // 2
        return send(
            self.grads[i].at[rows, cols((1 - ring.core) * half + start, width)], self.others[i].at[rows, cols(start, width)],
            self.core_send.at[i, kind, j], self.core_recv.at[i, kind, j], ring.sibling,
        )

    def loads(self, i, kind, j):
        start, width = self.span(i, kind)
        rows = self.rows(i, self.owner(kind, j))
        base = self.ring.core * (self.specs[i][1] // 2)
        return (
            pltpu.make_async_copy(
                self.grads[i].at[rows, cols(base + start, width)], self.mine[i][kind], self.load.at[i, kind, 0]
            ),
            pltpu.make_async_copy(self.others[i].at[rows, cols(start, width)], self.twin[i][kind], self.load.at[i, kind, 1]),
        )

    def fetch(self, i, kind, j):
        own, other = self.loads(i, kind, j)
        own.start()
        self.core_copy(i, kind, j).wait_recv()
        other.start()

    def ring_copy(self, i, d, j):
        ring = self.ring
        return send(
            self.slots[i][d].at[j], self.slots[i][d].at[j + 1],
            self.ring_send.at[i, d, j], self.ring_recv.at[i, d, j + 1], ring.left if d else ring.right,
        )

    def gap(self, i):
        w, part = carried(*self.specs[i][1:])
        x = self.ring.x
        return w - part, jnp.where(x == 0, part, 0), jnp.where(x == 0, w - part, 0), part

    def x_copy(self, i, j):
        _, _, at, part = self.gap(i)
        return send(
            self.x_out[i].at[lax.rem(j, 2)], self.x_slots[i].at[j, :, cols(at, part)],
            self.x_send.at[i, j], self.x_recv.at[i, j], self.ring.across,
        )

    def give(self, i, j):
        j = jnp.int32(j)
        for copy in self.loads(i, 2, j):
            copy.wait()

        @pl.when(j >= 2)
        def _():
            self.x_copy(i, j - 2).wait_send()

        self.x_out[i][lax.rem(j, 2)] = (self.mine[i][2][...].astype(F32) + self.twin[i][2][...].astype(F32)).astype(BF16)
        self.x_copy(i, j).start()
        self.hand_next(i, 2, j)

        @pl.when(j < self.ring.n - 1)
        def _():
            self.fetch(i, 2, j + 1)

    def each(self):
        return [(i, d) for i in range(len(self.grads)) for d in (1, 0)]

    def clear(self):
        for i in range(len(self.grads)):
            if self.kinds(i) == 3:
                width, at, _, _ = self.gap(i)
                if width:
                    rows = self.specs[i][0]
                    self.x_slots[i][:, :, cols(at, width)] = jnp.zeros((self.ring.n, rows, width), BF16)

    def all(self):
        return range(len(self.grads))

    def hand_over(self, which=None):
        for j in range(min(LEAD, self.ring.n)):
            for i in which or self.all():
                for kind in reversed(range(self.kinds(i))):
                    self.core_copy(i, kind, j).start()

    def hand_next(self, i, kind, j):
        pl.when(j + LEAD < self.ring.n)(lambda: self.core_copy(i, kind, j + LEAD).start())

    def fetch_first(self, which=None):
        for i in which or self.all():
            for kind in reversed(range(self.kinds(i))):
                self.fetch(i, kind, 0)

    def give_all(self, j, which=None):
        for i in which or self.all():
            if self.kinds(i) == 3:
                self.give(i, j)

    def opening(self, which=None):
        return [
            functools.partial(self.hand_over, which), functools.partial(self.fetch_first, which),
            functools.partial(self.give_all, 0, which), functools.partial(self.give_all, 1, which),
        ]

    def start(self):
        for step in self.opening():
            step()

    def item(self, j, work):
        last = self.ring.n - 1
        for i, d in work:
            for copy in self.loads(i, d, j):
                copy.wait()
            slot = self.slots[i][d]
            both = self.mine[i][d][...].astype(F32) + self.twin[i][d][...].astype(F32)
            if d == 0 and self.kinds(i) == 3:
                self.x_copy(i, j).wait_recv()
                both = both + self.x_slots[i][j].astype(F32)

            @pl.when(j == 0)
            def _():
                slot[j] = both.astype(BF16)

            @pl.when(j > 0)
            def _():
                self.ring_copy(i, d, j - 1).wait_recv()
                slot[j] = (slot[j].astype(F32) + both).astype(BF16)

            @pl.when(j < last)
            def _():
                self.ring_copy(i, d, j).start()
                self.fetch(i, d, j + 1)

            self.hand_next(i, d, j)
            if d == 0 and self.kinds(i) == 3:
                pl.when(j < last - 1)(functools.partial(self.give, i, j + 2))

            @pl.when(j == last)
            def _():
                self.keep_copy(i, d).start()

    def keep_copy(self, i, d):
        w = carried(*self.specs[i][1:])[0]
        at = jnp.where(self.ring.x == 0, d * w, (1 - d) * w)
        return pltpu.make_async_copy(self.slots[i][d].at[self.ring.n - 1], self.sums[i].at[:, cols(at, w)], self.keep.at[i, d])

    def finish(self):
        last = self.ring.n - 1
        for i, d in self.each():
            self.keep_copy(i, d).wait()

        def settle(j, carry):
            for i in range(len(self.grads)):
                for kind in range(self.kinds(i)):
                    self.core_copy(i, kind, j).wait_send()
                for d in range(2):
                    pl.when(j < last)(lambda i=i, d=d: self.ring_copy(i, d, j).wait_send())
                if self.kinds(i) == 3:
                    pl.when(j >= last - 1)(lambda i=i: self.x_copy(i, j).wait_send())
            return carry

        lax.fori_loop(0, self.ring.n, settle, 0)

    @staticmethod
    def specs_of(grads, n, portions):
        return [(g.shape[0] // n, g.shape[1], portion) for g, portion in zip(grads, portions)]

    @staticmethod
    def results(specs, n):
        return [
            jax.ShapeDtypeStruct((rows, 2 * carried(columns, shared)[0]), BF16) for rows, columns, shared in specs
        ] + [jax.ShapeDtypeStruct((n * rows, columns // 2), BF16) for rows, columns, _ in specs]

    @staticmethod
    def scratch(specs, n):
        dma = pltpu.SemaphoreType.DMA
        count = len(specs)
        buffers = []
        for rows, columns, shared in specs:
            w, part = carried(columns, shared)
            buffers += [pltpu.VMEM((n, rows, w), BF16)] * 2 + [pltpu.VMEM((rows, w), BF16)] * 4
            if part:
                buffers += [pltpu.VMEM((rows, part), BF16)] * 2
                buffers += [pltpu.VMEM((n, rows, w), BF16), pltpu.VMEM((2, rows, part), BF16)]
        return buffers + [
            dma((count, 3, 2)), dma((count, 2, n)), dma((count, 2, n)), dma((count, 3, n)), dma((count, 3, n)),
            dma((count, n)), dma((count, n)), dma((count, 2)),
        ]


class FinalSum:
    def __init__(self, ring, sums, totals, specs, scratch):
        self.ring, self.sums, self.totals, self.specs = ring, sums, totals, specs
        scratch = list(scratch)
        self.mine, self.plane, self.own = [], [], []
        for spec in specs:
            self.mine.append(scratch.pop(0))
            self.plane.append(scratch.pop(0))
            self.own.append(scratch.pop(0) if carried(spec[1], spec[2])[1] else None)
        self.local, self.remote_send, self.remote_recv = scratch

    def spans(self, i):
        columns, shared = self.specs[i][1:]
        w, part = carried(columns, shared)
        half, wide = columns // 2, 2 * w - part
        base = self.ring.core * half
        low = self.ring.x == 0
        return (
            (jnp.where(low, part, 0), base + part, wide),
            (jnp.where(low, 0, wide), base + jnp.where(low, 0, half - part), part),
            (0, base + jnp.where(low, half - part, 0), part),
        )

    def remote(self, i, at, src, dst, device):
        return send(src, dst, self.remote_send.at[i, at], self.remote_recv.at[i, at], device)

    def copy(self, i, name):
        ring, sums, totals = self.ring, self.sums[i], self.totals[i]
        (a, a_out, wide), (b, b_out, part), (_, c_out, _) = self.spans(i)
        local = {"load": 0, "save": 1, "load done": 2, "save done": 3}
        remote = {"across": 0, "sibling": 1, "done across": 2, "done sibling": 3, "pass on": 4}
        if name in ("load", "save", "across", "sibling"):
            src, dst, mid = sums.at[:, cols(a, wide)], totals.at[:, cols(a_out, wide)], self.mine[i]
        elif name == "pass on":
            src = dst = mid = totals.at[:, cols(c_out, part)]
        else:
            src, dst, mid = sums.at[:, cols(b, part)], totals.at[:, cols(b_out, part)], self.own[i]
        if name in local:
            ends = (src, mid) if name.startswith("load") else (mid, dst)
            return pltpu.make_async_copy(*ends, self.local.at[i, local[name]])
        ends = {"across": (src, self.plane[i]), "sibling": (mid, dst)}.get(name, (src, dst))
        device = ring.across if "across" in name else ring.sibling
        at = remote[name]
        return send(*ends, self.remote_send.at[i, at], self.remote_recv.at[i, at], device)

    def shares(self, i):
        return carried(*self.specs[i][1:])[1] > 0

    def start(self, i):
        for name in ("across", "load"):
            self.copy(i, name).start()
        if self.shares(i):
            for name in ("done across", "load done", "done sibling"):
                self.copy(i, name).start()

    def add(self, i):
        self.copy(i, "load").wait()
        self.copy(i, "across").wait_recv()
        self.mine[i][...] = (self.mine[i][...].astype(F32) + self.plane[i][...].astype(F32)).astype(BF16)
        self.copy(i, "sibling").start()
        self.copy(i, "save").start()
        if self.shares(i):
            self.copy(i, "load done").wait()
            self.copy(i, "save done").start()
            self.copy(i, "done across").wait_recv()
            self.copy(i, "pass on").start()

    def finish(self):
        for i in range(len(self.specs)):
            self.copy(i, "across").wait_send()
            self.copy(i, "sibling").wait()
            self.copy(i, "save").wait()
            if self.shares(i):
                self.copy(i, "done across").wait_send()
                for name in ("done sibling", "save done", "pass on"):
                    self.copy(i, name).wait()

    @staticmethod
    def scratch(specs):
        dma = pltpu.SemaphoreType.DMA
        count = len(specs)
        buffers = []
        for rows, columns, shared in specs:
            w, part = carried(columns, shared)
            buffers += [pltpu.VMEM((rows, 2 * w - part), BF16)] * 2
            if part:
                buffers += [pltpu.VMEM((rows, part), BF16)]
        return buffers + [dma((count, 4)), dma((count, 5)), dma((count, 5))]


class SmallSum:
    def __init__(self, ring, given, total, scratch):
        self.ring, self.given, self.total = ring, given, total
        self.mine, self.twin, self.plane, self.slots, self.pair, self.ring_send, self.ring_recv = scratch

    def copy(self, src, dst, at, device):
        return send(src, dst, self.pair.at[0, at], self.pair.at[1, at], device)

    def to_core(self):
        return self.copy(self.given, self.twin, 0, self.ring.sibling)

    def to_plane(self):
        return self.copy(self.mine, self.plane, 1, self.ring.across)

    def add_core(self):
        self.to_core().wait()
        self.mine[...] = self.given[...] + self.twin[...]
        self.to_plane().start()

    def add_plane(self):
        self.to_plane().wait()
        self.slots[0] = self.mine[...] + self.plane[...]

    def ring_copy(self, j):
        return send(
            self.slots.at[j], self.slots.at[j + 1], self.ring_send.at[j], self.ring_recv.at[j + 1], self.ring.right
        )

    def item(self, j):
        @pl.when(j > 0)
        def _():
            self.ring_copy(j - 1).wait_recv()

        @pl.when(j < self.ring.n - 1)
        def _():
            self.ring_copy(j).start()

    def finish(self):
        ring = self.ring
        total = jnp.zeros(self.total.shape, F32)
        for place in range(ring.n):
            total = total + self.slots[lax.rem(ring.place - place + ring.n, ring.n)]
        self.total[...] = total

        def settle(j, carry):
            self.ring_copy(j).wait_send()
            return carry

        lax.fori_loop(0, ring.n - 1, settle, 0)

    @staticmethod
    def scratch(rows, n):
        dma = pltpu.SemaphoreType.DMA
        block = pltpu.VMEM((rows, LANE), F32)
        return [block, block, block, pltpu.VMEM((n, rows, LANE), F32), dma((2, 2)), dma((n,)), dma((n,))]


SMALL_SCRATCH = 7


def pack(given, at, row):
    for r in range(row.shape[1] // LANE):
        given[at + r : at + r + 1, :] = row[:, r * LANE : (r + 1) * LANE]
    return at + row.shape[1] // LANE


SPOTS = 8


def pack_taps(given, at, taps_ref, mix_ref):
    rows = taps_ref.shape[1]
    for first in range(0, HEADS, SPOTS):
        together = taps_ref[first]
        for h in range(1, SPOTS):
            together = together + pltpu.roll(taps_ref[first + h], h * (LANE // SPOTS), axis=1)
        given[at : at + rows, :] = together
        at += rows
    together = mix_ref[0]
    for quad in range(1, mix_ref.shape[0]):
        together = together + pltpu.roll(mix_ref[quad], 2 * quad, axis=0)
    given[at : at + rows, :] = together


def unpack_taps(summed):
    rows = 8
    taps = jnp.roll(summed[: HEADS // SPOTS * rows], CK // 2 + 1, axis=1).reshape(-1, rows, SPOTS, LANE // SPOTS)
    taps = taps.transpose(0, 2, 1, 3).reshape(HEADS, rows, LANE // SPOTS)[:, :CQ, :CK]
    mixing = summed[HEADS // SPOTS * rows :][: HEADS // 2, :4]
    return taps[:, :, ::-1] * SCALE, mixing.reshape(HEADS // 2, 2, 2)


def last_kernel(n, specs, early_specs, chunk, small_count, *refs):
    count, early = len(specs), len(early_specs)
    ring = Ring(n)
    refs = list(refs)

    def take(size):
        taken = refs[:size]
        del refs[:size]
        return taken

    small_refs = take(small_count)
    input_ref, normed_ref, gain_ref, d_middle_ref, d_projected, weight = take(6)
    grads, early_sums = take(count - 1), take(early)
    grad_input_ref, total_ref, grad_qkv = take(3)
    totals, early_totals, sums, others = take(count), take(early), take(count), take(count)
    given, d_normed, in_left, in_right, turned, leaving, in_sem, leave_sem = take(8)
    small = SmallSum(ring, given, total_ref, take(SMALL_SCRATCH))
    last_sum = FinalSum(ring, sums, totals, specs, take(len(FinalSum.scratch(specs))))
    early_sum = FinalSum(ring, early_sums, early_totals, early_specs, take(len(FinalSum.scratch(early_specs))))
    reduce = Reduce(ring, [grad_qkv] + grads, sums, others, specs, refs)
    chunks = d_projected.shape[1] // chunk

    def arrive(t, slot):
        at = cols(t * chunk, chunk)
        return (
            pltpu.make_async_copy(d_projected.at[:, at], in_left.at[slot], in_sem.at[slot, 0]),
            pltpu.make_async_copy(weight.at[:, at], in_right.at[slot], in_sem.at[slot, 1]),
        )

    def leave(t):
        slot = lax.rem(t, 2)
        return pltpu.make_async_copy(leaving.at[slot], grad_qkv.at[:, cols(t * chunk, chunk)], leave_sem.at[slot])

    def turn(t, carry):
        slot = lax.rem(t, 2)
        for copy in arrive(t, slot):
            copy.wait()

        @pl.when(t < chunks - 1)
        def _():
            for copy in arrive(t + 1, 1 - slot):
                copy.start()

        pl.when(t >= 2)(lambda: leave(t - 2).wait())
        leaving[slot] = nn(turned[...], in_left[slot]).astype(BF16)
        leave(t).start()
        d_normed[...] += nt(in_left[slot], in_right[slot])
        return carry

    ahead = 3
    qkv, others_at = [0], list(range(1, count))
    behind = [(i, d) for i, d in reduce.each() if i > 0]

    for copy in arrive(0, 0):
        copy.start()
    reduce.clear()
    ring.meet()
    reduce.hand_over(others_at)
    d_normed[...] = jnp.zeros_like(d_normed)
    given[...] = jnp.zeros_like(given)
    turned[...] = normed_ref[...].T
    for step in reduce.opening(others_at)[1:]:
        step()
    for j in range(ahead):
        lax.fori_loop(j * chunks // ahead, (j + 1) * chunks // ahead, turn, 0)
        reduce.item(jnp.int32(j), behind)
    for t in (chunks - 2, chunks - 1):
        leave(jnp.int32(t)).wait()
    reduce.hand_over(qkv)
    values = input_ref[...].astype(F32)
    scale = lax.rsqrt(jnp.mean(values * values, axis=1, keepdims=True) + EPSILON)
    upstream = d_normed[...]
    grad_gain = jnp.sum(upstream * (values * scale), axis=0, keepdims=True)
    at = 0
    for row in [grad_gain] + [ref[...] for ref in small_refs[:2]]:
        at = pack(given, at, row)
    pack_taps(given, at, small_refs[2], small_refs[3])
    small.to_core().start()
    for step in reduce.opening(qkv)[1:]:
        step()

    def items(j):
        reduce.item(j, [(0, 1), (0, 0)])
        pl.when(j + ahead < n)(lambda: reduce.item(j + ahead, behind))

    items(jnp.int32(0))
    small.add_core()
    scaled = upstream * gain_ref[0:1, :]
    inner = jnp.mean(scaled * values, axis=1, keepdims=True)
    grad_input_ref[...] = d_middle_ref[...] + scale * scaled - values * (scale * scale * scale * inner)
    items(jnp.int32(1))
    small.add_plane()
    hops = -(-n // (n - 3))

    def rest(j, carry):
        for hop in range(hops):
            at = (j - 2) * hops + hop
            pl.when(at < n)(functools.partial(small.item, at))
        for i in range(early):
            pl.when(j == 2 + i)(functools.partial(early_sum.start, i))
        items(j)
        for i in range(early):
            pl.when(j == n - early + i)(functools.partial(early_sum.add, i))
        return carry

    lax.fori_loop(2, n, rest, 0)
    reduce.finish()
    for i in range(count):
        last_sum.start(i)
    small.finish()
    for i in range(count):
        last_sum.add(i)
    early_sum.finish()
    last_sum.finish()


def last_step(
    d_projected, qkv_weight, layer_input, normed, gains, d_middle, grads, smalls, early_sums, early_specs, n, collective
):
    count, early = 1 + len(grads), len(early_specs)
    seq, width = layer_input.shape
    chunk = 512
    grad_qkv = jax.ShapeDtypeStruct((width, d_projected.shape[1]), BF16)
    specs = Reduce.specs_of([grad_qkv] + grads, n, LAST_PORTIONS)
    sizes = [width // LANE] * 3 + [(HEADS // SPOTS + 1) * 8]
    rows = -(-sum(sizes) // 8) * 8
    anywhere = pl.BlockSpec(memory_space=pl.ANY)
    whole = pl.BlockSpec(memory_space=pltpu.VMEM)
    results = pl.pallas_call(
        functools.partial(last_kernel, n, specs, early_specs, chunk, len(smalls)),
        out_shape=[jax.ShapeDtypeStruct((seq, width), F32), jax.ShapeDtypeStruct((rows, LANE), F32), grad_qkv]
        + [jax.ShapeDtypeStruct(spec[:2], BF16) for spec in specs + early_specs]
        + Reduce.results(specs, n),
        in_specs=[whole] * (len(smalls) + 4) + [anywhere] * (1 + count + early),
        out_specs=[whole] * 2 + [anywhere] * (1 + 3 * count + early),
        scratch_shapes=[
            pltpu.VMEM((rows, LANE), F32),
            pltpu.VMEM((seq, width), F32),
            pltpu.VMEM((2, seq, chunk), BF16),
            pltpu.VMEM((2, width, chunk), BF16),
            pltpu.VMEM((width, seq), BF16),
            pltpu.VMEM((2, width, chunk), BF16),
            pltpu.SemaphoreType.DMA((2, 2)),
            pltpu.SemaphoreType.DMA((2,)),
        ]
        + SmallSum.scratch(rows, n)
        + FinalSum.scratch(specs)
        + FinalSum.scratch(early_specs)
        + Reduce.scratch(specs, n),
        compiler_params=pltpu.CompilerParams(
            collective_id=collective, has_side_effects=True, vmem_limit_bytes=60 * 1024 * 1024
        ),
    )(*smalls, layer_input, normed, gains, d_middle, d_projected, qkv_weight, *grads, *early_sums)
    out, at = [], 0
    for size in sizes:
        out.append(results[1][at : at + size])
        at += size
    return results[0], results[3 : 3 + count + early], out


TILES = 8
EARLY_TILES = 3
POINTS = 4
LATE_TILES = 3


def mlp_kernel(n, specs, tile, *refs):
    refs = list(refs)

    def take(size):
        taken = refs[:size]
        del refs[:size]
        return taken

    second_ref, upstream_ref, gain_ref, middle, out_weight, inner, down, coming = take(8)
    out_ref, d_middle_ref, d_grouped_ref, grad_gain_ref = take(4)
    (early, late, grad_down), sums, others, (came,) = take(3), take(1), take(1), take(1)
    turned, out_sum, d_second_ref, in_gate, in_up, in_down, to_gate, to_up, to_down = take(9)
    middle_sem, in_sem, to_sem, out_sem = take(4)
    ring = Ring(n)
    hidden_size = down.shape[0]
    cut = hidden_size - LATE_TILES * tile
    size = hidden_size - cut
    pieces = [coming.at[:, cut:hidden_size], coming.at[:, hidden_size + cut :]]
    gather = Gather(
        ring, pieces, [came.at[:, :size], came.at[:, size:]], [share((coming.shape[0], size))] * 2,
        take(len(Gather.scratch(2, n))),
    )
    reduce = Reduce(ring, [early], sums, others, specs, refs)
    tiles = hidden_size // tile
    begun = EARLY_TILES
    each = -(-n // (tiles - begun - 1))
    due = -(-each // 2)

    split = tiles - LATE_TILES

    def arrive(t, slot, weight, first, count):
        at = pl.multiple_of((t - first) * tile, tile)
        return (
            pltpu.make_async_copy(weight.at[:, pl.ds(at, tile)], in_gate.at[slot], in_sem.at[slot, 0]),
            pltpu.make_async_copy(
                weight.at[:, pl.ds(pl.multiple_of(count * tile + at, tile), tile)], in_up.at[slot], in_sem.at[slot, 1]
            ),
            pltpu.make_async_copy(
                down.at[pl.ds(pl.multiple_of(t * tile, tile), tile), :], in_down.at[slot], in_sem.at[slot, 2]
            ),
        )

    def arrivals(t, act):
        slot = lax.rem(t, 2)

        @pl.when(t < split)
        def _():
            for copy in arrive(t, slot, inner, 0, split):
                act(copy)

        @pl.when((t >= split) & (t < tiles))
        def _():
            for copy in arrive(t, slot, came, split, LATE_TILES):
                act(copy)

    def leave(grad, t, slot, first, count):
        at = pl.multiple_of((t - first) * tile, tile)
        return (
            pltpu.make_async_copy(to_gate.at[slot], grad.at[:, pl.ds(at, tile)], to_sem.at[slot, 0]),
            pltpu.make_async_copy(
                to_up.at[slot], grad.at[:, pl.ds(pl.multiple_of(count * tile + at, tile), tile)], to_sem.at[slot, 1]
            ),
            pltpu.make_async_copy(
                to_down.at[slot], grad_down.at[pl.ds(pl.multiple_of(t * tile, tile), tile), :], to_sem.at[slot, 2]
            ),
        )

    def leave_early(t):
        return leave(early, t, lax.rem(t, 2), 0, begun)

    def leave_late(t):
        return leave(late, t, lax.rem(t, 2), begun, tiles - begun)

    first = pltpu.make_async_copy(middle, out_sum, middle_sem.at[0])
    again = pltpu.make_async_copy(middle, d_middle_ref, middle_sem.at[1])
    first.start()
    again.start()
    arrivals(jnp.int32(0), lambda copy: copy.start())
    reduce.clear()
    ring.meet()
    gather.start()
    turned[...] = second_ref[...].T
    d_second_ref[...] = jnp.zeros_like(d_second_ref)
    first.wait()

    def serve(t, point):
        ends = (split - 1) * POINTS + 1
        turns = 7
        for turn in range(turns):
            at = 2 + turn * (ends - 3) // (turns - 1)
            if at % POINTS == point:
                for k in in_turn(turn, turns, n - 1):
                    if k < n - 1:
                        pl.when(t == at // POINTS)(functools.partial(gather.step, jnp.int32(k)))
        if ends % POINTS == point:
            pl.when(t == ends // POINTS)(gather.finish)

        @pl.when(t == begun)
        def _():
            if point == 0:
                for back in (2, 1):
                    for copy in leave_early(t - back):
                        copy.wait()
            reduce.opening()[point]()

        for step in range(due):
            if point // 2 * due + step < each:
                j = (t - begun - 1) * each + point // 2 * due + step
                pl.when((t > begun) & (j < n))(functools.partial(reduce.item, j, [(0, 1 - point % 2)]))

    def one(t, carry):
        slot = lax.rem(t, 2)
        arrivals(t, lambda copy: copy.wait())
        second, upstream = second_ref[...], upstream_ref[...]
        gate = nn(second, in_gate[slot])
        up = nn(second, in_up[slot])
        sigmoid = jax.nn.sigmoid(gate)
        silu = gate * sigmoid
        hidden = (silu * up).astype(BF16)
        serve(t, 0)
        d_hidden = nt(upstream, in_down[slot])
        out_sum[...] += nn(hidden, in_down[slot])

        @pl.when((t >= 2) & (t < begun))
        def _():
            for copy in leave_early(t - 2):
                copy.wait()

        @pl.when(t >= begun + 2)
        def _():
            for copy in leave_late(t - 2):
                copy.wait()

        to_down[slot] = nn(hidden.T, upstream).astype(BF16)
        d_gate = (d_hidden * up * sigmoid * (1.0 + gate * (1.0 - sigmoid))).astype(BF16)
        d_up = (d_hidden * silu).astype(BF16)
        serve(t, 1)
        d_second_ref[...] += nt(d_gate, in_gate[slot])
        to_gate[slot] = nn(turned[...], d_gate).astype(BF16)
        serve(t, 2)
        arrivals(t + 1, lambda copy: copy.start())
        d_second_ref[...] += nt(d_up, in_up[slot])
        to_up[slot] = nn(turned[...], d_up).astype(BF16)
        serve(t, 3)

        @pl.when(t < begun)
        def _():
            for copy in leave_early(t):
                copy.start()

        @pl.when(t >= begun)
        def _():
            for copy in leave_late(t):
                copy.start()

        return carry

    def out_piece(c):
        into = (in_gate.at[0], in_up.at[0], in_gate.at[1])[c]
        return pltpu.make_async_copy(out_weight.at[:, c * tile : (c + 1) * tile], into, out_sem.at[c])

    lax.fori_loop(0, tiles, one, 0)
    pieces = out_weight.shape[1] // tile
    for c in range(pieces):
        out_piece(c).start()
    out_ref[...] = out_sum[...].astype(BF16)
    again.wait()
    values = d_middle_ref[...]
    scale = lax.rsqrt(jnp.mean(values * values, axis=1, keepdims=True) + EPSILON)
    d_second = d_second_ref[...]
    grad_gain_ref[...] = jnp.sum(d_second * (values * scale), axis=0, keepdims=True)
    scaled = d_second * gain_ref[2:3, :]
    mean = jnp.mean(scaled * values, axis=1, keepdims=True)
    d_middle_ref[...] = (
        upstream_ref[...].astype(F32) + scale * scaled - values * (scale * scale * scale * mean)
    )
    for c in range(pieces):
        out_piece(c).wait()
        part = nt(
            d_middle_ref[:, c * tile : (c + 1) * tile].astype(BF16), (in_gate.at[0], in_up.at[0], in_gate.at[1])[c][...]
        )
        if c == 0:
            d_grouped_ref[...] = part
        else:
            d_grouped_ref[...] += part
    for t in (tiles - 2, tiles - 1):
        for copy in leave_late(t):
            copy.wait()
    reduce.finish()


def feed_forward(second, upstream, gains, middle, out_weight, inner, down, coming, n, collective):
    seq, width = second.shape
    hidden_size = down.shape[0]
    tile = hidden_size // TILES
    early = EARLY_TILES * tile
    specs = [(width // n, 2 * early, THIRD)]
    whole = pl.BlockSpec(memory_space=pltpu.VMEM)
    anywhere = pl.BlockSpec(memory_space=pl.ANY)
    dma = pltpu.SemaphoreType.DMA
    results = pl.pallas_call(
        functools.partial(mlp_kernel, n, specs, tile),
        out_shape=[
            jax.ShapeDtypeStruct((seq, width), BF16),
            jax.ShapeDtypeStruct((seq, width), F32),
            jax.ShapeDtypeStruct((seq, width), F32),
            jax.ShapeDtypeStruct((1, width), F32),
        ]
        + [
            jax.ShapeDtypeStruct((width, 2 * early), BF16),
            jax.ShapeDtypeStruct((width, 2 * (hidden_size - early)), BF16),
            jax.ShapeDtypeStruct((hidden_size, width), BF16),
        ]
        + Reduce.results(specs, n)
        + [jax.ShapeDtypeStruct((width, 2 * LATE_TILES * tile), BF16)],
        in_specs=[whole] * 3 + [anywhere] * 5,
        out_specs=[whole] * 4 + [anywhere] * 6,
        scratch_shapes=[
            pltpu.VMEM((width, seq), BF16),
            pltpu.VMEM((seq, width), F32),
            pltpu.VMEM((seq, width), F32),
            pltpu.VMEM((2, width, tile), BF16),
            pltpu.VMEM((2, width, tile), BF16),
            pltpu.VMEM((2, tile, width), BF16),
            pltpu.VMEM((2, width, tile), BF16),
            pltpu.VMEM((2, width, tile), BF16),
            pltpu.VMEM((2, tile, width), BF16),
            dma((2,)), dma((2, 3)), dma((2, 3)), dma((3,)),
        ]
        + Gather.scratch(2, n)
        + Reduce.scratch(specs, n),
        compiler_params=pltpu.CompilerParams(
            collective_id=collective, has_side_effects=True, vmem_limit_bytes=62 * 1024 * 1024
        ),
    )(second, upstream, gains, middle, out_weight, inner, down, coming)
    out, d_middle, d_grouped, grad_gain, _, late, grad_down, sums, _, _ = results
    return out, d_middle, d_grouped, grad_gain, late, grad_down, [sums], specs


def weight_grad(operand, upstream):
    return lax.dot_general(
        operand, upstream, (((0,), (0,)), ((), ())), preferred_element_type=F32
    ).astype(BF16)


def body(
    layer_input,
    first_gain,
    qkv_weight,
    conv_kernel,
    head_mixing,
    group_gain,
    out_weight,
    second_gain,
    inner_weight,
    down_weight,
    doc_lengths,
    cotangent,
):
    n = lax.axis_size("fsdp")
    gains = jnp.concatenate([first_gain, group_gain, second_gain]).reshape(3, -1)
    kept, (qkv_weight, out_weight), (inner_first, down_full) = attend_forward(
        layer_input, conv_kernel, head_mixing, doc_lengths, gains, [qkv_weight, out_weight], inner_weight, down_weight, n, 0,
    )
    grouped, attended, soft, normed, middle, second, projected = kept
    layer_output, d_middle, d_grouped, grad_second, late_inner, grad_down, early_sums, early_specs = feed_forward(
        second, cotangent, gains, middle, out_weight, inner_first, down_full, inner_weight, n, 2
    )
    (d_projected, grad_group, grad_kernel, grad_mixing), sums, specs, (early_inner,) = attend_backward(
        projected, conv_kernel, head_mixing, doc_lengths, gains, attended, d_grouped, soft,
        [late_inner, grad_down], early_sums, early_specs, n, 3,
    )
    grad_proj = weight_grad(grouped, d_middle.astype(BF16))
    grad_input, shards, small = last_step(
        d_projected, qkv_weight, layer_input, normed, gains, d_middle, [grad_proj],
        [grad_group, grad_second, grad_kernel, grad_mixing], sums, specs, n, 4,
    )
    grad_first, grad_group, grad_second = [g.reshape(-1) for g in small[:3]]
    grad_kernel, grad_mixing = unpack_taps(small[3])
    grad_qkv, grad_proj, late_inner, grad_down = shards
    cut, late_cut = early_inner.shape[1] // 2, late_inner.shape[1] // 2
    grad_inner = jnp.concatenate(
        [early_inner[:, :cut], late_inner[:, :late_cut], early_inner[:, cut:], late_inner[:, late_cut:]], axis=1
    )
    shards = [g.astype(F32) for g in (grad_qkv, grad_proj, grad_inner, grad_down)]
    return (
        layer_output, grad_input, grad_first, shards[0], grad_kernel, grad_mixing, grad_group, shards[1], grad_second,
        shards[2], shards[3],
    )


def solution(mesh):
    placed = (
        P(("rep", "fsdp"), None),
        P(),
        P("fsdp", None),
        P(),
        P(),
        P(),
        P("fsdp", None),
        P(),
        P("fsdp", None),
        P("fsdp", None),
        P(("rep", "fsdp"), None),
        P(("rep", "fsdp"), None),
    )
    return jax.shard_map(
        body,
        mesh=mesh,
        in_specs=placed,
        out_specs=(
            P(("rep", "fsdp"), None),
            P(("rep", "fsdp"), None),
            P(),
            P("fsdp", None),
            P(),
            P(),
            P(),
            P("fsdp", None),
            P(),
            P("fsdp", None),
            P("fsdp", None),
        ),
        check_vma=False,
    )
```
